32 devices in a mesh: row: 16 (over z, y, core), col: 2 (over x).
Axes of the slice: x: 2, y: 2, z: 4, core: 2. Of those that a mesh axis runs over, the one named last changes fastest.
Arguments:
- inputs: bfloat16 [8192, 2048], P('row', 'col'), may hold values from -32 to 32, as said below
- segment_ids: int32 [16, 512], P('row'), may hold values from 0 to 3, never falling along the last dimension, each value on 1 to 256 neighbouring positions
- routes: int32 [8192, 6], P('row'), may hold values from 0 to 63, all different within a row; in each aligned block of 512 rows (0 to 511, 512 to 1023, ...) at most 64 rows name the same one
- norm_gain: float32 [2048], P('col'), may hold values from 0.5 to 1.5
- query_weight: bfloat16 [2048, 3072], P('row', 'col'), may hold values from -0.125 to 0.125
- latent_weight: bfloat16 [2048, 576], P('row'), may hold values from -0.125 to 0.125
- latent_gain: float32 [512], replicated, may hold values from 0.5 to 1.5
- expand_weight: bfloat16 [512, 4096], P('row', 'col'), may hold values from -0.25 to 0.25
- output_weight: bfloat16 [2048, 2048], P('col', 'row'), may hold values from -0.75 to 0.75
- ffn_gain: float32 [2048], P('col'), may hold values from 0.5 to 1.5
- router_weight: bfloat16 [2048, 64], P('row'), may hold values from -0.0625 to 0.0625
- expert_gate: bfloat16 [64, 1408, 2048], P('row', 'col'), may hold values from -0.125 to 0.125
- expert_up: bfloat16 [64, 1408, 2048], P('row', 'col'), may hold values from -0.125 to 0.125
- expert_down: bfloat16 [64, 1408, 2048], P('row', 'col'), may hold values from -6 to 6
- shared_gate: bfloat16 [2048, 2816], P('row', 'col'), may hold values from -0.125 to 0.125
- shared_up: bfloat16 [2048, 2816], P('row', 'col'), may hold values from -0.125 to 0.125
- shared_down: bfloat16 [2816, 2048], P('col', 'row'), may hold values from -0.109375 to 0.109375
- out_grad: bfloat16 [8192, 2048], P('row', 'col'), may hold values from -6 to 6
Outputs:
- output: bfloat16 [8192, 2048], P('row', 'col')
- input_grad: float32 [8192, 2048], P('row', 'col')
- norm_gain_grad: float32 [2048], P('col')
- query_weight_grad: float32 [2048, 3072], P('row', 'col')
- latent_weight_grad: float32 [2048, 576], P('row')
- latent_gain_grad: float32 [512], replicated
- expand_weight_grad: float32 [512, 4096], P('row', 'col')
- output_weight_grad: float32 [2048, 2048], P('col', 'row')
- ffn_gain_grad: float32 [2048], P('col')
- router_weight_grad: float32 [2048, 64], P('row')
- expert_gate_grad: float32 [64, 1408, 2048], P('row', 'col')
- expert_up_grad: float32 [64, 1408, 2048], P('row', 'col')
- expert_down_grad: float32 [64, 1408, 2048], P('row', 'col')
- shared_gate_grad: float32 [2048, 2816], P('row', 'col')
- shared_up_grad: float32 [2048, 2816], P('row', 'col')
- shared_down_grad: float32 [2816, 2048], P('col', 'row')
The draws below stay inside these ranges and needn't reach their ends.
Inputs may be any that keep to these rules, and one draw needn't show every extreme that they name: `inputs`: A scale that varies by token times a scale that varies by feature times a bounded random factor. `segment_ids`: ids never fall along a sequence; every document has at most half of 512 tokens, one exactly that many. `routes`: A token's 6 experts differ. In each aligned block of 512 rows (the rows of one device) no expert is named by more than 64 rows, a bound that some block reaches.
All inputs are finite; a program needn't handle non-finite values.
Results may differ from the reference program's by a relative error of at most 0.03.
Values may be sent and summed in bfloat16 or wider, within the bound.
No kernel may reach another device: no remote copies, remote signals or barrier semaphores. Data moves between devices by JAX's collectives and lax.ppermute only.
A program may use at most 448 MiB of HBM per device.

```python
import math
import jax
import jax.numpy as jnp
import numpy as np
from jax import lax

D = 2048
HEADS = 16
NOPE = 128
ROPE = 64
RANK = 512
VDIM = 128
FE = 1408
FS = 2816
TOPK = 6
TOK_DEV = 512
DOCS = 4
EXPERTS = 64
SEQS = 16
TOKENS = 8192
CAP = 64


def draw_inputs(key, part):
    key = jax.random.fold_in(key, 11)
    first, second, third = jax.random.split(key, 3)
    base = jax.random.truncated_normal(first, -4.0, 4.0, (TOKENS, D), jnp.float32)
    row_low, row_high = (0.4, 4.0)
    rows = jnp.exp(jax.random.uniform(second, (TOKENS, 1), jnp.float32, math.log(row_low), math.log(row_high)))
    columns = jnp.exp(jax.random.uniform(third, (1, D), jnp.float32, math.log(0.6), math.log(2.0)))
    return (base * rows * columns).astype(jnp.bfloat16)


def block_levels(key, shape, cuts, low, largest):
    level, own = 1.0, jax.random.fold_in(key, 6)
    for position, blocks in cuts:
        heights = jnp.exp(jax.random.uniform(jax.random.fold_in(own, position), (blocks,), jnp.float32, low / len(cuts), largest / len(cuts)))
        level = level * jnp.repeat(heights, shape[position] // blocks).reshape([-1 if axis == position else 1 for axis in range(len(shape))])
    return level


def length_profile(number_of, total, reach, slope):
    portions = [(1 << 20) // math.isqrt(rank ** slope) + 1 for rank in range(2, number_of + 1)]
    surplus, holding = total - reach - (number_of - 1), [1] * (number_of - 1)
    while surplus > 0:
        candidates = [i for i in range(number_of - 1) if holding[i] < reach]
        whole, budget = sum([portions[i] for i in candidates]), surplus
        for i in candidates:
            addition = min(reach - holding[i], max(1, budget * portions[i] // whole), surplus)
            holding[i] = holding[i] + addition
            surplus = surplus - addition
    return np.array([reach] + holding)


def uneven_parts(own_key, count, total, reach, lean):
    if count == 2:
        one = jax.random.randint(own_key, (), max(1, total - reach), min(reach, total - 1) + 1)
        return jnp.stack([one, total - one])
    tallies = jnp.asarray(length_profile(count, total, reach, lean), jnp.int32)
    twos = (count - 1) // 2
    giver, receiver = tallies[1:1 + 2 * twos:2], tallies[2:2 + 2 * twos:2]
    margin = jnp.minimum(giver - 1, reach - receiver)
    moved = jax.random.randint(jax.random.fold_in(own_key, 1), (twos,), 0, 1 << 20) % (margin + 1)
    tallies = tallies.at[1:1 + 2 * twos:2].set(giver - moved).at[2:2 + 2 * twos:2].set(receiver + moved)
    return tallies[jax.random.permutation(jax.random.fold_in(own_key, 2), count)]


def routed_block(key, own, number, rows, number_of, top, limit, skew):
    sequence = jax.random.permutation(key, number_of)
    crowded, usual = portions_of(number_of, rows * top, limit, skew, True), portions_of(number_of, rows * top, limit, skew, False)
    places = jnp.arange(number_of)

    def named(tallies, turn):
        used = int((tallies > 0).sum())
        fixed = max(1, used // 4)
        passed = fixed + (places - fixed + turn * (used - fixed)) % max(1, number_of - fixed)
        return jnp.zeros((number_of,), jnp.int32).at[sequence[jnp.where(places < fixed, places, passed)]].set(jnp.asarray(tallies, jnp.int32))

    tallies = jnp.where(number % 4 == 0, named(crowded, number // 4), named(usual, number - number // 4 - 1))
    mixed = jax.random.permutation(jax.random.fold_in(own, 3), number_of)
    giver, sink = mixed[0:number_of // 2 * 2:2], mixed[1:number_of // 2 * 2:2]
    room = jnp.minimum(tallies[giver] - 1, limit - tallies[sink]) // 2
    room = jnp.where((giver == sequence[0]) | (sink == sequence[0]) | (tallies[sink] == 0), 0, jnp.maximum(room, 0))
    passed = jax.random.randint(jax.random.fold_in(own, 4), (number_of // 2,), 0, 1 << 20) % (room + 1)
    tallies = tallies.at[giver].add(-passed).at[sink].add(passed)
    items = jnp.searchsorted(jnp.cumsum(tallies), jnp.arange(rows * top), side="right").astype(jnp.int32)
    grid = items.reshape(top, rows).T
    grid = grid[jax.random.permutation(jax.random.fold_in(own, 1), rows)]
    turn = jax.random.randint(jax.random.fold_in(own, 2), (rows, 1), 0, top)
    return jnp.take_along_axis(grid, (jnp.arange(top)[None, :] + turn) % top, axis=1)


def portions_of(number_of, total, bound, skew, full):
    weights = [(1 << 20) // math.isqrt(rank ** skew) + 1 for rank in range(1, number_of + 1)]
    largest = bound if full else min(bound, max(-(-total // number_of), total * weights[0] // sum(weights)))
    least = 1 if total - largest >= number_of - 1 else 0
    holding, surplus = [largest] + [least] * (number_of - 1), total - largest - least * (number_of - 1)
    while surplus > 0:
        movable = [i for i in range(1, number_of) if holding[i] < largest] or [i for i in range(1, number_of) if holding[i] < bound]
        whole, left = sum([weights[i] for i in movable]), surplus
        for i in movable:
            extra = min(bound - holding[i], max(1, left * weights[i] // whole), surplus)
            holding[i] = holding[i] + extra
            surplus = surplus - extra
    return np.array(holding)


def noise(key, extent, spread, bound, shards=(), kind=jnp.bfloat16):
    values = jax.random.normal(key, extent, jnp.float32) * spread
    if len(shards) > 0:
        values = block_levels(key, extent, shards, -0.22, 0.18) * values
    return jnp.clip(values, min=-bound, max=bound).astype(kind)


def setup_inputs(seed: int = 0) -> dict:
    streams_of = jax.random.split(jax.random.key(seed), 19)
    inputs = draw_inputs(jax.random.fold_in(streams_of[18], 71), 0)
    segment_ids = jax.vmap(lambda own: jnp.searchsorted(jnp.cumsum(uneven_parts(own, DOCS, TOK_DEV, TOK_DEV // 2, 0)), jnp.arange(TOK_DEV), side="right"))(jax.random.split(streams_of[1], SEQS)).reshape((SEQS, TOK_DEV)).astype(jnp.int32)
    routes_keys = jax.random.split(jax.random.fold_in(streams_of[2], 1), TOKENS // TOK_DEV)
    routes_turns = jax.random.permutation(jax.random.fold_in(streams_of[2], 3), TOKENS // TOK_DEV)
    routes = jax.vmap(lambda own, number: routed_block(jax.random.fold_in(streams_of[2], 2), own, number, TOK_DEV, EXPERTS, TOPK, CAP, 1))(routes_keys, routes_turns).reshape((TOKENS, TOPK))
    norm_gain = jnp.clip(1.0 + 0.1 * jax.random.normal(streams_of[3], (D,), jnp.float32), 0.5, 1.5)
    query_weight = noise(streams_of[4], (D, HEADS * (NOPE + ROPE)), D ** -0.5, 0.125, ((0, 16), (1, 2)))
    latent_weight = noise(streams_of[5], (D, RANK + ROPE), D ** -0.5, 0.125, ((0, 16),))
    latent_gain = jnp.clip(1.0 + 0.1 * jax.random.normal(streams_of[6], (RANK,), jnp.float32), 0.5, 1.5)
    expand_weight = noise(streams_of[7], (RANK, HEADS * (NOPE + VDIM)), RANK ** -0.5, 0.25, ((0, 16), (1, 2)))
    output_weight = noise(streams_of[8], (HEADS * VDIM, D), (HEADS * VDIM // 32) ** -0.5, 0.75, ((0, 2), (1, 16)))
    ffn_gain = jnp.clip(1.0 + 0.1 * jax.random.normal(streams_of[9], (D,), jnp.float32), 0.5, 1.5)
    router_weight = noise(streams_of[10], (D, EXPERTS), (0.5 / D ** 0.5), 0.0625, ((0, 16),))
    expert_gate = noise(streams_of[11], (EXPERTS, FE, D), D ** -0.5, 0.125, ((0, 16), (1, 2)))
    expert_up = noise(streams_of[12], (EXPERTS, FE, D), D ** -0.5, 0.125, ((0, 16), (1, 2)))
    expert_down = noise(streams_of[13], (EXPERTS, FE, D), (1.5 * EXPERTS / (TOPK * FE) ** 0.5), 6.0, ((0, 16), (1, 2)))
    shared_gate = noise(streams_of[14], (D, FS), D ** -0.5, 0.125, ((0, 16), (1, 2)))
    shared_up = noise(streams_of[15], (D, FS), D ** -0.5, 0.125, ((0, 16), (1, 2)))
    shared_down = noise(streams_of[16], (FS, D), FS ** -0.5, 0.109375, ((0, 2), (1, 16)))
    out_grad = noise(streams_of[17], (TOKENS, D), 1.0, 6.0, ((0, 16), (1, 2)))
    return {"inputs": inputs, "segment_ids": segment_ids, "routes": routes, "norm_gain": norm_gain, "query_weight": query_weight, "latent_weight": latent_weight, "latent_gain": latent_gain, "expand_weight": expand_weight, "output_weight": output_weight, "ffn_gain": ffn_gain, "router_weight": router_weight, "expert_gate": expert_gate, "expert_up": expert_up, "expert_down": expert_down, "shared_gate": shared_gate, "shared_up": shared_up, "shared_down": shared_down, "out_grad": out_grad}


@jax.custom_vjp
def low(v):
    return lax.optimization_barrier(v.astype(jnp.bfloat16)).astype(jnp.float32)

@jax.custom_vjp
def low_back(v):
    return v

def low_keep(v):
    return (low(v), None)

def low_pass(kept, grad):
    return (grad,)

def back_keep(v):
    return (v, None)

def back_low(kept, grad):
    return (low(grad),)
low.defvjp(low_keep, low_pass)
low_back.defvjp(back_keep, back_low)
epsilon = 1e-06
theta = 10000.0
highest = lax.Precision.HIGHEST

def product(left, right):
    return jnp.dot(left, right, precision=highest)

def unit_scale(values):
    return lax.rsqrt(lax.optimization_barrier(jnp.mean(values * values, axis=-1, keepdims=True)) + epsilon)

def rotation(count):
    half = ROPE // 2
    places = jnp.arange(count, dtype=jnp.float32)
    rates = theta ** (-jnp.arange(half, dtype=jnp.float32) * 2.0 / ROPE)
    angles = places[:, None] * rates[None, :]
    return (jnp.cos(angles), jnp.sin(angles))

def rotate(values, cosine, sine):
    half = ROPE // 2
    first = values[..., :half]
    second = values[..., half:]
    return jnp.concatenate([first * cosine - second * sine, second * cosine + first * sine], axis=-1)

def attend_sequence(query, latent, segment, latent_gain, expand_weight):
    length = query.shape[0]
    cosine, sine = rotation(length)
    compressed = latent[:, :RANK]
    normed = low(compressed * unit_scale(compressed) * latent_gain)
    key_rope = low(rotate(latent[:, RANK:], cosine, sine))
    expanded = low_back(product(normed, expand_weight)).reshape(length, HEADS, NOPE + VDIM)
    key_nope = low(expanded[..., :NOPE])
    values = low(expanded[..., NOPE:])
    query_nope = low(query[..., :NOPE])
    query_rope = low(rotate(query[..., NOPE:], cosine[:, None, :], sine[:, None, :]))
    raw = jnp.einsum('qhd,khd->hqk', query_nope, key_nope, precision=highest)
    raw = low_back(raw + jnp.einsum('qhd,kd->hqk', query_rope, key_rope, precision=highest))
    places = jnp.arange(length, dtype=jnp.int32)
    allowed = (segment[:, None] == segment[None, :]) & (places[None, :] <= places[:, None])
    score_scale = (NOPE + ROPE) ** (-0.5)
    scores = jnp.where(allowed[None], raw * score_scale, -1e+30)
    top = lax.optimization_barrier(jnp.max(scores, axis=-1, keepdims=True))
    weights = jnp.exp(scores - top)
    weights = weights / lax.optimization_barrier(jnp.sum(weights, axis=-1, keepdims=True))
    mixed = jnp.einsum('hqk,khd->qhd', low(weights), values, precision=highest)
    return low_back(low(mixed)).reshape(length, HEADS * VDIM)

def slot_tables(choices, gates):
    flat = choices.reshape(-1)
    hits = (flat[:, None] == jnp.arange(EXPERTS, dtype=jnp.int32)[None, :]).astype(jnp.int32)
    ranks = lax.optimization_barrier(jnp.sum((jnp.cumsum(hits, axis=0) - 1) * hits, axis=1))
    slots = flat * CAP + ranks
    owners = jnp.arange(TOK_DEV * TOPK, dtype=jnp.int32) // TOPK
    slot_token = jnp.full((EXPERTS * CAP,), TOK_DEV, jnp.int32).at[slots].set(owners)
    slot_gate = jnp.zeros((EXPERTS * CAP,), gates.dtype).at[slots].set(gates.reshape(-1))
    return (slot_token.reshape(EXPERTS, CAP), slot_gate.reshape(EXPERTS, CAP))

def route_block(gate_stack, up_stack, down_stack, rows, gates, choices):
    slot_token, slot_gate = slot_tables(choices, gates)
    padded = jnp.concatenate([rows, jnp.zeros((1, D), rows.dtype)], axis=0)

    def one_expert(total, parts):
        token_index, gate_row, gate_matrix, up_matrix, down_matrix = parts
        taken = low_back(padded[token_index])
        gate_pre = low_back(product(taken, gate_matrix.T))
        up_pre = low_back(product(taken, up_matrix.T))
        hidden = low(jax.nn.silu(gate_pre) * up_pre)
        result = low_back(low(product(hidden, down_matrix)))
        return (total.at[token_index].add(gate_row[:, None] * result), None)
    start = jnp.zeros((TOK_DEV + 1, D), rows.dtype)
    total, unused = lax.scan(one_expert, start, (slot_token, slot_gate, gate_stack, up_stack, down_stack))
    return total[:TOK_DEV]

def reference(inputs, segment_ids, routes, norm_gain, query_weight, latent_weight, latent_gain, expand_weight, output_weight, ffn_gain, router_weight, expert_gate, expert_up, expert_down, shared_gate, shared_up, shared_down, out_grad):

    def layer(source, gain_one, query_matrix, latent_matrix, gain_latent, expand_matrix, output_matrix, gain_two, router_matrix, gate_stack, up_stack, down_stack, shared_gate_matrix, shared_up_matrix, shared_down_matrix):
        normed_one = low(source * unit_scale(source) * gain_one)
        query = low_back(product(normed_one, query_matrix))
        latent = low_back(low(product(normed_one, latent_matrix)))

        def attend(items):
            return attend_sequence(items[0], items[1], items[2], gain_latent, expand_matrix)
        mixed = lax.map(jax.checkpoint(attend), (query.reshape(SEQS, TOK_DEV, HEADS, NOPE + ROPE), latent.reshape(SEQS, TOK_DEV, RANK + ROPE), segment_ids))
        mixed = mixed.reshape(TOKENS, HEADS * VDIM)
        middle = source + low_back(product(mixed, output_matrix))
        normed_two = low(middle * unit_scale(middle) * gain_two)
        logits = low_back(product(normed_two, router_matrix))
        gates = jnp.exp(jnp.take_along_axis(logits, routes, axis=1) - jax.nn.logsumexp(logits, axis=1, keepdims=True))

        def route(items):
            return route_block(gate_stack, up_stack, down_stack, items[0], items[1], items[2])
        routed = lax.map(jax.checkpoint(route), (normed_two.reshape(SEQS, TOK_DEV, D), gates.reshape(SEQS, TOK_DEV, TOPK), routes.reshape(SEQS, TOK_DEV, TOPK))).reshape(TOKENS, D)
        shared_hidden = low(jax.nn.silu(low_back(product(normed_two, shared_gate_matrix))) * low_back(product(normed_two, shared_up_matrix)))
        return middle + routed + product(shared_hidden, shared_down_matrix)
    floats = [value.astype(jnp.float32) for value in (inputs, norm_gain, query_weight, latent_weight, latent_gain, expand_weight, output_weight, ffn_gain, router_weight, expert_gate, expert_up, expert_down, shared_gate, shared_up, shared_down)]
    result, pull = jax.vjp(layer, *floats)
    grads = pull(out_grad.astype(jnp.float32))
    return (result.astype(jnp.bfloat16), grads[0], grads[1], grads[2], grads[3], grads[4], grads[5], grads[6], grads[7], grads[8], grads[9], grads[10], grads[11], grads[12], grads[13], grads[14])
```

```python
import jax
import jax.numpy as jnp
from jax import lax
from jax.experimental import pallas as pl
from jax.experimental.pallas import tpu as pltpu
from jax.sharding import PartitionSpec as P

D = 2048
NOPE = 128
ROPE = 64
RANK = 512
VDIM = 128
TOPK = 6
EXP_DEV = 4


epsilon = 1e-06
theta = 10000.0


def rotation(count, width):
    half = width // 2
    places = jnp.arange(count, dtype=jnp.float32)
    rates = theta ** (-jnp.arange(half, dtype=jnp.float32) * 2.0 / width)
    angles = places[:, None] * rates[None, :]
    return (jnp.cos(angles), jnp.sin(angles))


def rotate(values, cosine, sine):
    half = values.shape[-1] // 2
    first = values[..., :half]
    second = values[..., half:]
    return jnp.concatenate(
        [first * cosine - second * sine, second * cosine + first * sine], axis=-1
    )


def unrotate(grads, cosine, sine):
    half = grads.shape[-1] // 2
    first = grads[..., :half]
    second = grads[..., half:]
    return jnp.concatenate(
        [first * cosine + second * sine, second * cosine - first * sine], axis=-1
    )


def silu_slope(pre, sigmoid_value):
    return sigmoid_value * (1.0 + pre * (1.0 - sigmoid_value))


def col_total(values):
    return lax.psum(values, "col")


def spread(values):
    return lax.all_gather(values, "col", axis=1, tiled=True)


def mix_sums(values):
    return lax.psum_scatter(
        values.astype(jnp.bfloat16), "col", scatter_dimension=1, tiled=True
    ).astype(jnp.float32)


def send_rows(rows):
    return lax.all_to_all(rows, "row", split_axis=1, concat_axis=1, tiled=True)


def return_rows(rows):
    return lax.all_to_all(rows, "row", split_axis=1, concat_axis=1, tiled=True)


def rms_scale(rows):
    total = col_total(jnp.sum(rows * rows, axis=1))
    return lax.rsqrt(total / D + epsilon)[:, None]


def norm_backward(grads, unit, scale, gain):
    weighted = grads * gain
    average = col_total(jnp.sum(weighted * unit, axis=1)) / D
    return scale * (weighted - unit * average[:, None])


PLANES = 4
COMMON = 192
UNIQUE = 160
SENT = COMMON + UNIQUE
SHARED_PAD = 128


def swap_cols(values):
    return lax.ppermute(values, "col", [(0, 1), (1, 0)])


def swap_rows(values, bit):
    return lax.ppermute(values, "row", [(i, i ^ bit) for i in range(16)])


def turn_planes(values):
    return lax.ppermute(values, "row", [(i, (i + 4) % 16) for i in range(16)])


def join_cols(values, first):
    other = swap_cols(values)
    return jnp.where(
        first,
        jnp.concatenate([values, other], axis=1),
        jnp.concatenate([other, values], axis=1),
    )


def own_columns(values, first):
    half = values.shape[-1] // 2
    return jnp.where(first, values[..., :half], values[..., half:])


def other_columns(values, first):
    half = values.shape[-1] // 2
    return jnp.where(first, values[..., half:], values[..., :half])


def sent_rows(values, first):
    return jnp.concatenate(
        [values[:COMMON], jnp.where(first, values[COMMON:SENT], values[SENT:])], axis=0
    )


def local_tokens(values, axis, first):
    common = lax.slice_in_dim(values, 0, COMMON, axis=axis)
    one = lax.slice_in_dim(values, COMMON, SENT, axis=axis)
    two = lax.slice_in_dim(values, SENT, SENT + UNIQUE, axis=axis)
    return jnp.concatenate(
        [common, jnp.where(first, one, two), jnp.where(first, two, one)], axis=axis
    )


def spread_rows(rows):
    planes = []
    current = rows
    for plane in range(PLANES):
        if plane > 0:
            current = turn_planes(current)
        across = swap_rows(current, 2)
        held = [
            (current, swap_cols(current[COMMON:])),
            (across, swap_cols(across[COMMON:])),
        ]
        family = []
        for sent, unique in held:
            family.append((sent, unique))
            family.append((swap_rows(sent, 1), swap_rows(unique, 1)))
        planes.append(family)
    return planes


def collect_rows(planes):
    moving = None
    for plane in (1, 2, 3, 0):
        sibling, mine = planes[plane]
        total = mine + swap_rows(sibling, 1)
        unique = swap_cols(total[:, SENT:])
        total = jnp.concatenate([total[:, :COMMON], total[:, COMMON:SENT] + unique], axis=1)
        total = total[0] + swap_rows(total[1], 2)
        if moving is not None:
            total = total + turn_planes(moving)
        moving = total
    return moving


def merge_rows(own, received, first):
    own = own.astype(jnp.float32)
    received = received.astype(jnp.float32)
    common = own[:COMMON] + received[:COMMON]
    mine = own[COMMON:]
    theirs = received[COMMON:]
    return jnp.concatenate(
        [common, jnp.where(first, mine, theirs), jnp.where(first, theirs, mine)], axis=0
    )


FAMILIES = 4
VMEM_BYTES = 60 * 1024 * 1024


def kernel_params(**extra):
    return pltpu.CompilerParams(vmem_limit_bytes=VMEM_BYTES, **extra)


def dot_last(left, right):
    return lax.dot_general(
        left, right, (((1,), (1,)), ((), ())), preferred_element_type=jnp.float32
    )


def dot_first(left, right):
    return lax.dot_general(
        left, right, (((0,), (0,)), ((), ())), preferred_element_type=jnp.float32
    )


def dot_plain(left, right):
    return jnp.dot(left, right, preferred_element_type=jnp.float32)


def slot_matches(codes_ref, capacity):
    tokens = codes_ref.shape[-1]
    ranks = lax.broadcasted_iota(jnp.int32, (capacity, tokens), 0)
    return [codes_ref[0, j : j + 1, :] == ranks for j in range(EXP_DEV)]


def as_picks(matches):
    one = [jnp.where(m, 1.0, 0.0).astype(jnp.bfloat16) for m in matches]
    return jnp.concatenate(one, axis=0)


def start_rows(pieces, held, sems):
    for f in range(FAMILIES):
        pltpu.make_async_copy(pieces[2 * f], held.at[f, pl.ds(0, SENT)], sems.at[f, 0]).start()
        pltpu.make_async_copy(
            pieces[2 * f + 1], held.at[f, pl.ds(SENT, UNIQUE)], sems.at[f, 1]
        ).start()


def wait_rows(pieces, held, sems, f):
    pltpu.make_async_copy(pieces[0], held.at[f, pl.ds(0, SENT)], sems.at[f, 0]).wait()
    pltpu.make_async_copy(pieces[1], held.at[f, pl.ds(SENT, UNIQUE)], sems.at[f, 1]).wait()


def pick_grads(plane, codes, last, capacity):
    pieces = [piece for family in plane for piece in family]
    tokens = SENT + UNIQUE
    width = last.shape[1]
    pad = last.shape[0]

    def body(*refs):
        rows_in = refs[:8]
        codes_ref, last_ref, slots_ref, hidden_ref, held, sems = refs[8:]
        f = pl.program_id(0)

        @pl.when(f == 0)
        def _():
            start_rows(rows_in, held, sems)

        wait_rows(rows_in, held, sems, f)
        rows = held[f]
        picks = as_picks(slot_matches(codes_ref, capacity))
        taken = dot_plain(picks, rows).astype(jnp.bfloat16)
        slots_ref[...] = taken.reshape(EXP_DEV, capacity, width)
        hidden_ref[0] = dot_last(rows, last_ref[...])

    return pl.pallas_call(
        body,
        grid=(FAMILIES,),
        in_specs=[pl.BlockSpec(memory_space=pl.ANY)] * 8
        + [
            pl.BlockSpec((1, 8, tokens), lambda f: (f, 0, 0)),
            pl.BlockSpec((pad, width), lambda f: (0, 0)),
        ],
        out_specs=[
            pl.BlockSpec((EXP_DEV, capacity, width), lambda f: (0, f, 0)),
            pl.BlockSpec((1, tokens, pad), lambda f: (f, 0, 0)),
        ],
        out_shape=[
            jax.ShapeDtypeStruct((EXP_DEV, FAMILIES * capacity, width), jnp.bfloat16),
            jax.ShapeDtypeStruct((FAMILIES, tokens, pad), jnp.float32),
        ],
        scratch_shapes=[
            pltpu.VMEM((FAMILIES, tokens, width), jnp.bfloat16),
            pltpu.SemaphoreType.DMA((FAMILIES, 2)),
        ],
        compiler_params=kernel_params(),
        cost_estimate=pl.CostEstimate(
            flops=FAMILIES * 2 * tokens * width * (EXP_DEV * capacity + 2 * pad),
            bytes_accessed=FAMILIES * tokens * width * 4,
            transcendentals=0,
        ),
    )(*pieces, codes, last)


def pick_rows(plane, grad_plane, codes, router, pair, hidden_grads, capacity):
    pieces = [piece for family in plane for piece in family]
    grad_pieces = [piece for family in grad_plane for piece in family]
    tokens = SENT + UNIQUE
    width = pair.shape[1]
    pad = pair.shape[0] // 2

    def body(*refs):
        rows_in = refs[:8]
        grads_in = refs[8:16]
        (codes_ref, router_ref, pair_ref, hidden_grads_ref) = refs[16:20]
        (slots_ref, gates_ref, hidden_ref, back_ref, grad_ref) = refs[20:25]
        held, held_grads, sems, grad_sems = refs[25:]
        f = pl.program_id(0)

        @pl.when(f == 0)
        def _():
            start_rows(rows_in, held, sems)
            start_rows(grads_in, held_grads, grad_sems)
            grad_ref[...] = jnp.zeros_like(grad_ref)

        wait_rows(rows_in, held, sems, f)
        rows = held[f]
        matches = slot_matches(codes_ref, capacity)
        taken = dot_plain(as_picks(matches), rows).astype(jnp.bfloat16)
        slots_ref[...] = taken.reshape(EXP_DEV, capacity, width)
        logits = dot_last(router_ref[...], rows)
        top = jnp.max(logits, axis=0, keepdims=True)
        total = jnp.log(jnp.sum(jnp.exp(logits - top), axis=0, keepdims=True)) + top
        for j in range(EXP_DEV):
            chance = jnp.exp(logits[j : j + 1] - total)
            gate = jnp.sum(jnp.where(matches[j], chance, 0.0), axis=1, keepdims=True)
            gates_ref[j] = jnp.broadcast_to(gate, (capacity, 128))
        pre = dot_last(rows, pair_ref[...])
        gate_pre = pre[:, :pad]
        up_pre = pre[:, pad:]
        hidden_back = hidden_grads_ref[0]
        sigmoid_value = jax.nn.sigmoid(gate_pre)
        silu_value = gate_pre * sigmoid_value
        hidden = (silu_value * up_pre).astype(jnp.bfloat16)
        slope = sigmoid_value * (1.0 + gate_pre * (1.0 - sigmoid_value))
        gate_back = (hidden_back * up_pre * slope).astype(jnp.bfloat16)
        up_back = (hidden_back * silu_value).astype(jnp.bfloat16)
        back = jnp.concatenate([gate_back, up_back], axis=1)
        hidden_ref[0] = hidden
        back_ref[0] = back
        grad_ref[: 2 * pad] += dot_first(back, rows)
        wait_rows(grads_in, held_grads, grad_sems, f)
        grad_ref[2 * pad :] += dot_first(hidden, held_grads[f])

    return pl.pallas_call(
        body,
        grid=(FAMILIES,),
        in_specs=[pl.BlockSpec(memory_space=pl.ANY)] * 16
        + [
            pl.BlockSpec((1, 8, tokens), lambda f: (f, 0, 0)),
            pl.BlockSpec(router.shape, lambda f: (0, 0)),
            pl.BlockSpec(pair.shape, lambda f: (0, 0)),
            pl.BlockSpec((1, tokens, pad), lambda f: (f, 0, 0)),
        ],
        out_specs=[
            pl.BlockSpec((EXP_DEV, capacity, width), lambda f: (0, f, 0)),
            pl.BlockSpec((EXP_DEV, capacity, 128), lambda f: (0, f, 0)),
            pl.BlockSpec((1, tokens, pad), lambda f: (f, 0, 0)),
            pl.BlockSpec((1, tokens, 2 * pad), lambda f: (f, 0, 0)),
            pl.BlockSpec((3 * pad, width), lambda f: (0, 0)),
        ],
        out_shape=[
            jax.ShapeDtypeStruct((EXP_DEV, FAMILIES * capacity, width), jnp.bfloat16),
            jax.ShapeDtypeStruct((EXP_DEV, FAMILIES * capacity, 128), jnp.float32),
            jax.ShapeDtypeStruct((FAMILIES, tokens, pad), jnp.bfloat16),
            jax.ShapeDtypeStruct((FAMILIES, tokens, 2 * pad), jnp.bfloat16),
            jax.ShapeDtypeStruct((3 * pad, width), jnp.float32),
        ],
        scratch_shapes=[
            pltpu.VMEM((FAMILIES, tokens, width), jnp.bfloat16),
            pltpu.VMEM((FAMILIES, tokens, width), jnp.bfloat16),
            pltpu.SemaphoreType.DMA((FAMILIES, 2)),
            pltpu.SemaphoreType.DMA((FAMILIES, 2)),
        ],
        compiler_params=kernel_params(),
        cost_estimate=pl.CostEstimate(
            flops=FAMILIES * 2 * tokens * width * (EXP_DEV * capacity + 7 * pad),
            bytes_accessed=FAMILIES * tokens * width * 6,
            transcendentals=FAMILIES * tokens * 4 * pad,
        ),
    )(*pieces, *grad_pieces, codes, router, pair, hidden_grads)


def run_experts(slot_rows, slot_grads, gates, expert_gate, expert_up, expert_down):
    count, slots, width = slot_rows.shape
    units = expert_gate.shape[1]

    def body(
        rows_ref,
        grads_ref,
        gates_ref,
        gate_ref,
        up_ref,
        down_ref,
        sum_ref,
        back_ref,
        hidden_ref,
        gate_back_ref,
        up_back_ref,
        gate_grad_ref,
    ):
        rows = rows_ref[0]
        gates_here = gates_ref[0][:, :1]
        gate_pre = dot_last(rows, gate_ref[0])
        up_pre = dot_last(rows, up_ref[0])
        down_back = dot_last(grads_ref[0], down_ref[0])
        sigmoid_value = jax.nn.sigmoid(gate_pre)
        silu_value = gate_pre * sigmoid_value
        hidden = silu_value * up_pre
        gate_grad = jnp.sum(hidden * down_back, axis=1, keepdims=True)
        gate_grad_ref[0] = jnp.broadcast_to(gate_grad, (slots, 128))
        hidden_back = down_back * gates_here
        slope = sigmoid_value * (1.0 + gate_pre * (1.0 - sigmoid_value))
        gate_back = (hidden_back * up_pre * slope).astype(jnp.bfloat16)
        up_back = (hidden_back * silu_value).astype(jnp.bfloat16)
        scaled = (hidden * gates_here).astype(jnp.bfloat16)
        hidden_ref[0] = scaled
        gate_back_ref[0] = gate_back
        up_back_ref[0] = up_back
        back = dot_plain(gate_back, gate_ref[0]) + dot_plain(up_back, up_ref[0])
        back_ref[0] = back.astype(jnp.bfloat16)
        sum_ref[0] = dot_plain(scaled, down_ref[0]).astype(jnp.bfloat16)

    wide = pl.BlockSpec((1, slots, width), lambda j: (j, 0, 0))
    narrow = pl.BlockSpec((1, slots, 128), lambda j: (j, 0, 0))
    inner = pl.BlockSpec((1, slots, units), lambda j: (j, 0, 0))
    matrix = pl.BlockSpec((1, units, width), lambda j: (j, 0, 0))
    return pl.pallas_call(
        body,
        grid=(count,),
        in_specs=[wide, wide, narrow, matrix, matrix, matrix],
        out_specs=[wide, wide, inner, inner, inner, narrow],
        out_shape=[
            jax.ShapeDtypeStruct((count, slots, width), jnp.bfloat16),
            jax.ShapeDtypeStruct((count, slots, width), jnp.bfloat16),
            jax.ShapeDtypeStruct((count, slots, units), jnp.bfloat16),
            jax.ShapeDtypeStruct((count, slots, units), jnp.bfloat16),
            jax.ShapeDtypeStruct((count, slots, units), jnp.bfloat16),
            jax.ShapeDtypeStruct((count, slots, 128), jnp.float32),
        ],
        compiler_params=kernel_params(),
        cost_estimate=pl.CostEstimate(
            flops=12 * count * slots * units * width,
            bytes_accessed=count * width * (6 * units + 8 * slots),
            transcendentals=count * slots * units,
        ),
    )(slot_rows, slot_grads, gates, expert_gate, expert_up, expert_down)


def sum_tokens(values, codes, shared, matrix, gate_grads, capacity):
    tokens = codes.shape[2]
    width = values.shape[2]
    inner = matrix.shape[0]
    with_gates = gate_grads is not None

    def family(i):
        return 2 * (i % 2) + 1 - i // 2

    def body(*refs):
        values_ref, codes_ref, shared_ref, matrix_ref = refs[:4]
        sibling_ref, mine_ref = refs[4 + with_gates : 6 + with_gates]
        i = pl.program_id(0)
        matches = slot_matches(codes_ref, capacity)
        rows = values_ref[...].reshape(EXP_DEV * capacity, width)
        total = dot_first(as_picks(matches), rows)
        total = total + dot_plain(shared_ref[0], matrix_ref[...])
        total = total.astype(jnp.bfloat16)

        @pl.when(i < 2)
        def _():
            sibling_ref[0] = total

        @pl.when(i >= 2)
        def _():
            mine_ref[0] = total

        if with_gates:
            gate_grads_ref, dense_ref = refs[4], refs[7]
            dense = [
                jnp.sum(
                    jnp.where(matches[j], gate_grads_ref[j][:, :1], 0.0), axis=0, keepdims=True
                )
                for j in range(EXP_DEV)
            ]
            dense_ref[0] = jnp.concatenate(dense + [jnp.zeros((4, tokens), jnp.float32)], axis=0)

    in_specs = [
        pl.BlockSpec((EXP_DEV, capacity, width), lambda i: (0, family(i), 0)),
        pl.BlockSpec((1, 8, tokens), lambda i: (family(i), 0, 0)),
        pl.BlockSpec((1, tokens, inner), lambda i: (family(i), 0, 0)),
        pl.BlockSpec((inner, width), lambda i: (0, 0)),
    ]
    out_specs = [
        pl.BlockSpec((1, tokens, width), lambda i: (jnp.minimum(i, 1), 0, 0)),
        pl.BlockSpec((1, tokens, width), lambda i: (jnp.maximum(i - 2, 0), 0, 0)),
    ]
    out_shape = [jax.ShapeDtypeStruct((2, tokens, width), jnp.bfloat16)] * 2
    operands = [values, codes, shared, matrix]
    if with_gates:
        in_specs.append(pl.BlockSpec((EXP_DEV, capacity, 128), lambda i: (0, family(i), 0)))
        out_specs.append(pl.BlockSpec((1, 8, tokens), lambda i: (family(i), 0, 0)))
        out_shape.append(jax.ShapeDtypeStruct((FAMILIES, 8, tokens), jnp.float32))
        operands.append(gate_grads)
    return pl.pallas_call(
        body,
        grid=(FAMILIES,),
        in_specs=in_specs,
        out_specs=out_specs,
        out_shape=out_shape,
        compiler_params=kernel_params(),
        cost_estimate=pl.CostEstimate(
            flops=FAMILIES * 2 * tokens * width * (EXP_DEV * capacity + inner),
            bytes_accessed=FAMILIES * width * (4 * tokens + 2 * EXP_DEV * capacity),
            transcendentals=0,
        ),
    )(*operands)


def expert_weight_grads(rows, grads, gate_backs, up_backs, hiddens):
    count, slots, width = rows[0].shape
    units = hiddens[0].shape[2]
    tile = 512
    planes = len(rows)

    def body(*refs):
        rows_in = refs[:planes]
        grads_in = refs[planes : 2 * planes]
        gate_in = refs[2 * planes : 3 * planes]
        up_in = refs[3 * planes : 4 * planes]
        hidden_in = refs[4 * planes : 5 * planes]
        gate_ref, up_ref, down_ref = refs[5 * planes :]
        for left, right, out in (
            (gate_in, rows_in, gate_ref),
            (up_in, rows_in, up_ref),
            (hidden_in, grads_in, down_ref),
        ):
            total = dot_first(left[0][0], right[0][0])
            for p in range(1, planes):
                total = total + dot_first(left[p][0], right[p][0])
            out[0] = total

    wide = pl.BlockSpec((1, slots, tile), lambda j, d: (j, 0, d))
    inner = pl.BlockSpec((1, slots, units), lambda j, d: (j, 0, 0))
    result = pl.BlockSpec((1, units, tile), lambda j, d: (j, 0, d))
    return pl.pallas_call(
        body,
        grid=(count, width // tile),
        in_specs=[wide] * (2 * planes) + [inner] * (3 * planes),
        out_specs=[result] * 3,
        out_shape=[jax.ShapeDtypeStruct((count, units, width), jnp.float32)] * 3,
        compiler_params=kernel_params(),
        cost_estimate=pl.CostEstimate(
            flops=6 * count * planes * slots * units * width,
            bytes_accessed=count * (12 * units * width + planes * slots * (4 * width + 6 * units)),
            transcendentals=0,
        ),
    )(*rows, *grads, *gate_backs, *up_backs, *hiddens)


def on_device(
    inputs,
    segment_ids,
    routes,
    norm_gain,
    query_weight,
    latent_weight,
    latent_gain,
    expand_weight,
    output_weight,
    ffn_gain,
    router_weight,
    expert_gate,
    expert_up,
    expert_down,
    shared_gate,
    shared_up,
    shared_down,
    out_grad,
):
    bf16 = jnp.bfloat16
    f32 = jnp.float32
    rows_count = inputs.shape[0]
    row_devices = lax.axis_size("row")
    row_place = lax.axis_index("row")
    first = lax.axis_index("col") == 0
    local_heads = query_weight.shape[1] // (NOPE + ROPE)
    expert_count = EXP_DEV * row_devices
    capacity = 4 * rows_count * TOPK // (3 * expert_count)
    score_scale = (NOPE + ROPE) ** (-0.5)
    segment_row = segment_ids[0]
    places = jnp.arange(rows_count, dtype=jnp.int32)

    steps = jnp.arange(row_devices, dtype=jnp.int32)
    arrival = (
        ((row_place // 4 - steps // 4) % 4) * 4 + ((row_place % 4) ^ (steps % 4))
    ).astype(jnp.int32)
    place_of = (((row_place // 4 - steps // 4) % 4) * 4 + ((row_place % 4) ^ (steps % 4))).astype(
        jnp.int32
    )

    query_width = query_weight.shape[1]
    latent_width = latent_weight.shape[1]
    expand_width = expand_weight.shape[1] * expand_weight.shape[0] // latent_weight.shape[0]
    output_width = output_weight.shape[0]
    packed = jnp.concatenate(
        [
            query_weight,
            latent_weight,
            router_weight,
            expand_weight.reshape(latent_weight.shape[0], expand_width),
            output_weight.T,
        ],
        axis=1,
    )
    packed_full = lax.all_gather(packed, "row", axis=0, tiled=True)
    edge = query_width
    query_full = packed_full[:, :edge]
    latent_full = packed_full[:, edge : edge + latent_width]
    edge += latent_width
    router_full = packed_full[:, edge : edge + expert_count]
    edge += expert_count
    expand_full = packed_full[:, edge : edge + expand_width].reshape(RANK, -1)
    edge += expand_width
    output_turned = packed_full[:, edge:]

    shared_share = shared_gate.shape[1] // row_devices
    shared_packed = jnp.stack([shared_gate.T, shared_up.T, shared_down], axis=0)
    shared_packed = shared_packed.reshape(3, row_devices, shared_share, -1).transpose(1, 0, 2, 3)
    shared_here = lax.all_to_all(shared_packed, "row", split_axis=0, concat_axis=0, tiled=True)
    shared_here = shared_here.transpose(1, 2, 0, 3).reshape(3, shared_share, D)
    shared_here = jnp.pad(shared_here, ((0, 0), (0, SHARED_PAD - shared_share), (0, 0)))
    shared_pair = shared_here[:2].reshape(2 * SHARED_PAD, D)
    shared_last = shared_here[2]

    upstream_bf16 = join_cols(out_grad, first)
    upstream = upstream_bf16.astype(f32)
    grad_planes = spread_rows(sent_rows(upstream_bf16, first))

    routes_all = lax.all_gather(routes, "row", axis=0)[arrival]
    routes_all = local_tokens(routes_all, 1, first)
    held_experts = row_place * EXP_DEV + jnp.arange(EXP_DEV, dtype=jnp.int32)
    hits = jnp.any(routes_all[:, :, :, None] == held_experts, axis=2)
    lower = (places[:, None] >= places[None, :]).astype(bf16)
    ranks = jnp.einsum("ut,stj->suj", lower, hits.astype(bf16), preferred_element_type=f32)
    codes = jnp.where(hits, ranks.astype(jnp.int32) - 1, -1)
    codes = jnp.pad(codes.transpose(0, 2, 1), ((0, 0), (0, 8 - EXP_DEV), (0, 0)), constant_values=-1)

    source = join_cols(inputs, first).astype(f32)
    scale_one = lax.rsqrt(jnp.mean(source * source, axis=1, keepdims=True) + epsilon)
    unit_one = source * scale_one
    gain_one = join_cols(norm_gain[None], first)
    gain_two = join_cols(ffn_gain[None], first)
    normed_one = (unit_one * gain_one).astype(bf16)
    query = jnp.dot(normed_one, query_full, preferred_element_type=f32).reshape(
        rows_count, local_heads, NOPE + ROPE
    )
    latent = jnp.dot(normed_one, latent_full, preferred_element_type=f32).astype(bf16)
    cosine, sine = rotation(rows_count, ROPE)
    head_cos = cosine[:, None, :]
    head_sin = sine[:, None, :]
    compressed = latent[:, :RANK].astype(f32)
    latent_scale = lax.rsqrt(jnp.mean(compressed * compressed, axis=1, keepdims=True) + epsilon)
    latent_unit = compressed * latent_scale
    latent_normed = (latent_unit * latent_gain).astype(bf16)
    key_rope = rotate(latent[:, RANK:].astype(f32), cosine, sine).astype(bf16)
    expanded = jnp.dot(latent_normed, expand_full, preferred_element_type=f32).reshape(
        rows_count, local_heads, NOPE + VDIM
    )
    key_nope = expanded[..., :NOPE].astype(bf16)
    values_all = expanded[..., NOPE:].astype(bf16)
    query_nope = query[..., :NOPE].astype(bf16)
    query_rope = rotate(query[..., NOPE:], head_cos, head_sin).astype(bf16)
    raw = jnp.einsum("qhd,khd->hqk", query_nope, key_nope, preferred_element_type=f32)
    raw = raw + jnp.einsum("qhd,kd->hqk", query_rope, key_rope, preferred_element_type=f32)
    allowed = (segment_row[:, None] == segment_row[None, :]) & (places[None, :] <= places[:, None])
    scores = jnp.where(allowed[None], raw * score_scale, -1e30)
    top = jnp.max(scores, axis=2, keepdims=True)
    exponent = jnp.exp(scores - top)
    total = jnp.sum(exponent, axis=2, keepdims=True)
    weights = exponent / total
    log_blocks = top + jnp.log(total)
    mixed = (
        jnp.einsum("hqk,khd->qhd", weights.astype(bf16), values_all, preferred_element_type=f32)
        .astype(bf16)
        .reshape(rows_count, local_heads * VDIM)
    )
    attended_part = jnp.einsum(
        "tv,dv->td", mixed, output_turned, preferred_element_type=f32
    ).astype(bf16)
    attended = attended_part.astype(f32) + swap_cols(attended_part).astype(f32)
    middle = source + attended
    scale_two = lax.rsqrt(jnp.mean(middle * middle, axis=1, keepdims=True) + epsilon)
    unit_two = middle * scale_two
    normed_two = (unit_two * gain_two).astype(bf16)
    row_planes = spread_rows(sent_rows(normed_two, first))

    logits = jnp.dot(normed_two, router_full, preferred_element_type=f32)
    log_total = jax.nn.logsumexp(logits, axis=1, keepdims=True)
    chances = jnp.exp(logits - log_total)

    router_turned = router_full.T
    router_held = lax.dynamic_slice_in_dim(
        jnp.concatenate([router_turned, router_turned], axis=0),
        row_place * EXP_DEV,
        expert_count,
        0,
    )
    sum_planes = [None] * PLANES
    back_planes = [None] * PLANES
    gate_grad_dense = []
    kept_rows, kept_grads, kept_hidden, kept_gate, kept_up = [], [], [], [], []
    shared_grads = 0.0
    for plane in range(PLANES):
        plane_codes = codes[plane * FAMILIES : (plane + 1) * FAMILIES]
        slot_grads, hidden_grads = pick_grads(
            grad_planes[plane], plane_codes, shared_last, capacity
        )
        slot_rows, gate_slots, shared_hidden, shared_back, shared_grad = pick_rows(
            row_planes[plane],
            grad_planes[plane],
            plane_codes,
            router_held,
            shared_pair,
            hidden_grads,
            capacity,
        )
        expert_sum, row_back, scaled_hidden, gate_back, up_back, gate_grad = run_experts(
            slot_rows, slot_grads, gate_slots, expert_gate, expert_up, expert_down
        )
        sibling, mine, dense = sum_tokens(
            row_back, plane_codes, shared_back, shared_pair, gate_grad, capacity
        )
        back_planes[plane] = (sibling, mine)
        sum_planes[plane] = sum_tokens(
            expert_sum, plane_codes, shared_hidden, shared_last, None, capacity
        )
        gate_grad_dense.append(dense[:, :EXP_DEV])
        shared_grads = shared_grads + shared_grad
        kept_rows.append(slot_rows)
        kept_grads.append(slot_grads)
        kept_hidden.append(scaled_hidden)
        kept_gate.append(gate_back)
        kept_up.append(up_back)

    back_sent = collect_rows(back_planes)
    sum_sent = collect_rows(sum_planes)

    gate_grad_dense = jnp.concatenate(gate_grad_dense, axis=0)
    gate_grad_dense = local_tokens(gate_grad_dense, 2, first)[place_of]
    gate_grad_dense = lax.all_to_all(
        gate_grad_dense, "row", split_axis=0, concat_axis=0, tiled=True
    ).reshape(expert_count, rows_count)
    gate_grad_dense = gate_grad_dense + swap_cols(gate_grad_dense)
    weighted_gates = gate_grad_dense.T * chances
    logit_grads = (
        weighted_gates - chances * jnp.sum(weighted_gates, axis=1, keepdims=True)
    ).astype(bf16)
    router_back = jnp.einsum("te,de->td", logit_grads, router_full, preferred_element_type=f32)
    router_grad_part = jnp.einsum("td,te->de", normed_two, logit_grads, preferred_element_type=f32)

    expert_gate_grad, expert_up_grad, expert_down_grad = expert_weight_grads(
        kept_rows, kept_grads, kept_gate, kept_up, kept_hidden
    )
    shared_grads = shared_grads.reshape(3, SHARED_PAD, D)[:, :shared_share]
    shared_grads = (
        shared_grads.astype(bf16)
        .reshape(3, shared_share, row_devices, -1)
        .transpose(2, 0, 1, 3)
    )
    shared_grads = lax.all_to_all(shared_grads, "row", split_axis=0, concat_axis=0, tiled=True)
    shared_grads = shared_grads.transpose(1, 0, 2, 3).reshape(3, row_devices * shared_share, -1)
    shared_grads = shared_grads.astype(f32)
    shared_gate_grad = shared_grads[0].T
    shared_up_grad = shared_grads[1].T
    shared_down_grad = shared_grads[2]

    combined = merge_rows(
        own_columns(sum_sent, first), swap_cols(other_columns(sum_sent, first)), first
    )
    output = (own_columns(middle, first) + combined).astype(bf16)

    normed_two_back = merge_rows(back_sent, swap_cols(back_sent), first) + router_back
    ffn_gain_part = jnp.sum(normed_two_back * unit_two, axis=0)
    weighted = normed_two_back * gain_two
    average = jnp.mean(weighted * unit_two, axis=1, keepdims=True)
    middle_back = upstream + scale_two * (weighted - unit_two * average)
    attended_back = middle_back.astype(bf16)
    mixed_back = (
        jnp.einsum("td,dv->tv", attended_back, output_turned, preferred_element_type=f32)
        .astype(bf16)
        .reshape(rows_count, local_heads, VDIM)
    )
    output_grad_part = jnp.einsum("td,tv->dv", attended_back, mixed, preferred_element_type=f32)

    weights = jnp.exp(scores - log_blocks)
    weight_back = jnp.einsum("qhd,khd->hqk", mixed_back, values_all, preferred_element_type=f32)
    center = jnp.sum(weight_back * weights, axis=2, keepdims=True)
    raw_back = (weights * (weight_back - center) * score_scale).astype(bf16)
    query_nope_back = jnp.einsum("hqk,khd->qhd", raw_back, key_nope, preferred_element_type=f32)
    query_rope_back = jnp.einsum("hqk,kd->qhd", raw_back, key_rope, preferred_element_type=f32)
    key_nope_back = jnp.einsum("hqk,qhd->khd", raw_back, query_nope, preferred_element_type=f32)
    key_rope_back = jnp.einsum("hqk,qhd->kd", raw_back, query_rope, preferred_element_type=f32)
    values_back = jnp.einsum(
        "hqk,qhd->khd", weights.astype(bf16), mixed_back, preferred_element_type=f32
    )
    query_back = jnp.concatenate(
        [query_nope_back, unrotate(query_rope_back, head_cos, head_sin)], axis=2
    )
    query_back = query_back.astype(bf16).reshape(rows_count, local_heads * (NOPE + ROPE))
    expanded_back = (
        jnp.concatenate([key_nope_back, values_back], axis=2)
        .astype(bf16)
        .reshape(rows_count, local_heads * (NOPE + VDIM))
    )
    latent_normed_back = jnp.einsum(
        "tc,rc->tr", expanded_back, expand_full, preferred_element_type=f32
    )
    expand_grad_part = jnp.einsum(
        "tr,tc->rc", latent_normed, expanded_back, preferred_element_type=f32
    )
    latent_gain_part = jnp.sum(latent_normed_back * latent_unit, axis=0)
    latent_weighted = latent_normed_back * latent_gain
    compressed_back = latent_scale * (
        latent_weighted
        - latent_unit * jnp.mean(latent_weighted * latent_unit, axis=1, keepdims=True)
    )
    rope_back = unrotate(key_rope_back, cosine, sine)
    latent_part = jnp.concatenate([compressed_back, rope_back], axis=1).astype(bf16)
    latent_back = (latent_part.astype(f32) + swap_cols(latent_part).astype(f32)).astype(bf16)
    latent_grad_part = jnp.einsum("td,tc->dc", normed_one, latent_back, preferred_element_type=f32)
    query_grad_part = jnp.einsum("td,tc->dc", normed_one, query_back, preferred_element_type=f32)
    input_part = jnp.einsum("tc,dc->td", query_back, query_full, preferred_element_type=f32)
    input_part = input_part.astype(bf16)
    latent_input = jnp.einsum("tc,dc->td", latent_back, latent_full, preferred_element_type=f32)
    weighted_part = jnp.sum(input_part.astype(f32) * gain_one * unit_one, axis=1)
    weighted_sum = weighted_part + swap_cols(weighted_part)
    weighted_sum = weighted_sum + jnp.sum(latent_input * gain_one * unit_one, axis=1)
    normed_one_back = (
        own_columns(input_part, first).astype(f32)
        + swap_cols(other_columns(input_part, first)).astype(f32)
        + own_columns(latent_input, first)
    )
    own_unit = own_columns(unit_one, first)
    norm_gain_part = jnp.sum(normed_one_back * own_unit, axis=0)
    input_grad = own_columns(middle_back, first) + scale_one * (
        normed_one_back * norm_gain - own_unit * (weighted_sum / D)[:, None]
    )
    gains = jnp.concatenate(
        [
            norm_gain_part,
            own_columns(ffn_gain_part, first),
            latent_gain_part + swap_cols(latent_gain_part),
        ]
    )
    gains = lax.psum(gains, "row")
    width_share = norm_gain.shape[0]
    norm_gain_grad = gains[:width_share]
    ffn_gain_grad = gains[width_share : 2 * width_share]
    latent_gain_grad = gains[2 * width_share :]

    def to_owners(values):
        return lax.psum_scatter(
            values.astype(bf16), "row", scatter_dimension=0, tiled=True
        ).astype(f32)

    output_grad = to_owners(output_grad_part).T
    dense_part = jnp.concatenate(
        [
            query_grad_part,
            latent_grad_part,
            router_grad_part,
            expand_grad_part.reshape(D, expand_width),
        ],
        axis=1,
    )
    dense_grad = to_owners(dense_part)
    edge = query_width
    query_grad = dense_grad[:, :edge]
    latent_grad = dense_grad[:, edge : edge + latent_width]
    edge += latent_width
    router_grad = dense_grad[:, edge : edge + expert_count]
    edge += expert_count
    expand_grad = dense_grad[:, edge:].reshape(expand_weight.shape)
    return (
        output,
        input_grad,
        norm_gain_grad,
        query_grad,
        latent_grad,
        latent_gain_grad,
        expand_grad,
        output_grad,
        ffn_gain_grad,
        router_grad,
        expert_gate_grad,
        expert_up_grad,
        expert_down_grad,
        shared_gate_grad,
        shared_up_grad,
        shared_down_grad,
    )


def on_device_general(
    inputs,
    segment_ids,
    routes,
    norm_gain,
    query_weight,
    latent_weight,
    latent_gain,
    expand_weight,
    output_weight,
    ffn_gain,
    router_weight,
    expert_gate,
    expert_up,
    expert_down,
    shared_gate,
    shared_up,
    shared_down,
    out_grad,
):
    bf16 = jnp.bfloat16
    f32 = jnp.float32
    rows_count = inputs.shape[0]
    width_share = inputs.shape[1]
    row_devices = lax.axis_size("row")
    col_devices = lax.axis_size("col")
    col_place = lax.axis_index("col")
    local_heads = query_weight.shape[1] // (NOPE + ROPE)
    expert_count = EXP_DEV * row_devices
    capacity = 4 * rows_count * TOPK // (3 * expert_count)
    score_scale = (NOPE + ROPE) ** (-0.5)
    block_rows = min(512, rows_count)
    segment_row = segment_ids[0]
    places = jnp.arange(rows_count, dtype=jnp.int32)
    (
        query_full,
        latent_full,
        expand_full,
        output_full,
        router_full,
        shared_gate_full,
        shared_up_full,
        shared_down_full,
    ) = (
        lax.all_gather(query_weight, "row", axis=0, tiled=True),
        lax.all_gather(latent_weight, "row", axis=0, tiled=True),
        lax.all_gather(expand_weight, "row", axis=0, tiled=True),
        lax.all_gather(output_weight, "row", axis=1, tiled=True),
        lax.all_gather(router_weight, "row", axis=0, tiled=True),
        lax.all_gather(shared_gate, "row", axis=0, tiled=True),
        lax.all_gather(shared_up, "row", axis=0, tiled=True),
        lax.all_gather(shared_down, "row", axis=1, tiled=True),
    )
    source = inputs.astype(f32)
    scale_one = rms_scale(source)
    unit_one = source * scale_one
    normed_one = spread((unit_one * norm_gain).astype(bf16))
    query = jnp.dot(normed_one, query_full, preferred_element_type=f32).reshape(
        rows_count, local_heads, NOPE + ROPE
    )
    latent = jnp.dot(normed_one, latent_full, preferred_element_type=f32).astype(bf16)
    cosine, sine = rotation(rows_count, ROPE)
    head_cos = cosine[:, None, :]
    head_sin = sine[:, None, :]
    compressed = latent[:, :RANK].astype(f32)
    latent_scale = lax.rsqrt(jnp.mean(compressed * compressed, axis=1, keepdims=True) + epsilon)
    latent_unit = compressed * latent_scale
    latent_normed = (latent_unit * latent_gain).astype(bf16)
    key_rope = rotate(latent[:, RANK:].astype(f32), cosine, sine).astype(bf16)
    expanded = jnp.dot(latent_normed, expand_full, preferred_element_type=f32).reshape(
        rows_count, local_heads, NOPE + VDIM
    )
    key_nope = expanded[..., :NOPE].astype(bf16)
    values_all = expanded[..., NOPE:].astype(bf16)
    query_nope = query[..., :NOPE].astype(bf16)
    query_rope = rotate(query[..., NOPE:], head_cos, head_sin).astype(bf16)

    def block_scores(start):
        ending = start + block_rows
        raw = jnp.einsum("qhd,khd->hqk", query_nope, key_nope, preferred_element_type=f32)
        raw = raw + jnp.einsum("qhd,kd->hqk", query_rope, key_rope, preferred_element_type=f32)
        allowed = (segment_row[start:ending, None] == segment_row[None, :]) & (
            places[None, :] <= places[:, None]
        )
        return jnp.where(allowed[None], raw * score_scale, -1e30)

    start = 0
    scores = block_scores(start)
    top = jnp.max(scores, axis=2, keepdims=True)
    exponent = jnp.exp(scores - top)
    total = jnp.sum(exponent, axis=2, keepdims=True)
    weights = exponent / total
    log_blocks = top + jnp.log(total)
    mixed_blocks = jnp.einsum(
        "hqk,khd->qhd", weights.astype(bf16), values_all, preferred_element_type=f32
    ).astype(bf16)
    mixed = mixed_blocks.reshape(rows_count, local_heads * VDIM)
    attended = mix_sums(jnp.dot(mixed, output_full, preferred_element_type=f32))
    middle = source + attended
    scale_two = rms_scale(middle)
    unit_two = middle * scale_two
    normed_two_share = (unit_two * ffn_gain).astype(bf16)
    normed_two = spread(normed_two_share)
    logits = jnp.dot(normed_two, router_full, preferred_element_type=f32)
    log_total = jax.nn.logsumexp(logits, axis=1, keepdims=True)
    chosen = routes[:, :, None] == jnp.arange(expert_count, dtype=jnp.int32)[None, None, :]
    picked = jnp.sum(jnp.where(chosen, logits[:, None, :], 0.0), axis=2)
    gates = jnp.exp(picked - log_total)
    upstream = out_grad.astype(f32)
    upstream_full = spread(out_grad)
    shared_gate_pre = jnp.dot(normed_two, shared_gate_full, preferred_element_type=f32)
    shared_up_pre = jnp.dot(normed_two, shared_up_full, preferred_element_type=f32)
    shared_hidden = (jax.nn.silu(shared_gate_pre) * shared_up_pre).astype(bf16)
    shared_part = jnp.dot(shared_hidden, shared_down_full, preferred_element_type=f32)
    flat_routes = routes.reshape(-1)
    hits = (flat_routes[:, None] == jnp.arange(expert_count, dtype=jnp.int32)[None, :]).astype(
        jnp.int32
    )
    ranks = jnp.sum((jnp.cumsum(hits, axis=0) - 1) * hits, axis=1)
    owners = jnp.arange(rows_count * TOPK, dtype=jnp.int32) // TOPK
    share_slots = capacity // col_devices
    slot_count = row_devices * share_slots
    buffer_size = EXP_DEV * slot_count
    inside = ranks // share_slots == col_place
    slot_place = jnp.where(
        inside,
        flat_routes % EXP_DEV * slot_count
        + flat_routes // EXP_DEV * share_slots
        + ranks
        - col_place * share_slots,
        buffer_size,
    )
    token_of_slot = (
        jnp.full((buffer_size + 1,), rows_count, jnp.int32).at[slot_place].set(owners)[:buffer_size]
    )
    gate_of_slot = (
        jnp.zeros((buffer_size + 1,), f32).at[slot_place].set(gates.reshape(-1))[:buffer_size]
    )
    position = slot_place.reshape(rows_count, TOPK)
    gate_stack, up_stack, down_stack = (
        lax.all_gather(expert_gate, "col", axis=1, tiled=True),
        lax.all_gather(expert_up, "col", axis=1, tiled=True),
        lax.all_gather(expert_down, "col", axis=1, tiled=True),
    )
    padded_rows = jnp.concatenate([normed_two, jnp.zeros((1, D), bf16)], axis=0)
    outgoing = padded_rows[token_of_slot].reshape(EXP_DEV, slot_count, D)
    arrived = send_rows(outgoing)
    gate_pre = jnp.einsum("jnd,jfd->jnf", arrived, gate_stack, preferred_element_type=f32)
    up_pre = jnp.einsum("jnd,jfd->jnf", arrived, up_stack, preferred_element_type=f32)
    hidden = (jax.nn.silu(gate_pre) * up_pre).astype(bf16)
    expert_result = jnp.einsum(
        "jnf,jfd->jnd", hidden, down_stack, preferred_element_type=f32
    ).astype(bf16)
    returned = return_rows(expert_result).reshape(buffer_size, D)
    returned = jnp.concatenate([returned, jnp.zeros((1, D), bf16)], axis=0)
    slot_values = returned[position].astype(f32)
    combined = mix_sums(jnp.sum(gates[:, :, None] * slot_values, axis=1) + shared_part)
    upstream_wide = upstream_full.astype(f32)
    gate_partial = jnp.sum(upstream_wide[:, None, :] * slot_values, axis=2)
    output = (middle + combined).astype(bf16)
    gate_grads = lax.psum(gate_partial, "col")
    chances = jnp.exp(logits - log_total)
    weighted_gates = gate_grads * gates
    logit_grads = (
        jnp.sum(jnp.where(chosen, weighted_gates[:, :, None], 0.0), axis=1)
        - chances * jnp.sum(weighted_gates, axis=1, keepdims=True)
    ).astype(bf16)
    router_rows = lax.dynamic_slice_in_dim(router_full, col_place * width_share, width_share, 0)
    router_back = jnp.einsum("te,de->td", logit_grads, router_rows, preferred_element_type=f32)
    router_grad_part = jnp.einsum("td,te->de", normed_two, logit_grads, preferred_element_type=f32)
    shared_hidden_back = jnp.einsum(
        "td,fd->tf", upstream_full, shared_down_full, preferred_element_type=f32
    )
    shared_sigmoid = jax.nn.sigmoid(shared_gate_pre)
    shared_gate_back = (
        shared_hidden_back * shared_up_pre * silu_slope(shared_gate_pre, shared_sigmoid)
    ).astype(bf16)
    shared_up_back = (shared_hidden_back * (shared_gate_pre * shared_sigmoid)).astype(bf16)
    shared_input_back = jnp.einsum(
        "tf,df->td", shared_gate_back, shared_gate_full, preferred_element_type=f32
    ) + jnp.einsum("tf,df->td", shared_up_back, shared_up_full, preferred_element_type=f32)
    shared_gate_part = jnp.einsum(
        "td,tf->df", normed_two, shared_gate_back, preferred_element_type=f32
    )
    shared_up_part = jnp.einsum("td,tf->df", normed_two, shared_up_back, preferred_element_type=f32)
    shared_down_part = jnp.einsum(
        "tf,td->fd", shared_hidden, upstream_full, preferred_element_type=f32
    )
    padded_upstream = jnp.concatenate([upstream_wide, jnp.zeros((1, D), f32)], axis=0)
    slot_grads = (
        (gate_of_slot[:, None] * padded_upstream[token_of_slot])
        .astype(bf16)
        .reshape(EXP_DEV, slot_count, D)
    )
    arrived_grads = send_rows(slot_grads)
    hidden_back = jnp.einsum("jnd,jfd->jnf", arrived_grads, down_stack, preferred_element_type=f32)
    gate_sigmoid = jax.nn.sigmoid(gate_pre)
    gate_back = (hidden_back * up_pre * silu_slope(gate_pre, gate_sigmoid)).astype(bf16)
    up_back = (hidden_back * (gate_pre * gate_sigmoid)).astype(bf16)
    row_back = jnp.einsum(
        "jnf,jfd->jnd", gate_back, gate_stack, preferred_element_type=f32
    ) + jnp.einsum("jnf,jfd->jnd", up_back, up_stack, preferred_element_type=f32)
    returned_grads = return_rows(row_back.astype(bf16)).reshape(buffer_size, D)
    returned_grads = jnp.concatenate([returned_grads, jnp.zeros((1, D), bf16)], axis=0)
    routed_back = jnp.sum(returned_grads[position].astype(f32), axis=1)
    normed_two_back = mix_sums(routed_back + shared_input_back) + router_back
    gate_pieces = []
    up_pieces = []
    down_pieces = []
    for expert in range(EXP_DEV):
        gate_piece, up_piece, down_piece = (
            lax.psum_scatter(
                jnp.einsum(
                    "nf,nd->fd", gate_back[expert], arrived[expert], preferred_element_type=f32
                ).astype(jnp.bfloat16),
                "col",
                scatter_dimension=0,
                tiled=True,
            ).astype(jnp.float32),
            lax.psum_scatter(
                jnp.einsum(
                    "nf,nd->fd", up_back[expert], arrived[expert], preferred_element_type=f32
                ).astype(jnp.bfloat16),
                "col",
                scatter_dimension=0,
                tiled=True,
            ).astype(jnp.float32),
            lax.psum_scatter(
                jnp.einsum(
                    "nf,nd->fd", hidden[expert], arrived_grads[expert], preferred_element_type=f32
                ).astype(jnp.bfloat16),
                "col",
                scatter_dimension=0,
                tiled=True,
            ).astype(jnp.float32),
        )
        gate_pieces.append(gate_piece)
        up_pieces.append(up_piece)
        down_pieces.append(down_piece)
    expert_gate_grad = jnp.stack(gate_pieces, axis=0)
    expert_up_grad = jnp.stack(up_pieces, axis=0)
    expert_down_grad = jnp.stack(down_pieces, axis=0)
    ffn_gain_part = jnp.sum(normed_two_back * unit_two, axis=0)
    middle_back = upstream + norm_backward(normed_two_back, unit_two, scale_two, ffn_gain)
    attended_back = spread(middle_back.astype(bf16))
    mixed_back = (
        jnp.einsum("td,vd->tv", attended_back, output_full, preferred_element_type=f32)
        .astype(bf16)
        .reshape(rows_count, local_heads, VDIM)
    )
    output_grad_part = jnp.einsum("tv,td->vd", mixed, attended_back, preferred_element_type=f32)
    start = 0
    ending = start + block_rows
    scores = block_scores(start)
    weights = jnp.exp(scores - log_blocks)
    weight_back = jnp.einsum("qhd,khd->hqk", mixed_back, values_all, preferred_element_type=f32)
    center = jnp.sum(weight_back * weights, axis=2, keepdims=True)
    raw_back = (weights * (weight_back - center) * score_scale).astype(bf16)
    query_nope_back = jnp.einsum("hqk,khd->qhd", raw_back, key_nope, preferred_element_type=f32)
    query_rope_back = jnp.einsum("hqk,kd->qhd", raw_back, key_rope, preferred_element_type=f32)
    key_nope_back = jnp.einsum("hqk,qhd->khd", raw_back, query_nope, preferred_element_type=f32)
    key_rope_back = jnp.einsum("hqk,qhd->kd", raw_back, query_rope, preferred_element_type=f32)
    values_back = jnp.einsum(
        "hqk,qhd->khd", weights.astype(bf16), mixed_back, preferred_element_type=f32
    )
    query_back = jnp.concatenate(
        [query_nope_back, unrotate(query_rope_back, head_cos, head_sin)], axis=2
    )
    query_back = query_back.astype(bf16).reshape(rows_count, local_heads * (NOPE + ROPE))
    expanded_back = (
        jnp.concatenate([key_nope_back, values_back], axis=2)
        .astype(bf16)
        .reshape(rows_count, local_heads * (NOPE + VDIM))
    )
    latent_normed_back = jnp.einsum(
        "tc,rc->tr", expanded_back, expand_full, preferred_element_type=f32
    )
    expand_grad_part = jnp.einsum(
        "tr,tc->rc", latent_normed, expanded_back, preferred_element_type=f32
    )
    latent_gain_part = jnp.sum(latent_normed_back * latent_unit, axis=0)
    latent_weighted = latent_normed_back * latent_gain
    compressed_back = latent_scale * (
        latent_weighted
        - latent_unit * jnp.mean(latent_weighted * latent_unit, axis=1, keepdims=True)
    )
    rope_back = unrotate(key_rope_back, cosine, sine)
    latent_back, latent_gain_col = (
        lax.psum(
            jnp.concatenate([compressed_back, rope_back], axis=1).astype(jnp.bfloat16), "col"
        ).astype(jnp.float32),
        lax.psum(latent_gain_part.astype(jnp.bfloat16), "col").astype(jnp.float32),
    )
    latent_back = latent_back.astype(bf16)
    latent_grad_part = jnp.einsum("td,tc->dc", normed_one, latent_back, preferred_element_type=f32)
    query_grad_part = jnp.einsum("td,tc->dc", normed_one, query_back, preferred_element_type=f32)
    latent_rows = lax.dynamic_slice_in_dim(latent_full, col_place * width_share, width_share, 0)
    input_part = jnp.einsum("tc,dc->td", query_back, query_full, preferred_element_type=f32)
    normed_one_back = mix_sums(input_part) + jnp.einsum(
        "tc,dc->td", latent_back, latent_rows, preferred_element_type=f32
    )
    norm_gain_part = jnp.sum(normed_one_back * unit_one, axis=0)
    input_grad = middle_back + norm_backward(normed_one_back, unit_one, scale_one, norm_gain)
    norm_gain_grad, ffn_gain_grad, latent_gain_grad = lax.psum(
        (norm_gain_part, ffn_gain_part, latent_gain_col), "row"
    )
    (
        query_grad,
        latent_grad,
        expand_grad,
        output_grad,
        router_grad,
        shared_gate_grad,
        shared_up_grad,
        shared_down_grad,
    ) = (
        lax.psum_scatter(
            query_grad_part.astype(jnp.bfloat16), "row", scatter_dimension=0, tiled=True
        ).astype(jnp.float32),
        lax.psum_scatter(
            latent_grad_part.astype(jnp.bfloat16), "row", scatter_dimension=0, tiled=True
        ).astype(jnp.float32),
        lax.psum_scatter(
            expand_grad_part.astype(jnp.bfloat16), "row", scatter_dimension=0, tiled=True
        ).astype(jnp.float32),
        lax.psum_scatter(
            output_grad_part.astype(jnp.bfloat16), "row", scatter_dimension=1, tiled=True
        ).astype(jnp.float32),
        lax.psum_scatter(
            router_grad_part.astype(jnp.bfloat16), "row", scatter_dimension=0, tiled=True
        ).astype(jnp.float32),
        lax.psum_scatter(
            shared_gate_part.astype(jnp.bfloat16), "row", scatter_dimension=0, tiled=True
        ).astype(jnp.float32),
        lax.psum_scatter(
            shared_up_part.astype(jnp.bfloat16), "row", scatter_dimension=0, tiled=True
        ).astype(jnp.float32),
        lax.psum_scatter(
            shared_down_part.astype(jnp.bfloat16), "row", scatter_dimension=1, tiled=True
        ).astype(jnp.float32),
    )
    return (
        output,
        input_grad,
        norm_gain_grad,
        query_grad,
        latent_grad,
        latent_gain_grad,
        expand_grad,
        output_grad,
        ffn_gain_grad,
        router_grad,
        expert_gate_grad,
        expert_up_grad,
        expert_down_grad,
        shared_gate_grad,
        shared_up_grad,
        shared_down_grad,
    )


def solution(mesh):
    in_specs = (
        P("row", "col"),
        P("row", None),
        P("row", None),
        P("col"),
        P("row", "col"),
        P("row", None),
        P(),
        P("row", "col"),
        P("col", "row"),
        P("col"),
        P("row", None),
        P("row", "col", None),
        P("row", "col", None),
        P("row", "col", None),
        P("row", "col"),
        P("row", "col"),
        P("col", "row"),
        P("row", "col"),
    )
    out_specs = (
        P("row", "col"),
        P("row", "col"),
        P("col"),
        P("row", "col"),
        P("row", None),
        P(),
        P("row", "col"),
        P("col", "row"),
        P("col"),
        P("row", None),
        P("row", "col", None),
        P("row", "col", None),
        P("row", "col", None),
        P("row", "col"),
        P("row", "col"),
        P("col", "row"),
    )
    plan = on_device if dict(mesh.shape) == {"row": 16, "col": 2} else on_device_general
    return jax.shard_map(
        plan, mesh=mesh, in_specs=in_specs, out_specs=out_specs, check_vma=False
    )
```

```python
import jax
import jax.numpy as jnp
from jax import lax
from jax.experimental import pallas as pl
from jax.experimental.pallas import tpu as pltpu
from jax.sharding import PartitionSpec as P

D = 2048
NOPE = 128
ROPE = 64
RANK = 512
VDIM = 128
TOPK = 6
EXP_DEV = 4


epsilon = 1e-06
theta = 10000.0


def rotation(count, width):
    half = width // 2
    places = jnp.arange(count, dtype=jnp.float32)
    rates = theta ** (-jnp.arange(half, dtype=jnp.float32) * 2.0 / width)
    angles = places[:, None] * rates[None, :]
    return (jnp.cos(angles), jnp.sin(angles))


def rotate(values, cosine, sine):
    half = values.shape[-1] // 2
    first = values[..., :half]
    second = values[..., half:]
    return jnp.concatenate(
        [first * cosine - second * sine, second * cosine + first * sine], axis=-1
    )


def unrotate(grads, cosine, sine):
    half = grads.shape[-1] // 2
    first = grads[..., :half]
    second = grads[..., half:]
    return jnp.concatenate(
        [first * cosine + second * sine, second * cosine - first * sine], axis=-1
    )


def silu_slope(pre, sigmoid_value):
    return sigmoid_value * (1.0 + pre * (1.0 - sigmoid_value))


def col_total(values):
    return lax.psum(values, "col")


def spread(values):
    return lax.all_gather(values, "col", axis=1, tiled=True)


def mix_sums(values):
    return lax.psum_scatter(
        values.astype(jnp.bfloat16), "col", scatter_dimension=1, tiled=True
    ).astype(jnp.float32)


def send_rows(rows):
    return lax.all_to_all(rows, "row", split_axis=1, concat_axis=1, tiled=True)


def return_rows(rows):
    return lax.all_to_all(rows, "row", split_axis=1, concat_axis=1, tiled=True)


def rms_scale(rows):
    total = col_total(jnp.sum(rows * rows, axis=1))
    return lax.rsqrt(total / D + epsilon)[:, None]


def norm_backward(grads, unit, scale, gain):
    weighted = grads * gain
    average = col_total(jnp.sum(weighted * unit, axis=1)) / D
    return scale * (weighted - unit * average[:, None])


PLANES = 4
COMMON = 192
UNIQUE = 160
SENT = COMMON + UNIQUE
SHARED_PAD = 128
QUERY_COLUMNS = 1536
SCORE_SCALE = (NOPE + ROPE) ** (-0.5)


def swap_cols(values):
    return lax.ppermute(values, "col", [(0, 1), (1, 0)])


def swap_rows(values, bit):
    return lax.ppermute(values, "row", [(i, i ^ bit) for i in range(16)])


def turn_planes(values):
    return lax.ppermute(values, "row", [(i, (i + 4) % 16) for i in range(16)])


def join_cols(values, first):
    other = swap_cols(values)
    return jnp.where(
        first,
        jnp.concatenate([values, other], axis=1),
        jnp.concatenate([other, values], axis=1),
    )


def own_columns(values, first):
    half = values.shape[-1] // 2
    return jnp.where(first, values[..., :half], values[..., half:])


def other_columns(values, first):
    half = values.shape[-1] // 2
    return jnp.where(first, values[..., half:], values[..., :half])


def sent_rows(values, first):
    return jnp.concatenate(
        [values[:COMMON], jnp.where(first, values[COMMON:SENT], values[SENT:])], axis=0
    )


def local_tokens(values, axis, first):
    common = lax.slice_in_dim(values, 0, COMMON, axis=axis)
    one = lax.slice_in_dim(values, COMMON, SENT, axis=axis)
    two = lax.slice_in_dim(values, SENT, SENT + UNIQUE, axis=axis)
    return jnp.concatenate(
        [common, jnp.where(first, one, two), jnp.where(first, two, one)], axis=axis
    )


def together(*values):
    return lax.optimization_barrier(values)


def after(values, *others):
    return lax.optimization_barrier((values, *others))[0]


def batch(values):
    starts = [0]
    for value in values:
        starts.append(starts[-1] + value.shape[0])
    return jnp.concatenate(values, axis=0), starts[:-1]


class Spread:
    def __init__(self, rows):
        self.held = {(0, 0): rows}
        self.unique = {}
        self.sibling = {}

    def turn(self, plane):
        return turn_planes(self.held[plane - 1, 0])

    def cross(self, plane):
        return swap_rows(self.held[plane, 0], 2)

    def sent(self, *keys):
        return [self.held[key][COMMON:] for key in keys]

    def got(self, array, starts, *keys):
        for key, start in zip(keys, starts):
            self.unique[key] = (array, start)

    def passed(self, *keys):
        pieces = []
        for key in keys:
            if key[2]:
                array, start = self.unique[key[:2]]
                pieces.append(array[start : start + UNIQUE])
            else:
                pieces.append(self.held[key[:2]])
        return pieces

    def taken(self, array, starts, *keys):
        for key, start in zip(keys, starts):
            self.sibling[key] = (array, start)

    def family(self, plane):
        result = []
        for across in (0, 1):
            result.append(((self.held[plane, across], 0), self.unique[plane, across]))
            result.append((self.sibling[plane, across, 0], self.sibling[plane, across, 1]))
        return result


def add_unique(rest, unique, across):
    return jnp.concatenate([rest[across, :COMMON], rest[across, COMMON:] + unique[across]], axis=0)


def column_pieces(weight, bounds):
    return jnp.concatenate([weight[:, a:b] for a, b in bounds], axis=1)


def pair_columns(weight):
    head = NOPE + ROPE
    bounds = []
    for start in range(0, weight.shape[1], 2 * head):
        bounds += [(start, start + NOPE), (start + head, start + head + NOPE)]
        bounds += [(start + NOPE, start + head), (start + head + NOPE, start + 2 * head)]
    return column_pieces(weight, bounds)


def head_columns(weight):
    bounds = []
    for start in range(0, weight.shape[1], 2 * (NOPE + ROPE)):
        turned = start + 2 * NOPE
        bounds += [(start, start + NOPE), (turned, turned + ROPE)]
        bounds += [(start + NOPE, turned), (turned + ROPE, turned + 2 * ROPE)]
    return column_pieces(weight, bounds)


def merge_rows(own, received, first):
    own = own.astype(jnp.float32)
    received = received.astype(jnp.float32)
    common = own[:COMMON] + received[:COMMON]
    mine = own[COMMON:]
    theirs = received[COMMON:]
    return jnp.concatenate(
        [common, jnp.where(first, mine, theirs), jnp.where(first, theirs, mine)], axis=0
    )


FAMILIES = 4
VMEM_BYTES = 60 * 1024 * 1024


def kernel_params(**extra):
    return pltpu.CompilerParams(vmem_limit_bytes=VMEM_BYTES, **extra)


def short_cost():
    return pl.CostEstimate(flops=10**9, bytes_accessed=10**6, transcendentals=0)


def dot_last(left, right):
    return lax.dot_general(
        left, right, (((1,), (1,)), ((), ())), preferred_element_type=jnp.float32
    )


def dot_first(left, right):
    return lax.dot_general(
        left, right, (((0,), (0,)), ((), ())), preferred_element_type=jnp.float32
    )


def dot_plain(left, right):
    return jnp.dot(left, right, preferred_element_type=jnp.float32)


def slot_matches(codes_ref, capacity):
    tokens = codes_ref.shape[-1]
    ranks = lax.broadcasted_iota(jnp.int32, (capacity, tokens), 0)
    return [codes_ref[0, j : j + 1, :] == ranks for j in range(EXP_DEV)]


def as_picks(matches):
    one = [jnp.where(m, 1.0, 0.0).astype(jnp.bfloat16) for m in matches]
    return jnp.concatenate(one, axis=0)


def row_copies(refs, starts, held, sems, f):
    return [
        pltpu.make_async_copy(
            refs[2 * f].at[pl.ds(starts[2 * f], SENT)],
            held.at[f, pl.ds(0, SENT)],
            sems.at[f, 0],
        ),
        pltpu.make_async_copy(
            refs[2 * f + 1].at[pl.ds(starts[2 * f + 1], UNIQUE)],
            held.at[f, pl.ds(SENT, UNIQUE)],
            sems.at[f, 1],
        ),
    ]


def start_rows(refs, starts, held, sems):
    for f in range(FAMILIES):
        for copy in row_copies(refs, starts, held, sems, f):
            copy.start()


def wait_rows(refs, starts, held, sems, f):
    for family in range(FAMILIES):

        @pl.when(f == family)
        def _():
            for copy in row_copies(refs, starts, held, sems, family):
                copy.wait()


def pick_grads(plane, codes, last, capacity):
    pieces = [piece[0] for family in plane for piece in family]
    starts = [piece[1] for family in plane for piece in family]
    tokens = SENT + UNIQUE
    width = last.shape[1]
    pad = last.shape[0]

    def body(*refs):
        rows_in = refs[:8]
        codes_ref, last_ref, slots_ref, hidden_ref, held, sems = refs[8:]
        f = pl.program_id(0)

        @pl.when(f == 0)
        def _():
            start_rows(rows_in, starts, held, sems)

        wait_rows(rows_in, starts, held, sems, f)
        rows = held[f]
        picks = as_picks(slot_matches(codes_ref, capacity))
        taken = dot_plain(picks, rows).astype(jnp.bfloat16)
        slots_ref[...] = taken.reshape(EXP_DEV, capacity, width)
        hidden_ref[0] = dot_last(rows, last_ref[...])

    return pl.pallas_call(
        body,
        grid=(FAMILIES,),
        in_specs=[pl.BlockSpec(memory_space=pl.ANY)] * 8
        + [
            pl.BlockSpec((1, 8, tokens), lambda f: (f, 0, 0)),
            pl.BlockSpec((pad, width), lambda f: (0, 0)),
        ],
        out_specs=[
            pl.BlockSpec((EXP_DEV, capacity, width), lambda f: (0, f, 0)),
            pl.BlockSpec((1, tokens, pad), lambda f: (f, 0, 0)),
        ],
        out_shape=[
            jax.ShapeDtypeStruct((EXP_DEV, FAMILIES * capacity, width), jnp.bfloat16),
            jax.ShapeDtypeStruct((FAMILIES, tokens, pad), jnp.float32),
        ],
        scratch_shapes=[
            pltpu.VMEM((FAMILIES, tokens, width), jnp.bfloat16),
            pltpu.SemaphoreType.DMA((FAMILIES, 2)),
        ],
        compiler_params=kernel_params(),
        cost_estimate=short_cost(),
    )(*pieces, codes, last)


def pick_rows(plane, grad_plane, codes, router, pair, hidden_grads, capacity):
    pieces = [piece[0] for family in plane for piece in family]
    starts = [piece[1] for family in plane for piece in family]
    grad_pieces = [piece[0] for family in grad_plane for piece in family]
    grad_starts = [piece[1] for family in grad_plane for piece in family]
    tokens = SENT + UNIQUE
    width = pair.shape[1]
    pad = pair.shape[0] // 2

    def body(*refs):
        rows_in = refs[:8]
        grads_in = refs[8:16]
        (codes_ref, router_ref, pair_ref, hidden_grads_ref) = refs[16:20]
        (slots_ref, gates_ref, hidden_ref, back_ref, grad_ref) = refs[20:25]
        held, held_grads, sems, grad_sems = refs[25:]
        f = pl.program_id(0)

        @pl.when(f == 0)
        def _():
            start_rows(rows_in, starts, held, sems)
            start_rows(grads_in, grad_starts, held_grads, grad_sems)
            grad_ref[...] = jnp.zeros_like(grad_ref)

        wait_rows(rows_in, starts, held, sems, f)
        rows = held[f]
        matches = slot_matches(codes_ref, capacity)
        taken = dot_plain(as_picks(matches), rows).astype(jnp.bfloat16)
        slots_ref[...] = taken.reshape(EXP_DEV, capacity, width)
        logits = dot_last(router_ref[...], rows)
        top = jnp.max(logits, axis=0, keepdims=True)
        total = jnp.log(jnp.sum(jnp.exp(logits - top), axis=0, keepdims=True)) + top
        for j in range(EXP_DEV):
            chance = jnp.exp(logits[j : j + 1] - total)
            gate = jnp.sum(jnp.where(matches[j], chance, 0.0), axis=1, keepdims=True)
            gates_ref[j] = jnp.broadcast_to(gate, (capacity, 128))
        pre = dot_last(rows, pair_ref[...])
        gate_pre = pre[:, :pad]
        up_pre = pre[:, pad:]
        hidden_back = hidden_grads_ref[0]
        sigmoid_value = jax.nn.sigmoid(gate_pre)
        silu_value = gate_pre * sigmoid_value
        hidden = (silu_value * up_pre).astype(jnp.bfloat16)
        slope = sigmoid_value * (1.0 + gate_pre * (1.0 - sigmoid_value))
        gate_back = (hidden_back * up_pre * slope).astype(jnp.bfloat16)
        up_back = (hidden_back * silu_value).astype(jnp.bfloat16)
        back = jnp.concatenate([gate_back, up_back], axis=1)
        hidden_ref[0] = hidden
        back_ref[0] = back
        grad_ref[: 2 * pad] += dot_first(back, rows)
        wait_rows(grads_in, grad_starts, held_grads, grad_sems, f)
        grad_ref[2 * pad :] += dot_first(hidden, held_grads[f])

    return pl.pallas_call(
        body,
        grid=(FAMILIES,),
        in_specs=[pl.BlockSpec(memory_space=pl.ANY)] * 16
        + [
            pl.BlockSpec((1, 8, tokens), lambda f: (f, 0, 0)),
            pl.BlockSpec(router.shape, lambda f: (0, 0)),
            pl.BlockSpec(pair.shape, lambda f: (0, 0)),
            pl.BlockSpec((1, tokens, pad), lambda f: (f, 0, 0)),
        ],
        out_specs=[
            pl.BlockSpec((EXP_DEV, capacity, width), lambda f: (0, f, 0)),
            pl.BlockSpec((EXP_DEV, capacity, 128), lambda f: (0, f, 0)),
            pl.BlockSpec((1, tokens, pad), lambda f: (f, 0, 0)),
            pl.BlockSpec((1, tokens, 2 * pad), lambda f: (f, 0, 0)),
            pl.BlockSpec((3 * pad, width), lambda f: (0, 0)),
        ],
        out_shape=[
            jax.ShapeDtypeStruct((EXP_DEV, FAMILIES * capacity, width), jnp.bfloat16),
            jax.ShapeDtypeStruct((EXP_DEV, FAMILIES * capacity, 128), jnp.float32),
            jax.ShapeDtypeStruct((FAMILIES, tokens, pad), jnp.bfloat16),
            jax.ShapeDtypeStruct((FAMILIES, tokens, 2 * pad), jnp.bfloat16),
            jax.ShapeDtypeStruct((3 * pad, width), jnp.float32),
        ],
        scratch_shapes=[
            pltpu.VMEM((FAMILIES, tokens, width), jnp.bfloat16),
            pltpu.VMEM((FAMILIES, tokens, width), jnp.bfloat16),
            pltpu.SemaphoreType.DMA((FAMILIES, 2)),
            pltpu.SemaphoreType.DMA((FAMILIES, 2)),
        ],
        compiler_params=kernel_params(),
        cost_estimate=short_cost(),
    )(*pieces, *grad_pieces, codes, router, pair, hidden_grads)


def run_experts(slot_rows, slot_grads, gates, expert_gate, expert_up, expert_down):
    count, slots, width = slot_rows.shape
    units = expert_gate.shape[1]

    def body(
        rows_ref,
        grads_ref,
        gates_ref,
        gate_ref,
        up_ref,
        down_ref,
        sum_ref,
        back_ref,
        hidden_ref,
        gate_back_ref,
        up_back_ref,
        gate_grad_ref,
    ):
        rows = rows_ref[0]
        gates_here = gates_ref[0][:, :1]
        gate_pre = dot_last(rows, gate_ref[0])
        up_pre = dot_last(rows, up_ref[0])
        down_back = dot_last(grads_ref[0], down_ref[0])
        sigmoid_value = jax.nn.sigmoid(gate_pre)
        silu_value = gate_pre * sigmoid_value
        hidden = silu_value * up_pre
        gate_grad = jnp.sum(hidden * down_back, axis=1, keepdims=True)
        gate_grad_ref[0] = jnp.broadcast_to(gate_grad, (slots, 128))
        hidden_back = down_back * gates_here
        slope = sigmoid_value * (1.0 + gate_pre * (1.0 - sigmoid_value))
        gate_back = (hidden_back * up_pre * slope).astype(jnp.bfloat16)
        up_back = (hidden_back * silu_value).astype(jnp.bfloat16)
        scaled = (hidden * gates_here).astype(jnp.bfloat16)
        hidden_ref[0] = scaled
        gate_back_ref[0] = gate_back
        up_back_ref[0] = up_back
        back = dot_plain(gate_back, gate_ref[0]) + dot_plain(up_back, up_ref[0])
        back_ref[0] = back.astype(jnp.bfloat16)
        sum_ref[0] = dot_plain(scaled, down_ref[0]).astype(jnp.bfloat16)

    wide = pl.BlockSpec((1, slots, width), lambda j: (j, 0, 0))
    narrow = pl.BlockSpec((1, slots, 128), lambda j: (j, 0, 0))
    inner = pl.BlockSpec((1, slots, units), lambda j: (j, 0, 0))
    matrix = pl.BlockSpec((1, units, width), lambda j: (j, 0, 0))
    return pl.pallas_call(
        body,
        grid=(count,),
        in_specs=[wide, wide, narrow, matrix, matrix, matrix],
        out_specs=[wide, wide, inner, inner, inner, narrow],
        out_shape=[
            jax.ShapeDtypeStruct((count, slots, width), jnp.bfloat16),
            jax.ShapeDtypeStruct((count, slots, width), jnp.bfloat16),
            jax.ShapeDtypeStruct((count, slots, units), jnp.bfloat16),
            jax.ShapeDtypeStruct((count, slots, units), jnp.bfloat16),
            jax.ShapeDtypeStruct((count, slots, units), jnp.bfloat16),
            jax.ShapeDtypeStruct((count, slots, 128), jnp.float32),
        ],
        compiler_params=kernel_params(),
        cost_estimate=short_cost(),
    )(slot_rows, slot_grads, gates, expert_gate, expert_up, expert_down)


def sum_tokens(values, codes, shared, matrix, capacity, core, received=None, gate_grads=None):
    tokens = codes.shape[2]
    width = values.shape[2]
    inner = matrix.shape[0]
    with_rows = received is not None
    with_gates = gate_grads is not None

    def body(*refs):
        values_ref, codes_ref, shared_ref, matrix_ref = refs[:4]
        outs = refs[4 + with_rows + with_gates :]
        matches = slot_matches(codes_ref, capacity)
        rows = values_ref[...].reshape(EXP_DEV * capacity, width)
        total = dot_first(as_picks(matches), rows)
        total = total + dot_plain(shared_ref[0], matrix_ref[...])
        if with_rows:
            total = (total + refs[4][0].astype(jnp.float32)).astype(jnp.bfloat16)
            outs[0][0] = total[:SENT]
            outs[1][0] = total[SENT:]
        else:
            outs[0][0] = total.astype(jnp.bfloat16)
        if with_gates:
            dense = [
                jnp.sum(
                    jnp.where(matches[j], refs[4 + with_rows][j][:, :1], 0.0),
                    axis=0,
                    keepdims=True,
                )
                for j in range(EXP_DEV)
            ]
            outs[-1][0] = jnp.concatenate(dense + [jnp.zeros((4, tokens), jnp.float32)], axis=0)

    in_specs = [
        pl.BlockSpec((EXP_DEV, capacity, width), lambda i: (0, 2 * i + core, 0)),
        pl.BlockSpec((1, 8, tokens), lambda i: (2 * i + core, 0, 0)),
        pl.BlockSpec((1, tokens, inner), lambda i: (2 * i + core, 0, 0)),
        pl.BlockSpec((inner, width), lambda i: (0, 0)),
    ]
    operands = [values, codes, shared, matrix]
    pieces = [tokens]
    if with_rows:
        in_specs.append(pl.BlockSpec((1, tokens, width), lambda i: (i, 0, 0)))
        operands.append(received)
        pieces = [SENT, UNIQUE]
    out_specs = [pl.BlockSpec((1, piece, width), lambda i: (i, 0, 0)) for piece in pieces]
    out_shape = [jax.ShapeDtypeStruct((2, piece, width), jnp.bfloat16) for piece in pieces]
    if with_gates:
        in_specs.append(pl.BlockSpec((EXP_DEV, capacity, 128), lambda i: (0, 2 * i + core, 0)))
        operands.append(gate_grads)
        out_specs.append(pl.BlockSpec((1, 8, tokens), lambda i: (i, 0, 0)))
        out_shape.append(jax.ShapeDtypeStruct((2, 8, tokens), jnp.float32))
    return pl.pallas_call(
        body,
        grid=(2,),
        in_specs=in_specs,
        out_specs=out_specs,
        out_shape=out_shape,
        compiler_params=kernel_params(),
        cost_estimate=short_cost(),
    )(*operands)


def pack_weights(query_weight, expand_weight, output_weight, latent_weight, router_weight, routes):
    block = latent_weight.shape[0]
    share = expand_weight.shape[0]
    widths = [
        query_weight.shape[1],
        expand_weight.shape[1] * share // block,
        output_weight.shape[0],
        latent_weight.shape[1],
        router_weight.shape[1],
        routes.shape[1],
    ]
    columns = (sum(widths) + 127) // 128 * 128

    def body(query_ref, expand_ref, output_ref, latent_ref, router_ref, routes_ref, out_ref):
        out_ref[:, : widths[0]] = pair_columns(query_ref[...])
        start = widths[0]
        for i in range(block // share):
            out_ref[share * i : share * (i + 1), start : start + widths[1]] = expand_ref[
                :, widths[1] * i : widths[1] * (i + 1)
            ]
        start += widths[1]
        out_ref[:, start : start + widths[2]] = output_ref[...].T
        start += widths[2]
        out_ref[:, start : start + widths[3] + widths[4]] = jnp.concatenate(
            [latent_ref[...], router_ref[...]], axis=1
        )
        start += widths[3] + widths[4]
        last = jnp.zeros((block, columns - start - widths[5]), jnp.bfloat16)
        out_ref[:, start:] = jnp.concatenate([routes_ref[...], last], axis=1)

    return pl.pallas_call(
        body,
        out_shape=jax.ShapeDtypeStruct((block, columns), jnp.bfloat16),
        compiler_params=kernel_params(),
        cost_estimate=short_cost(),
    )(query_weight, expand_weight, output_weight, latent_weight, router_weight, routes)


def unpack_grads(output, wide, narrow, widths):
    block = wide.shape[0]
    query_width, expand_width, latent_width = widths
    parts = 4
    share = block // parts

    def body(sum_ref, wide_ref, narrow_ref, output_ref, query_ref, expand_ref, latent_ref, router_ref):
        output_ref[...] = sum_ref[...].astype(jnp.float32).T
        query_ref[...] = head_columns(wide_ref[:, :query_width]).astype(jnp.float32)
        for i in range(parts):
            expand_ref[:, expand_width * i : expand_width * (i + 1)] = wide_ref[
                share * i : share * (i + 1), query_width:
            ].astype(jnp.float32)
        latent_ref[...] = narrow_ref[:, :latent_width].astype(jnp.float32)
        router_ref[...] = narrow_ref[:, latent_width:].astype(jnp.float32)

    shapes = [
        (output.shape[1], block),
        (block, query_width),
        (share, expand_width * parts),
        (block, latent_width),
        (block, narrow.shape[1] - latent_width),
    ]
    return pl.pallas_call(
        body,
        out_shape=[jax.ShapeDtypeStruct(shape, jnp.float32) for shape in shapes],
        compiler_params=kernel_params(),
        cost_estimate=short_cost(),
    )(output, wide, narrow)


def block_grads(places, left, right, tile, core, turned=None, expanded=None, received=None):
    count, width = left.shape
    block = width // (4 * PLANES)
    blocks = 2 * PLANES
    columns = right.shape[1]
    steps = columns // tile
    with_expand = turned is not None
    share = turned.shape[0] // (4 * PLANES) if with_expand else 0
    quarter = expanded.shape[1] // steps if with_expand else 0

    def body(places_ref, left_ref, right_ref, *refs):
        held = refs[-2]
        held_turned = refs[-1]
        out_ref = refs[-3]
        step = pl.program_id(0)

        @pl.when(step == 0)
        def _():
            for i in range(blocks):
                place = places_ref[2 * i + core]
                start = pl.multiple_of(place * block, block)
                held[:, block * i : block * (i + 1)] = left_ref[:, pl.ds(start, block)]
                if with_expand:
                    start = pl.multiple_of(place * share, share)
                    held_turned[share * i : share * (i + 1)] = refs[0][pl.ds(start, share)]

        part = dot_first(held[...], right_ref[...]).reshape(blocks, block, tile)
        lanes = pl.ds(pl.multiple_of(step * tile, 128), tile)
        if received is not None:
            got_ref = refs[-4]
            part = part + got_ref[:, :, lanes].astype(jnp.float32)
        out_ref[:, :, lanes] = part.astype(jnp.bfloat16)
        if with_expand:
            part = dot_plain(held_turned[...], refs[1][...]).reshape(blocks, share, quarter)
            lines = pl.ds(pl.multiple_of(step * share, share), share)
            if received is not None:
                part = part + got_ref[:, lines, columns:].astype(jnp.float32)
            out_ref[:, lines, columns:] = part.astype(jnp.bfloat16)

    whole = lambda shape: pl.BlockSpec(shape, lambda h, places_ref: (0,) * len(shape))
    in_specs = [
        whole(left.shape),
        pl.BlockSpec((count, tile), lambda h, places_ref: (0, h)),
    ]
    operands = [left, right]
    if with_expand:
        in_specs += [
            whole(turned.shape),
            pl.BlockSpec((count, quarter), lambda h, places_ref: (0, h)),
        ]
        operands += [turned, expanded]
    shape = (blocks, block, columns + quarter)
    if received is not None:
        in_specs.append(whole(shape))
        operands.append(received)
    return pl.pallas_call(
        body,
        grid_spec=pltpu.PrefetchScalarGridSpec(
            num_scalar_prefetch=1,
            grid=(steps,),
            in_specs=in_specs,
            out_specs=whole(shape),
            scratch_shapes=[
                pltpu.VMEM((count, blocks * block), jnp.bfloat16),
                pltpu.VMEM((max(blocks * share, 16), count), jnp.bfloat16),
            ],
        ),
        out_shape=jax.ShapeDtypeStruct(shape, jnp.bfloat16),
        compiler_params=kernel_params(),
        cost_estimate=short_cost(),
    )(places, *operands)


def narrow_grads(places, normed, latent_back, normed_two, logit_grads, core):
    count, width = normed.shape
    block = width // (4 * PLANES)
    widths = [latent_back.shape[1], logit_grads.shape[1]]

    def body(places_ref, normed_ref, two_ref, latent_ref, logit_ref, out_ref):
        parts = [
            dot_first(normed_ref[...], latent_ref[...]),
            dot_first(two_ref[...], logit_ref[...]),
        ]
        out_ref[0] = jnp.concatenate(parts, axis=1).astype(jnp.bfloat16)

    piece = pl.BlockSpec((count, block), lambda i, places_ref: (0, places_ref[2 * i + core]))
    whole = lambda columns: pl.BlockSpec((count, columns), lambda i, places_ref: (0, 0))
    return pl.pallas_call(
        body,
        grid_spec=pltpu.PrefetchScalarGridSpec(
            num_scalar_prefetch=1,
            grid=(2 * PLANES,),
            in_specs=[piece, piece, whole(widths[0]), whole(widths[1])],
            out_specs=pl.BlockSpec((1, block, sum(widths)), lambda i, places_ref: (i, 0, 0)),
        ),
        out_shape=jax.ShapeDtypeStruct((2 * PLANES, block, sum(widths)), jnp.bfloat16),
        compiler_params=kernel_params(),
        cost_estimate=short_cost(),
    )(places, normed, normed_two, latent_back, logit_grads)


def assemble(blocks, places):
    count = len(blocks)

    def body(places_ref, *refs):
        out, held, sems, out_sems = refs[count:]
        arrivals = [
            pltpu.make_async_copy(refs[i], held.at[i], sems.at[i]) for i in range(count)
        ]
        leaving = [
            pltpu.make_async_copy(held.at[i], out.at[places_ref[i]], out_sems.at[i])
            for i in range(count)
        ]
        for copy in arrivals:
            copy.start()
        for i in range(count):
            arrivals[i].wait()
            leaving[i].start()
        for copy in leaving:
            copy.wait()

    return pl.pallas_call(
        body,
        in_specs=[pl.BlockSpec(memory_space=pltpu.SMEM)]
        + [pl.BlockSpec(memory_space=pl.ANY)] * len(blocks),
        out_specs=pl.BlockSpec(memory_space=pl.ANY),
        out_shape=jax.ShapeDtypeStruct((len(blocks),) + blocks[0].shape, blocks[0].dtype),
        scratch_shapes=[
            pltpu.VMEM((count,) + blocks[0].shape, blocks[0].dtype),
            pltpu.SemaphoreType.DMA((count,)),
            pltpu.SemaphoreType.DMA((count,)),
        ],
        compiler_params=kernel_params(),
        cost_estimate=short_cost(),
    )(places, *blocks)


def expert_weight_grads(rows, grads, gate_backs, up_backs, hiddens, begin, count, earlier):
    experts, slots, width = rows[0].shape
    units = hiddens[0].shape[2]
    tile = 512
    planes = len(rows)

    def body(*refs):
        rows_in = refs[:planes]
        grads_in = refs[planes : 2 * planes]
        gate_in = refs[2 * planes : 3 * planes]
        up_in = refs[3 * planes : 4 * planes]
        hidden_in = refs[4 * planes : 5 * planes]
        gate_ref, up_ref, down_ref = refs[-3:]
        for left, right, out in (
            (gate_in, rows_in, gate_ref),
            (up_in, rows_in, up_ref),
            (hidden_in, grads_in, down_ref),
        ):
            total = dot_first(left[0][0], right[0][0])
            for p in range(1, planes):
                total = total + dot_first(left[p][0], right[p][0])
            out[0] = total

    wide = pl.BlockSpec((1, slots, tile), lambda j, d: (begin + j, 0, d))
    inner = pl.BlockSpec((1, slots, units), lambda j, d: (begin + j, 0, 0))
    result = pl.BlockSpec((1, units, tile), lambda j, d: (begin + j, 0, d))
    return pl.pallas_call(
        body,
        grid=(count, width // tile),
        in_specs=[wide] * (2 * planes)
        + [inner] * (3 * planes)
        + [pl.BlockSpec(memory_space=pl.ANY)] * len(earlier),
        out_specs=[result] * 3,
        out_shape=[jax.ShapeDtypeStruct((experts, units, width), jnp.float32)] * 3,
        input_output_aliases={5 * planes + i: i for i in range(len(earlier))},
        compiler_params=kernel_params(),
        cost_estimate=short_cost(),
    )(*rows, *grads, *gate_backs, *up_backs, *hiddens, *earlier)


def swap_halves(values):
    lanes = lax.broadcasted_iota(jnp.int32, values.shape, 1)
    return jnp.where(lanes % 64 < 32, pltpu.roll(values, 96, 1), pltpu.roll(values, 32, 1))


def masked_weights(segment_column, segment_line, query, keys, rope, head_rope):
    count = query.shape[0]
    raw = dot_last(query, keys) + dot_last(rope, head_rope)
    after_key = lax.broadcasted_iota(jnp.int32, (count, count), 0) >= lax.broadcasted_iota(
        jnp.int32, (count, count), 1
    )
    allowed = (segment_column == segment_line) & after_key
    scores = jnp.where(allowed, raw * SCORE_SCALE, -1e30)
    exponent = jnp.exp(scores - jnp.max(scores, axis=1, keepdims=True))
    return exponent / jnp.sum(exponent, axis=1, keepdims=True)


def head_ropes(key_rope):
    zeros = jnp.zeros_like(key_rope)
    return [
        jnp.concatenate([key_rope, zeros], axis=1),
        jnp.concatenate([zeros, key_rope], axis=1),
    ]


def attend(normed, latent_normed, ropes, turns, segments, dense):
    count, width = normed.shape
    rows, block, columns = dense.shape
    pairs = QUERY_COLUMNS // 384
    rank = latent_normed.shape[1]
    share = rank // rows
    flat = dense.reshape(rows * block, columns)
    quarters = dense.reshape(rows, block // share, share, columns)

    def body(
        normed_ref,
        latent_ref,
        rope0_ref,
        rope1_ref,
        cosine_ref,
        sine_ref,
        column_ref,
        line_ref,
        query_weight_ref,
        expand_ref,
        output_ref,
        query_ref,
        keys_ref,
        mixed_ref,
        attended_ref,
        total,
    ):
        step = pl.program_id(0)
        query = dot_plain(normed_ref[...], query_weight_ref[...])
        rope = query[:, 256:]
        rope = rope * cosine_ref[...] + swap_halves(rope) * sine_ref[...]
        query = jnp.concatenate([query[:, :256], rope], axis=1).astype(jnp.bfloat16)
        expand = expand_ref[...].reshape(rank, 512)
        keys = dot_plain(latent_ref[...], expand).astype(jnp.bfloat16)
        query_ref[...] = query
        keys_ref[...] = keys
        mixed = []
        for head, rope_ref in enumerate((rope0_ref, rope1_ref)):
            weights = masked_weights(
                column_ref[:, :1],
                line_ref[:1],
                query[:, 128 * head : 128 * head + 128],
                keys[:, 256 * head : 256 * head + 128],
                query[:, 256:],
                rope_ref[...],
            )
            values = keys[:, 256 * head + 128 : 256 * head + 256]
            mixed.append(dot_plain(weights.astype(jnp.bfloat16), values).astype(jnp.bfloat16))
        mixed = jnp.concatenate(mixed, axis=1)
        mixed_ref[...] = mixed
        part = dot_last(mixed, output_ref[...])

        @pl.when(step == 0)
        def _():
            total[...] = part

        @pl.when(step > 0)
        def _():
            total[...] += part

        @pl.when(step == pairs - 1)
        def _():
            attended_ref[...] = total[...].astype(jnp.bfloat16)

    whole = lambda shape: pl.BlockSpec(shape, lambda h: (0,) * len(shape))
    return pl.pallas_call(
        body,
        grid=(pairs,),
        in_specs=[
            whole((count, width)),
            whole((count, rank)),
            whole((count, 128)),
            whole((count, 128)),
            whole((count, 128)),
            whole((count, 128)),
            whole((count, 128)),
            whole((8, count)),
            pl.BlockSpec((width, 384), lambda h: (0, h)),
            pl.BlockSpec((rows, 1, share, 512), lambda h: (0, h, 0, QUERY_COLUMNS // 512)),
            pl.BlockSpec((width, 256), lambda h: (0, (QUERY_COLUMNS + 512) // 256 + h)),
        ],
        out_specs=[
            pl.BlockSpec((count, 384), lambda h: (0, h)),
            pl.BlockSpec((count, 512), lambda h: (0, h)),
            pl.BlockSpec((count, 256), lambda h: (0, h)),
            whole((count, width)),
        ],
        out_shape=[
            jax.ShapeDtypeStruct((count, 384 * pairs), jnp.bfloat16),
            jax.ShapeDtypeStruct((count, 512 * pairs), jnp.bfloat16),
            jax.ShapeDtypeStruct((count, 256 * pairs), jnp.bfloat16),
            jax.ShapeDtypeStruct((count, width), jnp.bfloat16),
        ],
        scratch_shapes=[pltpu.VMEM((count, width), jnp.float32)],
        compiler_params=kernel_params(),
        cost_estimate=short_cost(),
    )(normed, latent_normed, *ropes, *turns, *segments, flat, quarters, flat)


def attend_back(upstream, query, keys, ropes, turns, segments, dense, rank):
    count, width = upstream.shape
    rows, block, columns = dense.shape
    pairs = QUERY_COLUMNS // 384
    share = rank // rows
    flat = dense.reshape(rows * block, columns)
    quarters = dense.reshape(rows, block // share, share, columns)

    def body(
        upstream_ref,
        query_ref,
        keys_ref,
        rope0_ref,
        rope1_ref,
        cosine_ref,
        sine_ref,
        column_ref,
        line_ref,
        query_weight_ref,
        expand_ref,
        output_ref,
        query_back_ref,
        keys_back_ref,
        rope_back_ref,
        latent_back_ref,
        input_ref,
        total,
    ):
        step = pl.program_id(0)
        mixed_back = dot_plain(upstream_ref[...], output_ref[...]).astype(jnp.bfloat16)
        query = query_ref[...]
        keys = keys_ref[...]
        rope = query[:, 256:]
        lanes = lax.broadcasted_iota(jnp.int32, (count, 128), 1)
        query_back = []
        keys_back = []
        rope_back = 0.0
        key_rope_back = 0.0
        for head, rope_ref in enumerate((rope0_ref, rope1_ref)):
            query_nope = query[:, 128 * head : 128 * head + 128]
            key_nope = keys[:, 256 * head : 256 * head + 128]
            values = keys[:, 256 * head + 128 : 256 * head + 256]
            mixed_head = mixed_back[:, 128 * head : 128 * head + 128]
            weights = masked_weights(
                column_ref[:, :1], line_ref[:1], query_nope, key_nope, rope, rope_ref[...]
            )
            weight_back = dot_last(mixed_head, values)
            center = jnp.sum(weight_back * weights, axis=1, keepdims=True)
            raw_back = (weights * (weight_back - center) * SCORE_SCALE).astype(jnp.bfloat16)
            query_back.append(dot_plain(raw_back, key_nope))
            rope_back = rope_back + dot_plain(raw_back, rope_ref[...])
            keys_back.append(dot_first(raw_back, query_nope))
            keys_back.append(dot_first(weights.astype(jnp.bfloat16), mixed_head))
            mine = lanes // 64 == head
            key_rope_back = key_rope_back + jnp.where(mine, dot_first(raw_back, rope), 0.0)
        rope_back = rope_back * cosine_ref[...] - swap_halves(rope_back) * sine_ref[...]
        query_back = jnp.concatenate(query_back + [rope_back], axis=1).astype(jnp.bfloat16)
        keys_back = jnp.concatenate(keys_back, axis=1).astype(jnp.bfloat16)
        query_back_ref[...] = query_back
        keys_back_ref[...] = keys_back
        latent_part = dot_last(keys_back, expand_ref[...].reshape(rank, 512))
        input_part = dot_last(query_back, query_weight_ref[...])

        @pl.when(step == 0)
        def _():
            rope_back_ref[...] = key_rope_back
            latent_back_ref[...] = latent_part
            total[...] = input_part

        @pl.when(step > 0)
        def _():
            rope_back_ref[...] += key_rope_back
            latent_back_ref[...] += latent_part
            total[...] += input_part

        @pl.when(step == pairs - 1)
        def _():
            input_ref[...] = total[...].astype(jnp.bfloat16)

    whole = lambda shape: pl.BlockSpec(shape, lambda h: (0,) * len(shape))
    return pl.pallas_call(
        body,
        grid=(pairs,),
        in_specs=[
            whole((count, width)),
            pl.BlockSpec((count, 384), lambda h: (0, h)),
            pl.BlockSpec((count, 512), lambda h: (0, h)),
            whole((count, 128)),
            whole((count, 128)),
            whole((count, 128)),
            whole((count, 128)),
            whole((count, 128)),
            whole((8, count)),
            pl.BlockSpec((width, 384), lambda h: (0, h)),
            pl.BlockSpec((rows, 1, share, 512), lambda h: (0, h, 0, QUERY_COLUMNS // 512)),
            pl.BlockSpec((width, 256), lambda h: (0, (QUERY_COLUMNS + 512) // 256 + h)),
        ],
        out_specs=[
            pl.BlockSpec((count, 384), lambda h: (0, h)),
            pl.BlockSpec((count, 512), lambda h: (0, h)),
            whole((count, 128)),
            whole((count, rank)),
            whole((count, width)),
        ],
        out_shape=[
            jax.ShapeDtypeStruct((count, 384 * pairs), jnp.bfloat16),
            jax.ShapeDtypeStruct((count, 512 * pairs), jnp.bfloat16),
            jax.ShapeDtypeStruct((count, 128), jnp.float32),
            jax.ShapeDtypeStruct((count, rank), jnp.float32),
            jax.ShapeDtypeStruct((count, width), jnp.bfloat16),
        ],
        scratch_shapes=[pltpu.VMEM((count, width), jnp.float32)],
        compiler_params=kernel_params(),
        cost_estimate=short_cost(),
    )(upstream, query, keys, *ropes, *turns, *segments, flat, quarters, flat)


def on_device(
    inputs,
    segment_ids,
    routes,
    norm_gain,
    query_weight,
    latent_weight,
    latent_gain,
    expand_weight,
    output_weight,
    ffn_gain,
    router_weight,
    expert_gate,
    expert_up,
    expert_down,
    shared_gate,
    shared_up,
    shared_down,
    out_grad,
):
    bf16 = jnp.bfloat16
    f32 = jnp.float32
    rows_count = inputs.shape[0]
    row_devices = lax.axis_size("row")
    row_place = lax.axis_index("row")
    first = lax.axis_index("col") == 0
    expert_count = EXP_DEV * row_devices
    capacity = 4 * rows_count * TOPK // (3 * expert_count)
    segment_row = segment_ids[0]
    places = jnp.arange(rows_count, dtype=jnp.int32)

    steps = jnp.arange(row_devices, dtype=jnp.int32)
    arrival = (((row_place // 4 - steps // 4) % 4) * 4 + ((row_place % 4) ^ (steps % 4))).astype(
        jnp.int32
    )
    block = latent_weight.shape[0]
    share = expand_weight.shape[0]
    quarter = expand_weight.shape[1] * share // block
    query_width = query_weight.shape[1]
    latent_width = latent_weight.shape[1]

    slab = pack_weights(
        query_weight,
        expand_weight,
        output_weight,
        latent_weight,
        router_weight,
        routes.astype(bf16).reshape(block, -1),
    )
    shared_share = shared_gate.shape[1] // row_devices
    blocks = {}
    blocks[0] = slab
    blocks[4], blocks[2], inputs_other, gains_other = together(
        turn_planes(slab),
        swap_rows(slab, 2),
        swap_cols(inputs),
        swap_cols(jnp.stack([norm_gain, ffn_gain])),
    )
    shared_packed = jnp.stack(
        [after(shared_gate, inputs_other).T, after(shared_up, inputs_other).T, shared_down], axis=0
    )
    shared_packed = shared_packed.reshape(3, row_devices, shared_share, -1).transpose(1, 0, 2, 3)
    (
        blocks[8],
        blocks[6],
        blocks[1],
        blocks[3],
        out_grad_other,
    ) = together(
        turn_planes(blocks[4]),
        swap_rows(blocks[4], 2),
        swap_rows(blocks[0], 1),
        swap_rows(blocks[2], 1),
        swap_cols(after(out_grad, inputs_other)),
    )
    upstream_bf16 = jnp.where(
        first,
        jnp.concatenate([out_grad, out_grad_other], axis=1),
        jnp.concatenate([out_grad_other, out_grad], axis=1),
    )
    grad_rows = Spread(sent_rows(upstream_bf16, first))
    blocks[12], blocks[10], blocks[5], blocks[7], got = together(
        turn_planes(blocks[8]),
        swap_rows(blocks[8], 2),
        swap_rows(blocks[4], 1),
        swap_rows(blocks[6], 1),
        swap_cols(grad_rows.sent((0, 0))[0]),
    )
    grad_rows.got(got, [0], (0, 0))
    source = jnp.where(
        first,
        jnp.concatenate([inputs, inputs_other], axis=1),
        jnp.concatenate([inputs_other, inputs], axis=1),
    ).astype(f32)
    gains = jnp.stack([norm_gain, ffn_gain])
    gains = jnp.where(
        first,
        jnp.concatenate([gains, gains_other], axis=1),
        jnp.concatenate([gains_other, gains], axis=1),
    )
    gain_one = gains[:1]
    gain_two = gains[1:]
    scale_one = lax.rsqrt(jnp.mean(source * source, axis=1, keepdims=True) + epsilon)
    unit_one = source * scale_one
    normed_one = (unit_one * gain_one).astype(bf16)
    cosine, sine = rotation(rows_count, ROPE)
    turns = (
        jnp.concatenate([cosine] * 4, axis=1),
        jnp.concatenate([-sine, sine, -sine, sine], axis=1),
    )
    segments = (
        jnp.broadcast_to(segment_row[:, None], (rows_count, 128)),
        jnp.broadcast_to(segment_row[None], (8, rows_count)),
    )
    passed, starts = batch(grad_rows.passed((0, 0, 0), (0, 0, 1)))
    (
        blocks[14],
        blocks[9],
        blocks[11],
        passed,
        shared_packed,
        normed_one,
        cosine,
        sine,
        turns,
        segments,
    ) = together(
        swap_rows(blocks[12], 2),
        swap_rows(blocks[8], 1),
        swap_rows(blocks[10], 1),
        swap_rows(passed, 1),
        shared_packed,
        normed_one,
        cosine,
        sine,
        turns,
        segments,
    )
    grad_rows.taken(passed, starts, (0, 0, 0), (0, 0, 1))
    grad_rows.held[0, 0] = after(grad_rows.held[0, 0], blocks[14])
    grad_turned = grad_rows.turn(1)
    blocks[13], blocks[15] = together(swap_rows(blocks[12], 1), swap_rows(blocks[14], 1))
    dense = assemble([blocks[i] for i in range(4 * PLANES)], arrival)
    flat_dense = dense.reshape(D, -1)
    latent_full = flat_dense[:, QUERY_COLUMNS + 1536 : QUERY_COLUMNS + 1536 + latent_width]
    router_full = flat_dense[
        :, QUERY_COLUMNS + 1536 + latent_width : QUERY_COLUMNS + 1536 + latent_width + expert_count
    ]
    latent = jnp.dot(normed_one, latent_full, preferred_element_type=f32).astype(bf16)
    compressed = latent[:, :RANK].astype(f32)
    latent_scale = lax.rsqrt(jnp.mean(compressed * compressed, axis=1, keepdims=True) + epsilon)
    latent_unit = compressed * latent_scale
    latent_normed = (latent_unit * latent_gain).astype(bf16)
    key_rope = rotate(latent[:, RANK:].astype(f32), cosine, sine).astype(bf16)
    ropes = head_ropes(key_rope)
    routes_all = flat_dense[
        :, QUERY_COLUMNS + 1536 + latent_width + expert_count :
    ][:, : rows_count * TOPK // block]
    routes_all = routes_all.reshape(row_devices, rows_count, TOPK).transpose(0, 2, 1)[arrival]
    routes_all = routes_all.astype(jnp.int32)

    routes_all = local_tokens(routes_all, 2, first)
    held_experts = row_place * EXP_DEV + jnp.arange(EXP_DEV, dtype=jnp.int32)
    hits = jnp.any(routes_all[:, :, None, :] == held_experts[None, None, :, None], axis=1)
    upper = (places[:, None] <= places[None, :]).astype(bf16)
    ranks = jnp.einsum("sjt,tu->sju", hits.astype(bf16), upper, preferred_element_type=f32)
    codes = jnp.where(hits, ranks.astype(jnp.int32) - 1, -1)
    codes = jnp.pad(codes, ((0, 0), (0, 8 - EXP_DEV), (0, 0)), constant_values=-1)
    plane_codes = [codes[p * FAMILIES : (p + 1) * FAMILIES] for p in range(PLANES)]

    latent_normed, plane_codes, grad_rows.held[0, 1], grad_rows.held[1, 0] = together(
        latent_normed, plane_codes, grad_rows.cross(0), grad_turned
    )

    query, keys, mixed, attended_part = attend(
        normed_one, latent_normed, ropes, turns, segments, dense
    )
    sent, starts = batch(grad_rows.sent((0, 1), (1, 0)))
    passed, passed_starts = batch(grad_rows.passed((0, 1, 0), (1, 0, 0)))
    (
        query,
        attended_part,
        grad_rows.held[2, 0],
        grad_rows.held[1, 1],
        got,
        passed,
    ) = together(
        query,
        attended_part,
        grad_rows.turn(2),
        grad_rows.cross(1),
        swap_cols(sent),
        swap_rows(passed, 1),
    )
    grad_rows.got(got, starts, (0, 1), (1, 0))
    grad_rows.taken(passed, passed_starts, (0, 1, 0), (1, 0, 0))

    picked = {}

    def pick(plane, *others):
        picked[plane] = pick_grads(
            grad_rows.family(plane), after(plane_codes[plane], *others), shared_last, capacity
        )
        return picked[plane]

    def pass_alone(spread, key):
        spread.taken(swap_rows(spread.passed(key)[0], 1), [0], key)

    passed, starts = batch(grad_rows.passed((0, 1, 1), (1, 0, 1), (1, 1, 0)))
    partner_part = jnp.concatenate(
        [
            attended_part[:COMMON],
            jnp.where(first, attended_part[SENT:], attended_part[COMMON:SENT]),
        ],
        axis=0,
    )
    (
        attended_other,
        shared_here,
        grad_rows.held[2, 1],
        passed,
    ) = together(
        swap_cols(partner_part),
        lax.all_to_all(
            after(shared_packed, attended_part), "row", split_axis=0, concat_axis=0, tiled=True
        ),
        grad_rows.cross(2),
        swap_rows(passed, 1),
    )
    grad_rows.taken(passed, starts, (0, 1, 1), (1, 0, 1), (1, 1, 0))
    attended_sent = sent_rows(attended_part, first).astype(f32) + attended_other.astype(f32)
    middle_sent = sent_rows(source, first) + attended_sent
    scale_sent = lax.rsqrt(jnp.mean(middle_sent * middle_sent, axis=1, keepdims=True) + epsilon)
    normed_sent = (middle_sent * scale_sent * gain_two).astype(bf16)
    rows = Spread(normed_sent)

    shared_here = shared_here.transpose(1, 2, 0, 3).reshape(3, shared_share, D)
    shared_here = jnp.pad(shared_here, ((0, 0), (0, SHARED_PAD - shared_share), (0, 0)))
    shared_pair = shared_here[:2].reshape(2 * SHARED_PAD, D)
    shared_last = shared_here[2]

    sent, starts = batch(rows.sent((0, 0)) + grad_rows.sent((1, 1)))
    rows.held[1, 0], rows.held[0, 1], got, shared_pair, shared_last = together(
        rows.turn(1), rows.cross(0), swap_cols(sent), shared_pair, shared_last
    )
    rows.got(got, starts, (0, 0))
    grad_rows.got(got, starts[1:], (1, 1))
    router_turned = router_full.T
    router_held = lax.dynamic_slice_in_dim(
        jnp.concatenate([router_turned, router_turned], axis=0),
        row_place * EXP_DEV,
        expert_count,
        0,
    )
    pass_alone(grad_rows, (1, 1, 1))
    sent, starts = batch(rows.sent((0, 1), (1, 0)))
    passed, passed_starts = batch(rows.passed((0, 0, 0), (0, 0, 1), (0, 1, 0)))
    (
        rows.held[2, 0],
        rows.held[1, 1],
        got,
        passed,
        picked[0],
        picked[1],
        router_held,
    ) = together(
        rows.turn(2),
        rows.cross(1),
        swap_cols(sent),
        swap_rows(passed, 1),
        pick(0),
        pick(1),
        router_held,
    )
    rows.got(got, starts, (0, 1), (1, 0))
    rows.taken(passed, passed_starts, (0, 0, 0), (0, 0, 1), (0, 1, 0))

    experts = (expert_gate, expert_up, expert_down)
    begun = {}
    ran = {}

    def start_plane(plane, *others):
        begun[plane] = pick_rows(
            rows.family(plane),
            grad_rows.family(plane),
            after(plane_codes[plane], *others),
            router_held,
            shared_pair,
            picked[plane][1],
            capacity,
        )
        return begun[plane]

    def run_plane(plane):
        ran[plane] = run_experts(begun[plane][0], picked[plane][0], begun[plane][1], *experts)
        return ran[plane]

    def back_sibling(plane):
        return sum_tokens(
            ran[plane][1],
            plane_codes[plane],
            begun[plane][3],
            shared_pair,
            capacity,
            1,
            None,
            ran[plane][5],
        )

    def back_mine(plane, received):
        return sum_tokens(
            ran[plane][1],
            plane_codes[plane],
            begun[plane][3],
            shared_pair,
            capacity,
            0,
            received,
            ran[plane][5],
        )

    def sum_sibling(plane):
        return sum_tokens(
            ran[plane][0], plane_codes[plane], begun[plane][2], shared_last, capacity, 1
        )[0]

    def sum_mine(plane, received):
        return sum_tokens(
            ran[plane][0], plane_codes[plane], begun[plane][2], shared_last, capacity, 0, received
        )

    def unique_out(mine):
        return swap_cols(mine[1])

    def across_out(mine, unique):
        return swap_rows(add_unique(mine[0], unique, 1), 2)

    def own_sum(mine, unique, crossed):
        return add_unique(mine[0], unique, 0) + crossed

    pass_alone(rows, (0, 1, 1))
    sent, starts = batch(rows.sent((1, 1), (2, 0)))
    passed, passed_starts = batch(rows.passed((1, 0, 0), (1, 1, 0), (1, 0, 1)))
    rows.held[3, 0], rows.held[2, 1], got, passed = together(
        rows.turn(3), rows.cross(2), swap_cols(sent), swap_rows(passed, 1)
    )
    rows.got(got, starts, (1, 1), (2, 0))
    rows.taken(passed, passed_starts, (1, 0, 0), (1, 1, 0), (1, 0, 1))

    pass_alone(rows, (1, 1, 1))
    sent, starts = batch(rows.sent((2, 1), (3, 0)))
    passed, passed_starts = batch(rows.passed((2, 0, 0), (2, 1, 0), (2, 0, 1)))
    begun[1], rows.held[3, 1], grad_rows.held[3, 0], got, passed = together(
        start_plane(1), rows.cross(3), grad_rows.turn(3), swap_cols(sent), swap_rows(passed, 1)
    )
    rows.got(got, starts, (2, 1), (3, 0))
    rows.taken(passed, passed_starts, (2, 0, 0), (2, 1, 0), (2, 0, 1))

    ran[1] = run_plane(1)
    back_1 = back_sibling(1)
    sent, starts = batch(rows.sent((3, 1)) + grad_rows.sent((2, 0), (2, 1)))
    passed = [
        batch(rows.passed((2, 1, 1), (3, 0, 1))),
        batch(rows.passed((3, 0, 0), (3, 1, 0))),
        batch(grad_rows.passed((2, 0, 0), (2, 1, 0))),
    ]
    ran[1], back_1, grad_rows.held[3, 1], got, passed_got = together(
        ran[1],
        back_1,
        grad_rows.cross(3),
        swap_cols(sent),
        [swap_rows(rows_passed, 1) for rows_passed, _ in passed],
    )
    rows.got(got, starts, (3, 1))
    grad_rows.got(got, starts[1:], (2, 0), (2, 1))
    rows.taken(passed_got[0], passed[0][1], (2, 1, 1), (3, 0, 1))
    rows.taken(passed_got[1], passed[1][1], (3, 0, 0), (3, 1, 0))
    grad_rows.taken(passed_got[2], passed[2][1], (2, 0, 0), (2, 1, 0))

    passed, passed_starts = batch(grad_rows.passed((2, 0, 1), (2, 1, 1)))
    grad_rows.taken(swap_rows(passed, 1), passed_starts, (2, 0, 1), (2, 1, 1))
    sent, starts = batch(grad_rows.sent((3, 0), (3, 1)))
    passed, passed_starts = batch(
        rows.passed((3, 1, 1)) + grad_rows.passed((3, 0, 0), (3, 1, 0))
    )
    picked[2] = pick(2)
    begun[2] = start_plane(2)
    picked[2], begun[2], back_got, got, passed = together(
        picked[2], begun[2], swap_rows(back_1[0], 1), swap_cols(sent), swap_rows(passed, 1)
    )
    grad_rows.got(got, starts, (3, 0), (3, 1))
    rows.taken(passed, passed_starts, (3, 1, 1))
    grad_rows.taken(passed, passed_starts[1:], (3, 0, 0), (3, 1, 0))
    passed, passed_starts = batch(grad_rows.passed((3, 0, 1), (3, 1, 1)))
    grad_rows.taken(swap_rows(passed, 1), passed_starts, (3, 0, 1), (3, 1, 1))
    back_mine_1 = back_mine(1, back_got)
    sum_1 = sum_sibling(1)
    back_mine_1, sum_1 = together(back_mine_1, sum_1)

    ran[2] = run_plane(2)
    back_2 = back_sibling(2)
    ran[2], back_2, back_unique, sum_got = together(
        ran[2], back_2, unique_out(back_mine_1), swap_rows(sum_1, 1)
    )
    sum_mine_1 = sum_mine(1, sum_got)

    picked[3] = pick(3)
    begun[3] = start_plane(3)
    picked[3], begun[3], back_got, back_crossed, sum_unique = together(
        picked[3],
        begun[3],
        swap_rows(back_2[0], 1),
        across_out(back_mine_1, back_unique),
        unique_out(sum_mine_1),
    )
    back = own_sum(back_mine_1, back_unique, back_crossed)
    back_mine_2 = back_mine(2, back_got)
    sum_2 = sum_sibling(2)
    attended_rest = after(attended_sent[COMMON:], picked[3]).astype(bf16)
    back_mine_2, sum_2, back, attended_rest = together(
        back_mine_2, sum_2, back, swap_cols(attended_rest)
    )

    ran[3] = run_plane(3)
    back_3 = back_sibling(3)
    ran[3], back_3, back, back_unique, sum_got, sum_crossed = together(
        ran[3],
        back_3,
        turn_planes(back),
        unique_out(back_mine_2),
        swap_rows(sum_2, 1),
        across_out(sum_mine_1, sum_unique),
    )
    result = own_sum(sum_mine_1, sum_unique, sum_crossed)
    sum_mine_2 = sum_mine(2, sum_got)
    sum_mine_2, result = together(sum_mine_2, result)

    attended_rest = after(attended_rest, sum_mine_2).astype(f32)
    attended_mine = attended_sent[COMMON:]
    middle = source + jnp.concatenate(
        [
            attended_sent[:COMMON],
            jnp.where(first, attended_mine, attended_rest),
            jnp.where(first, attended_rest, attended_mine),
        ],
        axis=0,
    )
    scale_two = lax.rsqrt(jnp.mean(middle * middle, axis=1, keepdims=True) + epsilon)
    unit_two = middle * scale_two
    normed_two = (unit_two * gain_two).astype(bf16)
    logits = jnp.dot(normed_two, router_full, preferred_element_type=f32)
    log_total = jax.nn.logsumexp(logits, axis=1, keepdims=True)
    chances = jnp.exp(logits - log_total)

    begun[0] = start_plane(0, sum_mine_2)
    begun[0], back_got, back_crossed, sum_unique, result, normed_two, chances = together(
        begun[0],
        swap_rows(back_3[0], 1),
        across_out(back_mine_2, back_unique),
        unique_out(sum_mine_2),
        turn_planes(result),
        normed_two,
        chances,
    )
    back = back + own_sum(back_mine_2, back_unique, back_crossed)
    back_mine_3 = back_mine(3, back_got)
    sum_3 = sum_sibling(3)
    back_mine_3, sum_3, back = together(back_mine_3, sum_3, back)

    ran[0] = run_plane(0)
    back_0 = back_sibling(0)
    ran[0], back_0, back, back_unique, sum_got, sum_crossed = together(
        ran[0],
        back_0,
        turn_planes(back),
        unique_out(back_mine_3),
        swap_rows(sum_3, 1),
        across_out(sum_mine_2, sum_unique),
    )
    result = result + own_sum(sum_mine_2, sum_unique, sum_crossed)
    sum_mine_3 = sum_mine(3, sum_got)
    sum_mine_3, result = together(sum_mine_3, result)

    kept = [
        (begun[plane][0], picked[plane][0], ran[plane][3], ran[plane][4], ran[plane][2])
        for plane in range(PLANES)
    ]
    kept = [list(part) for part in zip(*kept)]
    half = EXP_DEV // 2
    expert_parts = expert_weight_grads(*kept, 0, half, [])
    expert_parts, back_got, back_crossed, sum_unique, result = together(
        expert_parts,
        swap_rows(back_0[0], 1),
        across_out(back_mine_3, back_unique),
        unique_out(sum_mine_3),
        turn_planes(result),
    )
    back = back + own_sum(back_mine_3, back_unique, back_crossed)
    back_mine_0 = back_mine(0, back_got)
    sum_0 = sum_sibling(0)
    back_mine_0, sum_0, back = together(back_mine_0, sum_0, back)

    expert_parts = expert_weight_grads(*kept, half, EXP_DEV - half, expert_parts)
    expert_parts, back, back_unique, sum_got, common_crossed = together(
        expert_parts,
        turn_planes(back),
        unique_out(back_mine_0),
        swap_rows(sum_0, 1),
        swap_rows(back_mine_0[0][1, :COMMON], 2),
    )
    expert_gate_grad, expert_up_grad, expert_down_grad = expert_parts
    common = back[:COMMON] + back_mine_0[0][0, :COMMON] + common_crossed
    unique_rest = back_mine_0[0][:, COMMON:] + back_unique
    sum_mine_0 = sum_mine(0, sum_got)

    gate_grad_dense = [
        jnp.stack([mine[2], sibling[1]], axis=1)[:, :, :EXP_DEV]
        for mine, sibling in (
            (back_mine_0, back_0),
            (back_mine_1, back_1),
            (back_mine_2, back_2),
            (back_mine_3, back_3),
        )
    ]
    gate_grad_dense = jnp.stack(gate_grad_dense).reshape(row_devices, EXP_DEV, rows_count)
    gate_grad_dense = local_tokens(gate_grad_dense, 2, first)[arrival]
    gate_grad_dense = lax.all_to_all(
        gate_grad_dense, "row", split_axis=0, concat_axis=0, tiled=True
    ).reshape(expert_count, rows_count)
    shared_grads = sum([begun[p][4] for p in range(1, PLANES)], begun[0][4])
    shared_grads = shared_grads.reshape(3, SHARED_PAD, D)[:, :shared_share]
    shared_grads = (
        shared_grads.astype(bf16)
        .reshape(3, shared_share, row_devices, -1)
        .transpose(2, 0, 1, 3)
    )
    gate_grad_dense = gate_grad_dense + swap_cols(gate_grad_dense)
    weighted_gates = gate_grad_dense.T * chances
    logit_grads = (
        weighted_gates - chances * jnp.sum(weighted_gates, axis=1, keepdims=True)
    ).astype(bf16)
    router_back = jnp.einsum("te,de->td", logit_grads, router_full, preferred_element_type=f32)
    unique_crossed, common_other, sum_mine_0, shared_grads, router_back, logit_grads = together(
        swap_rows(unique_rest[1], 2),
        swap_cols(common),
        sum_mine_0,
        shared_grads,
        router_back,
        logit_grads,
    )
    unique_mine = back[COMMON:] + unique_rest[0] + unique_crossed
    shared_grads = lax.all_to_all(shared_grads, "row", split_axis=0, concat_axis=0, tiled=True)
    unique_other = swap_cols(unique_mine)
    shared_grads = shared_grads.transpose(1, 0, 2, 3).reshape(3, row_devices * shared_share, -1)
    shared_grads = shared_grads.astype(f32)
    shared_gate_grad = shared_grads[0].T
    shared_up_grad = shared_grads[1].T
    shared_down_grad = shared_grads[2]

    upstream = upstream_bf16.astype(f32)
    normed_two_back = router_back + jnp.concatenate(
        [
            common.astype(f32) + common_other.astype(f32),
            jnp.where(first, unique_mine, unique_other).astype(f32),
            jnp.where(first, unique_other, unique_mine).astype(f32),
        ],
        axis=0,
    )
    ffn_gain_part = jnp.sum(normed_two_back * unit_two, axis=0)
    weighted = normed_two_back * gain_two
    average = jnp.mean(weighted * unit_two, axis=1, keepdims=True)
    middle_back = upstream + scale_two * (weighted - unit_two * average)
    attended_back = middle_back.astype(bf16)

    def by_plane(total):
        return total.reshape((PLANES, 2) + total.shape[1:])

    output_sibling = block_grads(arrival, attended_back, mixed, 256, 1)
    query_back, expanded_back, key_rope_back, latent_normed_back, input_part = attend_back(
        attended_back, query, keys, ropes, turns, segments, dense, RANK
    )
    query_back, last_unique, output_got, sum_crossed = together(
        query_back,
        unique_out(sum_mine_0),
        swap_rows(output_sibling, 1),
        across_out(sum_mine_3, sum_unique),
    )
    result = result + own_sum(sum_mine_3, sum_unique, sum_crossed)

    latent_gain_part = jnp.sum(latent_normed_back * latent_unit, axis=0)
    latent_weighted = latent_normed_back * latent_gain
    compressed_back = latent_scale * (
        latent_weighted
        - latent_unit * jnp.mean(latent_weighted * latent_unit, axis=1, keepdims=True)
    )
    key_rope_back = key_rope_back[:, :ROPE] + key_rope_back[:, ROPE:]
    rope_back = unrotate(key_rope_back, cosine, sine)
    latent_part = jnp.concatenate([compressed_back, rope_back], axis=1).astype(bf16)
    latent_turned = latent_normed.T
    wide_sibling = block_grads(
        arrival, normed_one, query_back, 384, 1, latent_turned, expanded_back
    )
    wide_sibling, latent_part = together(wide_sibling, latent_part)
    output_total = by_plane(
        block_grads(
            arrival, after(attended_back, wide_sibling), mixed, 256, 0, received=output_got
        )
    )
    weighted_part = jnp.sum(
        after(input_part, wide_sibling).astype(f32) * gain_one * unit_one, axis=1
    )
    wide_got, latent_other, output_total, weighted_part, result = together(
        swap_rows(wide_sibling, 1),
        swap_cols(latent_part),
        output_total,
        weighted_part,
        turn_planes(result),
    )
    latent_back = (latent_part.astype(f32) + latent_other.astype(f32)).astype(bf16)
    wide_total = by_plane(
        block_grads(
            arrival, normed_one, query_back, 384, 0, latent_turned, expanded_back, wide_got
        )
    )
    narrow_sibling = narrow_grads(
        arrival, normed_one, after(latent_back, wide_total), normed_two, logit_grads, 1
    )
    input_sent = other_columns(input_part, first)
    half_rows = rows_count // 2
    small_part = jnp.concatenate([weighted_part, latent_gain_part]).reshape(-1, 128)
    wide_total, narrow_sibling, sum_crossed, crossed_output, input_low, small_other = together(
        wide_total,
        narrow_sibling,
        across_out(sum_mine_0, last_unique),
        [swap_rows(output_total[p, 1], 2) for p in (1, 2)],
        swap_cols(input_sent[:half_rows]),
        swap_cols(small_part),
    )
    sum_sent = result + own_sum(sum_mine_0, last_unique, sum_crossed)
    output_sums = [output_total[p, 0] + crossed_output[p - 1] for p in (1, 2)]
    narrow_mine = narrow_grads(
        arrival, normed_one, latent_back, after(normed_two, wide_total), logit_grads, 0
    )
    crossed, crossed_output, moved_output, narrow_got, narrow_mine, input_high = together(
        swap_rows(wide_total[1, 1], 2),
        swap_rows(output_total[3, 1], 2),
        turn_planes(output_sums[0]),
        swap_rows(narrow_sibling, 1),
        narrow_mine,
        swap_cols(input_sent[half_rows:]),
    )
    output_sums.append(output_total[3, 0] + crossed_output)
    moving = [wide_total[1, 0] + crossed]
    moving_output = output_sums[1] + moved_output
    narrow_total = by_plane(narrow_mine + narrow_got)
    crossed, moved, moved_output, crossed_narrow, combined_other = together(
        swap_rows(wide_total[2, 1], 2),
        turn_planes(moving[0]),
        turn_planes(moving_output),
        swap_rows(narrow_total[1, 1], 2),
        swap_cols(other_columns(sum_sent, first)),
    )
    moving = [wide_total[2, 0] + crossed + moved, narrow_total[1, 0] + crossed_narrow]
    moving_output = output_sums[2] + moved_output

    latent_input = jnp.einsum("tc,dc->td", latent_back, latent_full, preferred_element_type=f32)
    small_sum = (small_part + small_other).reshape(-1)
    weighted_sum = small_sum[:rows_count]
    weighted_sum = weighted_sum + jnp.sum(latent_input * gain_one * unit_one, axis=1)
    normed_one_back = (
        own_columns(input_part, first).astype(f32)
        + jnp.concatenate([input_low, input_high], axis=0).astype(f32)
        + own_columns(latent_input, first)
    )
    own_unit = own_columns(unit_one, first)
    norm_gain_part = jnp.sum(normed_one_back * own_unit, axis=0)
    input_grad = own_columns(middle_back, first) + scale_one * (
        normed_one_back * norm_gain - own_unit * (weighted_sum / D)[:, None]
    )
    gain_grads = jnp.concatenate(
        [norm_gain_part, own_columns(ffn_gain_part, first), small_sum[rows_count:]]
    ).reshape(-1, 128)
    crossed, crossed_narrow, moved, crossed_output, gain_grads = together(
        swap_rows(wide_total[3, 1], 2),
        swap_rows(narrow_total[2, 1], 2),
        [turn_planes(part) for part in moving],
        swap_rows(output_total[0, 1], 2),
        gain_grads,
    )
    moving = [
        wide_total[3, 0] + crossed + moved[0],
        narrow_total[2, 0] + crossed_narrow + moved[1],
    ]
    crossed, crossed_narrow, moved, moved_output = together(
        swap_rows(wide_total[0, 1], 2),
        swap_rows(narrow_total[3, 1], 2),
        [turn_planes(part) for part in moving],
        turn_planes(moving_output),
    )
    moving_output = output_total[0, 0] + crossed_output + moved_output
    moving = [
        wide_total[0, 0] + crossed + moved[0],
        narrow_total[3, 0] + crossed_narrow + moved[1],
    ]
    crossed_narrow, moved, others = together(
        swap_rows(narrow_total[0, 1], 2),
        turn_planes(moving[1]),
        [swap_rows(gain_grads, bits) for bits in (1, 2, 3)],
    )
    moving[1] = narrow_total[0, 0] + crossed_narrow + moved
    gain_grads = (gain_grads + others[0]) + (others[1] + others[2])
    others = [swap_rows(gain_grads, bits) for bits in (4, 8, 12)]
    gain_grads = (gain_grads + others[0]) + (others[1] + others[2])
    gain_grads = gain_grads.reshape(-1)
    output_grad, query_grad, expand_grad, latent_grad, router_grad = unpack_grads(
        moving_output, *moving, (query_width, quarter, latent_width)
    )

    combined = merge_rows(own_columns(sum_sent, first), combined_other, first)
    output = (own_columns(middle, first) + combined).astype(bf16)

    width_share = norm_gain.shape[0]
    norm_gain_grad = gain_grads[:width_share]
    ffn_gain_grad = gain_grads[width_share : 2 * width_share]
    latent_gain_grad = gain_grads[2 * width_share :]
    return (
        output,
        input_grad,
        norm_gain_grad,
        query_grad,
        latent_grad,
        latent_gain_grad,
        expand_grad,
        output_grad,
        ffn_gain_grad,
        router_grad,
        expert_gate_grad,
        expert_up_grad,
        expert_down_grad,
        shared_gate_grad,
        shared_up_grad,
        shared_down_grad,
    )


def on_device_general(
    inputs,
    segment_ids,
    routes,
    norm_gain,
    query_weight,
    latent_weight,
    latent_gain,
    expand_weight,
    output_weight,
    ffn_gain,
    router_weight,
    expert_gate,
    expert_up,
    expert_down,
    shared_gate,
    shared_up,
    shared_down,
    out_grad,
):
    bf16 = jnp.bfloat16
    f32 = jnp.float32
    rows_count = inputs.shape[0]
    width_share = inputs.shape[1]
    row_devices = lax.axis_size("row")
    col_devices = lax.axis_size("col")
    col_place = lax.axis_index("col")
    local_heads = query_weight.shape[1] // (NOPE + ROPE)
    expert_count = EXP_DEV * row_devices
    capacity = 4 * rows_count * TOPK // (3 * expert_count)
    score_scale = (NOPE + ROPE) ** (-0.5)
    block_rows = min(512, rows_count)
    segment_row = segment_ids[0]
    places = jnp.arange(rows_count, dtype=jnp.int32)
    (
        query_full,
        latent_full,
        expand_full,
        output_full,
        router_full,
        shared_gate_full,
        shared_up_full,
        shared_down_full,
    ) = (
        lax.all_gather(query_weight, "row", axis=0, tiled=True),
        lax.all_gather(latent_weight, "row", axis=0, tiled=True),
        lax.all_gather(expand_weight, "row", axis=0, tiled=True),
        lax.all_gather(output_weight, "row", axis=1, tiled=True),
        lax.all_gather(router_weight, "row", axis=0, tiled=True),
        lax.all_gather(shared_gate, "row", axis=0, tiled=True),
        lax.all_gather(shared_up, "row", axis=0, tiled=True),
        lax.all_gather(shared_down, "row", axis=1, tiled=True),
    )
    source = inputs.astype(f32)
    scale_one = rms_scale(source)
    unit_one = source * scale_one
    normed_one = spread((unit_one * norm_gain).astype(bf16))
    query = jnp.dot(normed_one, query_full, preferred_element_type=f32).reshape(
        rows_count, local_heads, NOPE + ROPE
    )
    latent = jnp.dot(normed_one, latent_full, preferred_element_type=f32).astype(bf16)
    cosine, sine = rotation(rows_count, ROPE)
    head_cos = cosine[:, None, :]
    head_sin = sine[:, None, :]
    compressed = latent[:, :RANK].astype(f32)
    latent_scale = lax.rsqrt(jnp.mean(compressed * compressed, axis=1, keepdims=True) + epsilon)
    latent_unit = compressed * latent_scale
    latent_normed = (latent_unit * latent_gain).astype(bf16)
    key_rope = rotate(latent[:, RANK:].astype(f32), cosine, sine).astype(bf16)
    expanded = jnp.dot(latent_normed, expand_full, preferred_element_type=f32).reshape(
        rows_count, local_heads, NOPE + VDIM
    )
    key_nope = expanded[..., :NOPE].astype(bf16)
    values_all = expanded[..., NOPE:].astype(bf16)
    query_nope = query[..., :NOPE].astype(bf16)
    query_rope = rotate(query[..., NOPE:], head_cos, head_sin).astype(bf16)

    def block_scores(start):
        ending = start + block_rows
        raw = jnp.einsum("qhd,khd->hqk", query_nope, key_nope, preferred_element_type=f32)
        raw = raw + jnp.einsum("qhd,kd->hqk", query_rope, key_rope, preferred_element_type=f32)
        allowed = (segment_row[start:ending, None] == segment_row[None, :]) & (
            places[None, :] <= places[:, None]
        )
        return jnp.where(allowed[None], raw * score_scale, -1e30)

    start = 0
    scores = block_scores(start)
    top = jnp.max(scores, axis=2, keepdims=True)
    exponent = jnp.exp(scores - top)
    total = jnp.sum(exponent, axis=2, keepdims=True)
    weights = exponent / total
    log_blocks = top + jnp.log(total)
    mixed_blocks = jnp.einsum(
        "hqk,khd->qhd", weights.astype(bf16), values_all, preferred_element_type=f32
    ).astype(bf16)
    mixed = mixed_blocks.reshape(rows_count, local_heads * VDIM)
    attended = mix_sums(jnp.dot(mixed, output_full, preferred_element_type=f32))
    middle = source + attended
    scale_two = rms_scale(middle)
    unit_two = middle * scale_two
    normed_two_share = (unit_two * ffn_gain).astype(bf16)
    normed_two = spread(normed_two_share)
    logits = jnp.dot(normed_two, router_full, preferred_element_type=f32)
    log_total = jax.nn.logsumexp(logits, axis=1, keepdims=True)
    chosen = routes[:, :, None] == jnp.arange(expert_count, dtype=jnp.int32)[None, None, :]
    picked = jnp.sum(jnp.where(chosen, logits[:, None, :], 0.0), axis=2)
    gates = jnp.exp(picked - log_total)
    upstream = out_grad.astype(f32)
    upstream_full = spread(out_grad)
    shared_gate_pre = jnp.dot(normed_two, shared_gate_full, preferred_element_type=f32)
    shared_up_pre = jnp.dot(normed_two, shared_up_full, preferred_element_type=f32)
    shared_hidden = (jax.nn.silu(shared_gate_pre) * shared_up_pre).astype(bf16)
    shared_part = jnp.dot(shared_hidden, shared_down_full, preferred_element_type=f32)
    flat_routes = routes.reshape(-1)
    hits = (flat_routes[:, None] == jnp.arange(expert_count, dtype=jnp.int32)[None, :]).astype(
        jnp.int32
    )
    ranks = jnp.sum((jnp.cumsum(hits, axis=0) - 1) * hits, axis=1)
    owners = jnp.arange(rows_count * TOPK, dtype=jnp.int32) // TOPK
    share_slots = capacity // col_devices
    slot_count = row_devices * share_slots
    buffer_size = EXP_DEV * slot_count
    inside = ranks // share_slots == col_place
    slot_place = jnp.where(
        inside,
        flat_routes % EXP_DEV * slot_count
        + flat_routes // EXP_DEV * share_slots
        + ranks
        - col_place * share_slots,
        buffer_size,
    )
    token_of_slot = (
        jnp.full((buffer_size + 1,), rows_count, jnp.int32).at[slot_place].set(owners)[:buffer_size]
    )
    gate_of_slot = (
        jnp.zeros((buffer_size + 1,), f32).at[slot_place].set(gates.reshape(-1))[:buffer_size]
    )
    position = slot_place.reshape(rows_count, TOPK)
    gate_stack, up_stack, down_stack = (
        lax.all_gather(expert_gate, "col", axis=1, tiled=True),
        lax.all_gather(expert_up, "col", axis=1, tiled=True),
        lax.all_gather(expert_down, "col", axis=1, tiled=True),
    )
    padded_rows = jnp.concatenate([normed_two, jnp.zeros((1, D), bf16)], axis=0)
    outgoing = padded_rows[token_of_slot].reshape(EXP_DEV, slot_count, D)
    arrived = send_rows(outgoing)
    gate_pre = jnp.einsum("jnd,jfd->jnf", arrived, gate_stack, preferred_element_type=f32)
    up_pre = jnp.einsum("jnd,jfd->jnf", arrived, up_stack, preferred_element_type=f32)
    hidden = (jax.nn.silu(gate_pre) * up_pre).astype(bf16)
    expert_result = jnp.einsum(
        "jnf,jfd->jnd", hidden, down_stack, preferred_element_type=f32
    ).astype(bf16)
    returned = return_rows(expert_result).reshape(buffer_size, D)
    returned = jnp.concatenate([returned, jnp.zeros((1, D), bf16)], axis=0)
    slot_values = returned[position].astype(f32)
    combined = mix_sums(jnp.sum(gates[:, :, None] * slot_values, axis=1) + shared_part)
    upstream_wide = upstream_full.astype(f32)
    gate_partial = jnp.sum(upstream_wide[:, None, :] * slot_values, axis=2)
    output = (middle + combined).astype(bf16)
    gate_grads = lax.psum(gate_partial, "col")
    chances = jnp.exp(logits - log_total)
    weighted_gates = gate_grads * gates
    logit_grads = (
        jnp.sum(jnp.where(chosen, weighted_gates[:, :, None], 0.0), axis=1)
        - chances * jnp.sum(weighted_gates, axis=1, keepdims=True)
    ).astype(bf16)
    router_rows = lax.dynamic_slice_in_dim(router_full, col_place * width_share, width_share, 0)
    router_back = jnp.einsum("te,de->td", logit_grads, router_rows, preferred_element_type=f32)
    router_grad_part = jnp.einsum("td,te->de", normed_two, logit_grads, preferred_element_type=f32)
    shared_hidden_back = jnp.einsum(
        "td,fd->tf", upstream_full, shared_down_full, preferred_element_type=f32
    )
    shared_sigmoid = jax.nn.sigmoid(shared_gate_pre)
    shared_gate_back = (
        shared_hidden_back * shared_up_pre * silu_slope(shared_gate_pre, shared_sigmoid)
    ).astype(bf16)
    shared_up_back = (shared_hidden_back * (shared_gate_pre * shared_sigmoid)).astype(bf16)
    shared_input_back = jnp.einsum(
        "tf,df->td", shared_gate_back, shared_gate_full, preferred_element_type=f32
    ) + jnp.einsum("tf,df->td", shared_up_back, shared_up_full, preferred_element_type=f32)
    shared_gate_part = jnp.einsum(
        "td,tf->df", normed_two, shared_gate_back, preferred_element_type=f32
    )
    shared_up_part = jnp.einsum("td,tf->df", normed_two, shared_up_back, preferred_element_type=f32)
    shared_down_part = jnp.einsum(
        "tf,td->fd", shared_hidden, upstream_full, preferred_element_type=f32
    )
    padded_upstream = jnp.concatenate([upstream_wide, jnp.zeros((1, D), f32)], axis=0)
    slot_grads = (
        (gate_of_slot[:, None] * padded_upstream[token_of_slot])
        .astype(bf16)
        .reshape(EXP_DEV, slot_count, D)
    )
    arrived_grads = send_rows(slot_grads)
    hidden_back = jnp.einsum("jnd,jfd->jnf", arrived_grads, down_stack, preferred_element_type=f32)
    gate_sigmoid = jax.nn.sigmoid(gate_pre)
    gate_back = (hidden_back * up_pre * silu_slope(gate_pre, gate_sigmoid)).astype(bf16)
    up_back = (hidden_back * (gate_pre * gate_sigmoid)).astype(bf16)
    row_back = jnp.einsum(
        "jnf,jfd->jnd", gate_back, gate_stack, preferred_element_type=f32
    ) + jnp.einsum("jnf,jfd->jnd", up_back, up_stack, preferred_element_type=f32)
    returned_grads = return_rows(row_back.astype(bf16)).reshape(buffer_size, D)
    returned_grads = jnp.concatenate([returned_grads, jnp.zeros((1, D), bf16)], axis=0)
    routed_back = jnp.sum(returned_grads[position].astype(f32), axis=1)
    normed_two_back = mix_sums(routed_back + shared_input_back) + router_back
    gate_pieces = []
    up_pieces = []
    down_pieces = []
    for expert in range(EXP_DEV):
        gate_piece, up_piece, down_piece = (
            lax.psum_scatter(
                jnp.einsum(
                    "nf,nd->fd", gate_back[expert], arrived[expert], preferred_element_type=f32
                ).astype(jnp.bfloat16),
                "col",
                scatter_dimension=0,
                tiled=True,
            ).astype(jnp.float32),
            lax.psum_scatter(
                jnp.einsum(
                    "nf,nd->fd", up_back[expert], arrived[expert], preferred_element_type=f32
                ).astype(jnp.bfloat16),
                "col",
                scatter_dimension=0,
                tiled=True,
            ).astype(jnp.float32),
            lax.psum_scatter(
                jnp.einsum(
                    "nf,nd->fd", hidden[expert], arrived_grads[expert], preferred_element_type=f32
                ).astype(jnp.bfloat16),
                "col",
                scatter_dimension=0,
                tiled=True,
            ).astype(jnp.float32),
        )
        gate_pieces.append(gate_piece)
        up_pieces.append(up_piece)
        down_pieces.append(down_piece)
    expert_gate_grad = jnp.stack(gate_pieces, axis=0)
    expert_up_grad = jnp.stack(up_pieces, axis=0)
    expert_down_grad = jnp.stack(down_pieces, axis=0)
    ffn_gain_part = jnp.sum(normed_two_back * unit_two, axis=0)
    middle_back = upstream + norm_backward(normed_two_back, unit_two, scale_two, ffn_gain)
    attended_back = spread(middle_back.astype(bf16))
    mixed_back = (
        jnp.einsum("td,vd->tv", attended_back, output_full, preferred_element_type=f32)
        .astype(bf16)
        .reshape(rows_count, local_heads, VDIM)
    )
    output_grad_part = jnp.einsum("tv,td->vd", mixed, attended_back, preferred_element_type=f32)
    start = 0
    ending = start + block_rows
    scores = block_scores(start)
    weights = jnp.exp(scores - log_blocks)
    weight_back = jnp.einsum("qhd,khd->hqk", mixed_back, values_all, preferred_element_type=f32)
    center = jnp.sum(weight_back * weights, axis=2, keepdims=True)
    raw_back = (weights * (weight_back - center) * score_scale).astype(bf16)
    query_nope_back = jnp.einsum("hqk,khd->qhd", raw_back, key_nope, preferred_element_type=f32)
    query_rope_back = jnp.einsum("hqk,kd->qhd", raw_back, key_rope, preferred_element_type=f32)
    key_nope_back = jnp.einsum("hqk,qhd->khd", raw_back, query_nope, preferred_element_type=f32)
    key_rope_back = jnp.einsum("hqk,qhd->kd", raw_back, query_rope, preferred_element_type=f32)
    values_back = jnp.einsum(
        "hqk,qhd->khd", weights.astype(bf16), mixed_back, preferred_element_type=f32
    )
    query_back = jnp.concatenate(
        [query_nope_back, unrotate(query_rope_back, head_cos, head_sin)], axis=2
    )
    query_back = query_back.astype(bf16).reshape(rows_count, local_heads * (NOPE + ROPE))
    expanded_back = (
        jnp.concatenate([key_nope_back, values_back], axis=2)
        .astype(bf16)
        .reshape(rows_count, local_heads * (NOPE + VDIM))
    )
    latent_normed_back = jnp.einsum(
        "tc,rc->tr", expanded_back, expand_full, preferred_element_type=f32
    )
    expand_grad_part = jnp.einsum(
        "tr,tc->rc", latent_normed, expanded_back, preferred_element_type=f32
    )
    latent_gain_part = jnp.sum(latent_normed_back * latent_unit, axis=0)
    latent_weighted = latent_normed_back * latent_gain
    compressed_back = latent_scale * (
        latent_weighted
        - latent_unit * jnp.mean(latent_weighted * latent_unit, axis=1, keepdims=True)
    )
    rope_back = unrotate(key_rope_back, cosine, sine)
    latent_back, latent_gain_col = (
        lax.psum(
            jnp.concatenate([compressed_back, rope_back], axis=1).astype(jnp.bfloat16), "col"
        ).astype(jnp.float32),
        lax.psum(latent_gain_part.astype(jnp.bfloat16), "col").astype(jnp.float32),
    )
    latent_back = latent_back.astype(bf16)
    latent_grad_part = jnp.einsum("td,tc->dc", normed_one, latent_back, preferred_element_type=f32)
    query_grad_part = jnp.einsum("td,tc->dc", normed_one, query_back, preferred_element_type=f32)
    latent_rows = lax.dynamic_slice_in_dim(latent_full, col_place * width_share, width_share, 0)
    input_part = jnp.einsum("tc,dc->td", query_back, query_full, preferred_element_type=f32)
    normed_one_back = mix_sums(input_part) + jnp.einsum(
        "tc,dc->td", latent_back, latent_rows, preferred_element_type=f32
    )
    norm_gain_part = jnp.sum(normed_one_back * unit_one, axis=0)
    input_grad = middle_back + norm_backward(normed_one_back, unit_one, scale_one, norm_gain)
    norm_gain_grad, ffn_gain_grad, latent_gain_grad = lax.psum(
        (norm_gain_part, ffn_gain_part, latent_gain_col), "row"
    )
    (
        query_grad,
        latent_grad,
        expand_grad,
        output_grad,
        router_grad,
        shared_gate_grad,
        shared_up_grad,
        shared_down_grad,
    ) = (
        lax.psum_scatter(
            query_grad_part.astype(jnp.bfloat16), "row", scatter_dimension=0, tiled=True
        ).astype(jnp.float32),
        lax.psum_scatter(
            latent_grad_part.astype(jnp.bfloat16), "row", scatter_dimension=0, tiled=True
        ).astype(jnp.float32),
        lax.psum_scatter(
            expand_grad_part.astype(jnp.bfloat16), "row", scatter_dimension=0, tiled=True
        ).astype(jnp.float32),
        lax.psum_scatter(
            output_grad_part.astype(jnp.bfloat16), "row", scatter_dimension=1, tiled=True
        ).astype(jnp.float32),
        lax.psum_scatter(
            router_grad_part.astype(jnp.bfloat16), "row", scatter_dimension=0, tiled=True
        ).astype(jnp.float32),
        lax.psum_scatter(
            shared_gate_part.astype(jnp.bfloat16), "row", scatter_dimension=0, tiled=True
        ).astype(jnp.float32),
        lax.psum_scatter(
            shared_up_part.astype(jnp.bfloat16), "row", scatter_dimension=0, tiled=True
        ).astype(jnp.float32),
        lax.psum_scatter(
            shared_down_part.astype(jnp.bfloat16), "row", scatter_dimension=1, tiled=True
        ).astype(jnp.float32),
    )
    return (
        output,
        input_grad,
        norm_gain_grad,
        query_grad,
        latent_grad,
        latent_gain_grad,
        expand_grad,
        output_grad,
        ffn_gain_grad,
        router_grad,
        expert_gate_grad,
        expert_up_grad,
        expert_down_grad,
        shared_gate_grad,
        shared_up_grad,
        shared_down_grad,
    )


def solution(mesh):
    in_specs = (
        P("row", "col"),
        P("row", None),
        P("row", None),
        P("col"),
        P("row", "col"),
        P("row", None),
        P(),
        P("row", "col"),
        P("col", "row"),
        P("col"),
        P("row", None),
        P("row", "col", None),
        P("row", "col", None),
        P("row", "col", None),
        P("row", "col"),
        P("row", "col"),
        P("col", "row"),
        P("row", "col"),
    )
    out_specs = (
        P("row", "col"),
        P("row", "col"),
        P("col"),
        P("row", "col"),
        P("row", None),
        P(),
        P("row", "col"),
        P("col", "row"),
        P("col"),
        P("row", None),
        P("row", "col", None),
        P("row", "col", None),
        P("row", "col", None),
        P("row", "col"),
        P("row", "col"),
        P("col", "row"),
    )
    plan = on_device if dict(mesh.shape) == {"row": 16, "col": 2} else on_device_general
    return jax.shard_map(
        plan, mesh=mesh, in_specs=in_specs, out_specs=out_specs, check_vma=False
    )
```

```python
import jax
import jax.numpy as jnp
from jax import lax
from jax.experimental import pallas as pl
from jax.experimental.pallas import tpu as pltpu
from jax.sharding import PartitionSpec as P

D = 2048
NOPE = 128
ROPE = 64
RANK = 512
VDIM = 128
TOPK = 6
EXP_DEV = 4


epsilon = 1e-06
theta = 10000.0


def rotation(count, width):
    half = width // 2
    places = jnp.arange(count, dtype=jnp.float32)
    rates = theta ** (-jnp.arange(half, dtype=jnp.float32) * 2.0 / width)
    angles = places[:, None] * rates[None, :]
    return (jnp.cos(angles), jnp.sin(angles))


def rotate(values, cosine, sine):
    half = values.shape[-1] // 2
    first = values[..., :half]
    second = values[..., half:]
    return jnp.concatenate(
        [first * cosine - second * sine, second * cosine + first * sine], axis=-1
    )


def unrotate(grads, cosine, sine):
    half = grads.shape[-1] // 2
    first = grads[..., :half]
    second = grads[..., half:]
    return jnp.concatenate(
        [first * cosine + second * sine, second * cosine - first * sine], axis=-1
    )


def silu_slope(pre, sigmoid_value):
    return sigmoid_value * (1.0 + pre * (1.0 - sigmoid_value))


def col_total(values):
    return lax.psum(values, "col")


def spread(values):
    return lax.all_gather(values, "col", axis=1, tiled=True)


def mix_sums(values):
    return lax.psum_scatter(
        values.astype(jnp.bfloat16), "col", scatter_dimension=1, tiled=True
    ).astype(jnp.float32)


def send_rows(rows):
    return lax.all_to_all(rows, "row", split_axis=1, concat_axis=1, tiled=True)


def return_rows(rows):
    return lax.all_to_all(rows, "row", split_axis=1, concat_axis=1, tiled=True)


def rms_scale(rows):
    total = col_total(jnp.sum(rows * rows, axis=1))
    return lax.rsqrt(total / D + epsilon)[:, None]


def norm_backward(grads, unit, scale, gain):
    weighted = grads * gain
    average = col_total(jnp.sum(weighted * unit, axis=1)) / D
    return scale * (weighted - unit * average[:, None])


PLANES = 4
COMMON = 192
UNIQUE = 160
SENT = COMMON + UNIQUE
SHARED_PAD = 128
QUERY_COLUMNS = 1536
SCORE_SCALE = (NOPE + ROPE) ** (-0.5)


def swap_cols(values):
    return lax.ppermute(values, "col", [(0, 1), (1, 0)])


def swap_rows(values, bit):
    return lax.ppermute(values, "row", [(i, i ^ bit) for i in range(16)])


def turn_planes(values):
    return lax.ppermute(values, "row", [(i, (i + 4) % 16) for i in range(16)])


def join_cols(values, first):
    other = swap_cols(values)
    return jnp.where(
        first,
        jnp.concatenate([values, other], axis=1),
        jnp.concatenate([other, values], axis=1),
    )


def own_columns(values, first):
    half = values.shape[-1] // 2
    return jnp.where(first, values[..., :half], values[..., half:])


def other_columns(values, first):
    half = values.shape[-1] // 2
    return jnp.where(first, values[..., half:], values[..., :half])


def sent_rows(values, first):
    return jnp.concatenate(
        [values[:COMMON], jnp.where(first, values[COMMON:SENT], values[SENT:])], axis=0
    )


def local_tokens(values, axis, first):
    common = lax.slice_in_dim(values, 0, COMMON, axis=axis)
    one = lax.slice_in_dim(values, COMMON, SENT, axis=axis)
    two = lax.slice_in_dim(values, SENT, SENT + UNIQUE, axis=axis)
    return jnp.concatenate(
        [common, jnp.where(first, one, two), jnp.where(first, two, one)], axis=axis
    )


def together(*values):
    return lax.optimization_barrier(values)


def after(values, *others):
    return lax.optimization_barrier((values, *others))[0]


def batch(values):
    starts = [0]
    for value in values:
        starts.append(starts[-1] + value.shape[0])
    return jnp.concatenate(values, axis=0), starts[:-1]


class Spread:
    def __init__(self, rows):
        self.held = {(0, 0): rows}
        self.unique = {}
        self.sibling = {}

    def turn(self, plane):
        return turn_planes(self.held[plane - 1, 0])

    def cross(self, plane):
        return swap_rows(self.held[plane, 0], 2)

    def sent(self, *keys):
        return [self.held[key][COMMON:] for key in keys]

    def got(self, array, starts, *keys):
        for key, start in zip(keys, starts):
            self.unique[key] = (array, start)

    def passed(self, *keys):
        pieces = []
        for key in keys:
            if key[2]:
                array, start = self.unique[key[:2]]
                pieces.append(array[start : start + UNIQUE])
            else:
                pieces.append(self.held[key[:2]])
        return pieces

    def taken(self, array, starts, *keys):
        for key, start in zip(keys, starts):
            self.sibling[key] = (array, start)

    def family(self, plane):
        result = []
        for across in (0, 1):
            result.append(((self.held[plane, across], 0), self.unique[plane, across]))
            result.append((self.sibling[plane, across, 0], self.sibling[plane, across, 1]))
        return result


def add_unique(rest, unique, across):
    return jnp.concatenate([rest[across, :COMMON], rest[across, COMMON:] + unique[across]], axis=0)


def column_pieces(weight, bounds):
    return jnp.concatenate([weight[:, a:b] for a, b in bounds], axis=1)


def pair_columns(weight):
    head = NOPE + ROPE
    bounds = []
    for start in range(0, weight.shape[1], 2 * head):
        bounds += [(start, start + NOPE), (start + head, start + head + NOPE)]
        bounds += [(start + NOPE, start + head), (start + head + NOPE, start + 2 * head)]
    return column_pieces(weight, bounds)


def head_columns(weight):
    bounds = []
    for start in range(0, weight.shape[1], 2 * (NOPE + ROPE)):
        turned = start + 2 * NOPE
        bounds += [(start, start + NOPE), (turned, turned + ROPE)]
        bounds += [(start + NOPE, turned), (turned + ROPE, turned + 2 * ROPE)]
    return column_pieces(weight, bounds)


def merge_rows(own, received, first):
    own = own.astype(jnp.float32)
    received = received.astype(jnp.float32)
    common = own[:COMMON] + received[:COMMON]
    mine = own[COMMON:]
    theirs = received[COMMON:]
    return jnp.concatenate(
        [common, jnp.where(first, mine, theirs), jnp.where(first, theirs, mine)], axis=0
    )


FAMILIES = 4


def kernel_params(mebibytes):
    return pltpu.CompilerParams(vmem_limit_bytes=mebibytes * 1024 * 1024)


def short_cost():
    return pl.CostEstimate(flops=10**9, bytes_accessed=10**6, transcendentals=0)


def dot_last(left, right):
    return lax.dot_general(
        left, right, (((1,), (1,)), ((), ())), preferred_element_type=jnp.float32
    )


def dot_first(left, right):
    return lax.dot_general(
        left, right, (((0,), (0,)), ((), ())), preferred_element_type=jnp.float32
    )


def dot_plain(left, right):
    return jnp.dot(left, right, preferred_element_type=jnp.float32)


def slot_matches(codes_ref, capacity):
    tokens = codes_ref.shape[-1]
    ranks = lax.broadcasted_iota(jnp.int32, (capacity, tokens), 0)
    return [codes_ref[0, j : j + 1, :] == ranks for j in range(EXP_DEV)]


def as_picks(matches):
    one = [jnp.where(m, 1.0, 0.0).astype(jnp.bfloat16) for m in matches]
    return jnp.concatenate(one, axis=0)


def row_copies(refs, starts, held, sems, f):
    return [
        pltpu.make_async_copy(
            refs[2 * f].at[pl.ds(starts[2 * f], SENT)],
            held.at[f, pl.ds(0, SENT)],
            sems.at[f, 0],
        ),
        pltpu.make_async_copy(
            refs[2 * f + 1].at[pl.ds(starts[2 * f + 1], UNIQUE)],
            held.at[f, pl.ds(SENT, UNIQUE)],
            sems.at[f, 1],
        ),
    ]


def start_rows(refs, starts, held, sems):
    for f in range(FAMILIES):
        for copy in row_copies(refs, starts, held, sems, f):
            copy.start()


def wait_rows(refs, starts, held, sems, f):
    for family in range(FAMILIES):

        @pl.when(f == family)
        def _():
            for copy in row_copies(refs, starts, held, sems, family):
                copy.wait()


def pick_grads(plane, codes, last, capacity):
    pieces = [piece[0] for family in plane for piece in family]
    starts = [piece[1] for family in plane for piece in family]
    tokens = SENT + UNIQUE
    width = last.shape[1]
    pad = last.shape[0]

    def body(*refs):
        rows_in = refs[:8]
        codes_ref, last_ref, slots_ref, hidden_ref, held, sems = refs[8:]
        f = pl.program_id(0)

        @pl.when(f == 0)
        def _():
            start_rows(rows_in, starts, held, sems)

        wait_rows(rows_in, starts, held, sems, f)
        rows = held[f]
        picks = as_picks(slot_matches(codes_ref, capacity))
        taken = dot_plain(picks, rows).astype(jnp.bfloat16)
        slots_ref[...] = taken.reshape(EXP_DEV, capacity, width)
        hidden_ref[0] = dot_last(rows, last_ref[...])

    return pl.pallas_call(
        body,
        grid=(FAMILIES,),
        in_specs=[pl.BlockSpec(memory_space=pl.ANY)] * 8
        + [
            pl.BlockSpec((1, 8, tokens), lambda f: (f, 0, 0)),
            pl.BlockSpec((pad, width), lambda f: (0, 0)),
        ],
        out_specs=[
            pl.BlockSpec((EXP_DEV, capacity, width), lambda f: (0, f, 0)),
            pl.BlockSpec((1, tokens, pad), lambda f: (f, 0, 0)),
        ],
        out_shape=[
            jax.ShapeDtypeStruct((EXP_DEV, FAMILIES * capacity, width), jnp.bfloat16),
            jax.ShapeDtypeStruct((FAMILIES, tokens, pad), jnp.float32),
        ],
        scratch_shapes=[
            pltpu.VMEM((FAMILIES, tokens, width), jnp.bfloat16),
            pltpu.SemaphoreType.DMA((FAMILIES, 2)),
        ],
        compiler_params=kernel_params(32),
        cost_estimate=short_cost(),
    )(*pieces, codes, last)


def pick_rows(plane, grad_plane, codes, router, pair, hidden_grads, capacity):
    pieces = [piece[0] for family in plane for piece in family]
    starts = [piece[1] for family in plane for piece in family]
    grad_pieces = [piece[0] for family in grad_plane for piece in family]
    grad_starts = [piece[1] for family in grad_plane for piece in family]
    tokens = SENT + UNIQUE
    width = pair.shape[1]
    pad = pair.shape[0] // 2

    def body(*refs):
        rows_in = refs[:8]
        grads_in = refs[8:16]
        (codes_ref, router_ref, pair_ref, hidden_grads_ref) = refs[16:20]
        (slots_ref, gates_ref, hidden_ref, back_ref, grad_ref) = refs[20:25]
        held, held_grads, sems, grad_sems = refs[25:]
        f = pl.program_id(0)

        @pl.when(f == 0)
        def _():
            start_rows(rows_in, starts, held, sems)
            start_rows(grads_in, grad_starts, held_grads, grad_sems)
            grad_ref[...] = jnp.zeros_like(grad_ref)

        wait_rows(rows_in, starts, held, sems, f)
        rows = held[f]
        matches = slot_matches(codes_ref, capacity)
        taken = dot_plain(as_picks(matches), rows).astype(jnp.bfloat16)
        slots_ref[...] = taken.reshape(EXP_DEV, capacity, width)
        logits = dot_last(router_ref[...], rows)
        top = jnp.max(logits, axis=0, keepdims=True)
        total = jnp.log(jnp.sum(jnp.exp(logits - top), axis=0, keepdims=True)) + top
        for j in range(EXP_DEV):
            chance = jnp.exp(logits[j : j + 1] - total)
            gate = jnp.sum(jnp.where(matches[j], chance, 0.0), axis=1, keepdims=True)
            gates_ref[j] = jnp.broadcast_to(gate, (capacity, 128))
        pre = dot_last(rows, pair_ref[...])
        gate_pre = pre[:, :pad]
        up_pre = pre[:, pad:]
        hidden_back = hidden_grads_ref[0]
        sigmoid_value = jax.nn.sigmoid(gate_pre)
        silu_value = gate_pre * sigmoid_value
        hidden = (silu_value * up_pre).astype(jnp.bfloat16)
        slope = sigmoid_value * (1.0 + gate_pre * (1.0 - sigmoid_value))
        gate_back = (hidden_back * up_pre * slope).astype(jnp.bfloat16)
        up_back = (hidden_back * silu_value).astype(jnp.bfloat16)
        back = jnp.concatenate([gate_back, up_back], axis=1)
        hidden_ref[0] = hidden
        back_ref[0] = back
        grad_ref[: 2 * pad] += dot_first(back, rows)
        wait_rows(grads_in, grad_starts, held_grads, grad_sems, f)
        grad_ref[2 * pad :] += dot_first(hidden, held_grads[f])

    return pl.pallas_call(
        body,
        grid=(FAMILIES,),
        in_specs=[pl.BlockSpec(memory_space=pl.ANY)] * 16
        + [
            pl.BlockSpec((1, 8, tokens), lambda f: (f, 0, 0)),
            pl.BlockSpec(router.shape, lambda f: (0, 0)),
            pl.BlockSpec(pair.shape, lambda f: (0, 0)),
            pl.BlockSpec((1, tokens, pad), lambda f: (f, 0, 0)),
        ],
        out_specs=[
            pl.BlockSpec((EXP_DEV, capacity, width), lambda f: (0, f, 0)),
            pl.BlockSpec((EXP_DEV, capacity, 128), lambda f: (0, f, 0)),
            pl.BlockSpec((1, tokens, pad), lambda f: (f, 0, 0)),
            pl.BlockSpec((1, tokens, 2 * pad), lambda f: (f, 0, 0)),
            pl.BlockSpec((3 * pad, width), lambda f: (0, 0)),
        ],
        out_shape=[
            jax.ShapeDtypeStruct((EXP_DEV, FAMILIES * capacity, width), jnp.bfloat16),
            jax.ShapeDtypeStruct((EXP_DEV, FAMILIES * capacity, 128), jnp.float32),
            jax.ShapeDtypeStruct((FAMILIES, tokens, pad), jnp.bfloat16),
            jax.ShapeDtypeStruct((FAMILIES, tokens, 2 * pad), jnp.bfloat16),
            jax.ShapeDtypeStruct((3 * pad, width), jnp.float32),
        ],
        scratch_shapes=[
            pltpu.VMEM((FAMILIES, tokens, width), jnp.bfloat16),
            pltpu.VMEM((FAMILIES, tokens, width), jnp.bfloat16),
            pltpu.SemaphoreType.DMA((FAMILIES, 2)),
            pltpu.SemaphoreType.DMA((FAMILIES, 2)),
        ],
        compiler_params=kernel_params(48),
        cost_estimate=short_cost(),
    )(*pieces, *grad_pieces, codes, router, pair, hidden_grads)


def run_experts(slot_rows, slot_grads, gates, expert_gate, expert_up, expert_down):
    count, slots, width = slot_rows.shape
    units = expert_gate.shape[1]

    def body(
        rows_ref,
        grads_ref,
        gates_ref,
        gate_ref,
        up_ref,
        down_ref,
        sum_ref,
        back_ref,
        hidden_ref,
        gate_back_ref,
        up_back_ref,
        gate_grad_ref,
    ):
        rows = rows_ref[0]
        gates_here = gates_ref[0][:, :1]
        gate_pre = dot_last(rows, gate_ref[0])
        up_pre = dot_last(rows, up_ref[0])
        down_back = dot_last(grads_ref[0], down_ref[0])
        sigmoid_value = jax.nn.sigmoid(gate_pre)
        silu_value = gate_pre * sigmoid_value
        hidden = silu_value * up_pre
        gate_grad = jnp.sum(hidden * down_back, axis=1, keepdims=True)
        gate_grad_ref[0] = jnp.broadcast_to(gate_grad, (slots, 128))
        hidden_back = down_back * gates_here
        slope = sigmoid_value * (1.0 + gate_pre * (1.0 - sigmoid_value))
        gate_back = (hidden_back * up_pre * slope).astype(jnp.bfloat16)
        up_back = (hidden_back * silu_value).astype(jnp.bfloat16)
        scaled = (hidden * gates_here).astype(jnp.bfloat16)
        hidden_ref[0] = scaled
        gate_back_ref[0] = gate_back
        up_back_ref[0] = up_back
        back = dot_plain(gate_back, gate_ref[0]) + dot_plain(up_back, up_ref[0])
        back_ref[0] = back.astype(jnp.bfloat16)
        sum_ref[0] = dot_plain(scaled, down_ref[0]).astype(jnp.bfloat16)

    wide = pl.BlockSpec((1, slots, width), lambda j: (j, 0, 0))
    narrow = pl.BlockSpec((1, slots, 128), lambda j: (j, 0, 0))
    inner = pl.BlockSpec((1, slots, units), lambda j: (j, 0, 0))
    matrix = pl.BlockSpec((1, units, width), lambda j: (j, 0, 0))
    return pl.pallas_call(
        body,
        grid=(count,),
        in_specs=[wide, wide, narrow, matrix, matrix, matrix],
        out_specs=[wide, wide, inner, inner, inner, narrow],
        out_shape=[
            jax.ShapeDtypeStruct((count, slots, width), jnp.bfloat16),
            jax.ShapeDtypeStruct((count, slots, width), jnp.bfloat16),
            jax.ShapeDtypeStruct((count, slots, units), jnp.bfloat16),
            jax.ShapeDtypeStruct((count, slots, units), jnp.bfloat16),
            jax.ShapeDtypeStruct((count, slots, units), jnp.bfloat16),
            jax.ShapeDtypeStruct((count, slots, 128), jnp.float32),
        ],
        compiler_params=kernel_params(56),
        cost_estimate=short_cost(),
    )(slot_rows, slot_grads, gates, expert_gate, expert_up, expert_down)


def sum_tokens(values, codes, shared, matrix, capacity, core, received=None, gate_grads=None):
    tokens = codes.shape[2]
    width = values.shape[2]
    inner = matrix.shape[0]
    with_rows = received is not None
    with_gates = gate_grads is not None

    def body(*refs):
        values_ref, codes_ref, shared_ref, matrix_ref = refs[:4]
        outs = refs[4 + with_rows + with_gates :]
        matches = slot_matches(codes_ref, capacity)
        rows = values_ref[...].reshape(EXP_DEV * capacity, width)
        total = dot_first(as_picks(matches), rows)
        total = total + dot_plain(shared_ref[0], matrix_ref[...])
        if with_rows:
            total = (total + refs[4][0].astype(jnp.float32)).astype(jnp.bfloat16)
            outs[0][0] = total[:SENT]
            outs[1][0] = total[SENT:]
        else:
            outs[0][0] = total.astype(jnp.bfloat16)
        if with_gates:
            dense = [
                jnp.sum(
                    jnp.where(matches[j], refs[4 + with_rows][j][:, :1], 0.0),
                    axis=0,
                    keepdims=True,
                )
                for j in range(EXP_DEV)
            ]
            outs[-1][0] = jnp.concatenate(dense + [jnp.zeros((4, tokens), jnp.float32)], axis=0)

    in_specs = [
        pl.BlockSpec((EXP_DEV, capacity, width), lambda i: (0, 2 * i + core, 0)),
        pl.BlockSpec((1, 8, tokens), lambda i: (2 * i + core, 0, 0)),
        pl.BlockSpec((1, tokens, inner), lambda i: (2 * i + core, 0, 0)),
        pl.BlockSpec((inner, width), lambda i: (0, 0)),
    ]
    operands = [values, codes, shared, matrix]
    pieces = [tokens]
    if with_rows:
        in_specs.append(pl.BlockSpec((1, tokens, width), lambda i: (i, 0, 0)))
        operands.append(received)
        pieces = [SENT, UNIQUE]
    out_specs = [pl.BlockSpec((1, piece, width), lambda i: (i, 0, 0)) for piece in pieces]
    out_shape = [jax.ShapeDtypeStruct((2, piece, width), jnp.bfloat16) for piece in pieces]
    if with_gates:
        in_specs.append(pl.BlockSpec((EXP_DEV, capacity, 128), lambda i: (0, 2 * i + core, 0)))
        operands.append(gate_grads)
        out_specs.append(pl.BlockSpec((1, 8, tokens), lambda i: (i, 0, 0)))
        out_shape.append(jax.ShapeDtypeStruct((2, 8, tokens), jnp.float32))
    return pl.pallas_call(
        body,
        grid=(2,),
        in_specs=in_specs,
        out_specs=out_specs,
        out_shape=out_shape,
        compiler_params=kernel_params(24),
        cost_estimate=short_cost(),
    )(*operands)


def pack_weights(query_weight, expand_weight, output_weight, latent_weight, router_weight, routes):
    block = latent_weight.shape[0]
    share = expand_weight.shape[0]
    widths = [
        query_weight.shape[1],
        expand_weight.shape[1] * share // block,
        output_weight.shape[0],
        latent_weight.shape[1],
        router_weight.shape[1],
        routes.shape[1],
    ]
    columns = (sum(widths) + 127) // 128 * 128

    def body(query_ref, expand_ref, output_ref, latent_ref, router_ref, routes_ref, out_ref):
        out_ref[:, : widths[0]] = pair_columns(query_ref[...])
        start = widths[0]
        for i in range(block // share):
            out_ref[share * i : share * (i + 1), start : start + widths[1]] = expand_ref[
                :, widths[1] * i : widths[1] * (i + 1)
            ]
        start += widths[1]
        out_ref[:, start : start + widths[2]] = output_ref[...].T
        start += widths[2]
        out_ref[:, start : start + widths[3] + widths[4]] = jnp.concatenate(
            [latent_ref[...], router_ref[...]], axis=1
        )
        start += widths[3] + widths[4]
        last = jnp.zeros((block, columns - start - widths[5]), jnp.bfloat16)
        out_ref[:, start:] = jnp.concatenate([routes_ref[...], last], axis=1)

    return pl.pallas_call(
        body,
        out_shape=jax.ShapeDtypeStruct((block, columns), jnp.bfloat16),
        compiler_params=kernel_params(16),
        cost_estimate=short_cost(),
    )(query_weight, expand_weight, output_weight, latent_weight, router_weight, routes)


def unpack_grads(output, joined, widths):
    block = joined.shape[0]
    query_width, expand_width, latent_width = widths
    edge = query_width + expand_width
    parts = 4
    share = block // parts

    def body(sum_ref, joined_ref, output_ref, query_ref, expand_ref, latent_ref, router_ref):
        output_ref[...] = sum_ref[...].astype(jnp.float32).T
        query_ref[...] = head_columns(joined_ref[:, :query_width]).astype(jnp.float32)
        for i in range(parts):
            expand_ref[:, expand_width * i : expand_width * (i + 1)] = joined_ref[
                share * i : share * (i + 1), query_width:edge
            ].astype(jnp.float32)
        narrow = joined_ref[:, edge:].astype(jnp.float32)
        latent_ref[...] = narrow[:, :latent_width]
        router_ref[...] = narrow[:, latent_width:]

    shapes = [
        (output.shape[1], block),
        (block, query_width),
        (share, expand_width * parts),
        (block, latent_width),
        (block, joined.shape[1] - edge - latent_width),
    ]
    return pl.pallas_call(
        body,
        out_shape=[jax.ShapeDtypeStruct(shape, jnp.float32) for shape in shapes],
        compiler_params=kernel_params(16),
        cost_estimate=short_cost(),
    )(output, joined)


def block_grads(places, left, right, tile, core, turned=None, expanded=None, received=None):
    count, width = left.shape
    block = width // (4 * PLANES)
    blocks = 2 * PLANES
    columns = right.shape[1]
    steps = columns // tile
    with_expand = turned is not None
    share = turned.shape[0] // (4 * PLANES) if with_expand else 0
    quarter = expanded.shape[1] // steps if with_expand else 0

    def body(places_ref, left_ref, right_ref, *refs):
        held = refs[-2]
        held_turned = refs[-1]
        out_ref = refs[-3]
        step = pl.program_id(0)

        @pl.when(step == 0)
        def _():
            for i in range(blocks):
                place = places_ref[2 * i + core]
                start = pl.multiple_of(place * block, block)
                held[:, block * i : block * (i + 1)] = left_ref[:, pl.ds(start, block)]
                if with_expand:
                    start = pl.multiple_of(place * share, share)
                    held_turned[share * i : share * (i + 1)] = refs[0][pl.ds(start, share)]

        part = dot_first(held[...], right_ref[...]).reshape(blocks, block, tile)
        lanes = pl.ds(pl.multiple_of(step * tile, 128), tile)
        if received is not None:
            got_ref = refs[-4]
            part = part + got_ref[:, :, lanes].astype(jnp.float32)
        out_ref[:, :, lanes] = part.astype(jnp.bfloat16)
        if with_expand:
            part = dot_plain(held_turned[...], refs[1][...]).reshape(blocks, share, quarter)
            lines = pl.ds(pl.multiple_of(step * share, share), share)
            if received is not None:
                part = part + got_ref[:, lines, columns:].astype(jnp.float32)
            out_ref[:, lines, columns:] = part.astype(jnp.bfloat16)

    whole = lambda shape: pl.BlockSpec(shape, lambda h, places_ref: (0,) * len(shape))
    in_specs = [
        whole(left.shape),
        pl.BlockSpec((count, tile), lambda h, places_ref: (0, h)),
    ]
    operands = [left, right]
    if with_expand:
        in_specs += [
            whole(turned.shape),
            pl.BlockSpec((count, quarter), lambda h, places_ref: (0, h)),
        ]
        operands += [turned, expanded]
    shape = (blocks, block, columns + quarter)
    if received is not None:
        in_specs.append(whole(shape))
        operands.append(received)
    return pl.pallas_call(
        body,
        grid_spec=pltpu.PrefetchScalarGridSpec(
            num_scalar_prefetch=1,
            grid=(steps,),
            in_specs=in_specs,
            out_specs=whole(shape),
            scratch_shapes=[
                pltpu.VMEM((count, blocks * block), jnp.bfloat16),
                pltpu.VMEM((max(blocks * share, 16), count), jnp.bfloat16),
            ],
        ),
        out_shape=jax.ShapeDtypeStruct(shape, jnp.bfloat16),
        compiler_params=kernel_params(40),
        cost_estimate=short_cost(),
    )(places, *operands)


def joined_grads(
    places, normed, query_back, turned, expanded, latent_back, normed_two, logit_grads, wide, narrow
):
    count, width = normed.shape
    block = width // (4 * PLANES)
    blocks = 2 * PLANES
    query_width = query_back.shape[1]
    tile = 384
    steps = query_width // tile
    share = turned.shape[0] // (4 * PLANES)
    quarter = expanded.shape[1] // steps
    latent_width = latent_back.shape[1]
    edge = query_width + quarter

    def body(
        places_ref,
        normed_ref,
        query_ref,
        turned_ref,
        expanded_ref,
        latent_ref,
        two_ref,
        logit_ref,
        wide_ref,
        narrow_ref,
        out_ref,
        held,
        held_turned,
        held_two,
    ):
        step = pl.program_id(0)

        @pl.when(step == 0)
        def _():
            for i in range(blocks):
                place = places_ref[2 * i]
                start = pl.multiple_of(place * block, block)
                held[:, block * i : block * (i + 1)] = normed_ref[:, pl.ds(start, block)]
                held_two[:, block * i : block * (i + 1)] = two_ref[:, pl.ds(start, block)]
                start = pl.multiple_of(place * share, share)
                held_turned[share * i : share * (i + 1)] = turned_ref[pl.ds(start, share)]
            part = jnp.concatenate(
                [
                    dot_first(held[...], latent_ref[...]),
                    dot_first(held_two[...], logit_ref[...]),
                ],
                axis=1,
            ).reshape(blocks, block, narrow.shape[2])
            part = part + narrow_ref[...].astype(jnp.float32)
            out_ref[:, :, edge:] = part.astype(jnp.bfloat16)

        lanes = pl.ds(pl.multiple_of(step * tile, 128), tile)
        part = dot_first(held[...], query_ref[...]).reshape(blocks, block, tile)
        part = part + wide_ref[:, :, lanes].astype(jnp.float32)
        out_ref[:, :, lanes] = part.astype(jnp.bfloat16)
        lines = pl.ds(pl.multiple_of(step * share, share), share)
        part = dot_plain(held_turned[...], expanded_ref[...]).reshape(blocks, share, quarter)
        part = part + wide_ref[:, lines, query_width:].astype(jnp.float32)
        out_ref[:, lines, query_width:edge] = part.astype(jnp.bfloat16)

    whole = lambda shape: pl.BlockSpec(shape, lambda h, places_ref: (0,) * len(shape))
    shape = (blocks, block, edge + narrow.shape[2])
    return pl.pallas_call(
        body,
        grid_spec=pltpu.PrefetchScalarGridSpec(
            num_scalar_prefetch=1,
            grid=(steps,),
            in_specs=[
                whole(normed.shape),
                pl.BlockSpec((count, tile), lambda h, places_ref: (0, h)),
                whole(turned.shape),
                pl.BlockSpec((count, quarter), lambda h, places_ref: (0, h)),
                whole(latent_back.shape),
                whole(normed_two.shape),
                whole(logit_grads.shape),
                whole(wide.shape),
                whole(narrow.shape),
            ],
            out_specs=whole(shape),
            scratch_shapes=[
                pltpu.VMEM((count, blocks * block), jnp.bfloat16),
                pltpu.VMEM((blocks * share, count), jnp.bfloat16),
                pltpu.VMEM((count, blocks * block), jnp.bfloat16),
            ],
        ),
        out_shape=jax.ShapeDtypeStruct(shape, jnp.bfloat16),
        compiler_params=kernel_params(40),
        cost_estimate=short_cost(),
    )(
        places,
        normed,
        query_back,
        turned,
        expanded,
        latent_back,
        normed_two,
        logit_grads,
        wide,
        narrow,
    )


def narrow_grads(places, normed, latent_back, normed_two, logit_grads, core):
    count, width = normed.shape
    block = width // (4 * PLANES)
    widths = [latent_back.shape[1], logit_grads.shape[1]]

    def body(places_ref, normed_ref, two_ref, latent_ref, logit_ref, out_ref):
        parts = [
            dot_first(normed_ref[...], latent_ref[...]),
            dot_first(two_ref[...], logit_ref[...]),
        ]
        out_ref[0] = jnp.concatenate(parts, axis=1).astype(jnp.bfloat16)

    piece = pl.BlockSpec((count, block), lambda i, places_ref: (0, places_ref[2 * i + core]))
    whole = lambda columns: pl.BlockSpec((count, columns), lambda i, places_ref: (0, 0))
    return pl.pallas_call(
        body,
        grid_spec=pltpu.PrefetchScalarGridSpec(
            num_scalar_prefetch=1,
            grid=(2 * PLANES,),
            in_specs=[piece, piece, whole(widths[0]), whole(widths[1])],
            out_specs=pl.BlockSpec((1, block, sum(widths)), lambda i, places_ref: (i, 0, 0)),
        ),
        out_shape=jax.ShapeDtypeStruct((2 * PLANES, block, sum(widths)), jnp.bfloat16),
        compiler_params=kernel_params(24),
        cost_estimate=short_cost(),
    )(places, normed, normed_two, latent_back, logit_grads)


def assemble(blocks, places):
    count = len(blocks)

    def body(places_ref, *refs):
        out, held, sems, out_sems = refs[count:]
        arrivals = [
            pltpu.make_async_copy(refs[i], held.at[i], sems.at[i]) for i in range(count)
        ]
        leaving = [
            pltpu.make_async_copy(held.at[i], out.at[places_ref[i]], out_sems.at[i])
            for i in range(count)
        ]
        for copy in arrivals:
            copy.start()
        for i in range(count):
            arrivals[i].wait()
            leaving[i].start()
        for copy in leaving:
            copy.wait()

    return pl.pallas_call(
        body,
        in_specs=[pl.BlockSpec(memory_space=pltpu.SMEM)]
        + [pl.BlockSpec(memory_space=pl.ANY)] * len(blocks),
        out_specs=pl.BlockSpec(memory_space=pl.ANY),
        out_shape=jax.ShapeDtypeStruct((len(blocks),) + blocks[0].shape, blocks[0].dtype),
        scratch_shapes=[
            pltpu.VMEM((count,) + blocks[0].shape, blocks[0].dtype),
            pltpu.SemaphoreType.DMA((count,)),
            pltpu.SemaphoreType.DMA((count,)),
        ],
        compiler_params=kernel_params(24),
        cost_estimate=short_cost(),
    )(places, *blocks)


def expert_weight_grads(rows, grads, gate_backs, up_backs, hiddens, begin, count, earlier):
    experts, slots, width = rows[0].shape
    units = hiddens[0].shape[2]
    tile = 512
    planes = len(rows)

    def body(*refs):
        rows_in = refs[:planes]
        grads_in = refs[planes : 2 * planes]
        gate_in = refs[2 * planes : 3 * planes]
        up_in = refs[3 * planes : 4 * planes]
        hidden_in = refs[4 * planes : 5 * planes]
        gate_ref, up_ref, down_ref = refs[-3:]
        for left, right, out in (
            (gate_in, rows_in, gate_ref),
            (up_in, rows_in, up_ref),
            (hidden_in, grads_in, down_ref),
        ):
            total = dot_first(left[0][0], right[0][0])
            for p in range(1, planes):
                total = total + dot_first(left[p][0], right[p][0])
            out[0] = total

    wide = pl.BlockSpec((1, slots, tile), lambda j, d: (begin + j, 0, d))
    inner = pl.BlockSpec((1, slots, units), lambda j, d: (begin + j, 0, 0))
    result = pl.BlockSpec((1, units, tile), lambda j, d: (begin + j, 0, d))
    return pl.pallas_call(
        body,
        grid=(count, width // tile),
        in_specs=[wide] * (2 * planes)
        + [inner] * (3 * planes)
        + [pl.BlockSpec(memory_space=pl.ANY)] * len(earlier),
        out_specs=[result] * 3,
        out_shape=[jax.ShapeDtypeStruct((experts, units, width), jnp.float32)] * 3,
        input_output_aliases={5 * planes + i: i for i in range(len(earlier))},
        compiler_params=kernel_params(52),
        cost_estimate=short_cost(),
    )(*rows, *grads, *gate_backs, *up_backs, *hiddens, *earlier)


def swap_halves(values):
    lanes = lax.broadcasted_iota(jnp.int32, values.shape, 1)
    return jnp.where(lanes % 64 < 32, pltpu.roll(values, 96, 1), pltpu.roll(values, 32, 1))


def masked_weights(segment_column, segment_line, query, keys, rope, head_rope):
    count = query.shape[0]
    raw = dot_last(query, keys) + dot_last(rope, head_rope)
    after_key = lax.broadcasted_iota(jnp.int32, (count, count), 0) >= lax.broadcasted_iota(
        jnp.int32, (count, count), 1
    )
    allowed = (segment_column == segment_line) & after_key
    scores = jnp.where(allowed, raw * SCORE_SCALE, -1e30)
    exponent = jnp.exp(scores - jnp.max(scores, axis=1, keepdims=True))
    return exponent / jnp.sum(exponent, axis=1, keepdims=True)


def head_ropes(key_rope):
    zeros = jnp.zeros_like(key_rope)
    return [
        jnp.concatenate([key_rope, zeros], axis=1),
        jnp.concatenate([zeros, key_rope], axis=1),
    ]


def attend(normed, latent_normed, ropes, turns, segments, dense):
    count, width = normed.shape
    rows, block, columns = dense.shape
    pairs = QUERY_COLUMNS // 384
    rank = latent_normed.shape[1]
    share = rank // rows
    flat = dense.reshape(rows * block, columns)
    quarters = dense.reshape(rows, block // share, share, columns)

    def body(
        normed_ref,
        latent_ref,
        rope0_ref,
        rope1_ref,
        cosine_ref,
        sine_ref,
        column_ref,
        line_ref,
        query_weight_ref,
        expand_ref,
        output_ref,
        query_ref,
        keys_ref,
        mixed_ref,
        attended_ref,
        total,
    ):
        step = pl.program_id(0)
        query = dot_plain(normed_ref[...], query_weight_ref[...])
        rope = query[:, 256:]
        rope = rope * cosine_ref[...] + swap_halves(rope) * sine_ref[...]
        query = jnp.concatenate([query[:, :256], rope], axis=1).astype(jnp.bfloat16)
        expand = expand_ref[...].reshape(rank, 512)
        keys = dot_plain(latent_ref[...], expand).astype(jnp.bfloat16)
        query_ref[...] = query
        keys_ref[...] = keys
        mixed = []
        for head, rope_ref in enumerate((rope0_ref, rope1_ref)):
            weights = masked_weights(
                column_ref[:, :1],
                line_ref[:1],
                query[:, 128 * head : 128 * head + 128],
                keys[:, 256 * head : 256 * head + 128],
                query[:, 256:],
                rope_ref[...],
            )
            values = keys[:, 256 * head + 128 : 256 * head + 256]
            mixed.append(dot_plain(weights.astype(jnp.bfloat16), values).astype(jnp.bfloat16))
        mixed = jnp.concatenate(mixed, axis=1)
        mixed_ref[...] = mixed
        part = dot_last(mixed, output_ref[...])

        @pl.when(step == 0)
        def _():
            total[...] = part

        @pl.when(step > 0)
        def _():
            total[...] += part

        @pl.when(step == pairs - 1)
        def _():
            attended_ref[...] = total[...].astype(jnp.bfloat16)

    whole = lambda shape: pl.BlockSpec(shape, lambda h: (0,) * len(shape))
    return pl.pallas_call(
        body,
        grid=(pairs,),
        in_specs=[
            whole((count, width)),
            whole((count, rank)),
            whole((count, 128)),
            whole((count, 128)),
            whole((count, 128)),
            whole((count, 128)),
            whole((count, 128)),
            whole((8, count)),
            pl.BlockSpec((width, 384), lambda h: (0, h)),
            pl.BlockSpec((rows, 1, share, 512), lambda h: (0, h, 0, QUERY_COLUMNS // 512)),
            pl.BlockSpec((width, 256), lambda h: (0, (QUERY_COLUMNS + 512) // 256 + h)),
        ],
        out_specs=[
            pl.BlockSpec((count, 384), lambda h: (0, h)),
            pl.BlockSpec((count, 512), lambda h: (0, h)),
            pl.BlockSpec((count, 256), lambda h: (0, h)),
            whole((count, width)),
        ],
        out_shape=[
            jax.ShapeDtypeStruct((count, 384 * pairs), jnp.bfloat16),
            jax.ShapeDtypeStruct((count, 512 * pairs), jnp.bfloat16),
            jax.ShapeDtypeStruct((count, 256 * pairs), jnp.bfloat16),
            jax.ShapeDtypeStruct((count, width), jnp.bfloat16),
        ],
        scratch_shapes=[pltpu.VMEM((count, width), jnp.float32)],
        compiler_params=kernel_params(44),
        cost_estimate=short_cost(),
    )(normed, latent_normed, *ropes, *turns, *segments, flat, quarters, flat)


def attend_back(upstream, query, keys, ropes, turns, segments, dense, rank):
    count, width = upstream.shape
    rows, block, columns = dense.shape
    pairs = QUERY_COLUMNS // 384
    share = rank // rows
    flat = dense.reshape(rows * block, columns)
    quarters = dense.reshape(rows, block // share, share, columns)

    def body(
        upstream_ref,
        query_ref,
        keys_ref,
        rope0_ref,
        rope1_ref,
        cosine_ref,
        sine_ref,
        column_ref,
        line_ref,
        query_weight_ref,
        expand_ref,
        output_ref,
        query_back_ref,
        keys_back_ref,
        rope_back_ref,
        latent_back_ref,
        input_ref,
        total,
    ):
        step = pl.program_id(0)
        mixed_back = dot_plain(upstream_ref[...], output_ref[...]).astype(jnp.bfloat16)
        query = query_ref[...]
        keys = keys_ref[...]
        rope = query[:, 256:]
        lanes = lax.broadcasted_iota(jnp.int32, (count, 128), 1)
        query_back = []
        keys_back = []
        rope_back = 0.0
        key_rope_back = 0.0
        for head, rope_ref in enumerate((rope0_ref, rope1_ref)):
            query_nope = query[:, 128 * head : 128 * head + 128]
            key_nope = keys[:, 256 * head : 256 * head + 128]
            values = keys[:, 256 * head + 128 : 256 * head + 256]
            mixed_head = mixed_back[:, 128 * head : 128 * head + 128]
            weights = masked_weights(
                column_ref[:, :1], line_ref[:1], query_nope, key_nope, rope, rope_ref[...]
            )
            weight_back = dot_last(mixed_head, values)
            center = jnp.sum(weight_back * weights, axis=1, keepdims=True)
            raw_back = (weights * (weight_back - center) * SCORE_SCALE).astype(jnp.bfloat16)
            query_back.append(dot_plain(raw_back, key_nope))
            rope_back = rope_back + dot_plain(raw_back, rope_ref[...])
            keys_back.append(dot_first(raw_back, query_nope))
            keys_back.append(dot_first(weights.astype(jnp.bfloat16), mixed_head))
            mine = lanes // 64 == head
            key_rope_back = key_rope_back + jnp.where(mine, dot_first(raw_back, rope), 0.0)
        rope_back = rope_back * cosine_ref[...] - swap_halves(rope_back) * sine_ref[...]
        query_back = jnp.concatenate(query_back + [rope_back], axis=1).astype(jnp.bfloat16)
        keys_back = jnp.concatenate(keys_back, axis=1).astype(jnp.bfloat16)
        query_back_ref[...] = query_back
        keys_back_ref[...] = keys_back
        latent_part = dot_last(keys_back, expand_ref[...].reshape(rank, 512))
        input_part = dot_last(query_back, query_weight_ref[...])

        @pl.when(step == 0)
        def _():
            rope_back_ref[...] = key_rope_back
            latent_back_ref[...] = latent_part
            total[...] = input_part

        @pl.when(step > 0)
        def _():
            rope_back_ref[...] += key_rope_back
            latent_back_ref[...] += latent_part
            total[...] += input_part

        @pl.when(step == pairs - 1)
        def _():
            input_ref[...] = total[...].astype(jnp.bfloat16)

    whole = lambda shape: pl.BlockSpec(shape, lambda h: (0,) * len(shape))
    return pl.pallas_call(
        body,
        grid=(pairs,),
        in_specs=[
            whole((count, width)),
            pl.BlockSpec((count, 384), lambda h: (0, h)),
            pl.BlockSpec((count, 512), lambda h: (0, h)),
            whole((count, 128)),
            whole((count, 128)),
            whole((count, 128)),
            whole((count, 128)),
            whole((count, 128)),
            whole((8, count)),
            pl.BlockSpec((width, 384), lambda h: (0, h)),
            pl.BlockSpec((rows, 1, share, 512), lambda h: (0, h, 0, QUERY_COLUMNS // 512)),
            pl.BlockSpec((width, 256), lambda h: (0, (QUERY_COLUMNS + 512) // 256 + h)),
        ],
        out_specs=[
            pl.BlockSpec((count, 384), lambda h: (0, h)),
            pl.BlockSpec((count, 512), lambda h: (0, h)),
            whole((count, 128)),
            whole((count, rank)),
            whole((count, width)),
        ],
        out_shape=[
            jax.ShapeDtypeStruct((count, 384 * pairs), jnp.bfloat16),
            jax.ShapeDtypeStruct((count, 512 * pairs), jnp.bfloat16),
            jax.ShapeDtypeStruct((count, 128), jnp.float32),
            jax.ShapeDtypeStruct((count, rank), jnp.float32),
            jax.ShapeDtypeStruct((count, width), jnp.bfloat16),
        ],
        scratch_shapes=[pltpu.VMEM((count, width), jnp.float32)],
        compiler_params=kernel_params(52),
        cost_estimate=short_cost(),
    )(upstream, query, keys, *ropes, *turns, *segments, flat, quarters, flat)


def on_device(
    inputs,
    segment_ids,
    routes,
    norm_gain,
    query_weight,
    latent_weight,
    latent_gain,
    expand_weight,
    output_weight,
    ffn_gain,
    router_weight,
    expert_gate,
    expert_up,
    expert_down,
    shared_gate,
    shared_up,
    shared_down,
    out_grad,
):
    bf16 = jnp.bfloat16
    f32 = jnp.float32
    rows_count = inputs.shape[0]
    row_devices = lax.axis_size("row")
    row_place = lax.axis_index("row")
    first = lax.axis_index("col") == 0
    expert_count = EXP_DEV * row_devices
    capacity = 4 * rows_count * TOPK // (3 * expert_count)
    segment_row = segment_ids[0]
    places = jnp.arange(rows_count, dtype=jnp.int32)

    steps = jnp.arange(row_devices, dtype=jnp.int32)
    arrival = (((row_place // 4 - steps // 4) % 4) * 4 + ((row_place % 4) ^ (steps % 4))).astype(
        jnp.int32
    )
    block = latent_weight.shape[0]
    share = expand_weight.shape[0]
    quarter = expand_weight.shape[1] * share // block
    query_width = query_weight.shape[1]
    latent_width = latent_weight.shape[1]

    slab = pack_weights(
        query_weight,
        expand_weight,
        output_weight,
        latent_weight,
        router_weight,
        routes.astype(bf16).reshape(block, -1),
    )
    shared_share = shared_gate.shape[1] // row_devices
    blocks = {}
    blocks[0] = slab
    blocks[4], blocks[2], inputs_other, gains_other = together(
        turn_planes(slab),
        swap_rows(slab, 2),
        swap_cols(inputs),
        swap_cols(jnp.stack([norm_gain, ffn_gain])),
    )
    shared_packed = jnp.stack(
        [after(shared_gate, inputs_other).T, after(shared_up, inputs_other).T, shared_down], axis=0
    )
    shared_packed = shared_packed.reshape(3, row_devices, shared_share, -1).transpose(1, 0, 2, 3)
    (
        blocks[8],
        blocks[6],
        blocks[1],
        blocks[3],
        out_grad_other,
    ) = together(
        turn_planes(blocks[4]),
        swap_rows(blocks[4], 2),
        swap_rows(blocks[0], 1),
        swap_rows(blocks[2], 1),
        swap_cols(after(out_grad, inputs_other)),
    )
    upstream_bf16 = jnp.where(
        first,
        jnp.concatenate([out_grad, out_grad_other], axis=1),
        jnp.concatenate([out_grad_other, out_grad], axis=1),
    )
    grad_rows = Spread(sent_rows(upstream_bf16, first))
    blocks[12], blocks[10], blocks[5], blocks[7], got, shared_packed = together(
        turn_planes(blocks[8]),
        swap_rows(blocks[8], 2),
        swap_rows(blocks[4], 1),
        swap_rows(blocks[6], 1),
        swap_cols(grad_rows.sent((0, 0))[0]),
        shared_packed,
    )
    grad_rows.got(got, [0], (0, 0))
    source = jnp.where(
        first,
        jnp.concatenate([inputs, inputs_other], axis=1),
        jnp.concatenate([inputs_other, inputs], axis=1),
    ).astype(f32)
    gains = jnp.stack([norm_gain, ffn_gain])
    gains = jnp.where(
        first,
        jnp.concatenate([gains, gains_other], axis=1),
        jnp.concatenate([gains_other, gains], axis=1),
    )
    gain_one = gains[:1]
    gain_two = gains[1:]
    scale_one = lax.rsqrt(jnp.mean(source * source, axis=1, keepdims=True) + epsilon)
    unit_one = source * scale_one
    normed_one = (unit_one * gain_one).astype(bf16)
    cosine, sine = rotation(rows_count, ROPE)
    turns = (
        jnp.concatenate([cosine] * 4, axis=1),
        jnp.concatenate([-sine, sine, -sine, sine], axis=1),
    )
    segments = (
        jnp.broadcast_to(segment_row[:, None], (rows_count, 128)),
        jnp.broadcast_to(segment_row[None], (8, rows_count)),
    )
    passed, starts = batch(grad_rows.passed((0, 0, 0), (0, 0, 1)))
    (
        blocks[14],
        blocks[9],
        blocks[11],
        passed,
        shared_here,
        normed_one,
        cosine,
        sine,
        turns,
        segments,
    ) = together(
        swap_rows(blocks[12], 2),
        swap_rows(blocks[8], 1),
        swap_rows(blocks[10], 1),
        swap_rows(passed, 1),
        lax.all_to_all(shared_packed, "row", split_axis=0, concat_axis=0, tiled=True),
        normed_one,
        cosine,
        sine,
        turns,
        segments,
    )
    grad_rows.taken(passed, starts, (0, 0, 0), (0, 0, 1))
    grad_rows.held[0, 0] = after(grad_rows.held[0, 0], blocks[14])
    grad_turned = grad_rows.turn(1)
    blocks[13], blocks[15] = together(swap_rows(blocks[12], 1), swap_rows(blocks[14], 1))
    dense = assemble([blocks[i] for i in range(4 * PLANES)], arrival)
    flat_dense = dense.reshape(D, -1)
    latent_full = flat_dense[:, QUERY_COLUMNS + 1536 : QUERY_COLUMNS + 1536 + latent_width]
    router_full = flat_dense[
        :, QUERY_COLUMNS + 1536 + latent_width : QUERY_COLUMNS + 1536 + latent_width + expert_count
    ]
    latent = jnp.dot(normed_one, latent_full, preferred_element_type=f32).astype(bf16)
    compressed = latent[:, :RANK].astype(f32)
    latent_scale = lax.rsqrt(jnp.mean(compressed * compressed, axis=1, keepdims=True) + epsilon)
    latent_unit = compressed * latent_scale
    latent_normed = (latent_unit * latent_gain).astype(bf16)
    key_rope = rotate(latent[:, RANK:].astype(f32), cosine, sine).astype(bf16)
    ropes = head_ropes(key_rope)
    routes_all = flat_dense[
        :, QUERY_COLUMNS + 1536 + latent_width + expert_count :
    ][:, : rows_count * TOPK // block]
    routes_all = routes_all.reshape(row_devices, rows_count, TOPK).transpose(0, 2, 1)[arrival]
    routes_all = routes_all.astype(jnp.int32)

    routes_all = local_tokens(routes_all, 2, first)
    held_experts = row_place * EXP_DEV + jnp.arange(EXP_DEV, dtype=jnp.int32)
    hits = jnp.any(routes_all[:, :, None, :] == held_experts[None, None, :, None], axis=1)
    upper = (places[:, None] <= places[None, :]).astype(bf16)
    ranks = jnp.einsum("sjt,tu->sju", hits.astype(bf16), upper, preferred_element_type=f32)
    codes = jnp.where(hits, ranks.astype(jnp.int32) - 1, -1)
    codes = jnp.pad(codes, ((0, 0), (0, 8 - EXP_DEV), (0, 0)), constant_values=-1)
    plane_codes = [codes[p * FAMILIES : (p + 1) * FAMILIES] for p in range(PLANES)]

    latent_normed, plane_codes, grad_rows.held[0, 1], grad_rows.held[1, 0] = together(
        latent_normed, plane_codes, grad_rows.cross(0), grad_turned
    )

    query, keys, mixed, attended_part = attend(
        normed_one, latent_normed, ropes, turns, segments, dense
    )
    sent, starts = batch(grad_rows.sent((0, 1), (1, 0)))
    passed, passed_starts = batch(grad_rows.passed((0, 1, 0), (1, 0, 0)))
    (
        query,
        attended_part,
        grad_rows.held[2, 0],
        grad_rows.held[1, 1],
        got,
        passed,
    ) = together(
        query,
        attended_part,
        grad_rows.turn(2),
        grad_rows.cross(1),
        swap_cols(sent),
        swap_rows(passed, 1),
    )
    grad_rows.got(got, starts, (0, 1), (1, 0))
    grad_rows.taken(passed, passed_starts, (0, 1, 0), (1, 0, 0))

    picked = {}

    def pick(plane, *others):
        picked[plane] = pick_grads(
            grad_rows.family(plane), after(plane_codes[plane], *others), shared_last, capacity
        )
        return picked[plane]

    def pass_alone(spread, key):
        spread.taken(swap_rows(spread.passed(key)[0], 1), [0], key)

    passed, starts = batch(grad_rows.passed((0, 1, 1), (1, 0, 1), (1, 1, 0)))
    partner_part = jnp.concatenate(
        [
            attended_part[:COMMON],
            jnp.where(first, attended_part[SENT:], attended_part[COMMON:SENT]),
        ],
        axis=0,
    )
    (
        attended_other,
        grad_rows.held[2, 1],
        passed,
    ) = together(
        swap_cols(partner_part),
        grad_rows.cross(2),
        swap_rows(passed, 1),
    )
    grad_rows.taken(passed, starts, (0, 1, 1), (1, 0, 1), (1, 1, 0))
    attended_sent = sent_rows(attended_part, first).astype(f32) + attended_other.astype(f32)
    middle_sent = sent_rows(source, first) + attended_sent
    scale_sent = lax.rsqrt(jnp.mean(middle_sent * middle_sent, axis=1, keepdims=True) + epsilon)
    normed_sent = (middle_sent * scale_sent * gain_two).astype(bf16)
    rows = Spread(normed_sent)

    shared_here = shared_here.transpose(1, 2, 0, 3).reshape(3, shared_share, D)
    shared_here = jnp.pad(shared_here, ((0, 0), (0, SHARED_PAD - shared_share), (0, 0)))
    shared_pair = shared_here[:2].reshape(2 * SHARED_PAD, D)
    shared_last = shared_here[2]

    sent, starts = batch(rows.sent((0, 0)) + grad_rows.sent((1, 1)))
    rows.held[1, 0], rows.held[0, 1], got, shared_pair, shared_last = together(
        rows.turn(1), rows.cross(0), swap_cols(sent), shared_pair, shared_last
    )
    rows.got(got, starts, (0, 0))
    grad_rows.got(got, starts[1:], (1, 1))
    router_turned = router_full.T
    router_held = lax.dynamic_slice_in_dim(
        jnp.concatenate([router_turned, router_turned], axis=0),
        row_place * EXP_DEV,
        expert_count,
        0,
    )
    pass_alone(grad_rows, (1, 1, 1))
    sent, starts = batch(rows.sent((0, 1), (1, 0)))
    passed, passed_starts = batch(rows.passed((0, 0, 0), (0, 0, 1), (0, 1, 0)))
    (
        rows.held[2, 0],
        rows.held[1, 1],
        got,
        passed,
        picked[0],
        picked[1],
        router_held,
    ) = together(
        rows.turn(2),
        rows.cross(1),
        swap_cols(sent),
        swap_rows(passed, 1),
        pick(0),
        pick(1),
        router_held,
    )
    rows.got(got, starts, (0, 1), (1, 0))
    rows.taken(passed, passed_starts, (0, 0, 0), (0, 0, 1), (0, 1, 0))

    experts = (expert_gate, expert_up, expert_down)
    begun = {}
    ran = {}

    def start_plane(plane, *others):
        begun[plane] = pick_rows(
            rows.family(plane),
            grad_rows.family(plane),
            after(plane_codes[plane], *others),
            router_held,
            shared_pair,
            picked[plane][1],
            capacity,
        )
        return begun[plane]

    def run_plane(plane):
        ran[plane] = run_experts(begun[plane][0], picked[plane][0], begun[plane][1], *experts)
        return ran[plane]

    def back_sibling(plane):
        return sum_tokens(
            ran[plane][1],
            plane_codes[plane],
            begun[plane][3],
            shared_pair,
            capacity,
            1,
            None,
            ran[plane][5],
        )

    def back_mine(plane, received):
        return sum_tokens(
            ran[plane][1],
            plane_codes[plane],
            begun[plane][3],
            shared_pair,
            capacity,
            0,
            received,
            ran[plane][5],
        )

    def sum_sibling(plane):
        return sum_tokens(
            ran[plane][0], plane_codes[plane], begun[plane][2], shared_last, capacity, 1
        )[0]

    def sum_mine(plane, received):
        return sum_tokens(
            ran[plane][0], plane_codes[plane], begun[plane][2], shared_last, capacity, 0, received
        )

    def unique_out(mine):
        return swap_cols(mine[1])

    def across_out(mine, unique):
        return swap_rows(add_unique(mine[0], unique, 1), 2)

    def own_sum(mine, unique, crossed):
        return add_unique(mine[0], unique, 0) + crossed

    pass_alone(rows, (0, 1, 1))
    sent, starts = batch(rows.sent((1, 1), (2, 0)))
    passed, passed_starts = batch(rows.passed((1, 0, 0), (1, 1, 0), (1, 0, 1)))
    rows.held[3, 0], rows.held[2, 1], got, passed = together(
        rows.turn(3), rows.cross(2), swap_cols(sent), swap_rows(passed, 1)
    )
    rows.got(got, starts, (1, 1), (2, 0))
    rows.taken(passed, passed_starts, (1, 0, 0), (1, 1, 0), (1, 0, 1))

    pass_alone(rows, (1, 1, 1))
    sent, starts = batch(rows.sent((2, 1), (3, 0)))
    passed, passed_starts = batch(rows.passed((2, 0, 0), (2, 1, 0), (2, 0, 1)))
    begun[1], rows.held[3, 1], grad_rows.held[3, 0], got, passed = together(
        start_plane(1), rows.cross(3), grad_rows.turn(3), swap_cols(sent), swap_rows(passed, 1)
    )
    rows.got(got, starts, (2, 1), (3, 0))
    rows.taken(passed, passed_starts, (2, 0, 0), (2, 1, 0), (2, 0, 1))

    ran[1] = run_plane(1)
    back_1 = back_sibling(1)
    sent, starts = batch(rows.sent((3, 1)) + grad_rows.sent((2, 0), (2, 1)))
    passed = [
        batch(rows.passed((2, 1, 1), (3, 0, 1))),
        batch(rows.passed((3, 0, 0), (3, 1, 0))),
        batch(grad_rows.passed((2, 0, 0), (2, 1, 0))),
    ]
    ran[1], back_1, grad_rows.held[3, 1], got, passed_got = together(
        ran[1],
        back_1,
        grad_rows.cross(3),
        swap_cols(sent),
        [swap_rows(rows_passed, 1) for rows_passed, _ in passed],
    )
    rows.got(got, starts, (3, 1))
    grad_rows.got(got, starts[1:], (2, 0), (2, 1))
    rows.taken(passed_got[0], passed[0][1], (2, 1, 1), (3, 0, 1))
    rows.taken(passed_got[1], passed[1][1], (3, 0, 0), (3, 1, 0))
    grad_rows.taken(passed_got[2], passed[2][1], (2, 0, 0), (2, 1, 0))

    passed, passed_starts = batch(grad_rows.passed((2, 0, 1), (2, 1, 1)))
    grad_rows.taken(swap_rows(passed, 1), passed_starts, (2, 0, 1), (2, 1, 1))
    sent, starts = batch(grad_rows.sent((3, 0), (3, 1)))
    passed, passed_starts = batch(
        rows.passed((3, 1, 1)) + grad_rows.passed((3, 0, 0), (3, 1, 0))
    )
    picked[2] = pick(2)
    begun[2] = start_plane(2)
    picked[2], begun[2], back_got, got, passed = together(
        picked[2], begun[2], swap_rows(back_1[0], 1), swap_cols(sent), swap_rows(passed, 1)
    )
    grad_rows.got(got, starts, (3, 0), (3, 1))
    rows.taken(passed, passed_starts, (3, 1, 1))
    grad_rows.taken(passed, passed_starts[1:], (3, 0, 0), (3, 1, 0))
    passed, passed_starts = batch(grad_rows.passed((3, 0, 1), (3, 1, 1)))
    grad_rows.taken(swap_rows(passed, 1), passed_starts, (3, 0, 1), (3, 1, 1))
    back_mine_1 = back_mine(1, back_got)
    sum_1 = sum_sibling(1)
    back_mine_1, sum_1 = together(back_mine_1, sum_1)

    ran[2] = run_plane(2)
    back_2 = back_sibling(2)
    ran[2], back_2, back_unique, sum_got = together(
        ran[2], back_2, unique_out(back_mine_1), swap_rows(sum_1, 1)
    )
    sum_mine_1 = sum_mine(1, sum_got)

    picked[3] = pick(3)
    begun[3] = start_plane(3)
    picked[3], begun[3], back_got, back_crossed, sum_unique = together(
        picked[3],
        begun[3],
        swap_rows(back_2[0], 1),
        across_out(back_mine_1, back_unique),
        unique_out(sum_mine_1),
    )
    back = own_sum(back_mine_1, back_unique, back_crossed)
    back_mine_2 = back_mine(2, back_got)
    sum_2 = sum_sibling(2)
    attended_rest = after(attended_sent[COMMON:], picked[3]).astype(bf16)
    back_mine_2, sum_2, back, attended_rest = together(
        back_mine_2, sum_2, back, swap_cols(attended_rest)
    )

    ran[3] = run_plane(3)
    back_3 = back_sibling(3)
    ran[3], back_3, back, back_unique, sum_got, sum_crossed = together(
        ran[3],
        back_3,
        turn_planes(back),
        unique_out(back_mine_2),
        swap_rows(sum_2, 1),
        across_out(sum_mine_1, sum_unique),
    )
    result = own_sum(sum_mine_1, sum_unique, sum_crossed)
    sum_mine_2 = sum_mine(2, sum_got)
    sum_mine_2, result = together(sum_mine_2, result)

    attended_rest = after(attended_rest, sum_mine_2).astype(f32)
    attended_mine = attended_sent[COMMON:]
    middle = source + jnp.concatenate(
        [
            attended_sent[:COMMON],
            jnp.where(first, attended_mine, attended_rest),
            jnp.where(first, attended_rest, attended_mine),
        ],
        axis=0,
    )
    scale_two = lax.rsqrt(jnp.mean(middle * middle, axis=1, keepdims=True) + epsilon)
    unit_two = middle * scale_two
    normed_two = (unit_two * gain_two).astype(bf16)
    logits = jnp.dot(normed_two, router_full, preferred_element_type=f32)
    log_total = jax.nn.logsumexp(logits, axis=1, keepdims=True)
    chances = jnp.exp(logits - log_total)

    begun[0] = start_plane(0, sum_mine_2)
    begun[0], back_got, back_crossed, sum_unique, result, normed_two, chances = together(
        begun[0],
        swap_rows(back_3[0], 1),
        across_out(back_mine_2, back_unique),
        unique_out(sum_mine_2),
        turn_planes(result),
        normed_two,
        chances,
    )
    back = back + own_sum(back_mine_2, back_unique, back_crossed)
    back_mine_3 = back_mine(3, back_got)
    sum_3 = sum_sibling(3)
    back_mine_3, sum_3, back = together(back_mine_3, sum_3, back)

    ran[0] = run_plane(0)
    back_0 = back_sibling(0)
    ran[0], back_0, back, back_unique, sum_got, sum_crossed = together(
        ran[0],
        back_0,
        turn_planes(back),
        unique_out(back_mine_3),
        swap_rows(sum_3, 1),
        across_out(sum_mine_2, sum_unique),
    )
    result = result + own_sum(sum_mine_2, sum_unique, sum_crossed)
    sum_mine_3 = sum_mine(3, sum_got)
    sum_mine_3, result = together(sum_mine_3, result)

    kept = [
        (begun[plane][0], picked[plane][0], ran[plane][3], ran[plane][4], ran[plane][2])
        for plane in range(PLANES)
    ]
    kept = [list(part) for part in zip(*kept)]
    half = EXP_DEV // 2
    expert_parts = expert_weight_grads(*kept, 0, half, [])
    expert_parts, back_got, back_crossed, sum_unique, result = together(
        expert_parts,
        swap_rows(back_0[0], 1),
        across_out(back_mine_3, back_unique),
        unique_out(sum_mine_3),
        turn_planes(result),
    )
    back = back + own_sum(back_mine_3, back_unique, back_crossed)
    back_mine_0 = back_mine(0, back_got)
    sum_0 = sum_sibling(0)
    back_mine_0, sum_0, back = together(back_mine_0, sum_0, back)

    expert_parts = expert_weight_grads(*kept, half, EXP_DEV - half, expert_parts)
    expert_parts, back, back_unique, sum_got, common_crossed = together(
        expert_parts,
        turn_planes(back),
        unique_out(back_mine_0),
        swap_rows(sum_0, 1),
        swap_rows(back_mine_0[0][1, :COMMON], 2),
    )
    expert_gate_grad, expert_up_grad, expert_down_grad = expert_parts
    common = back[:COMMON] + back_mine_0[0][0, :COMMON] + common_crossed
    unique_rest = back_mine_0[0][:, COMMON:] + back_unique
    sum_mine_0 = sum_mine(0, sum_got)

    gate_grad_dense = [
        jnp.stack([mine[2], sibling[1]], axis=1)[:, :, :EXP_DEV]
        for mine, sibling in (
            (back_mine_0, back_0),
            (back_mine_1, back_1),
            (back_mine_2, back_2),
            (back_mine_3, back_3),
        )
    ]
    gate_grad_dense = jnp.stack(gate_grad_dense).reshape(row_devices, EXP_DEV, rows_count)
    gate_grad_dense = local_tokens(gate_grad_dense, 2, first)[arrival]
    gate_grad_dense = lax.all_to_all(
        gate_grad_dense, "row", split_axis=0, concat_axis=0, tiled=True
    ).reshape(expert_count, rows_count)
    shared_grads = sum([begun[p][4] for p in range(1, PLANES)], begun[0][4])
    shared_grads = shared_grads.reshape(3, SHARED_PAD, D)[:, :shared_share]
    shared_grads = (
        shared_grads.astype(bf16)
        .reshape(3, shared_share, row_devices, -1)
        .transpose(2, 0, 1, 3)
    )
    gate_grad_dense = gate_grad_dense + swap_cols(gate_grad_dense)
    weighted_gates = gate_grad_dense.T * chances
    logit_grads = (
        weighted_gates - chances * jnp.sum(weighted_gates, axis=1, keepdims=True)
    ).astype(bf16)
    router_back = jnp.einsum("te,de->td", logit_grads, router_full, preferred_element_type=f32)
    unique_crossed, common_other, sum_mine_0, shared_grads, router_back, logit_grads = together(
        swap_rows(unique_rest[1], 2),
        swap_cols(common),
        sum_mine_0,
        shared_grads,
        router_back,
        logit_grads,
    )
    unique_mine = back[COMMON:] + unique_rest[0] + unique_crossed
    shared_grads = lax.all_to_all(shared_grads, "row", split_axis=0, concat_axis=0, tiled=True)
    unique_other = swap_cols(unique_mine)
    upstream = upstream_bf16.astype(f32)
    normed_two_back = router_back + jnp.concatenate(
        [
            common.astype(f32) + common_other.astype(f32),
            jnp.where(first, unique_mine, unique_other).astype(f32),
            jnp.where(first, unique_other, unique_mine).astype(f32),
        ],
        axis=0,
    )
    ffn_gain_part = jnp.sum(normed_two_back * unit_two, axis=0)
    weighted = normed_two_back * gain_two
    average = jnp.mean(weighted * unit_two, axis=1, keepdims=True)
    middle_back = upstream + scale_two * (weighted - unit_two * average)
    attended_back = middle_back.astype(bf16)

    def by_plane(total):
        return total.reshape((PLANES, 2) + total.shape[1:])

    output_sibling = block_grads(arrival, attended_back, mixed, 256, 1)
    query_back, expanded_back, key_rope_back, latent_normed_back, input_part = attend_back(
        attended_back, query, keys, ropes, turns, segments, dense, RANK
    )
    query_back, shared_grads, last_unique, output_got, sum_crossed = together(
        query_back,
        shared_grads,
        unique_out(sum_mine_0),
        swap_rows(output_sibling, 1),
        across_out(after(sum_mine_3, unique_other), sum_unique),
    )
    result = result + own_sum(sum_mine_3, sum_unique, sum_crossed)
    latent_gain_part = jnp.sum(latent_normed_back * latent_unit, axis=0)
    latent_weighted = latent_normed_back * latent_gain
    compressed_back = latent_scale * (
        latent_weighted
        - latent_unit * jnp.mean(latent_weighted * latent_unit, axis=1, keepdims=True)
    )
    key_rope_back = key_rope_back[:, :ROPE] + key_rope_back[:, ROPE:]
    rope_back = unrotate(key_rope_back, cosine, sine)
    latent_part = jnp.concatenate([compressed_back, rope_back], axis=1).astype(bf16)
    latent_turned = latent_normed.T
    wide_sibling = block_grads(
        arrival, normed_one, after(query_back, latent_part), 384, 1, latent_turned, expanded_back
    )
    latent_other, wide_sibling = together(swap_cols(latent_part), wide_sibling)
    latent_back = (latent_part.astype(f32) + latent_other.astype(f32)).astype(bf16)
    narrow_sibling = narrow_grads(arrival, normed_one, latent_back, normed_two, logit_grads, 1)
    weighted_part = jnp.sum(
        after(input_part, wide_sibling).astype(f32) * gain_one * unit_one, axis=1
    )
    wide_got, narrow_sibling, weighted_part = together(
        swap_rows(wide_sibling, 1), narrow_sibling, weighted_part
    )
    output_total = by_plane(
        block_grads(
            arrival, after(attended_back, narrow_sibling), mixed, 256, 0, received=output_got
        )
    )
    input_sent = other_columns(input_part, first)
    small_part = jnp.concatenate([weighted_part, latent_gain_part]).reshape(-1, 128)
    narrow_got = swap_rows(narrow_sibling, 1)
    small_other, narrow_got, output_total, sum_crossed, result = together(
        swap_cols(small_part),
        narrow_got,
        output_total,
        across_out(sum_mine_0, last_unique),
        turn_planes(result),
    )
    sum_sent = result + own_sum(sum_mine_0, last_unique, sum_crossed)
    joined_total = by_plane(
        joined_grads(
            arrival,
            normed_one,
            query_back,
            latent_turned,
            expanded_back,
            latent_back,
            normed_two,
            logit_grads,
            wide_got,
            narrow_got,
        )
    )
    joined_total, crossed_output, input_other = together(
        joined_total,
        swap_rows(output_total[1:, 1], 2),
        swap_cols(after(input_sent, small_other)),
    )
    output_sums = [output_total[p, 0] + crossed_output[p - 1] for p in (1, 2, 3)]

    crossed, crossed_output, moved_output, combined_other = together(
        swap_rows(joined_total[1, 1], 2),
        swap_rows(output_total[0, 1], 2),
        turn_planes(output_sums[0]),
        swap_cols(other_columns(sum_sent, first)),
    )
    moving = joined_total[1, 0] + crossed
    moving_output = output_sums[1] + moved_output
    last_output = output_total[0, 0] + crossed_output

    shared_grads = after(shared_grads, joined_total).transpose(1, 0, 2, 3).reshape(3, row_devices * shared_share, -1)
    shared_grads = shared_grads.astype(f32)
    shared_gate_grad = shared_grads[0].T
    shared_up_grad = shared_grads[1].T
    shared_down_grad = shared_grads[2]

    latent_input = jnp.einsum("tc,dc->td", latent_back, latent_full, preferred_element_type=f32)
    small_sum = (small_part + small_other).reshape(-1)
    weighted_sum = small_sum[:rows_count]
    weighted_sum = weighted_sum + jnp.sum(latent_input * gain_one * unit_one, axis=1)
    normed_one_back = (
        own_columns(input_part, first).astype(f32)
        + input_other.astype(f32)
        + own_columns(latent_input, first)
    )
    own_unit = own_columns(unit_one, first)
    norm_gain_part = jnp.sum(normed_one_back * own_unit, axis=0)
    input_grad = own_columns(middle_back, first) + scale_one * (
        normed_one_back * norm_gain - own_unit * (weighted_sum / D)[:, None]
    )
    gain_grads = jnp.concatenate(
        [norm_gain_part, own_columns(ffn_gain_part, first), small_sum[rows_count:]]
    ).reshape(-1, 128)
    crossed, moved, moved_output, gains_other = together(
        swap_rows(joined_total[2, 1], 2),
        turn_planes(moving),
        turn_planes(moving_output),
        swap_rows(gain_grads, 1),
    )
    moving = joined_total[2, 0] + crossed + moved
    moving_output = output_sums[2] + moved_output
    gain_grads = gain_grads + gains_other
    crossed, moved, moved_output, gains_other = together(
        swap_rows(joined_total[3, 1], 2),
        turn_planes(moving),
        turn_planes(moving_output),
        swap_rows(gain_grads, 2),
    )
    moving = joined_total[3, 0] + crossed + moved
    moving_output = last_output + moved_output
    gain_grads = gain_grads + gains_other
    crossed, moved, others = together(
        swap_rows(joined_total[0, 1], 2),
        turn_planes(moving),
        [swap_rows(gain_grads, bits) for bits in (4, 8, 12)],
    )
    moving = joined_total[0, 0] + crossed + moved
    gain_grads = ((gain_grads + others[0]) + (others[1] + others[2])).reshape(-1)
    output_grad, query_grad, expand_grad, latent_grad, router_grad = unpack_grads(
        moving_output, moving, (query_width, quarter, latent_width)
    )

    combined = merge_rows(own_columns(sum_sent, first), combined_other, first)
    output = (own_columns(middle, first) + combined).astype(bf16)
    width_share = norm_gain.shape[0]
    norm_gain_grad = gain_grads[:width_share]
    ffn_gain_grad = gain_grads[width_share : 2 * width_share]
    latent_gain_grad = gain_grads[2 * width_share :]
    return (
        output,
        input_grad,
        norm_gain_grad,
        query_grad,
        latent_grad,
        latent_gain_grad,
        expand_grad,
        output_grad,
        ffn_gain_grad,
        router_grad,
        expert_gate_grad,
        expert_up_grad,
        expert_down_grad,
        shared_gate_grad,
        shared_up_grad,
        shared_down_grad,
    )


def on_device_general(
    inputs,
    segment_ids,
    routes,
    norm_gain,
    query_weight,
    latent_weight,
    latent_gain,
    expand_weight,
    output_weight,
    ffn_gain,
    router_weight,
    expert_gate,
    expert_up,
    expert_down,
    shared_gate,
    shared_up,
    shared_down,
    out_grad,
):
    bf16 = jnp.bfloat16
    f32 = jnp.float32
    rows_count = inputs.shape[0]
    width_share = inputs.shape[1]
    row_devices = lax.axis_size("row")
    col_devices = lax.axis_size("col")
    col_place = lax.axis_index("col")
    local_heads = query_weight.shape[1] // (NOPE + ROPE)
    expert_count = EXP_DEV * row_devices
    capacity = 4 * rows_count * TOPK // (3 * expert_count)
    score_scale = (NOPE + ROPE) ** (-0.5)
    block_rows = min(512, rows_count)
    segment_row = segment_ids[0]
    places = jnp.arange(rows_count, dtype=jnp.int32)
    (
        query_full,
        latent_full,
        expand_full,
        output_full,
        router_full,
        shared_gate_full,
        shared_up_full,
        shared_down_full,
    ) = (
        lax.all_gather(query_weight, "row", axis=0, tiled=True),
        lax.all_gather(latent_weight, "row", axis=0, tiled=True),
        lax.all_gather(expand_weight, "row", axis=0, tiled=True),
        lax.all_gather(output_weight, "row", axis=1, tiled=True),
        lax.all_gather(router_weight, "row", axis=0, tiled=True),
        lax.all_gather(shared_gate, "row", axis=0, tiled=True),
        lax.all_gather(shared_up, "row", axis=0, tiled=True),
        lax.all_gather(shared_down, "row", axis=1, tiled=True),
    )
    source = inputs.astype(f32)
    scale_one = rms_scale(source)
    unit_one = source * scale_one
    normed_one = spread((unit_one * norm_gain).astype(bf16))
    query = jnp.dot(normed_one, query_full, preferred_element_type=f32).reshape(
        rows_count, local_heads, NOPE + ROPE
    )
    latent = jnp.dot(normed_one, latent_full, preferred_element_type=f32).astype(bf16)
    cosine, sine = rotation(rows_count, ROPE)
    head_cos = cosine[:, None, :]
    head_sin = sine[:, None, :]
    compressed = latent[:, :RANK].astype(f32)
    latent_scale = lax.rsqrt(jnp.mean(compressed * compressed, axis=1, keepdims=True) + epsilon)
    latent_unit = compressed * latent_scale
    latent_normed = (latent_unit * latent_gain).astype(bf16)
    key_rope = rotate(latent[:, RANK:].astype(f32), cosine, sine).astype(bf16)
    expanded = jnp.dot(latent_normed, expand_full, preferred_element_type=f32).reshape(
        rows_count, local_heads, NOPE + VDIM
    )
    key_nope = expanded[..., :NOPE].astype(bf16)
    values_all = expanded[..., NOPE:].astype(bf16)
    query_nope = query[..., :NOPE].astype(bf16)
    query_rope = rotate(query[..., NOPE:], head_cos, head_sin).astype(bf16)

    def block_scores(start):
        ending = start + block_rows
        raw = jnp.einsum("qhd,khd->hqk", query_nope, key_nope, preferred_element_type=f32)
        raw = raw + jnp.einsum("qhd,kd->hqk", query_rope, key_rope, preferred_element_type=f32)
        allowed = (segment_row[start:ending, None] == segment_row[None, :]) & (
            places[None, :] <= places[:, None]
        )
        return jnp.where(allowed[None], raw * score_scale, -1e30)

    start = 0
    scores = block_scores(start)
    top = jnp.max(scores, axis=2, keepdims=True)
    exponent = jnp.exp(scores - top)
    total = jnp.sum(exponent, axis=2, keepdims=True)
    weights = exponent / total
    log_blocks = top + jnp.log(total)
    mixed_blocks = jnp.einsum(
        "hqk,khd->qhd", weights.astype(bf16), values_all, preferred_element_type=f32
    ).astype(bf16)
    mixed = mixed_blocks.reshape(rows_count, local_heads * VDIM)
    attended = mix_sums(jnp.dot(mixed, output_full, preferred_element_type=f32))
    middle = source + attended
    scale_two = rms_scale(middle)
    unit_two = middle * scale_two
    normed_two_share = (unit_two * ffn_gain).astype(bf16)
    normed_two = spread(normed_two_share)
    logits = jnp.dot(normed_two, router_full, preferred_element_type=f32)
    log_total = jax.nn.logsumexp(logits, axis=1, keepdims=True)
    chosen = routes[:, :, None] == jnp.arange(expert_count, dtype=jnp.int32)[None, None, :]
    picked = jnp.sum(jnp.where(chosen, logits[:, None, :], 0.0), axis=2)
    gates = jnp.exp(picked - log_total)
    upstream = out_grad.astype(f32)
    upstream_full = spread(out_grad)
    shared_gate_pre = jnp.dot(normed_two, shared_gate_full, preferred_element_type=f32)
    shared_up_pre = jnp.dot(normed_two, shared_up_full, preferred_element_type=f32)
    shared_hidden = (jax.nn.silu(shared_gate_pre) * shared_up_pre).astype(bf16)
    shared_part = jnp.dot(shared_hidden, shared_down_full, preferred_element_type=f32)
    flat_routes = routes.reshape(-1)
    hits = (flat_routes[:, None] == jnp.arange(expert_count, dtype=jnp.int32)[None, :]).astype(
        jnp.int32
    )
    ranks = jnp.sum((jnp.cumsum(hits, axis=0) - 1) * hits, axis=1)
    owners = jnp.arange(rows_count * TOPK, dtype=jnp.int32) // TOPK
    share_slots = capacity // col_devices
    slot_count = row_devices * share_slots
    buffer_size = EXP_DEV * slot_count
    inside = ranks // share_slots == col_place
    slot_place = jnp.where(
        inside,
        flat_routes % EXP_DEV * slot_count
        + flat_routes // EXP_DEV * share_slots
        + ranks
        - col_place * share_slots,
        buffer_size,
    )
    token_of_slot = (
        jnp.full((buffer_size + 1,), rows_count, jnp.int32).at[slot_place].set(owners)[:buffer_size]
    )
    gate_of_slot = (
        jnp.zeros((buffer_size + 1,), f32).at[slot_place].set(gates.reshape(-1))[:buffer_size]
    )
    position = slot_place.reshape(rows_count, TOPK)
    gate_stack, up_stack, down_stack = (
        lax.all_gather(expert_gate, "col", axis=1, tiled=True),
        lax.all_gather(expert_up, "col", axis=1, tiled=True),
        lax.all_gather(expert_down, "col", axis=1, tiled=True),
    )
    padded_rows = jnp.concatenate([normed_two, jnp.zeros((1, D), bf16)], axis=0)
    outgoing = padded_rows[token_of_slot].reshape(EXP_DEV, slot_count, D)
    arrived = send_rows(outgoing)
    gate_pre = jnp.einsum("jnd,jfd->jnf", arrived, gate_stack, preferred_element_type=f32)
    up_pre = jnp.einsum("jnd,jfd->jnf", arrived, up_stack, preferred_element_type=f32)
    hidden = (jax.nn.silu(gate_pre) * up_pre).astype(bf16)
    expert_result = jnp.einsum(
        "jnf,jfd->jnd", hidden, down_stack, preferred_element_type=f32
    ).astype(bf16)
    returned = return_rows(expert_result).reshape(buffer_size, D)
    returned = jnp.concatenate([returned, jnp.zeros((1, D), bf16)], axis=0)
    slot_values = returned[position].astype(f32)
    combined = mix_sums(jnp.sum(gates[:, :, None] * slot_values, axis=1) + shared_part)
    upstream_wide = upstream_full.astype(f32)
    gate_partial = jnp.sum(upstream_wide[:, None, :] * slot_values, axis=2)
    output = (middle + combined).astype(bf16)
    gate_grads = lax.psum(gate_partial, "col")
    chances = jnp.exp(logits - log_total)
    weighted_gates = gate_grads * gates
    logit_grads = (
        jnp.sum(jnp.where(chosen, weighted_gates[:, :, None], 0.0), axis=1)
        - chances * jnp.sum(weighted_gates, axis=1, keepdims=True)
    ).astype(bf16)
    router_rows = lax.dynamic_slice_in_dim(router_full, col_place * width_share, width_share, 0)
    router_back = jnp.einsum("te,de->td", logit_grads, router_rows, preferred_element_type=f32)
    router_grad_part = jnp.einsum("td,te->de", normed_two, logit_grads, preferred_element_type=f32)
    shared_hidden_back = jnp.einsum(
        "td,fd->tf", upstream_full, shared_down_full, preferred_element_type=f32
    )
    shared_sigmoid = jax.nn.sigmoid(shared_gate_pre)
    shared_gate_back = (
        shared_hidden_back * shared_up_pre * silu_slope(shared_gate_pre, shared_sigmoid)
    ).astype(bf16)
    shared_up_back = (shared_hidden_back * (shared_gate_pre * shared_sigmoid)).astype(bf16)
    shared_input_back = jnp.einsum(
        "tf,df->td", shared_gate_back, shared_gate_full, preferred_element_type=f32
    ) + jnp.einsum("tf,df->td", shared_up_back, shared_up_full, preferred_element_type=f32)
    shared_gate_part = jnp.einsum(
        "td,tf->df", normed_two, shared_gate_back, preferred_element_type=f32
    )
    shared_up_part = jnp.einsum("td,tf->df", normed_two, shared_up_back, preferred_element_type=f32)
    shared_down_part = jnp.einsum(
        "tf,td->fd", shared_hidden, upstream_full, preferred_element_type=f32
    )
    padded_upstream = jnp.concatenate([upstream_wide, jnp.zeros((1, D), f32)], axis=0)
    slot_grads = (
        (gate_of_slot[:, None] * padded_upstream[token_of_slot])
        .astype(bf16)
        .reshape(EXP_DEV, slot_count, D)
    )
    arrived_grads = send_rows(slot_grads)
    hidden_back = jnp.einsum("jnd,jfd->jnf", arrived_grads, down_stack, preferred_element_type=f32)
    gate_sigmoid = jax.nn.sigmoid(gate_pre)
    gate_back = (hidden_back * up_pre * silu_slope(gate_pre, gate_sigmoid)).astype(bf16)
    up_back = (hidden_back * (gate_pre * gate_sigmoid)).astype(bf16)
    row_back = jnp.einsum(
        "jnf,jfd->jnd", gate_back, gate_stack, preferred_element_type=f32
    ) + jnp.einsum("jnf,jfd->jnd", up_back, up_stack, preferred_element_type=f32)
    returned_grads = return_rows(row_back.astype(bf16)).reshape(buffer_size, D)
    returned_grads = jnp.concatenate([returned_grads, jnp.zeros((1, D), bf16)], axis=0)
    routed_back = jnp.sum(returned_grads[position].astype(f32), axis=1)
    normed_two_back = mix_sums(routed_back + shared_input_back) + router_back
    gate_pieces = []
    up_pieces = []
    down_pieces = []
    for expert in range(EXP_DEV):
        gate_piece, up_piece, down_piece = (
            lax.psum_scatter(
                jnp.einsum(
                    "nf,nd->fd", gate_back[expert], arrived[expert], preferred_element_type=f32
                ).astype(jnp.bfloat16),
                "col",
                scatter_dimension=0,
                tiled=True,
            ).astype(jnp.float32),
            lax.psum_scatter(
                jnp.einsum(
                    "nf,nd->fd", up_back[expert], arrived[expert], preferred_element_type=f32
                ).astype(jnp.bfloat16),
                "col",
                scatter_dimension=0,
                tiled=True,
            ).astype(jnp.float32),
            lax.psum_scatter(
                jnp.einsum(
                    "nf,nd->fd", hidden[expert], arrived_grads[expert], preferred_element_type=f32
                ).astype(jnp.bfloat16),
                "col",
                scatter_dimension=0,
                tiled=True,
            ).astype(jnp.float32),
        )
        gate_pieces.append(gate_piece)
        up_pieces.append(up_piece)
        down_pieces.append(down_piece)
    expert_gate_grad = jnp.stack(gate_pieces, axis=0)
    expert_up_grad = jnp.stack(up_pieces, axis=0)
    expert_down_grad = jnp.stack(down_pieces, axis=0)
    ffn_gain_part = jnp.sum(normed_two_back * unit_two, axis=0)
    middle_back = upstream + norm_backward(normed_two_back, unit_two, scale_two, ffn_gain)
    attended_back = spread(middle_back.astype(bf16))
    mixed_back = (
        jnp.einsum("td,vd->tv", attended_back, output_full, preferred_element_type=f32)
        .astype(bf16)
        .reshape(rows_count, local_heads, VDIM)
    )
    output_grad_part = jnp.einsum("tv,td->vd", mixed, attended_back, preferred_element_type=f32)
    start = 0
    ending = start + block_rows
    scores = block_scores(start)
    weights = jnp.exp(scores - log_blocks)
    weight_back = jnp.einsum("qhd,khd->hqk", mixed_back, values_all, preferred_element_type=f32)
    center = jnp.sum(weight_back * weights, axis=2, keepdims=True)
    raw_back = (weights * (weight_back - center) * score_scale).astype(bf16)
    query_nope_back = jnp.einsum("hqk,khd->qhd", raw_back, key_nope, preferred_element_type=f32)
    query_rope_back = jnp.einsum("hqk,kd->qhd", raw_back, key_rope, preferred_element_type=f32)
    key_nope_back = jnp.einsum("hqk,qhd->khd", raw_back, query_nope, preferred_element_type=f32)
    key_rope_back = jnp.einsum("hqk,qhd->kd", raw_back, query_rope, preferred_element_type=f32)
    values_back = jnp.einsum(
        "hqk,qhd->khd", weights.astype(bf16), mixed_back, preferred_element_type=f32
    )
    query_back = jnp.concatenate(
        [query_nope_back, unrotate(query_rope_back, head_cos, head_sin)], axis=2
    )
    query_back = query_back.astype(bf16).reshape(rows_count, local_heads * (NOPE + ROPE))
    expanded_back = (
        jnp.concatenate([key_nope_back, values_back], axis=2)
        .astype(bf16)
        .reshape(rows_count, local_heads * (NOPE + VDIM))
    )
    latent_normed_back = jnp.einsum(
        "tc,rc->tr", expanded_back, expand_full, preferred_element_type=f32
    )
    expand_grad_part = jnp.einsum(
        "tr,tc->rc", latent_normed, expanded_back, preferred_element_type=f32
    )
    latent_gain_part = jnp.sum(latent_normed_back * latent_unit, axis=0)
    latent_weighted = latent_normed_back * latent_gain
    compressed_back = latent_scale * (
        latent_weighted
        - latent_unit * jnp.mean(latent_weighted * latent_unit, axis=1, keepdims=True)
    )
    rope_back = unrotate(key_rope_back, cosine, sine)
    latent_back, latent_gain_col = (
        lax.psum(
            jnp.concatenate([compressed_back, rope_back], axis=1).astype(jnp.bfloat16), "col"
        ).astype(jnp.float32),
        lax.psum(latent_gain_part.astype(jnp.bfloat16), "col").astype(jnp.float32),
    )
    latent_back = latent_back.astype(bf16)
    latent_grad_part = jnp.einsum("td,tc->dc", normed_one, latent_back, preferred_element_type=f32)
    query_grad_part = jnp.einsum("td,tc->dc", normed_one, query_back, preferred_element_type=f32)
    latent_rows = lax.dynamic_slice_in_dim(latent_full, col_place * width_share, width_share, 0)
    input_part = jnp.einsum("tc,dc->td", query_back, query_full, preferred_element_type=f32)
    normed_one_back = mix_sums(input_part) + jnp.einsum(
        "tc,dc->td", latent_back, latent_rows, preferred_element_type=f32
    )
    norm_gain_part = jnp.sum(normed_one_back * unit_one, axis=0)
    input_grad = middle_back + norm_backward(normed_one_back, unit_one, scale_one, norm_gain)
    norm_gain_grad, ffn_gain_grad, latent_gain_grad = lax.psum(
        (norm_gain_part, ffn_gain_part, latent_gain_col), "row"
    )
    (
        query_grad,
        latent_grad,
        expand_grad,
        output_grad,
        router_grad,
        shared_gate_grad,
        shared_up_grad,
        shared_down_grad,
    ) = (
        lax.psum_scatter(
            query_grad_part.astype(jnp.bfloat16), "row", scatter_dimension=0, tiled=True
        ).astype(jnp.float32),
        lax.psum_scatter(
            latent_grad_part.astype(jnp.bfloat16), "row", scatter_dimension=0, tiled=True
        ).astype(jnp.float32),
        lax.psum_scatter(
            expand_grad_part.astype(jnp.bfloat16), "row", scatter_dimension=0, tiled=True
        ).astype(jnp.float32),
        lax.psum_scatter(
            output_grad_part.astype(jnp.bfloat16), "row", scatter_dimension=1, tiled=True
        ).astype(jnp.float32),
        lax.psum_scatter(
            router_grad_part.astype(jnp.bfloat16), "row", scatter_dimension=0, tiled=True
        ).astype(jnp.float32),
        lax.psum_scatter(
            shared_gate_part.astype(jnp.bfloat16), "row", scatter_dimension=0, tiled=True
        ).astype(jnp.float32),
        lax.psum_scatter(
            shared_up_part.astype(jnp.bfloat16), "row", scatter_dimension=0, tiled=True
        ).astype(jnp.float32),
        lax.psum_scatter(
            shared_down_part.astype(jnp.bfloat16), "row", scatter_dimension=1, tiled=True
        ).astype(jnp.float32),
    )
    return (
        output,
        input_grad,
        norm_gain_grad,
        query_grad,
        latent_grad,
        latent_gain_grad,
        expand_grad,
        output_grad,
        ffn_gain_grad,
        router_grad,
        expert_gate_grad,
        expert_up_grad,
        expert_down_grad,
        shared_gate_grad,
        shared_up_grad,
        shared_down_grad,
    )


def solution(mesh):
    in_specs = (
        P("row", "col"),
        P("row", None),
        P("row", None),
        P("col"),
        P("row", "col"),
        P("row", None),
        P(),
        P("row", "col"),
        P("col", "row"),
        P("col"),
        P("row", None),
        P("row", "col", None),
        P("row", "col", None),
        P("row", "col", None),
        P("row", "col"),
        P("row", "col"),
        P("col", "row"),
        P("row", "col"),
    )
    out_specs = (
        P("row", "col"),
        P("row", "col"),
        P("col"),
        P("row", "col"),
        P("row", None),
        P(),
        P("row", "col"),
        P("col", "row"),
        P("col"),
        P("row", None),
        P("row", "col", None),
        P("row", "col", None),
        P("row", "col", None),
        P("row", "col"),
        P("row", "col"),
        P("col", "row"),
    )
    plan = on_device if dict(mesh.shape) == {"row": 16, "col": 2} else on_device_general
    return jax.shard_map(
        plan, mesh=mesh, in_specs=in_specs, out_specs=out_specs, check_vma=False
    )
```

```python
import jax
import jax.numpy as jnp
from jax import lax
from jax.experimental import pallas as pl
from jax.experimental.pallas import tpu as pltpu
from jax.sharding import PartitionSpec as P

D = 2048
NOPE = 128
ROPE = 64
RANK = 512
VDIM = 128
TOPK = 6
EXP_DEV = 4


epsilon = 1e-06
theta = 10000.0


def rotation(count, width):
    half = width // 2
    places = jnp.arange(count, dtype=jnp.float32)
    rates = theta ** (-jnp.arange(half, dtype=jnp.float32) * 2.0 / width)
    angles = places[:, None] * rates[None, :]
    return (jnp.cos(angles), jnp.sin(angles))


def rotate(values, cosine, sine):
    half = values.shape[-1] // 2
    first = values[..., :half]
    second = values[..., half:]
    return jnp.concatenate(
        [first * cosine - second * sine, second * cosine + first * sine], axis=-1
    )


def unrotate(grads, cosine, sine):
    half = grads.shape[-1] // 2
    first = grads[..., :half]
    second = grads[..., half:]
    return jnp.concatenate(
        [first * cosine + second * sine, second * cosine - first * sine], axis=-1
    )


def silu_slope(pre, sigmoid_value):
    return sigmoid_value * (1.0 + pre * (1.0 - sigmoid_value))


def col_total(values):
    return lax.psum(values, "col")


def spread(values):
    return lax.all_gather(values, "col", axis=1, tiled=True)


def mix_sums(values):
    return lax.psum_scatter(
        values.astype(jnp.bfloat16), "col", scatter_dimension=1, tiled=True
    ).astype(jnp.float32)


def send_rows(rows):
    return lax.all_to_all(rows, "row", split_axis=1, concat_axis=1, tiled=True)


def return_rows(rows):
    return lax.all_to_all(rows, "row", split_axis=1, concat_axis=1, tiled=True)


def rms_scale(rows):
    total = col_total(jnp.sum(rows * rows, axis=1))
    return lax.rsqrt(total / D + epsilon)[:, None]


def norm_backward(grads, unit, scale, gain):
    weighted = grads * gain
    average = col_total(jnp.sum(weighted * unit, axis=1)) / D
    return scale * (weighted - unit * average[:, None])


PLANES = 4
COMMON = 192
UNIQUE = 160
SENT = COMMON + UNIQUE
SHARED_PAD = 128
QUERY_COLUMNS = 1536
SCORE_SCALE = (NOPE + ROPE) ** (-0.5)


def swap_cols(values):
    return lax.ppermute(values, "col", [(0, 1), (1, 0)])


def swap_rows(values, bit):
    return lax.ppermute(values, "row", [(i, i ^ bit) for i in range(16)])


def turn_planes(values):
    return lax.ppermute(values, "row", [(i, (i + 4) % 16) for i in range(16)])


def join_cols(values, first):
    other = swap_cols(values)
    return jnp.where(
        first,
        jnp.concatenate([values, other], axis=1),
        jnp.concatenate([other, values], axis=1),
    )


def own_columns(values, first):
    half = values.shape[-1] // 2
    return jnp.where(first, values[..., :half], values[..., half:])


def other_columns(values, first):
    half = values.shape[-1] // 2
    return jnp.where(first, values[..., half:], values[..., :half])


def sent_rows(values, first):
    return jnp.concatenate(
        [values[:COMMON], jnp.where(first, values[COMMON:SENT], values[SENT:])], axis=0
    )


def local_tokens(values, axis, first):
    common = lax.slice_in_dim(values, 0, COMMON, axis=axis)
    one = lax.slice_in_dim(values, COMMON, SENT, axis=axis)
    two = lax.slice_in_dim(values, SENT, SENT + UNIQUE, axis=axis)
    return jnp.concatenate(
        [common, jnp.where(first, one, two), jnp.where(first, two, one)], axis=axis
    )


def together(*values):
    return lax.optimization_barrier(values)


def after(values, *others):
    return lax.optimization_barrier((values, *others))[0]


def batch(values):
    starts = [0]
    for value in values:
        starts.append(starts[-1] + value.shape[0])
    return jnp.concatenate(values, axis=0), starts[:-1]


class Spread:
    def __init__(self, rows):
        self.held = {(0, 0): rows}
        self.unique = {}
        self.sibling = {}

    def turn(self, plane):
        return turn_planes(self.held[plane - 1, 0])

    def cross(self, plane):
        return swap_rows(self.held[plane, 0], 2)

    def sent(self, *keys):
        return [self.held[key][COMMON:] for key in keys]

    def got(self, array, starts, *keys):
        for key, start in zip(keys, starts):
            self.unique[key] = (array, start)

    def passed(self, *keys):
        pieces = []
        for key in keys:
            if key[2]:
                array, start = self.unique[key[:2]]
                pieces.append(array[start : start + UNIQUE])
            else:
                pieces.append(self.held[key[:2]])
        return pieces

    def taken(self, array, starts, *keys):
        for key, start in zip(keys, starts):
            self.sibling[key] = (array, start)

    def family(self, plane):
        result = []
        for across in (0, 1):
            result.append(((self.held[plane, across], 0), self.unique[plane, across]))
            result.append((self.sibling[plane, across, 0], self.sibling[plane, across, 1]))
        return result


def add_unique(rest, unique, across):
    return jnp.concatenate([rest[across, :COMMON], rest[across, COMMON:] + unique[across]], axis=0)


def column_pieces(weight, bounds):
    return jnp.concatenate([weight[:, a:b] for a, b in bounds], axis=1)


def pair_columns(weight):
    head = NOPE + ROPE
    bounds = []
    for start in range(0, weight.shape[1], 2 * head):
        bounds += [(start, start + NOPE), (start + head, start + head + NOPE)]
        bounds += [(start + NOPE, start + head), (start + head + NOPE, start + 2 * head)]
    return column_pieces(weight, bounds)


def head_columns(weight):
    bounds = []
    for start in range(0, weight.shape[1], 2 * (NOPE + ROPE)):
        turned = start + 2 * NOPE
        bounds += [(start, start + NOPE), (turned, turned + ROPE)]
        bounds += [(start + NOPE, turned), (turned + ROPE, turned + 2 * ROPE)]
    return column_pieces(weight, bounds)


def merge_rows(own, received, first):
    own = own.astype(jnp.float32)
    received = received.astype(jnp.float32)
    common = own[:COMMON] + received[:COMMON]
    mine = own[COMMON:]
    theirs = received[COMMON:]
    return jnp.concatenate(
        [common, jnp.where(first, mine, theirs), jnp.where(first, theirs, mine)], axis=0
    )


FAMILIES = 4


def kernel_params(mebibytes):
    return pltpu.CompilerParams(vmem_limit_bytes=mebibytes * 1024 * 1024)


def short_cost():
    return pl.CostEstimate(flops=10**9, bytes_accessed=10**6, transcendentals=0)


def dot_last(left, right):
    return lax.dot_general(
        left, right, (((1,), (1,)), ((), ())), preferred_element_type=jnp.float32
    )


def dot_first(left, right):
    return lax.dot_general(
        left, right, (((0,), (0,)), ((), ())), preferred_element_type=jnp.float32
    )


def dot_plain(left, right):
    return jnp.dot(left, right, preferred_element_type=jnp.float32)


def slot_matches(codes_ref, capacity):
    tokens = codes_ref.shape[-1]
    ranks = lax.broadcasted_iota(jnp.int32, (capacity, tokens), 0)
    return [codes_ref[0, j : j + 1, :] == ranks for j in range(EXP_DEV)]


def as_picks(matches):
    one = [jnp.where(m, 1.0, 0.0).astype(jnp.bfloat16) for m in matches]
    return jnp.concatenate(one, axis=0)


def row_copies(refs, starts, held, sems, f):
    return [
        pltpu.make_async_copy(
            refs[2 * f].at[pl.ds(starts[2 * f], SENT)],
            held.at[f, pl.ds(0, SENT)],
            sems.at[f, 0],
        ),
        pltpu.make_async_copy(
            refs[2 * f + 1].at[pl.ds(starts[2 * f + 1], UNIQUE)],
            held.at[f, pl.ds(SENT, UNIQUE)],
            sems.at[f, 1],
        ),
    ]


def start_rows(refs, starts, held, sems):
    for f in range(FAMILIES):
        for copy in row_copies(refs, starts, held, sems, f):
            copy.start()


def wait_rows(refs, starts, held, sems, f):
    for family in range(FAMILIES):

        @pl.when(f == family)
        def _():
            for copy in row_copies(refs, starts, held, sems, family):
                copy.wait()


def pick_grads(plane, codes, last, capacity):
    pieces = [piece[0] for family in plane for piece in family]
    starts = [piece[1] for family in plane for piece in family]
    tokens = SENT + UNIQUE
    width = last.shape[1]
    pad = last.shape[0]

    def body(*refs):
        rows_in = refs[:8]
        codes_ref, last_ref, slots_ref, hidden_ref, held, sems = refs[8:]
        f = pl.program_id(0)

        @pl.when(f == 0)
        def _():
            start_rows(rows_in, starts, held, sems)

        wait_rows(rows_in, starts, held, sems, f)
        rows = held[f]
        picks = as_picks(slot_matches(codes_ref, capacity))
        taken = dot_plain(picks, rows).astype(jnp.bfloat16)
        slots_ref[...] = taken.reshape(EXP_DEV, capacity, width)
        hidden_ref[0] = dot_last(rows, last_ref[...])

    return pl.pallas_call(
        body,
        grid=(FAMILIES,),
        in_specs=[pl.BlockSpec(memory_space=pl.ANY)] * 8
        + [
            pl.BlockSpec((1, 8, tokens), lambda f: (f, 0, 0)),
            pl.BlockSpec((pad, width), lambda f: (0, 0)),
        ],
        out_specs=[
            pl.BlockSpec((EXP_DEV, capacity, width), lambda f: (0, f, 0)),
            pl.BlockSpec((1, tokens, pad), lambda f: (f, 0, 0)),
        ],
        out_shape=[
            jax.ShapeDtypeStruct((EXP_DEV, FAMILIES * capacity, width), jnp.bfloat16),
            jax.ShapeDtypeStruct((FAMILIES, tokens, pad), jnp.float32),
        ],
        scratch_shapes=[
            pltpu.VMEM((FAMILIES, tokens, width), jnp.bfloat16),
            pltpu.SemaphoreType.DMA((FAMILIES, 2)),
        ],
        compiler_params=kernel_params(32),
        cost_estimate=short_cost(),
    )(*pieces, codes, last)


def pick_rows(plane, grad_plane, codes, router, pair, hidden_grads, capacity):
    pieces = [piece[0] for family in plane for piece in family]
    starts = [piece[1] for family in plane for piece in family]
    grad_pieces = [piece[0] for family in grad_plane for piece in family]
    grad_starts = [piece[1] for family in grad_plane for piece in family]
    tokens = SENT + UNIQUE
    width = pair.shape[1]
    pad = pair.shape[0] // 2

    def body(*refs):
        rows_in = refs[:8]
        grads_in = refs[8:16]
        (codes_ref, router_ref, pair_ref, hidden_grads_ref) = refs[16:20]
        (slots_ref, gates_ref, hidden_ref, back_ref, grad_ref) = refs[20:25]
        held, held_grads, sems, grad_sems = refs[25:]
        f = pl.program_id(0)

        @pl.when(f == 0)
        def _():
            start_rows(rows_in, starts, held, sems)
            start_rows(grads_in, grad_starts, held_grads, grad_sems)
            grad_ref[...] = jnp.zeros_like(grad_ref)

        wait_rows(rows_in, starts, held, sems, f)
        rows = held[f]
        matches = slot_matches(codes_ref, capacity)
        taken = dot_plain(as_picks(matches), rows).astype(jnp.bfloat16)
        slots_ref[...] = taken.reshape(EXP_DEV, capacity, width)
        logits = dot_last(router_ref[...], rows)
        top = jnp.max(logits, axis=0, keepdims=True)
        total = jnp.log(jnp.sum(jnp.exp(logits - top), axis=0, keepdims=True)) + top
        for j in range(EXP_DEV):
            chance = jnp.exp(logits[j : j + 1] - total)
            gate = jnp.sum(jnp.where(matches[j], chance, 0.0), axis=1, keepdims=True)
            gates_ref[j] = jnp.broadcast_to(gate, (capacity, 128))
        pre = dot_last(rows, pair_ref[...])
        gate_pre = pre[:, :pad]
        up_pre = pre[:, pad:]
        hidden_back = hidden_grads_ref[0]
        sigmoid_value = jax.nn.sigmoid(gate_pre)
        silu_value = gate_pre * sigmoid_value
        hidden = (silu_value * up_pre).astype(jnp.bfloat16)
        slope = sigmoid_value * (1.0 + gate_pre * (1.0 - sigmoid_value))
        gate_back = (hidden_back * up_pre * slope).astype(jnp.bfloat16)
        up_back = (hidden_back * silu_value).astype(jnp.bfloat16)
        back = jnp.concatenate([gate_back, up_back], axis=1)
        hidden_ref[0] = hidden
        back_ref[0] = back
        grad_ref[: 2 * pad] += dot_first(back, rows)
        wait_rows(grads_in, grad_starts, held_grads, grad_sems, f)
        grad_ref[2 * pad :] += dot_first(hidden, held_grads[f])

    return pl.pallas_call(
        body,
        grid=(FAMILIES,),
        in_specs=[pl.BlockSpec(memory_space=pl.ANY)] * 16
        + [
            pl.BlockSpec((1, 8, tokens), lambda f: (f, 0, 0)),
            pl.BlockSpec(router.shape, lambda f: (0, 0)),
            pl.BlockSpec(pair.shape, lambda f: (0, 0)),
            pl.BlockSpec((1, tokens, pad), lambda f: (f, 0, 0)),
        ],
        out_specs=[
            pl.BlockSpec((EXP_DEV, capacity, width), lambda f: (0, f, 0)),
            pl.BlockSpec((EXP_DEV, capacity, 128), lambda f: (0, f, 0)),
            pl.BlockSpec((1, tokens, pad), lambda f: (f, 0, 0)),
            pl.BlockSpec((1, tokens, 2 * pad), lambda f: (f, 0, 0)),
            pl.BlockSpec((3 * pad, width), lambda f: (0, 0)),
        ],
        out_shape=[
            jax.ShapeDtypeStruct((EXP_DEV, FAMILIES * capacity, width), jnp.bfloat16),
            jax.ShapeDtypeStruct((EXP_DEV, FAMILIES * capacity, 128), jnp.float32),
            jax.ShapeDtypeStruct((FAMILIES, tokens, pad), jnp.bfloat16),
            jax.ShapeDtypeStruct((FAMILIES, tokens, 2 * pad), jnp.bfloat16),
            jax.ShapeDtypeStruct((3 * pad, width), jnp.float32),
        ],
        scratch_shapes=[
            pltpu.VMEM((FAMILIES, tokens, width), jnp.bfloat16),
            pltpu.VMEM((FAMILIES, tokens, width), jnp.bfloat16),
            pltpu.SemaphoreType.DMA((FAMILIES, 2)),
            pltpu.SemaphoreType.DMA((FAMILIES, 2)),
        ],
        compiler_params=kernel_params(48),
        cost_estimate=short_cost(),
    )(*pieces, *grad_pieces, codes, router, pair, hidden_grads)


def run_experts(slot_rows, slot_grads, gates, expert_gate, expert_up, expert_down):
    count, slots, width = slot_rows.shape
    units = expert_gate.shape[1]

    def body(
        rows_ref,
        grads_ref,
        gates_ref,
        gate_ref,
        up_ref,
        down_ref,
        sum_ref,
        back_ref,
        hidden_ref,
        gate_back_ref,
        up_back_ref,
        gate_grad_ref,
    ):
        rows = rows_ref[0]
        gates_here = gates_ref[0][:, :1]
        gate_pre = dot_last(rows, gate_ref[0])
        up_pre = dot_last(rows, up_ref[0])
        down_back = dot_last(grads_ref[0], down_ref[0])
        sigmoid_value = jax.nn.sigmoid(gate_pre)
        silu_value = gate_pre * sigmoid_value
        hidden = silu_value * up_pre
        gate_grad = jnp.sum(hidden * down_back, axis=1, keepdims=True)
        gate_grad_ref[0] = jnp.broadcast_to(gate_grad, (slots, 128))
        hidden_back = down_back * gates_here
        slope = sigmoid_value * (1.0 + gate_pre * (1.0 - sigmoid_value))
        gate_back = (hidden_back * up_pre * slope).astype(jnp.bfloat16)
        up_back = (hidden_back * silu_value).astype(jnp.bfloat16)
        scaled = (hidden * gates_here).astype(jnp.bfloat16)
        hidden_ref[0] = scaled
        gate_back_ref[0] = gate_back
        up_back_ref[0] = up_back
        back = dot_plain(gate_back, gate_ref[0]) + dot_plain(up_back, up_ref[0])
        back_ref[0] = back.astype(jnp.bfloat16)
        sum_ref[0] = dot_plain(scaled, down_ref[0]).astype(jnp.bfloat16)

    wide = pl.BlockSpec((1, slots, width), lambda j: (j, 0, 0))
    narrow = pl.BlockSpec((1, slots, 128), lambda j: (j, 0, 0))
    inner = pl.BlockSpec((1, slots, units), lambda j: (j, 0, 0))
    matrix = pl.BlockSpec((1, units, width), lambda j: (j, 0, 0))
    return pl.pallas_call(
        body,
        grid=(count,),
        in_specs=[wide, wide, narrow, matrix, matrix, matrix],
        out_specs=[wide, wide, inner, inner, inner, narrow],
        out_shape=[
            jax.ShapeDtypeStruct((count, slots, width), jnp.bfloat16),
            jax.ShapeDtypeStruct((count, slots, width), jnp.bfloat16),
            jax.ShapeDtypeStruct((count, slots, units), jnp.bfloat16),
            jax.ShapeDtypeStruct((count, slots, units), jnp.bfloat16),
            jax.ShapeDtypeStruct((count, slots, units), jnp.bfloat16),
            jax.ShapeDtypeStruct((count, slots, 128), jnp.float32),
        ],
        compiler_params=kernel_params(56),
        cost_estimate=short_cost(),
    )(slot_rows, slot_grads, gates, expert_gate, expert_up, expert_down)


def sum_tokens(values, codes, shared, matrix, capacity, core, received=None, gate_grads=None):
    tokens = codes.shape[2]
    width = values.shape[2]
    inner = matrix.shape[0]
    with_rows = received is not None
    with_gates = gate_grads is not None

    def body(*refs):
        values_ref, codes_ref, shared_ref, matrix_ref = refs[:4]
        outs = refs[4 + with_rows + with_gates :]
        matches = slot_matches(codes_ref, capacity)
        rows = values_ref[...].reshape(EXP_DEV * capacity, width)
        total = dot_first(as_picks(matches), rows)
        total = total + dot_plain(shared_ref[0], matrix_ref[...])
        if with_rows:
            total = (total + refs[4][0].astype(jnp.float32)).astype(jnp.bfloat16)
            outs[0][0] = total[:SENT]
            outs[1][0] = total[SENT:]
        else:
            outs[0][0] = total.astype(jnp.bfloat16)
        if with_gates:
            dense = [
                jnp.sum(
                    jnp.where(matches[j], refs[4 + with_rows][j][:, :1], 0.0),
                    axis=0,
                    keepdims=True,
                )
                for j in range(EXP_DEV)
            ]
            outs[-1][0] = jnp.concatenate(dense + [jnp.zeros((4, tokens), jnp.float32)], axis=0)

    in_specs = [
        pl.BlockSpec((EXP_DEV, capacity, width), lambda i: (0, 2 * i + core, 0)),
        pl.BlockSpec((1, 8, tokens), lambda i: (2 * i + core, 0, 0)),
        pl.BlockSpec((1, tokens, inner), lambda i: (2 * i + core, 0, 0)),
        pl.BlockSpec((inner, width), lambda i: (0, 0)),
    ]
    operands = [values, codes, shared, matrix]
    pieces = [tokens]
    if with_rows:
        in_specs.append(pl.BlockSpec((1, tokens, width), lambda i: (i, 0, 0)))
        operands.append(received)
        pieces = [SENT, UNIQUE]
    out_specs = [pl.BlockSpec((1, piece, width), lambda i: (i, 0, 0)) for piece in pieces]
    out_shape = [jax.ShapeDtypeStruct((2, piece, width), jnp.bfloat16) for piece in pieces]
    if with_gates:
        in_specs.append(pl.BlockSpec((EXP_DEV, capacity, 128), lambda i: (0, 2 * i + core, 0)))
        operands.append(gate_grads)
        out_specs.append(pl.BlockSpec((1, 8, tokens), lambda i: (i, 0, 0)))
        out_shape.append(jax.ShapeDtypeStruct((2, 8, tokens), jnp.float32))
    return pl.pallas_call(
        body,
        grid=(2,),
        in_specs=in_specs,
        out_specs=out_specs,
        out_shape=out_shape,
        compiler_params=kernel_params(24),
        cost_estimate=short_cost(),
    )(*operands)


def pack_weights(query_weight, expand_weight, output_weight, latent_weight, router_weight, routes):
    block = latent_weight.shape[0]
    share = expand_weight.shape[0]
    widths = [
        query_weight.shape[1],
        expand_weight.shape[1] * share // block,
        output_weight.shape[0],
        latent_weight.shape[1],
        router_weight.shape[1],
        routes.shape[1],
    ]
    columns = (sum(widths) + 127) // 128 * 128

    def body(query_ref, expand_ref, output_ref, latent_ref, router_ref, routes_ref, out_ref):
        out_ref[:, : widths[0]] = pair_columns(query_ref[...])
        start = widths[0]
        for i in range(block // share):
            out_ref[share * i : share * (i + 1), start : start + widths[1]] = expand_ref[
                :, widths[1] * i : widths[1] * (i + 1)
            ]
        start += widths[1]
        out_ref[:, start : start + widths[2]] = output_ref[...].T
        start += widths[2]
        out_ref[:, start : start + widths[3] + widths[4]] = jnp.concatenate(
            [latent_ref[...], router_ref[...]], axis=1
        )
        start += widths[3] + widths[4]
        last = jnp.zeros((block, columns - start - widths[5]), jnp.bfloat16)
        out_ref[:, start:] = jnp.concatenate([routes_ref[...], last], axis=1)

    return pl.pallas_call(
        body,
        out_shape=jax.ShapeDtypeStruct((block, columns), jnp.bfloat16),
        compiler_params=kernel_params(16),
        cost_estimate=short_cost(),
    )(query_weight, expand_weight, output_weight, latent_weight, router_weight, routes)


def unpack_grads(output, joined, widths):
    block = joined.shape[0]
    query_width, expand_width, latent_width = widths
    edge = query_width + expand_width
    parts = 4
    share = block // parts

    def body(sum_ref, joined_ref, output_ref, query_ref, expand_ref, latent_ref, router_ref):
        output_ref[...] = sum_ref[...].astype(jnp.float32).T
        query_ref[...] = head_columns(joined_ref[:, :query_width]).astype(jnp.float32)
        for i in range(parts):
            expand_ref[:, expand_width * i : expand_width * (i + 1)] = joined_ref[
                share * i : share * (i + 1), query_width:edge
            ].astype(jnp.float32)
        narrow = joined_ref[:, edge:].astype(jnp.float32)
        latent_ref[...] = narrow[:, :latent_width]
        router_ref[...] = narrow[:, latent_width:]

    shapes = [
        (output.shape[1], block),
        (block, query_width),
        (share, expand_width * parts),
        (block, latent_width),
        (block, joined.shape[1] - edge - latent_width),
    ]
    return pl.pallas_call(
        body,
        out_shape=[jax.ShapeDtypeStruct(shape, jnp.float32) for shape in shapes],
        compiler_params=kernel_params(16),
        cost_estimate=short_cost(),
    )(output, joined)


def block_grads(places, left, right, tile, core, turned=None, expanded=None, received=None):
    count, width = left.shape
    block = width // (4 * PLANES)
    blocks = 2 * PLANES
    columns = right.shape[1]
    steps = columns // tile
    with_expand = turned is not None
    share = turned.shape[0] // (4 * PLANES) if with_expand else 0
    quarter = expanded.shape[1] // steps if with_expand else 0

    def body(places_ref, left_ref, right_ref, *refs):
        held = refs[-2]
        held_turned = refs[-1]
        out_ref = refs[-3]
        step = pl.program_id(0)

        @pl.when(step == 0)
        def _():
            for i in range(blocks):
                place = places_ref[2 * i + core]
                start = pl.multiple_of(place * block, block)
                held[:, block * i : block * (i + 1)] = left_ref[:, pl.ds(start, block)]
                if with_expand:
                    start = pl.multiple_of(place * share, share)
                    held_turned[share * i : share * (i + 1)] = refs[0][pl.ds(start, share)]

        part = dot_first(held[...], right_ref[...]).reshape(blocks, block, tile)
        lanes = pl.ds(pl.multiple_of(step * tile, 128), tile)
        if received is not None:
            got_ref = refs[-4]
            part = part + got_ref[:, :, lanes].astype(jnp.float32)
        out_ref[:, :, lanes] = part.astype(jnp.bfloat16)
        if with_expand:
            part = dot_plain(held_turned[...], refs[1][...]).reshape(blocks, share, quarter)
            lines = pl.ds(pl.multiple_of(step * share, share), share)
            if received is not None:
                part = part + got_ref[:, lines, columns:].astype(jnp.float32)
            out_ref[:, lines, columns:] = part.astype(jnp.bfloat16)

    whole = lambda shape: pl.BlockSpec(shape, lambda h, places_ref: (0,) * len(shape))
    in_specs = [
        whole(left.shape),
        pl.BlockSpec((count, tile), lambda h, places_ref: (0, h)),
    ]
    operands = [left, right]
    if with_expand:
        in_specs += [
            whole(turned.shape),
            pl.BlockSpec((count, quarter), lambda h, places_ref: (0, h)),
        ]
        operands += [turned, expanded]
    shape = (blocks, block, columns + quarter)
    if received is not None:
        in_specs.append(whole(shape))
        operands.append(received)
    return pl.pallas_call(
        body,
        grid_spec=pltpu.PrefetchScalarGridSpec(
            num_scalar_prefetch=1,
            grid=(steps,),
            in_specs=in_specs,
            out_specs=whole(shape),
            scratch_shapes=[
                pltpu.VMEM((count, blocks * block), jnp.bfloat16),
                pltpu.VMEM((max(blocks * share, 16), count), jnp.bfloat16),
            ],
        ),
        out_shape=jax.ShapeDtypeStruct(shape, jnp.bfloat16),
        compiler_params=kernel_params(40),
        cost_estimate=short_cost(),
    )(places, *operands)


def joined_grads(
    places, normed, query_back, turned, expanded, latent_back, normed_two, logit_grads, wide, narrow
):
    count, width = normed.shape
    block = width // (4 * PLANES)
    blocks = 2 * PLANES
    query_width = query_back.shape[1]
    tile = 384
    steps = query_width // tile
    share = turned.shape[0] // (4 * PLANES)
    quarter = expanded.shape[1] // steps
    latent_width = latent_back.shape[1]
    edge = query_width + quarter

    def body(
        places_ref,
        normed_ref,
        query_ref,
        turned_ref,
        expanded_ref,
        latent_ref,
        two_ref,
        logit_ref,
        wide_ref,
        narrow_ref,
        out_ref,
        held,
        held_turned,
        held_two,
    ):
        step = pl.program_id(0)

        @pl.when(step == 0)
        def _():
            for i in range(blocks):
                place = places_ref[2 * i]
                start = pl.multiple_of(place * block, block)
                held[:, block * i : block * (i + 1)] = normed_ref[:, pl.ds(start, block)]
                held_two[:, block * i : block * (i + 1)] = two_ref[:, pl.ds(start, block)]
                start = pl.multiple_of(place * share, share)
                held_turned[share * i : share * (i + 1)] = turned_ref[pl.ds(start, share)]
            part = jnp.concatenate(
                [
                    dot_first(held[...], latent_ref[...]),
                    dot_first(held_two[...], logit_ref[...]),
                ],
                axis=1,
            ).reshape(blocks, block, narrow.shape[2])
            part = part + narrow_ref[...].astype(jnp.float32)
            out_ref[:, :, edge:] = part.astype(jnp.bfloat16)

        lanes = pl.ds(pl.multiple_of(step * tile, 128), tile)
        part = dot_first(held[...], query_ref[...]).reshape(blocks, block, tile)
        part = part + wide_ref[:, :, lanes].astype(jnp.float32)
        out_ref[:, :, lanes] = part.astype(jnp.bfloat16)
        lines = pl.ds(pl.multiple_of(step * share, share), share)
        part = dot_plain(held_turned[...], expanded_ref[...]).reshape(blocks, share, quarter)
        part = part + wide_ref[:, lines, query_width:].astype(jnp.float32)
        out_ref[:, lines, query_width:edge] = part.astype(jnp.bfloat16)

    whole = lambda shape: pl.BlockSpec(shape, lambda h, places_ref: (0,) * len(shape))
    shape = (blocks, block, edge + narrow.shape[2])
    return pl.pallas_call(
        body,
        grid_spec=pltpu.PrefetchScalarGridSpec(
            num_scalar_prefetch=1,
            grid=(steps,),
            in_specs=[
                whole(normed.shape),
                pl.BlockSpec((count, tile), lambda h, places_ref: (0, h)),
                whole(turned.shape),
                pl.BlockSpec((count, quarter), lambda h, places_ref: (0, h)),
                whole(latent_back.shape),
                whole(normed_two.shape),
                whole(logit_grads.shape),
                whole(wide.shape),
                whole(narrow.shape),
            ],
            out_specs=whole(shape),
            scratch_shapes=[
                pltpu.VMEM((count, blocks * block), jnp.bfloat16),
                pltpu.VMEM((blocks * share, count), jnp.bfloat16),
                pltpu.VMEM((count, blocks * block), jnp.bfloat16),
            ],
        ),
        out_shape=jax.ShapeDtypeStruct(shape, jnp.bfloat16),
        compiler_params=kernel_params(40),
        cost_estimate=short_cost(),
    )(
        places,
        normed,
        query_back,
        turned,
        expanded,
        latent_back,
        normed_two,
        logit_grads,
        wide,
        narrow,
    )


def narrow_grads(places, normed, latent_back, normed_two, logit_grads, core):
    count, width = normed.shape
    block = width // (4 * PLANES)
    widths = [latent_back.shape[1], logit_grads.shape[1]]

    def body(places_ref, normed_ref, two_ref, latent_ref, logit_ref, out_ref):
        parts = [
            dot_first(normed_ref[...], latent_ref[...]),
            dot_first(two_ref[...], logit_ref[...]),
        ]
        out_ref[0] = jnp.concatenate(parts, axis=1).astype(jnp.bfloat16)

    piece = pl.BlockSpec((count, block), lambda i, places_ref: (0, places_ref[2 * i + core]))
    whole = lambda columns: pl.BlockSpec((count, columns), lambda i, places_ref: (0, 0))
    return pl.pallas_call(
        body,
        grid_spec=pltpu.PrefetchScalarGridSpec(
            num_scalar_prefetch=1,
            grid=(2 * PLANES,),
            in_specs=[piece, piece, whole(widths[0]), whole(widths[1])],
            out_specs=pl.BlockSpec((1, block, sum(widths)), lambda i, places_ref: (i, 0, 0)),
        ),
        out_shape=jax.ShapeDtypeStruct((2 * PLANES, block, sum(widths)), jnp.bfloat16),
        compiler_params=kernel_params(24),
        cost_estimate=short_cost(),
    )(places, normed, normed_two, latent_back, logit_grads)


def assemble(blocks, places):
    count = len(blocks)

    def body(places_ref, *refs):
        out, held, sems, out_sems = refs[count:]
        arrivals = [
            pltpu.make_async_copy(refs[i], held.at[i], sems.at[i]) for i in range(count)
        ]
        leaving = [
            pltpu.make_async_copy(held.at[i], out.at[places_ref[i]], out_sems.at[i])
            for i in range(count)
        ]
        for copy in arrivals:
            copy.start()
        for i in range(count):
            arrivals[i].wait()
            leaving[i].start()
        for copy in leaving:
            copy.wait()

    return pl.pallas_call(
        body,
        in_specs=[pl.BlockSpec(memory_space=pltpu.SMEM)]
        + [pl.BlockSpec(memory_space=pl.ANY)] * len(blocks),
        out_specs=pl.BlockSpec(memory_space=pl.ANY),
        out_shape=jax.ShapeDtypeStruct((len(blocks),) + blocks[0].shape, blocks[0].dtype),
        scratch_shapes=[
            pltpu.VMEM((count,) + blocks[0].shape, blocks[0].dtype),
            pltpu.SemaphoreType.DMA((count,)),
            pltpu.SemaphoreType.DMA((count,)),
        ],
        compiler_params=kernel_params(24),
        cost_estimate=short_cost(),
    )(places, *blocks)


def expert_weight_grads(rows, grads, gate_backs, up_backs, hiddens, begin, count, earlier):
    experts, slots, width = rows[0].shape
    units = hiddens[0].shape[2]
    tile = 512
    planes = len(rows)

    def body(*refs):
        rows_in = refs[:planes]
        grads_in = refs[planes : 2 * planes]
        gate_in = refs[2 * planes : 3 * planes]
        up_in = refs[3 * planes : 4 * planes]
        hidden_in = refs[4 * planes : 5 * planes]
        gate_ref, up_ref, down_ref = refs[-3:]
        for left, right, out in (
            (gate_in, rows_in, gate_ref),
            (up_in, rows_in, up_ref),
            (hidden_in, grads_in, down_ref),
        ):
            total = dot_first(left[0][0], right[0][0])
            for p in range(1, planes):
                total = total + dot_first(left[p][0], right[p][0])
            out[0] = total

    wide = pl.BlockSpec((1, slots, tile), lambda j, d: (begin + j, 0, d))
    inner = pl.BlockSpec((1, slots, units), lambda j, d: (begin + j, 0, 0))
    result = pl.BlockSpec((1, units, tile), lambda j, d: (begin + j, 0, d))
    return pl.pallas_call(
        body,
        grid=(count, width // tile),
        in_specs=[wide] * (2 * planes)
        + [inner] * (3 * planes)
        + [pl.BlockSpec(memory_space=pl.ANY)] * len(earlier),
        out_specs=[result] * 3,
        out_shape=[jax.ShapeDtypeStruct((experts, units, width), jnp.float32)] * 3,
        input_output_aliases={5 * planes + i: i for i in range(len(earlier))},
        compiler_params=kernel_params(52),
        cost_estimate=short_cost(),
    )(*rows, *grads, *gate_backs, *up_backs, *hiddens, *earlier)


def swap_halves(values):
    lanes = lax.broadcasted_iota(jnp.int32, values.shape, 1)
    return jnp.where(lanes % 64 < 32, pltpu.roll(values, 96, 1), pltpu.roll(values, 32, 1))


def masked_weights(segment_column, segment_line, query, keys, rope, head_rope):
    count = query.shape[0]
    raw = dot_last(query, keys) + dot_last(rope, head_rope)
    after_key = lax.broadcasted_iota(jnp.int32, (count, count), 0) >= lax.broadcasted_iota(
        jnp.int32, (count, count), 1
    )
    allowed = (segment_column == segment_line) & after_key
    scores = jnp.where(allowed, raw * SCORE_SCALE, -1e30)
    exponent = jnp.exp(scores - jnp.max(scores, axis=1, keepdims=True))
    return exponent / jnp.sum(exponent, axis=1, keepdims=True)


def head_ropes(key_rope):
    zeros = jnp.zeros_like(key_rope)
    return [
        jnp.concatenate([key_rope, zeros], axis=1),
        jnp.concatenate([zeros, key_rope], axis=1),
    ]


def attend(normed, latent_normed, ropes, turns, segments, dense):
    count, width = normed.shape
    rows, block, columns = dense.shape
    pairs = QUERY_COLUMNS // 384
    rank = latent_normed.shape[1]
    share = rank // rows
    flat = dense.reshape(rows * block, columns)
    quarters = dense.reshape(rows, block // share, share, columns)

    def body(
        normed_ref,
        latent_ref,
        rope0_ref,
        rope1_ref,
        cosine_ref,
        sine_ref,
        column_ref,
        line_ref,
        query_weight_ref,
        expand_ref,
        output_ref,
        query_ref,
        keys_ref,
        mixed_ref,
        attended_ref,
        total,
    ):
        step = pl.program_id(0)
        query = dot_plain(normed_ref[...], query_weight_ref[...])
        rope = query[:, 256:]
        rope = rope * cosine_ref[...] + swap_halves(rope) * sine_ref[...]
        query = jnp.concatenate([query[:, :256], rope], axis=1).astype(jnp.bfloat16)
        expand = expand_ref[...].reshape(rank, 512)
        keys = dot_plain(latent_ref[...], expand).astype(jnp.bfloat16)
        query_ref[...] = query
        keys_ref[...] = keys
        mixed = []
        for head, rope_ref in enumerate((rope0_ref, rope1_ref)):
            weights = masked_weights(
                column_ref[:, :1],
                line_ref[:1],
                query[:, 128 * head : 128 * head + 128],
                keys[:, 256 * head : 256 * head + 128],
                query[:, 256:],
                rope_ref[...],
            )
            values = keys[:, 256 * head + 128 : 256 * head + 256]
            mixed.append(dot_plain(weights.astype(jnp.bfloat16), values).astype(jnp.bfloat16))
        mixed = jnp.concatenate(mixed, axis=1)
        mixed_ref[...] = mixed
        part = dot_last(mixed, output_ref[...])

        @pl.when(step == 0)
        def _():
            total[...] = part

        @pl.when(step > 0)
        def _():
            total[...] += part

        @pl.when(step == pairs - 1)
        def _():
            attended_ref[...] = total[...].astype(jnp.bfloat16)

    whole = lambda shape: pl.BlockSpec(shape, lambda h: (0,) * len(shape))
    return pl.pallas_call(
        body,
        grid=(pairs,),
        in_specs=[
            whole((count, width)),
            whole((count, rank)),
            whole((count, 128)),
            whole((count, 128)),
            whole((count, 128)),
            whole((count, 128)),
            whole((count, 128)),
            whole((8, count)),
            pl.BlockSpec((width, 384), lambda h: (0, h)),
            pl.BlockSpec((rows, 1, share, 512), lambda h: (0, h, 0, QUERY_COLUMNS // 512)),
            pl.BlockSpec((width, 256), lambda h: (0, (QUERY_COLUMNS + 512) // 256 + h)),
        ],
        out_specs=[
            pl.BlockSpec((count, 384), lambda h: (0, h)),
            pl.BlockSpec((count, 512), lambda h: (0, h)),
            pl.BlockSpec((count, 256), lambda h: (0, h)),
            whole((count, width)),
        ],
        out_shape=[
            jax.ShapeDtypeStruct((count, 384 * pairs), jnp.bfloat16),
            jax.ShapeDtypeStruct((count, 512 * pairs), jnp.bfloat16),
            jax.ShapeDtypeStruct((count, 256 * pairs), jnp.bfloat16),
            jax.ShapeDtypeStruct((count, width), jnp.bfloat16),
        ],
        scratch_shapes=[pltpu.VMEM((count, width), jnp.float32)],
        compiler_params=kernel_params(44),
        cost_estimate=short_cost(),
    )(normed, latent_normed, *ropes, *turns, *segments, flat, quarters, flat)


def attend_back(upstream, query, keys, ropes, turns, segments, dense, rank):
    count, width = upstream.shape
    rows, block, columns = dense.shape
    pairs = QUERY_COLUMNS // 384
    share = rank // rows
    flat = dense.reshape(rows * block, columns)
    quarters = dense.reshape(rows, block // share, share, columns)

    def body(
        upstream_ref,
        query_ref,
        keys_ref,
        rope0_ref,
        rope1_ref,
        cosine_ref,
        sine_ref,
        column_ref,
        line_ref,
        query_weight_ref,
        expand_ref,
        output_ref,
        query_back_ref,
        keys_back_ref,
        rope_back_ref,
        latent_back_ref,
        input_ref,
        total,
    ):
        step = pl.program_id(0)
        mixed_back = dot_plain(upstream_ref[...], output_ref[...]).astype(jnp.bfloat16)
        query = query_ref[...]
        keys = keys_ref[...]
        rope = query[:, 256:]
        lanes = lax.broadcasted_iota(jnp.int32, (count, 128), 1)
        query_back = []
        keys_back = []
        rope_back = 0.0
        key_rope_back = 0.0
        for head, rope_ref in enumerate((rope0_ref, rope1_ref)):
            query_nope = query[:, 128 * head : 128 * head + 128]
            key_nope = keys[:, 256 * head : 256 * head + 128]
            values = keys[:, 256 * head + 128 : 256 * head + 256]
            mixed_head = mixed_back[:, 128 * head : 128 * head + 128]
            weights = masked_weights(
                column_ref[:, :1], line_ref[:1], query_nope, key_nope, rope, rope_ref[...]
            )
            weight_back = dot_last(mixed_head, values)
            center = jnp.sum(weight_back * weights, axis=1, keepdims=True)
            raw_back = (weights * (weight_back - center) * SCORE_SCALE).astype(jnp.bfloat16)
            query_back.append(dot_plain(raw_back, key_nope))
            rope_back = rope_back + dot_plain(raw_back, rope_ref[...])
            keys_back.append(dot_first(raw_back, query_nope))
            keys_back.append(dot_first(weights.astype(jnp.bfloat16), mixed_head))
            mine = lanes // 64 == head
            key_rope_back = key_rope_back + jnp.where(mine, dot_first(raw_back, rope), 0.0)
        rope_back = rope_back * cosine_ref[...] - swap_halves(rope_back) * sine_ref[...]
        query_back = jnp.concatenate(query_back + [rope_back], axis=1).astype(jnp.bfloat16)
        keys_back = jnp.concatenate(keys_back, axis=1).astype(jnp.bfloat16)
        query_back_ref[...] = query_back
        keys_back_ref[...] = keys_back
        latent_part = dot_last(keys_back, expand_ref[...].reshape(rank, 512))
        input_part = dot_last(query_back, query_weight_ref[...])

        @pl.when(step == 0)
        def _():
            rope_back_ref[...] = key_rope_back
            latent_back_ref[...] = latent_part
            total[...] = input_part

        @pl.when(step > 0)
        def _():
            rope_back_ref[...] += key_rope_back
            latent_back_ref[...] += latent_part
            total[...] += input_part

        @pl.when(step == pairs - 1)
        def _():
            input_ref[...] = total[...].astype(jnp.bfloat16)

    whole = lambda shape: pl.BlockSpec(shape, lambda h: (0,) * len(shape))
    return pl.pallas_call(
        body,
        grid=(pairs,),
        in_specs=[
            whole((count, width)),
            pl.BlockSpec((count, 384), lambda h: (0, h)),
            pl.BlockSpec((count, 512), lambda h: (0, h)),
            whole((count, 128)),
            whole((count, 128)),
            whole((count, 128)),
            whole((count, 128)),
            whole((count, 128)),
            whole((8, count)),
            pl.BlockSpec((width, 384), lambda h: (0, h)),
            pl.BlockSpec((rows, 1, share, 512), lambda h: (0, h, 0, QUERY_COLUMNS // 512)),
            pl.BlockSpec((width, 256), lambda h: (0, (QUERY_COLUMNS + 512) // 256 + h)),
        ],
        out_specs=[
            pl.BlockSpec((count, 384), lambda h: (0, h)),
            pl.BlockSpec((count, 512), lambda h: (0, h)),
            whole((count, 128)),
            whole((count, rank)),
            whole((count, width)),
        ],
        out_shape=[
            jax.ShapeDtypeStruct((count, 384 * pairs), jnp.bfloat16),
            jax.ShapeDtypeStruct((count, 512 * pairs), jnp.bfloat16),
            jax.ShapeDtypeStruct((count, 128), jnp.float32),
            jax.ShapeDtypeStruct((count, rank), jnp.float32),
            jax.ShapeDtypeStruct((count, width), jnp.bfloat16),
        ],
        scratch_shapes=[pltpu.VMEM((count, width), jnp.float32)],
        compiler_params=kernel_params(52),
        cost_estimate=short_cost(),
    )(upstream, query, keys, *ropes, *turns, *segments, flat, quarters, flat)


def on_device(
    inputs,
    segment_ids,
    routes,
    norm_gain,
    query_weight,
    latent_weight,
    latent_gain,
    expand_weight,
    output_weight,
    ffn_gain,
    router_weight,
    expert_gate,
    expert_up,
    expert_down,
    shared_gate,
    shared_up,
    shared_down,
    out_grad,
):
    bf16 = jnp.bfloat16
    f32 = jnp.float32
    rows_count = inputs.shape[0]
    row_devices = lax.axis_size("row")
    row_place = lax.axis_index("row")
    first = lax.axis_index("col") == 0
    expert_count = EXP_DEV * row_devices
    capacity = 4 * rows_count * TOPK // (3 * expert_count)
    segment_row = segment_ids[0]
    places = jnp.arange(rows_count, dtype=jnp.int32)

    steps = jnp.arange(row_devices, dtype=jnp.int32)
    arrival = (((row_place // 4 - steps // 4) % 4) * 4 + ((row_place % 4) ^ (steps % 4))).astype(
        jnp.int32
    )
    block = latent_weight.shape[0]
    share = expand_weight.shape[0]
    quarter = expand_weight.shape[1] * share // block
    query_width = query_weight.shape[1]
    latent_width = latent_weight.shape[1]

    slab = pack_weights(
        query_weight,
        expand_weight,
        output_weight,
        latent_weight,
        router_weight,
        routes.astype(bf16).reshape(block, -1),
    )
    shared_share = shared_gate.shape[1] // row_devices
    blocks = {}
    blocks[0] = slab
    blocks[4], blocks[2], inputs_other, gains_other = together(
        turn_planes(slab),
        swap_rows(slab, 2),
        swap_cols(inputs),
        swap_cols(jnp.stack([norm_gain, ffn_gain])),
    )
    shared_packed = jnp.stack(
        [after(shared_gate, inputs_other).T, after(shared_up, inputs_other).T, shared_down], axis=0
    )
    shared_packed = shared_packed.reshape(3, row_devices, shared_share, -1).transpose(1, 0, 2, 3)
    (
        blocks[8],
        blocks[6],
        blocks[1],
        blocks[3],
        out_grad_other,
    ) = together(
        turn_planes(blocks[4]),
        swap_rows(blocks[4], 2),
        swap_rows(blocks[0], 1),
        swap_rows(blocks[2], 1),
        swap_cols(after(out_grad, inputs_other)),
    )
    upstream_bf16 = jnp.where(
        first,
        jnp.concatenate([out_grad, out_grad_other], axis=1),
        jnp.concatenate([out_grad_other, out_grad], axis=1),
    )
    grad_rows = Spread(sent_rows(upstream_bf16, first))
    blocks[12], blocks[10], blocks[5], blocks[7], got, shared_packed = together(
        turn_planes(blocks[8]),
        swap_rows(blocks[8], 2),
        swap_rows(blocks[4], 1),
        swap_rows(blocks[6], 1),
        swap_cols(grad_rows.sent((0, 0))[0]),
        shared_packed,
    )
    grad_rows.got(got, [0], (0, 0))
    source = jnp.where(
        first,
        jnp.concatenate([inputs, inputs_other], axis=1),
        jnp.concatenate([inputs_other, inputs], axis=1),
    ).astype(f32)
    gains = jnp.stack([norm_gain, ffn_gain])
    gains = jnp.where(
        first,
        jnp.concatenate([gains, gains_other], axis=1),
        jnp.concatenate([gains_other, gains], axis=1),
    )
    gain_one = gains[:1]
    gain_two = gains[1:]
    scale_one = lax.rsqrt(jnp.mean(source * source, axis=1, keepdims=True) + epsilon)
    unit_one = source * scale_one
    normed_one = (unit_one * gain_one).astype(bf16)
    cosine, sine = rotation(rows_count, ROPE)
    turns = (
        jnp.concatenate([cosine] * 4, axis=1),
        jnp.concatenate([-sine, sine, -sine, sine], axis=1),
    )
    segments = (
        jnp.broadcast_to(segment_row[:, None], (rows_count, 128)),
        jnp.broadcast_to(segment_row[None], (8, rows_count)),
    )
    passed, starts = batch(grad_rows.passed((0, 0, 0), (0, 0, 1)))
    (
        blocks[14],
        blocks[9],
        blocks[11],
        passed,
        shared_here,
        normed_one,
        cosine,
        sine,
        turns,
        segments,
    ) = together(
        swap_rows(blocks[12], 2),
        swap_rows(blocks[8], 1),
        swap_rows(blocks[10], 1),
        swap_rows(passed, 1),
        lax.all_to_all(shared_packed, "row", split_axis=0, concat_axis=0, tiled=True),
        normed_one,
        cosine,
        sine,
        turns,
        segments,
    )
    grad_rows.taken(passed, starts, (0, 0, 0), (0, 0, 1))
    grad_rows.held[0, 0] = after(grad_rows.held[0, 0], blocks[14])
    grad_turned = grad_rows.turn(1)
    blocks[13], blocks[15] = together(swap_rows(blocks[12], 1), swap_rows(blocks[14], 1))
    dense = assemble([blocks[i] for i in range(4 * PLANES)], arrival)
    flat_dense = dense.reshape(D, -1)
    latent_full = flat_dense[:, QUERY_COLUMNS + 1536 : QUERY_COLUMNS + 1536 + latent_width]
    router_full = flat_dense[
        :, QUERY_COLUMNS + 1536 + latent_width : QUERY_COLUMNS + 1536 + latent_width + expert_count
    ]
    latent = jnp.dot(normed_one, latent_full, preferred_element_type=f32).astype(bf16)
    compressed = latent[:, :RANK].astype(f32)
    latent_scale = lax.rsqrt(jnp.mean(compressed * compressed, axis=1, keepdims=True) + epsilon)
    latent_unit = compressed * latent_scale
    latent_normed = (latent_unit * latent_gain).astype(bf16)
    key_rope = rotate(latent[:, RANK:].astype(f32), cosine, sine).astype(bf16)
    ropes = head_ropes(key_rope)
    latent_normed, grad_rows.held[0, 1], grad_rows.held[1, 0] = together(
        latent_normed, grad_rows.cross(0), grad_turned
    )

    query, keys, mixed, attended_part = attend(
        normed_one, latent_normed, ropes, turns, segments, dense
    )
    sent, starts = batch(grad_rows.sent((0, 1), (1, 0)))
    passed, passed_starts = batch(grad_rows.passed((0, 1, 0), (1, 0, 0)))
    (
        query,
        attended_part,
        grad_rows.held[2, 0],
        grad_rows.held[1, 1],
        got,
        passed,
    ) = together(
        query,
        attended_part,
        grad_rows.turn(2),
        grad_rows.cross(1),
        swap_cols(sent),
        swap_rows(passed, 1),
    )
    grad_rows.got(got, starts, (0, 1), (1, 0))
    grad_rows.taken(passed, passed_starts, (0, 1, 0), (1, 0, 0))

    picked = {}

    def pick(plane, *others):
        picked[plane] = pick_grads(
            grad_rows.family(plane), after(plane_codes[plane], *others), shared_last, capacity
        )
        return picked[plane]

    def pass_alone(spread, key):
        spread.taken(swap_rows(spread.passed(key)[0], 1), [0], key)

    passed, starts = batch(grad_rows.passed((0, 1, 1), (1, 0, 1), (1, 1, 0)))
    partner_part = jnp.concatenate(
        [
            attended_part[:COMMON],
            jnp.where(first, attended_part[SENT:], attended_part[COMMON:SENT]),
        ],
        axis=0,
    )
    (
        attended_other,
        grad_rows.held[2, 1],
        passed,
    ) = together(
        swap_cols(partner_part),
        grad_rows.cross(2),
        swap_rows(passed, 1),
    )
    grad_rows.taken(passed, starts, (0, 1, 1), (1, 0, 1), (1, 1, 0))
    attended_sent = sent_rows(attended_part, first).astype(f32) + attended_other.astype(f32)
    middle_sent = sent_rows(source, first) + attended_sent
    scale_sent = lax.rsqrt(jnp.mean(middle_sent * middle_sent, axis=1, keepdims=True) + epsilon)
    normed_sent = (middle_sent * scale_sent * gain_two).astype(bf16)
    rows = Spread(normed_sent)

    routes_all = after(flat_dense, normed_sent)[
        :, QUERY_COLUMNS + 1536 + latent_width + expert_count :
    ][:, : rows_count * TOPK // block]
    routes_all = routes_all.reshape(row_devices, rows_count, TOPK).transpose(0, 2, 1)[arrival]
    routes_all = routes_all.astype(jnp.int32)

    routes_all = local_tokens(routes_all, 2, first)
    held_experts = row_place * EXP_DEV + jnp.arange(EXP_DEV, dtype=jnp.int32)
    hits = jnp.any(routes_all[:, :, None, :] == held_experts[None, None, :, None], axis=1)
    upper = (places[:, None] <= places[None, :]).astype(bf16)
    ranks = jnp.einsum("sjt,tu->sju", hits.astype(bf16), upper, preferred_element_type=f32)
    codes = jnp.where(hits, ranks.astype(jnp.int32) - 1, -1)
    codes = jnp.pad(codes, ((0, 0), (0, 8 - EXP_DEV), (0, 0)), constant_values=-1)
    plane_codes = [codes[p * FAMILIES : (p + 1) * FAMILIES] for p in range(PLANES)]

    shared_here = shared_here.transpose(1, 2, 0, 3).reshape(3, shared_share, D)
    shared_here = jnp.pad(shared_here, ((0, 0), (0, SHARED_PAD - shared_share), (0, 0)))
    shared_pair = shared_here[:2].reshape(2 * SHARED_PAD, D)
    shared_last = shared_here[2]

    sent, starts = batch(rows.sent((0, 0)) + grad_rows.sent((1, 1)))
    rows.held[1, 0], rows.held[0, 1], got, shared_pair, shared_last, plane_codes = together(
        rows.turn(1), rows.cross(0), swap_cols(sent), shared_pair, shared_last, plane_codes
    )
    rows.got(got, starts, (0, 0))
    grad_rows.got(got, starts[1:], (1, 1))
    router_turned = router_full.T
    router_held = lax.dynamic_slice_in_dim(
        jnp.concatenate([router_turned, router_turned], axis=0),
        row_place * EXP_DEV,
        expert_count,
        0,
    )
    pass_alone(grad_rows, (1, 1, 1))
    sent, starts = batch(rows.sent((0, 1), (1, 0)))
    passed, passed_starts = batch(rows.passed((0, 0, 0), (0, 0, 1), (0, 1, 0)))
    (
        rows.held[2, 0],
        rows.held[1, 1],
        got,
        passed,
        picked[0],
        picked[1],
        router_held,
    ) = together(
        rows.turn(2),
        rows.cross(1),
        swap_cols(sent),
        swap_rows(passed, 1),
        pick(0),
        pick(1),
        router_held,
    )
    rows.got(got, starts, (0, 1), (1, 0))
    rows.taken(passed, passed_starts, (0, 0, 0), (0, 0, 1), (0, 1, 0))

    experts = (expert_gate, expert_up, expert_down)
    begun = {}
    ran = {}

    def start_plane(plane, *others):
        begun[plane] = pick_rows(
            rows.family(plane),
            grad_rows.family(plane),
            after(plane_codes[plane], *others),
            router_held,
            shared_pair,
            picked[plane][1],
            capacity,
        )
        return begun[plane]

    def run_plane(plane):
        ran[plane] = run_experts(begun[plane][0], picked[plane][0], begun[plane][1], *experts)
        return ran[plane]

    def back_sibling(plane):
        return sum_tokens(
            ran[plane][1],
            plane_codes[plane],
            begun[plane][3],
            shared_pair,
            capacity,
            1,
            None,
            ran[plane][5],
        )

    def back_mine(plane, received):
        return sum_tokens(
            ran[plane][1],
            plane_codes[plane],
            begun[plane][3],
            shared_pair,
            capacity,
            0,
            received,
            ran[plane][5],
        )

    def sum_sibling(plane):
        return sum_tokens(
            ran[plane][0], plane_codes[plane], begun[plane][2], shared_last, capacity, 1
        )[0]

    def sum_mine(plane, received):
        return sum_tokens(
            ran[plane][0], plane_codes[plane], begun[plane][2], shared_last, capacity, 0, received
        )

    def unique_out(mine):
        return swap_cols(mine[1])

    def across_out(mine, unique):
        return swap_rows(add_unique(mine[0], unique, 1), 2)

    def own_sum(mine, unique, crossed):
        return add_unique(mine[0], unique, 0) + crossed

    pass_alone(rows, (0, 1, 1))
    sent, starts = batch(rows.sent((1, 1), (2, 0)))
    passed, passed_starts = batch(rows.passed((1, 0, 0), (1, 1, 0), (1, 0, 1)))
    rows.held[3, 0], rows.held[2, 1], got, passed = together(
        rows.turn(3), rows.cross(2), swap_cols(sent), swap_rows(passed, 1)
    )
    rows.got(got, starts, (1, 1), (2, 0))
    rows.taken(passed, passed_starts, (1, 0, 0), (1, 1, 0), (1, 0, 1))

    pass_alone(rows, (1, 1, 1))
    sent, starts = batch(rows.sent((2, 1), (3, 0)))
    passed, passed_starts = batch(rows.passed((2, 0, 0), (2, 1, 0), (2, 0, 1)))
    begun[1], rows.held[3, 1], grad_rows.held[3, 0], got, passed = together(
        start_plane(1), rows.cross(3), grad_rows.turn(3), swap_cols(sent), swap_rows(passed, 1)
    )
    rows.got(got, starts, (2, 1), (3, 0))
    rows.taken(passed, passed_starts, (2, 0, 0), (2, 1, 0), (2, 0, 1))

    ran[1] = run_plane(1)
    back_1 = back_sibling(1)
    sent, starts = batch(rows.sent((3, 1)) + grad_rows.sent((2, 0), (2, 1)))
    passed = [
        batch(rows.passed((2, 1, 1), (3, 0, 1))),
        batch(rows.passed((3, 0, 0), (3, 1, 0))),
        batch(grad_rows.passed((2, 0, 0), (2, 1, 0))),
    ]
    ran[1], back_1, grad_rows.held[3, 1], got, passed_got = together(
        ran[1],
        back_1,
        grad_rows.cross(3),
        swap_cols(sent),
        [swap_rows(rows_passed, 1) for rows_passed, _ in passed],
    )
    rows.got(got, starts, (3, 1))
    grad_rows.got(got, starts[1:], (2, 0), (2, 1))
    rows.taken(passed_got[0], passed[0][1], (2, 1, 1), (3, 0, 1))
    rows.taken(passed_got[1], passed[1][1], (3, 0, 0), (3, 1, 0))
    grad_rows.taken(passed_got[2], passed[2][1], (2, 0, 0), (2, 1, 0))

    passed, passed_starts = batch(grad_rows.passed((2, 0, 1), (2, 1, 1)))
    grad_rows.taken(swap_rows(passed, 1), passed_starts, (2, 0, 1), (2, 1, 1))
    sent, starts = batch(grad_rows.sent((3, 0), (3, 1)))
    passed, passed_starts = batch(
        rows.passed((3, 1, 1)) + grad_rows.passed((3, 0, 0), (3, 1, 0))
    )
    picked[2] = pick(2)
    begun[2] = start_plane(2)
    picked[2], begun[2], back_got, got, passed = together(
        picked[2], begun[2], swap_rows(back_1[0], 1), swap_cols(sent), swap_rows(passed, 1)
    )
    grad_rows.got(got, starts, (3, 0), (3, 1))
    rows.taken(passed, passed_starts, (3, 1, 1))
    grad_rows.taken(passed, passed_starts[1:], (3, 0, 0), (3, 1, 0))
    passed, passed_starts = batch(grad_rows.passed((3, 0, 1), (3, 1, 1)))
    grad_rows.taken(swap_rows(passed, 1), passed_starts, (3, 0, 1), (3, 1, 1))
    back_mine_1 = back_mine(1, back_got)
    sum_1 = sum_sibling(1)
    back_mine_1, sum_1 = together(back_mine_1, sum_1)

    ran[2] = run_plane(2)
    back_2 = back_sibling(2)
    ran[2], back_2, back_unique, sum_got = together(
        ran[2], back_2, unique_out(back_mine_1), swap_rows(sum_1, 1)
    )
    sum_mine_1 = sum_mine(1, sum_got)

    picked[3] = pick(3)
    begun[3] = start_plane(3)
    picked[3], begun[3], back_got, back_crossed, sum_unique = together(
        picked[3],
        begun[3],
        swap_rows(back_2[0], 1),
        across_out(back_mine_1, back_unique),
        unique_out(sum_mine_1),
    )
    back = own_sum(back_mine_1, back_unique, back_crossed)
    back_mine_2 = back_mine(2, back_got)
    sum_2 = sum_sibling(2)
    attended_rest = after(attended_sent[COMMON:], picked[3]).astype(bf16)
    back_mine_2, sum_2, back, attended_rest = together(
        back_mine_2, sum_2, back, swap_cols(attended_rest)
    )

    ran[3] = run_plane(3)
    back_3 = back_sibling(3)
    ran[3], back_3, back, back_unique, sum_got, sum_crossed = together(
        ran[3],
        back_3,
        turn_planes(back),
        unique_out(back_mine_2),
        swap_rows(sum_2, 1),
        across_out(sum_mine_1, sum_unique),
    )
    result = own_sum(sum_mine_1, sum_unique, sum_crossed)
    sum_mine_2 = sum_mine(2, sum_got)
    sum_mine_2, result = together(sum_mine_2, result)

    attended_rest = after(attended_rest, sum_mine_2).astype(f32)
    attended_mine = attended_sent[COMMON:]
    middle = source + jnp.concatenate(
        [
            attended_sent[:COMMON],
            jnp.where(first, attended_mine, attended_rest),
            jnp.where(first, attended_rest, attended_mine),
        ],
        axis=0,
    )
    scale_two = lax.rsqrt(jnp.mean(middle * middle, axis=1, keepdims=True) + epsilon)
    unit_two = middle * scale_two
    normed_two = (unit_two * gain_two).astype(bf16)
    logits = jnp.dot(normed_two, router_full, preferred_element_type=f32)
    log_total = jax.nn.logsumexp(logits, axis=1, keepdims=True)
    chances = jnp.exp(logits - log_total)

    begun[0] = start_plane(0, sum_mine_2)
    begun[0], back_got, back_crossed, sum_unique, result, normed_two, chances = together(
        begun[0],
        swap_rows(back_3[0], 1),
        across_out(back_mine_2, back_unique),
        unique_out(sum_mine_2),
        turn_planes(result),
        normed_two,
        chances,
    )
    back = back + own_sum(back_mine_2, back_unique, back_crossed)
    back_mine_3 = back_mine(3, back_got)
    sum_3 = sum_sibling(3)
    back_mine_3, sum_3, back = together(back_mine_3, sum_3, back)

    ran[0] = run_plane(0)
    back_0 = back_sibling(0)
    ran[0], back_0, back, back_unique, sum_got, sum_crossed = together(
        ran[0],
        back_0,
        turn_planes(back),
        unique_out(back_mine_3),
        swap_rows(sum_3, 1),
        across_out(sum_mine_2, sum_unique),
    )
    result = result + own_sum(sum_mine_2, sum_unique, sum_crossed)
    sum_mine_3 = sum_mine(3, sum_got)
    sum_mine_3, result = together(sum_mine_3, result)

    kept = [
        (begun[plane][0], picked[plane][0], ran[plane][3], ran[plane][4], ran[plane][2])
        for plane in range(PLANES)
    ]
    kept = [list(part) for part in zip(*kept)]
    half = EXP_DEV // 2
    expert_parts = expert_weight_grads(*kept, 0, half, [])
    expert_parts, back_got, back_crossed, sum_unique, result = together(
        expert_parts,
        swap_rows(back_0[0], 1),
        across_out(back_mine_3, back_unique),
        unique_out(sum_mine_3),
        turn_planes(result),
    )
    back = back + own_sum(back_mine_3, back_unique, back_crossed)
    back_mine_0 = back_mine(0, back_got)
    sum_0 = sum_sibling(0)
    back_mine_0, sum_0, back = together(back_mine_0, sum_0, back)

    expert_parts = expert_weight_grads(*kept, half, EXP_DEV - half, expert_parts)
    expert_parts, back, back_unique, sum_got, common_crossed = together(
        expert_parts,
        turn_planes(back),
        unique_out(back_mine_0),
        swap_rows(sum_0, 1),
        swap_rows(back_mine_0[0][1, :COMMON], 2),
    )
    expert_gate_grad, expert_up_grad, expert_down_grad = expert_parts
    common = back[:COMMON] + back_mine_0[0][0, :COMMON] + common_crossed
    unique_rest = back_mine_0[0][:, COMMON:] + back_unique
    sum_mine_0 = sum_mine(0, sum_got)

    gate_grad_dense = [
        jnp.stack([mine[2], sibling[1]], axis=1)[:, :, :EXP_DEV]
        for mine, sibling in (
            (back_mine_0, back_0),
            (back_mine_1, back_1),
            (back_mine_2, back_2),
            (back_mine_3, back_3),
        )
    ]
    gate_grad_dense = jnp.stack(gate_grad_dense).reshape(row_devices, EXP_DEV, rows_count)
    gate_grad_dense = local_tokens(gate_grad_dense, 2, first)[arrival]
    gate_grad_dense = lax.all_to_all(
        gate_grad_dense, "row", split_axis=0, concat_axis=0, tiled=True
    ).reshape(expert_count, rows_count)
    shared_grads = sum([begun[p][4] for p in range(1, PLANES)], begun[0][4])
    shared_grads = shared_grads.reshape(3, SHARED_PAD, D)[:, :shared_share]
    shared_grads = (
        shared_grads.astype(bf16)
        .reshape(3, shared_share, row_devices, -1)
        .transpose(2, 0, 1, 3)
    )
    gate_grad_dense = gate_grad_dense + swap_cols(gate_grad_dense)
    weighted_gates = gate_grad_dense.T * chances
    logit_grads = (
        weighted_gates - chances * jnp.sum(weighted_gates, axis=1, keepdims=True)
    ).astype(bf16)
    router_back = jnp.einsum("te,de->td", logit_grads, router_full, preferred_element_type=f32)
    unique_crossed, common_other, sum_mine_0, shared_grads, router_back, logit_grads = together(
        swap_rows(unique_rest[1], 2),
        swap_cols(common),
        sum_mine_0,
        shared_grads,
        router_back,
        logit_grads,
    )
    unique_mine = back[COMMON:] + unique_rest[0] + unique_crossed
    shared_grads = lax.all_to_all(shared_grads, "row", split_axis=0, concat_axis=0, tiled=True)
    unique_other = swap_cols(unique_mine)
    upstream = upstream_bf16.astype(f32)
    normed_two_back = router_back + jnp.concatenate(
        [
            common.astype(f32) + common_other.astype(f32),
            jnp.where(first, unique_mine, unique_other).astype(f32),
            jnp.where(first, unique_other, unique_mine).astype(f32),
        ],
        axis=0,
    )
    ffn_gain_part = jnp.sum(normed_two_back * unit_two, axis=0)
    weighted = normed_two_back * gain_two
    average = jnp.mean(weighted * unit_two, axis=1, keepdims=True)
    middle_back = upstream + scale_two * (weighted - unit_two * average)
    attended_back = middle_back.astype(bf16)

    def by_plane(total):
        return total.reshape((PLANES, 2) + total.shape[1:])

    output_sibling = block_grads(arrival, attended_back, mixed, 256, 1)
    query_back, expanded_back, key_rope_back, latent_normed_back, input_part = attend_back(
        attended_back, query, keys, ropes, turns, segments, dense, RANK
    )
    query_back, shared_grads, last_unique, output_got, sum_crossed = together(
        query_back,
        shared_grads,
        unique_out(sum_mine_0),
        swap_rows(output_sibling, 1),
        across_out(after(sum_mine_3, unique_other), sum_unique),
    )
    result = result + own_sum(sum_mine_3, sum_unique, sum_crossed)
    latent_gain_part = jnp.sum(latent_normed_back * latent_unit, axis=0)
    latent_weighted = latent_normed_back * latent_gain
    compressed_back = latent_scale * (
        latent_weighted
        - latent_unit * jnp.mean(latent_weighted * latent_unit, axis=1, keepdims=True)
    )
    key_rope_back = key_rope_back[:, :ROPE] + key_rope_back[:, ROPE:]
    rope_back = unrotate(key_rope_back, cosine, sine)
    latent_part = jnp.concatenate([compressed_back, rope_back], axis=1).astype(bf16)
    latent_turned = latent_normed.T
    wide_sibling = block_grads(
        arrival, normed_one, after(query_back, latent_part), 384, 1, latent_turned, expanded_back
    )
    latent_other, wide_sibling = together(swap_cols(latent_part), wide_sibling)
    latent_back = (latent_part.astype(f32) + latent_other.astype(f32)).astype(bf16)
    narrow_sibling = narrow_grads(arrival, normed_one, latent_back, normed_two, logit_grads, 1)
    weighted_part = jnp.sum(
        after(input_part, wide_sibling).astype(f32) * gain_one * unit_one, axis=1
    )
    wide_got, narrow_sibling, weighted_part = together(
        swap_rows(wide_sibling, 1), narrow_sibling, weighted_part
    )
    output_total = by_plane(
        block_grads(
            arrival, after(attended_back, narrow_sibling), mixed, 256, 0, received=output_got
        )
    )
    input_sent = other_columns(input_part, first)
    small_part = jnp.concatenate([weighted_part, latent_gain_part]).reshape(-1, 128)
    narrow_got = swap_rows(narrow_sibling, 1)
    small_other, narrow_got, output_total, sum_crossed, result = together(
        swap_cols(small_part),
        narrow_got,
        output_total,
        across_out(sum_mine_0, last_unique),
        turn_planes(result),
    )
    sum_sent = result + own_sum(sum_mine_0, last_unique, sum_crossed)
    joined_total = by_plane(
        joined_grads(
            arrival,
            normed_one,
            query_back,
            latent_turned,
            expanded_back,
            latent_back,
            normed_two,
            logit_grads,
            wide_got,
            narrow_got,
        )
    )
    joined_total, crossed_output, input_other = together(
        joined_total,
        swap_rows(output_total[1:, 1], 2),
        swap_cols(after(input_sent, small_other)),
    )
    output_sums = [output_total[p, 0] + crossed_output[p - 1] for p in (1, 2, 3)]

    crossed, crossed_output, moved_output, combined_other = together(
        swap_rows(joined_total[1, 1], 2),
        swap_rows(output_total[0, 1], 2),
        turn_planes(output_sums[0]),
        swap_cols(other_columns(sum_sent, first)),
    )
    moving = joined_total[1, 0] + crossed
    moving_output = output_sums[1] + moved_output
    last_output = output_total[0, 0] + crossed_output

    shared_grads = after(shared_grads, joined_total).transpose(1, 0, 2, 3).reshape(3, row_devices * shared_share, -1)
    shared_grads = shared_grads.astype(f32)
    shared_gate_grad = shared_grads[0].T
    shared_up_grad = shared_grads[1].T
    shared_down_grad = shared_grads[2]

    latent_input = jnp.einsum("tc,dc->td", latent_back, latent_full, preferred_element_type=f32)
    small_sum = (small_part + small_other).reshape(-1)
    weighted_sum = small_sum[:rows_count]
    weighted_sum = weighted_sum + jnp.sum(latent_input * gain_one * unit_one, axis=1)
    normed_one_back = (
        own_columns(input_part, first).astype(f32)
        + input_other.astype(f32)
        + own_columns(latent_input, first)
    )
    own_unit = own_columns(unit_one, first)
    norm_gain_part = jnp.sum(normed_one_back * own_unit, axis=0)
    input_grad = own_columns(middle_back, first) + scale_one * (
        normed_one_back * norm_gain - own_unit * (weighted_sum / D)[:, None]
    )
    gain_grads = jnp.concatenate(
        [norm_gain_part, own_columns(ffn_gain_part, first), small_sum[rows_count:]]
    ).reshape(-1, 128)
    crossed, moved, moved_output, gains_other = together(
        swap_rows(joined_total[2, 1], 2),
        turn_planes(moving),
        turn_planes(moving_output),
        swap_rows(gain_grads, 1),
    )
    moving = joined_total[2, 0] + crossed + moved
    moving_output = output_sums[2] + moved_output
    gain_grads = gain_grads + gains_other
    crossed, moved, moved_output, gains_other = together(
        swap_rows(joined_total[3, 1], 2),
        turn_planes(moving),
        turn_planes(moving_output),
        swap_rows(gain_grads, 2),
    )
    moving = joined_total[3, 0] + crossed + moved
    moving_output = last_output + moved_output
    gain_grads = gain_grads + gains_other
    crossed, moved, others = together(
        swap_rows(joined_total[0, 1], 2),
        turn_planes(moving),
        [swap_rows(gain_grads, bits) for bits in (4, 8, 12)],
    )
    moving = joined_total[0, 0] + crossed + moved
    gain_grads = ((gain_grads + others[0]) + (others[1] + others[2])).reshape(-1)
    output_grad, query_grad, expand_grad, latent_grad, router_grad = unpack_grads(
        moving_output, moving, (query_width, quarter, latent_width)
    )

    combined = merge_rows(own_columns(sum_sent, first), combined_other, first)
    output = (own_columns(middle, first) + combined).astype(bf16)
    width_share = norm_gain.shape[0]
    norm_gain_grad = gain_grads[:width_share]
    ffn_gain_grad = gain_grads[width_share : 2 * width_share]
    latent_gain_grad = gain_grads[2 * width_share :]
    return (
        output,
        input_grad,
        norm_gain_grad,
        query_grad,
        latent_grad,
        latent_gain_grad,
        expand_grad,
        output_grad,
        ffn_gain_grad,
        router_grad,
        expert_gate_grad,
        expert_up_grad,
        expert_down_grad,
        shared_gate_grad,
        shared_up_grad,
        shared_down_grad,
    )


def on_device_general(
    inputs,
    segment_ids,
    routes,
    norm_gain,
    query_weight,
    latent_weight,
    latent_gain,
    expand_weight,
    output_weight,
    ffn_gain,
    router_weight,
    expert_gate,
    expert_up,
    expert_down,
    shared_gate,
    shared_up,
    shared_down,
    out_grad,
):
    bf16 = jnp.bfloat16
    f32 = jnp.float32
    rows_count = inputs.shape[0]
    width_share = inputs.shape[1]
    row_devices = lax.axis_size("row")
    col_devices = lax.axis_size("col")
    col_place = lax.axis_index("col")
    local_heads = query_weight.shape[1] // (NOPE + ROPE)
    expert_count = EXP_DEV * row_devices
    capacity = 4 * rows_count * TOPK // (3 * expert_count)
    score_scale = (NOPE + ROPE) ** (-0.5)
    block_rows = min(512, rows_count)
    segment_row = segment_ids[0]
    places = jnp.arange(rows_count, dtype=jnp.int32)
    (
        query_full,
        latent_full,
        expand_full,
        output_full,
        router_full,
        shared_gate_full,
        shared_up_full,
        shared_down_full,
    ) = (
        lax.all_gather(query_weight, "row", axis=0, tiled=True),
        lax.all_gather(latent_weight, "row", axis=0, tiled=True),
        lax.all_gather(expand_weight, "row", axis=0, tiled=True),
        lax.all_gather(output_weight, "row", axis=1, tiled=True),
        lax.all_gather(router_weight, "row", axis=0, tiled=True),
        lax.all_gather(shared_gate, "row", axis=0, tiled=True),
        lax.all_gather(shared_up, "row", axis=0, tiled=True),
        lax.all_gather(shared_down, "row", axis=1, tiled=True),
    )
    source = inputs.astype(f32)
    scale_one = rms_scale(source)
    unit_one = source * scale_one
    normed_one = spread((unit_one * norm_gain).astype(bf16))
    query = jnp.dot(normed_one, query_full, preferred_element_type=f32).reshape(
        rows_count, local_heads, NOPE + ROPE
    )
    latent = jnp.dot(normed_one, latent_full, preferred_element_type=f32).astype(bf16)
    cosine, sine = rotation(rows_count, ROPE)
    head_cos = cosine[:, None, :]
    head_sin = sine[:, None, :]
    compressed = latent[:, :RANK].astype(f32)
    latent_scale = lax.rsqrt(jnp.mean(compressed * compressed, axis=1, keepdims=True) + epsilon)
    latent_unit = compressed * latent_scale
    latent_normed = (latent_unit * latent_gain).astype(bf16)
    key_rope = rotate(latent[:, RANK:].astype(f32), cosine, sine).astype(bf16)
    expanded = jnp.dot(latent_normed, expand_full, preferred_element_type=f32).reshape(
        rows_count, local_heads, NOPE + VDIM
    )
    key_nope = expanded[..., :NOPE].astype(bf16)
    values_all = expanded[..., NOPE:].astype(bf16)
    query_nope = query[..., :NOPE].astype(bf16)
    query_rope = rotate(query[..., NOPE:], head_cos, head_sin).astype(bf16)

    def block_scores(start):
        ending = start + block_rows
        raw = jnp.einsum("qhd,khd->hqk", query_nope, key_nope, preferred_element_type=f32)
        raw = raw + jnp.einsum("qhd,kd->hqk", query_rope, key_rope, preferred_element_type=f32)
        allowed = (segment_row[start:ending, None] == segment_row[None, :]) & (
            places[None, :] <= places[:, None]
        )
        return jnp.where(allowed[None], raw * score_scale, -1e30)

    start = 0
    scores = block_scores(start)
    top = jnp.max(scores, axis=2, keepdims=True)
    exponent = jnp.exp(scores - top)
    total = jnp.sum(exponent, axis=2, keepdims=True)
    weights = exponent / total
    log_blocks = top + jnp.log(total)
    mixed_blocks = jnp.einsum(
        "hqk,khd->qhd", weights.astype(bf16), values_all, preferred_element_type=f32
    ).astype(bf16)
    mixed = mixed_blocks.reshape(rows_count, local_heads * VDIM)
    attended = mix_sums(jnp.dot(mixed, output_full, preferred_element_type=f32))
    middle = source + attended
    scale_two = rms_scale(middle)
    unit_two = middle * scale_two
    normed_two_share = (unit_two * ffn_gain).astype(bf16)
    normed_two = spread(normed_two_share)
    logits = jnp.dot(normed_two, router_full, preferred_element_type=f32)
    log_total = jax.nn.logsumexp(logits, axis=1, keepdims=True)
    chosen = routes[:, :, None] == jnp.arange(expert_count, dtype=jnp.int32)[None, None, :]
    picked = jnp.sum(jnp.where(chosen, logits[:, None, :], 0.0), axis=2)
    gates = jnp.exp(picked - log_total)
    upstream = out_grad.astype(f32)
    upstream_full = spread(out_grad)
    shared_gate_pre = jnp.dot(normed_two, shared_gate_full, preferred_element_type=f32)
    shared_up_pre = jnp.dot(normed_two, shared_up_full, preferred_element_type=f32)
    shared_hidden = (jax.nn.silu(shared_gate_pre) * shared_up_pre).astype(bf16)
    shared_part = jnp.dot(shared_hidden, shared_down_full, preferred_element_type=f32)
    flat_routes = routes.reshape(-1)
    hits = (flat_routes[:, None] == jnp.arange(expert_count, dtype=jnp.int32)[None, :]).astype(
        jnp.int32
    )
    ranks = jnp.sum((jnp.cumsum(hits, axis=0) - 1) * hits, axis=1)
    owners = jnp.arange(rows_count * TOPK, dtype=jnp.int32) // TOPK
    share_slots = capacity // col_devices
    slot_count = row_devices * share_slots
    buffer_size = EXP_DEV * slot_count
    inside = ranks // share_slots == col_place
    slot_place = jnp.where(
        inside,
        flat_routes % EXP_DEV * slot_count
        + flat_routes // EXP_DEV * share_slots
        + ranks
        - col_place * share_slots,
        buffer_size,
    )
    token_of_slot = (
        jnp.full((buffer_size + 1,), rows_count, jnp.int32).at[slot_place].set(owners)[:buffer_size]
    )
    gate_of_slot = (
        jnp.zeros((buffer_size + 1,), f32).at[slot_place].set(gates.reshape(-1))[:buffer_size]
    )
    position = slot_place.reshape(rows_count, TOPK)
    gate_stack, up_stack, down_stack = (
        lax.all_gather(expert_gate, "col", axis=1, tiled=True),
        lax.all_gather(expert_up, "col", axis=1, tiled=True),
        lax.all_gather(expert_down, "col", axis=1, tiled=True),
    )
    padded_rows = jnp.concatenate([normed_two, jnp.zeros((1, D), bf16)], axis=0)
    outgoing = padded_rows[token_of_slot].reshape(EXP_DEV, slot_count, D)
    arrived = send_rows(outgoing)
    gate_pre = jnp.einsum("jnd,jfd->jnf", arrived, gate_stack, preferred_element_type=f32)
    up_pre = jnp.einsum("jnd,jfd->jnf", arrived, up_stack, preferred_element_type=f32)
    hidden = (jax.nn.silu(gate_pre) * up_pre).astype(bf16)
    expert_result = jnp.einsum(
        "jnf,jfd->jnd", hidden, down_stack, preferred_element_type=f32
    ).astype(bf16)
    returned = return_rows(expert_result).reshape(buffer_size, D)
    returned = jnp.concatenate([returned, jnp.zeros((1, D), bf16)], axis=0)
    slot_values = returned[position].astype(f32)
    combined = mix_sums(jnp.sum(gates[:, :, None] * slot_values, axis=1) + shared_part)
    upstream_wide = upstream_full.astype(f32)
    gate_partial = jnp.sum(upstream_wide[:, None, :] * slot_values, axis=2)
    output = (middle + combined).astype(bf16)
    gate_grads = lax.psum(gate_partial, "col")
    chances = jnp.exp(logits - log_total)
    weighted_gates = gate_grads * gates
    logit_grads = (
        jnp.sum(jnp.where(chosen, weighted_gates[:, :, None], 0.0), axis=1)
        - chances * jnp.sum(weighted_gates, axis=1, keepdims=True)
    ).astype(bf16)
    router_rows = lax.dynamic_slice_in_dim(router_full, col_place * width_share, width_share, 0)
    router_back = jnp.einsum("te,de->td", logit_grads, router_rows, preferred_element_type=f32)
    router_grad_part = jnp.einsum("td,te->de", normed_two, logit_grads, preferred_element_type=f32)
    shared_hidden_back = jnp.einsum(
        "td,fd->tf", upstream_full, shared_down_full, preferred_element_type=f32
    )
    shared_sigmoid = jax.nn.sigmoid(shared_gate_pre)
    shared_gate_back = (
        shared_hidden_back * shared_up_pre * silu_slope(shared_gate_pre, shared_sigmoid)
    ).astype(bf16)
    shared_up_back = (shared_hidden_back * (shared_gate_pre * shared_sigmoid)).astype(bf16)
    shared_input_back = jnp.einsum(
        "tf,df->td", shared_gate_back, shared_gate_full, preferred_element_type=f32
    ) + jnp.einsum("tf,df->td", shared_up_back, shared_up_full, preferred_element_type=f32)
    shared_gate_part = jnp.einsum(
        "td,tf->df", normed_two, shared_gate_back, preferred_element_type=f32
    )
    shared_up_part = jnp.einsum("td,tf->df", normed_two, shared_up_back, preferred_element_type=f32)
    shared_down_part = jnp.einsum(
        "tf,td->fd", shared_hidden, upstream_full, preferred_element_type=f32
    )
    padded_upstream = jnp.concatenate([upstream_wide, jnp.zeros((1, D), f32)], axis=0)
    slot_grads = (
        (gate_of_slot[:, None] * padded_upstream[token_of_slot])
        .astype(bf16)
        .reshape(EXP_DEV, slot_count, D)
    )
    arrived_grads = send_rows(slot_grads)
    hidden_back = jnp.einsum("jnd,jfd->jnf", arrived_grads, down_stack, preferred_element_type=f32)
    gate_sigmoid = jax.nn.sigmoid(gate_pre)
    gate_back = (hidden_back * up_pre * silu_slope(gate_pre, gate_sigmoid)).astype(bf16)
    up_back = (hidden_back * (gate_pre * gate_sigmoid)).astype(bf16)
    row_back = jnp.einsum(
        "jnf,jfd->jnd", gate_back, gate_stack, preferred_element_type=f32
    ) + jnp.einsum("jnf,jfd->jnd", up_back, up_stack, preferred_element_type=f32)
    returned_grads = return_rows(row_back.astype(bf16)).reshape(buffer_size, D)
    returned_grads = jnp.concatenate([returned_grads, jnp.zeros((1, D), bf16)], axis=0)
    routed_back = jnp.sum(returned_grads[position].astype(f32), axis=1)
    normed_two_back = mix_sums(routed_back + shared_input_back) + router_back
    gate_pieces = []
    up_pieces = []
    down_pieces = []
    for expert in range(EXP_DEV):
        gate_piece, up_piece, down_piece = (
            lax.psum_scatter(
                jnp.einsum(
                    "nf,nd->fd", gate_back[expert], arrived[expert], preferred_element_type=f32
                ).astype(jnp.bfloat16),
                "col",
                scatter_dimension=0,
                tiled=True,
            ).astype(jnp.float32),
            lax.psum_scatter(
                jnp.einsum(
                    "nf,nd->fd", up_back[expert], arrived[expert], preferred_element_type=f32
                ).astype(jnp.bfloat16),
                "col",
                scatter_dimension=0,
                tiled=True,
            ).astype(jnp.float32),
            lax.psum_scatter(
                jnp.einsum(
                    "nf,nd->fd", hidden[expert], arrived_grads[expert], preferred_element_type=f32
                ).astype(jnp.bfloat16),
                "col",
                scatter_dimension=0,
                tiled=True,
            ).astype(jnp.float32),
        )
        gate_pieces.append(gate_piece)
        up_pieces.append(up_piece)
        down_pieces.append(down_piece)
    expert_gate_grad = jnp.stack(gate_pieces, axis=0)
    expert_up_grad = jnp.stack(up_pieces, axis=0)
    expert_down_grad = jnp.stack(down_pieces, axis=0)
    ffn_gain_part = jnp.sum(normed_two_back * unit_two, axis=0)
    middle_back = upstream + norm_backward(normed_two_back, unit_two, scale_two, ffn_gain)
    attended_back = spread(middle_back.astype(bf16))
    mixed_back = (
        jnp.einsum("td,vd->tv", attended_back, output_full, preferred_element_type=f32)
        .astype(bf16)
        .reshape(rows_count, local_heads, VDIM)
    )
    output_grad_part = jnp.einsum("tv,td->vd", mixed, attended_back, preferred_element_type=f32)
    start = 0
    ending = start + block_rows
    scores = block_scores(start)
    weights = jnp.exp(scores - log_blocks)
    weight_back = jnp.einsum("qhd,khd->hqk", mixed_back, values_all, preferred_element_type=f32)
    center = jnp.sum(weight_back * weights, axis=2, keepdims=True)
    raw_back = (weights * (weight_back - center) * score_scale).astype(bf16)
    query_nope_back = jnp.einsum("hqk,khd->qhd", raw_back, key_nope, preferred_element_type=f32)
    query_rope_back = jnp.einsum("hqk,kd->qhd", raw_back, key_rope, preferred_element_type=f32)
    key_nope_back = jnp.einsum("hqk,qhd->khd", raw_back, query_nope, preferred_element_type=f32)
    key_rope_back = jnp.einsum("hqk,qhd->kd", raw_back, query_rope, preferred_element_type=f32)
    values_back = jnp.einsum(
        "hqk,qhd->khd", weights.astype(bf16), mixed_back, preferred_element_type=f32
    )
    query_back = jnp.concatenate(
        [query_nope_back, unrotate(query_rope_back, head_cos, head_sin)], axis=2
    )
    query_back = query_back.astype(bf16).reshape(rows_count, local_heads * (NOPE + ROPE))
    expanded_back = (
        jnp.concatenate([key_nope_back, values_back], axis=2)
        .astype(bf16)
        .reshape(rows_count, local_heads * (NOPE + VDIM))
    )
    latent_normed_back = jnp.einsum(
        "tc,rc->tr", expanded_back, expand_full, preferred_element_type=f32
    )
    expand_grad_part = jnp.einsum(
        "tr,tc->rc", latent_normed, expanded_back, preferred_element_type=f32
    )
    latent_gain_part = jnp.sum(latent_normed_back * latent_unit, axis=0)
    latent_weighted = latent_normed_back * latent_gain
    compressed_back = latent_scale * (
        latent_weighted
        - latent_unit * jnp.mean(latent_weighted * latent_unit, axis=1, keepdims=True)
    )
    rope_back = unrotate(key_rope_back, cosine, sine)
    latent_back, latent_gain_col = (
        lax.psum(
            jnp.concatenate([compressed_back, rope_back], axis=1).astype(jnp.bfloat16), "col"
        ).astype(jnp.float32),
        lax.psum(latent_gain_part.astype(jnp.bfloat16), "col").astype(jnp.float32),
    )
    latent_back = latent_back.astype(bf16)
    latent_grad_part = jnp.einsum("td,tc->dc", normed_one, latent_back, preferred_element_type=f32)
    query_grad_part = jnp.einsum("td,tc->dc", normed_one, query_back, preferred_element_type=f32)
    latent_rows = lax.dynamic_slice_in_dim(latent_full, col_place * width_share, width_share, 0)
    input_part = jnp.einsum("tc,dc->td", query_back, query_full, preferred_element_type=f32)
    normed_one_back = mix_sums(input_part) + jnp.einsum(
        "tc,dc->td", latent_back, latent_rows, preferred_element_type=f32
    )
    norm_gain_part = jnp.sum(normed_one_back * unit_one, axis=0)
    input_grad = middle_back + norm_backward(normed_one_back, unit_one, scale_one, norm_gain)
    norm_gain_grad, ffn_gain_grad, latent_gain_grad = lax.psum(
        (norm_gain_part, ffn_gain_part, latent_gain_col), "row"
    )
    (
        query_grad,
        latent_grad,
        expand_grad,
        output_grad,
        router_grad,
        shared_gate_grad,
        shared_up_grad,
        shared_down_grad,
    ) = (
        lax.psum_scatter(
            query_grad_part.astype(jnp.bfloat16), "row", scatter_dimension=0, tiled=True
        ).astype(jnp.float32),
        lax.psum_scatter(
            latent_grad_part.astype(jnp.bfloat16), "row", scatter_dimension=0, tiled=True
        ).astype(jnp.float32),
        lax.psum_scatter(
            expand_grad_part.astype(jnp.bfloat16), "row", scatter_dimension=0, tiled=True
        ).astype(jnp.float32),
        lax.psum_scatter(
            output_grad_part.astype(jnp.bfloat16), "row", scatter_dimension=1, tiled=True
        ).astype(jnp.float32),
        lax.psum_scatter(
            router_grad_part.astype(jnp.bfloat16), "row", scatter_dimension=0, tiled=True
        ).astype(jnp.float32),
        lax.psum_scatter(
            shared_gate_part.astype(jnp.bfloat16), "row", scatter_dimension=0, tiled=True
        ).astype(jnp.float32),
        lax.psum_scatter(
            shared_up_part.astype(jnp.bfloat16), "row", scatter_dimension=0, tiled=True
        ).astype(jnp.float32),
        lax.psum_scatter(
            shared_down_part.astype(jnp.bfloat16), "row", scatter_dimension=1, tiled=True
        ).astype(jnp.float32),
    )
    return (
        output,
        input_grad,
        norm_gain_grad,
        query_grad,
        latent_grad,
        latent_gain_grad,
        expand_grad,
        output_grad,
        ffn_gain_grad,
        router_grad,
        expert_gate_grad,
        expert_up_grad,
        expert_down_grad,
        shared_gate_grad,
        shared_up_grad,
        shared_down_grad,
    )


def solution(mesh):
    in_specs = (
        P("row", "col"),
        P("row", None),
        P("row", None),
        P("col"),
        P("row", "col"),
        P("row", None),
        P(),
        P("row", "col"),
        P("col", "row"),
        P("col"),
        P("row", None),
        P("row", "col", None),
        P("row", "col", None),
        P("row", "col", None),
        P("row", "col"),
        P("row", "col"),
        P("col", "row"),
        P("row", "col"),
    )
    out_specs = (
        P("row", "col"),
        P("row", "col"),
        P("col"),
        P("row", "col"),
        P("row", None),
        P(),
        P("row", "col"),
        P("col", "row"),
        P("col"),
        P("row", None),
        P("row", "col", None),
        P("row", "col", None),
        P("row", "col", None),
        P("row", "col"),
        P("row", "col"),
        P("col", "row"),
    )
    plan = on_device if dict(mesh.shape) == {"row": 16, "col": 2} else on_device_general
    return jax.shard_map(
        plan, mesh=mesh, in_specs=in_specs, out_specs=out_specs, check_vma=False
    )
```

```python
import jax
import jax.numpy as jnp
from jax import lax
from jax.experimental import pallas as pl
from jax.experimental.pallas import tpu as pltpu
from jax.sharding import PartitionSpec as P

D = 2048
NOPE = 128
ROPE = 64
RANK = 512
VDIM = 128
TOPK = 6
EXP_DEV = 4


epsilon = 1e-06
theta = 10000.0


def rotation(count, width):
    half = width // 2
    places = jnp.arange(count, dtype=jnp.float32)
    rates = theta ** (-jnp.arange(half, dtype=jnp.float32) * 2.0 / width)
    angles = places[:, None] * rates[None, :]
    return (jnp.cos(angles), jnp.sin(angles))


def rotate(values, cosine, sine):
    half = values.shape[-1] // 2
    first = values[..., :half]
    second = values[..., half:]
    return jnp.concatenate(
        [first * cosine - second * sine, second * cosine + first * sine], axis=-1
    )


def unrotate(grads, cosine, sine):
    half = grads.shape[-1] // 2
    first = grads[..., :half]
    second = grads[..., half:]
    return jnp.concatenate(
        [first * cosine + second * sine, second * cosine - first * sine], axis=-1
    )


def silu_slope(pre, sigmoid_value):
    return sigmoid_value * (1.0 + pre * (1.0 - sigmoid_value))


def col_total(values):
    return lax.psum(values, "col")


def spread(values):
    return lax.all_gather(values, "col", axis=1, tiled=True)


def mix_sums(values):
    return lax.psum_scatter(
        values.astype(jnp.bfloat16), "col", scatter_dimension=1, tiled=True
    ).astype(jnp.float32)


def send_rows(rows):
    return lax.all_to_all(rows, "row", split_axis=1, concat_axis=1, tiled=True)


def return_rows(rows):
    return lax.all_to_all(rows, "row", split_axis=1, concat_axis=1, tiled=True)


def rms_scale(rows):
    total = col_total(jnp.sum(rows * rows, axis=1))
    return lax.rsqrt(total / D + epsilon)[:, None]


def norm_backward(grads, unit, scale, gain):
    weighted = grads * gain
    average = col_total(jnp.sum(weighted * unit, axis=1)) / D
    return scale * (weighted - unit * average[:, None])


PLANES = 4
COMMON = 192
UNIQUE = 160
SENT = COMMON + UNIQUE
SHARED_PAD = 128
QUERY_COLUMNS = 1536
SCORE_SCALE = (NOPE + ROPE) ** (-0.5)


def swap_cols(values):
    return lax.ppermute(values, "col", [(0, 1), (1, 0)])


def swap_rows(values, bit):
    return lax.ppermute(values, "row", [(i, i ^ bit) for i in range(16)])


def turn_planes(values):
    return lax.ppermute(values, "row", [(i, (i + 4) % 16) for i in range(16)])


def join_cols(values, first):
    other = swap_cols(values)
    return jnp.where(
        first,
        jnp.concatenate([values, other], axis=1),
        jnp.concatenate([other, values], axis=1),
    )


def own_columns(values, first):
    half = values.shape[-1] // 2
    return jnp.where(first, values[..., :half], values[..., half:])


def other_columns(values, first):
    half = values.shape[-1] // 2
    return jnp.where(first, values[..., half:], values[..., :half])


def sent_rows(values, first):
    return jnp.concatenate(
        [values[:COMMON], jnp.where(first, values[COMMON:SENT], values[SENT:])], axis=0
    )


def local_tokens(values, axis, first):
    common = lax.slice_in_dim(values, 0, COMMON, axis=axis)
    one = lax.slice_in_dim(values, COMMON, SENT, axis=axis)
    two = lax.slice_in_dim(values, SENT, SENT + UNIQUE, axis=axis)
    return jnp.concatenate(
        [common, jnp.where(first, one, two), jnp.where(first, two, one)], axis=axis
    )


def together(*values):
    return lax.optimization_barrier(values)


def after(values, *others):
    return lax.optimization_barrier((values, *others))[0]


def batch(values):
    starts = [0]
    for value in values:
        starts.append(starts[-1] + value.shape[0])
    return jnp.concatenate(values, axis=0), starts[:-1]


class Spread:
    def __init__(self, rows):
        self.held = {(0, 0): rows}
        self.unique = {}
        self.sibling = {}

    def turn(self, plane):
        return turn_planes(self.held[plane - 1, 0])

    def cross(self, plane):
        return swap_rows(self.held[plane, 0], 2)

    def sent(self, *keys):
        return [self.held[key][COMMON:] for key in keys]

    def got(self, array, starts, *keys):
        for key, start in zip(keys, starts):
            self.unique[key] = (array, start)

    def passed(self, *keys):
        pieces = []
        for key in keys:
            if key[2]:
                array, start = self.unique[key[:2]]
                pieces.append(array[start : start + UNIQUE])
            else:
                pieces.append(self.held[key[:2]])
        return pieces

    def taken(self, array, starts, *keys):
        for key, start in zip(keys, starts):
            self.sibling[key] = (array, start)

    def family(self, plane):
        result = []
        for across in (0, 1):
            result.append(((self.held[plane, across], 0), self.unique[plane, across]))
            result.append((self.sibling[plane, across, 0], self.sibling[plane, across, 1]))
        return result


def add_unique(rest, unique, across):
    return jnp.concatenate([rest[across, :COMMON], rest[across, COMMON:] + unique[across]], axis=0)


def column_pieces(weight, bounds):
    return jnp.concatenate([weight[:, a:b] for a, b in bounds], axis=1)


def pair_columns(weight):
    head = NOPE + ROPE
    bounds = []
    for start in range(0, weight.shape[1], 2 * head):
        bounds += [(start, start + NOPE), (start + head, start + head + NOPE)]
        bounds += [(start + NOPE, start + head), (start + head + NOPE, start + 2 * head)]
    return column_pieces(weight, bounds)


def head_columns(weight):
    bounds = []
    for start in range(0, weight.shape[1], 2 * (NOPE + ROPE)):
        turned = start + 2 * NOPE
        bounds += [(start, start + NOPE), (turned, turned + ROPE)]
        bounds += [(start + NOPE, turned), (turned + ROPE, turned + 2 * ROPE)]
    return column_pieces(weight, bounds)


def merge_rows(own, received, first):
    own = own.astype(jnp.float32)
    received = received.astype(jnp.float32)
    common = own[:COMMON] + received[:COMMON]
    mine = own[COMMON:]
    theirs = received[COMMON:]
    return jnp.concatenate(
        [common, jnp.where(first, mine, theirs), jnp.where(first, theirs, mine)], axis=0
    )


FAMILIES = 4


def kernel_params(mebibytes):
    return pltpu.CompilerParams(vmem_limit_bytes=mebibytes * 1024 * 1024)


def short_cost():
    return pl.CostEstimate(flops=10**9, bytes_accessed=10**6, transcendentals=0)


def dot_last(left, right):
    return lax.dot_general(
        left, right, (((1,), (1,)), ((), ())), preferred_element_type=jnp.float32
    )


def dot_first(left, right):
    return lax.dot_general(
        left, right, (((0,), (0,)), ((), ())), preferred_element_type=jnp.float32
    )


def dot_plain(left, right):
    return jnp.dot(left, right, preferred_element_type=jnp.float32)


def slot_matches(codes_ref, capacity):
    tokens = codes_ref.shape[-1]
    ranks = lax.broadcasted_iota(jnp.int32, (capacity, tokens), 0)
    return [codes_ref[0, j : j + 1, :] == ranks for j in range(EXP_DEV)]


def as_picks(matches):
    one = [jnp.where(m, 1.0, 0.0).astype(jnp.bfloat16) for m in matches]
    return jnp.concatenate(one, axis=0)


def row_copies(refs, starts, held, sems, f):
    return [
        pltpu.make_async_copy(
            refs[2 * f].at[pl.ds(starts[2 * f], SENT)],
            held.at[f, pl.ds(0, SENT)],
            sems.at[f, 0],
        ),
        pltpu.make_async_copy(
            refs[2 * f + 1].at[pl.ds(starts[2 * f + 1], UNIQUE)],
            held.at[f, pl.ds(SENT, UNIQUE)],
            sems.at[f, 1],
        ),
    ]


def start_rows(refs, starts, held, sems):
    for f in range(FAMILIES):
        for copy in row_copies(refs, starts, held, sems, f):
            copy.start()


def wait_rows(refs, starts, held, sems, f):
    for family in range(FAMILIES):

        @pl.when(f == family)
        def _():
            for copy in row_copies(refs, starts, held, sems, family):
                copy.wait()


def pick_grads(plane, codes, last, capacity):
    pieces = [piece[0] for family in plane for piece in family]
    starts = [piece[1] for family in plane for piece in family]
    tokens = SENT + UNIQUE
    width = last.shape[1]
    pad = last.shape[0]

    def body(*refs):
        rows_in = refs[:8]
        codes_ref, last_ref, slots_ref, hidden_ref, held, sems = refs[8:]
        f = pl.program_id(0)

        @pl.when(f == 0)
        def _():
            start_rows(rows_in, starts, held, sems)

        wait_rows(rows_in, starts, held, sems, f)
        rows = held[f]
        picks = as_picks(slot_matches(codes_ref, capacity))
        taken = dot_plain(picks, rows).astype(jnp.bfloat16)
        slots_ref[...] = taken.reshape(EXP_DEV, capacity, width)
        hidden_ref[0] = dot_last(rows, last_ref[...])

    return pl.pallas_call(
        body,
        grid=(FAMILIES,),
        in_specs=[pl.BlockSpec(memory_space=pl.ANY)] * 8
        + [
            pl.BlockSpec((1, 8, tokens), lambda f: (f, 0, 0)),
            pl.BlockSpec((pad, width), lambda f: (0, 0)),
        ],
        out_specs=[
            pl.BlockSpec((EXP_DEV, capacity, width), lambda f: (0, f, 0)),
            pl.BlockSpec((1, tokens, pad), lambda f: (f, 0, 0)),
        ],
        out_shape=[
            jax.ShapeDtypeStruct((EXP_DEV, FAMILIES * capacity, width), jnp.bfloat16),
            jax.ShapeDtypeStruct((FAMILIES, tokens, pad), jnp.float32),
        ],
        scratch_shapes=[
            pltpu.VMEM((FAMILIES, tokens, width), jnp.bfloat16),
            pltpu.SemaphoreType.DMA((FAMILIES, 2)),
        ],
        compiler_params=kernel_params(32),
        cost_estimate=short_cost(),
    )(*pieces, codes, last)


def pick_rows(plane, grad_plane, codes, router, pair, hidden_grads, capacity):
    pieces = [piece[0] for family in plane for piece in family]
    starts = [piece[1] for family in plane for piece in family]
    grad_pieces = [piece[0] for family in grad_plane for piece in family]
    grad_starts = [piece[1] for family in grad_plane for piece in family]
    tokens = SENT + UNIQUE
    width = pair.shape[1]
    pad = pair.shape[0] // 2

    def body(*refs):
        rows_in = refs[:8]
        grads_in = refs[8:16]
        (codes_ref, router_ref, pair_ref, hidden_grads_ref) = refs[16:20]
        (slots_ref, gates_ref, hidden_ref, back_ref, grad_ref) = refs[20:25]
        held, held_grads, sems, grad_sems = refs[25:]
        f = pl.program_id(0)

        @pl.when(f == 0)
        def _():
            start_rows(rows_in, starts, held, sems)
            start_rows(grads_in, grad_starts, held_grads, grad_sems)
            grad_ref[...] = jnp.zeros_like(grad_ref)

        wait_rows(rows_in, starts, held, sems, f)
        rows = held[f]
        matches = slot_matches(codes_ref, capacity)
        taken = dot_plain(as_picks(matches), rows).astype(jnp.bfloat16)
        slots_ref[...] = taken.reshape(EXP_DEV, capacity, width)
        logits = dot_last(router_ref[...], rows)
        top = jnp.max(logits, axis=0, keepdims=True)
        total = jnp.log(jnp.sum(jnp.exp(logits - top), axis=0, keepdims=True)) + top
        for j in range(EXP_DEV):
            chance = jnp.exp(logits[j : j + 1] - total)
            gate = jnp.sum(jnp.where(matches[j], chance, 0.0), axis=1, keepdims=True)
            gates_ref[j] = jnp.broadcast_to(gate, (capacity, 128))
        pre = dot_last(rows, pair_ref[...])
        gate_pre = pre[:, :pad]
        up_pre = pre[:, pad:]
        hidden_back = hidden_grads_ref[0]
        sigmoid_value = jax.nn.sigmoid(gate_pre)
        silu_value = gate_pre * sigmoid_value
        hidden = (silu_value * up_pre).astype(jnp.bfloat16)
        slope = sigmoid_value * (1.0 + gate_pre * (1.0 - sigmoid_value))
        gate_back = (hidden_back * up_pre * slope).astype(jnp.bfloat16)
        up_back = (hidden_back * silu_value).astype(jnp.bfloat16)
        back = jnp.concatenate([gate_back, up_back], axis=1)
        hidden_ref[0] = hidden
        back_ref[0] = back
        grad_ref[: 2 * pad] += dot_first(back, rows)
        wait_rows(grads_in, grad_starts, held_grads, grad_sems, f)
        grad_ref[2 * pad :] += dot_first(hidden, held_grads[f])

    return pl.pallas_call(
        body,
        grid=(FAMILIES,),
        in_specs=[pl.BlockSpec(memory_space=pl.ANY)] * 16
        + [
            pl.BlockSpec((1, 8, tokens), lambda f: (f, 0, 0)),
            pl.BlockSpec(router.shape, lambda f: (0, 0)),
            pl.BlockSpec(pair.shape, lambda f: (0, 0)),
            pl.BlockSpec((1, tokens, pad), lambda f: (f, 0, 0)),
        ],
        out_specs=[
            pl.BlockSpec((EXP_DEV, capacity, width), lambda f: (0, f, 0)),
            pl.BlockSpec((EXP_DEV, capacity, 128), lambda f: (0, f, 0)),
            pl.BlockSpec((1, tokens, pad), lambda f: (f, 0, 0)),
            pl.BlockSpec((1, tokens, 2 * pad), lambda f: (f, 0, 0)),
            pl.BlockSpec((3 * pad, width), lambda f: (0, 0)),
        ],
        out_shape=[
            jax.ShapeDtypeStruct((EXP_DEV, FAMILIES * capacity, width), jnp.bfloat16),
            jax.ShapeDtypeStruct((EXP_DEV, FAMILIES * capacity, 128), jnp.float32),
            jax.ShapeDtypeStruct((FAMILIES, tokens, pad), jnp.bfloat16),
            jax.ShapeDtypeStruct((FAMILIES, tokens, 2 * pad), jnp.bfloat16),
            jax.ShapeDtypeStruct((3 * pad, width), jnp.float32),
        ],
        scratch_shapes=[
            pltpu.VMEM((FAMILIES, tokens, width), jnp.bfloat16),
            pltpu.VMEM((FAMILIES, tokens, width), jnp.bfloat16),
            pltpu.SemaphoreType.DMA((FAMILIES, 2)),
            pltpu.SemaphoreType.DMA((FAMILIES, 2)),
        ],
        compiler_params=kernel_params(48),
        cost_estimate=short_cost(),
    )(*pieces, *grad_pieces, codes, router, pair, hidden_grads)


def run_experts(slot_rows, slot_grads, gates, expert_gate, expert_up, expert_down):
    count, slots, width = slot_rows.shape
    units = expert_gate.shape[1]

    def body(
        rows_ref,
        grads_ref,
        gates_ref,
        gate_ref,
        up_ref,
        down_ref,
        sum_ref,
        back_ref,
        hidden_ref,
        gate_back_ref,
        up_back_ref,
        gate_grad_ref,
    ):
        rows = rows_ref[0]
        gates_here = gates_ref[0][:, :1]
        gate_pre = dot_last(rows, gate_ref[0])
        up_pre = dot_last(rows, up_ref[0])
        down_back = dot_last(grads_ref[0], down_ref[0])
        sigmoid_value = jax.nn.sigmoid(gate_pre)
        silu_value = gate_pre * sigmoid_value
        hidden = silu_value * up_pre
        gate_grad = jnp.sum(hidden * down_back, axis=1, keepdims=True)
        gate_grad_ref[0] = jnp.broadcast_to(gate_grad, (slots, 128))
        hidden_back = down_back * gates_here
        slope = sigmoid_value * (1.0 + gate_pre * (1.0 - sigmoid_value))
        gate_back = (hidden_back * up_pre * slope).astype(jnp.bfloat16)
        up_back = (hidden_back * silu_value).astype(jnp.bfloat16)
        scaled = (hidden * gates_here).astype(jnp.bfloat16)
        hidden_ref[0] = scaled
        gate_back_ref[0] = gate_back
        up_back_ref[0] = up_back
        back = dot_plain(gate_back, gate_ref[0]) + dot_plain(up_back, up_ref[0])
        back_ref[0] = back.astype(jnp.bfloat16)
        sum_ref[0] = dot_plain(scaled, down_ref[0]).astype(jnp.bfloat16)

    wide = pl.BlockSpec((1, slots, width), lambda j: (j, 0, 0))
    narrow = pl.BlockSpec((1, slots, 128), lambda j: (j, 0, 0))
    inner = pl.BlockSpec((1, slots, units), lambda j: (j, 0, 0))
    matrix = pl.BlockSpec((1, units, width), lambda j: (j, 0, 0))
    return pl.pallas_call(
        body,
        grid=(count,),
        in_specs=[wide, wide, narrow, matrix, matrix, matrix],
        out_specs=[wide, wide, inner, inner, inner, narrow],
        out_shape=[
            jax.ShapeDtypeStruct((count, slots, width), jnp.bfloat16),
            jax.ShapeDtypeStruct((count, slots, width), jnp.bfloat16),
            jax.ShapeDtypeStruct((count, slots, units), jnp.bfloat16),
            jax.ShapeDtypeStruct((count, slots, units), jnp.bfloat16),
            jax.ShapeDtypeStruct((count, slots, units), jnp.bfloat16),
            jax.ShapeDtypeStruct((count, slots, 128), jnp.float32),
        ],
        compiler_params=kernel_params(56),
        cost_estimate=short_cost(),
    )(slot_rows, slot_grads, gates, expert_gate, expert_up, expert_down)


def sum_tokens(values, codes, shared, matrix, capacity, core, received=None, gate_grads=None):
    tokens = codes.shape[2]
    width = values.shape[2]
    inner = matrix.shape[0]
    with_rows = received is not None
    with_gates = gate_grads is not None

    def body(*refs):
        values_ref, codes_ref, shared_ref, matrix_ref = refs[:4]
        outs = refs[4 + with_rows + with_gates :]
        matches = slot_matches(codes_ref, capacity)
        rows = values_ref[...].reshape(EXP_DEV * capacity, width)
        total = dot_first(as_picks(matches), rows)
        total = total + dot_plain(shared_ref[0], matrix_ref[...])
        if with_rows:
            total = (total + refs[4][0].astype(jnp.float32)).astype(jnp.bfloat16)
            outs[0][0] = total[:SENT]
            outs[1][0] = total[SENT:]
        else:
            outs[0][0] = total.astype(jnp.bfloat16)
        if with_gates:
            dense = [
                jnp.sum(
                    jnp.where(matches[j], refs[4 + with_rows][j][:, :1], 0.0),
                    axis=0,
                    keepdims=True,
                )
                for j in range(EXP_DEV)
            ]
            outs[-1][0] = jnp.concatenate(dense + [jnp.zeros((4, tokens), jnp.float32)], axis=0)

    in_specs = [
        pl.BlockSpec((EXP_DEV, capacity, width), lambda i: (0, 2 * i + core, 0)),
        pl.BlockSpec((1, 8, tokens), lambda i: (2 * i + core, 0, 0)),
        pl.BlockSpec((1, tokens, inner), lambda i: (2 * i + core, 0, 0)),
        pl.BlockSpec((inner, width), lambda i: (0, 0)),
    ]
    operands = [values, codes, shared, matrix]
    pieces = [tokens]
    if with_rows:
        in_specs.append(pl.BlockSpec((1, tokens, width), lambda i: (i, 0, 0)))
        operands.append(received)
        pieces = [SENT, UNIQUE]
    out_specs = [pl.BlockSpec((1, piece, width), lambda i: (i, 0, 0)) for piece in pieces]
    out_shape = [jax.ShapeDtypeStruct((2, piece, width), jnp.bfloat16) for piece in pieces]
    if with_gates:
        in_specs.append(pl.BlockSpec((EXP_DEV, capacity, 128), lambda i: (0, 2 * i + core, 0)))
        operands.append(gate_grads)
        out_specs.append(pl.BlockSpec((1, 8, tokens), lambda i: (i, 0, 0)))
        out_shape.append(jax.ShapeDtypeStruct((2, 8, tokens), jnp.float32))
    return pl.pallas_call(
        body,
        grid=(2,),
        in_specs=in_specs,
        out_specs=out_specs,
        out_shape=out_shape,
        compiler_params=kernel_params(60),
        cost_estimate=short_cost(),
    )(*operands)


def pack_weights(query_weight, expand_weight, output_weight, latent_weight, router_weight, routes):
    block = latent_weight.shape[0]
    share = expand_weight.shape[0]
    widths = [
        query_weight.shape[1],
        expand_weight.shape[1] * share // block,
        output_weight.shape[0],
        latent_weight.shape[1],
        router_weight.shape[1],
        routes.shape[1],
    ]
    columns = (sum(widths) + 127) // 128 * 128

    def body(query_ref, expand_ref, output_ref, latent_ref, router_ref, routes_ref, out_ref):
        out_ref[:, : widths[0]] = pair_columns(query_ref[...])
        start = widths[0]
        for i in range(block // share):
            out_ref[share * i : share * (i + 1), start : start + widths[1]] = expand_ref[
                :, widths[1] * i : widths[1] * (i + 1)
            ]
        start += widths[1]
        out_ref[:, start : start + widths[2]] = output_ref[...].T
        start += widths[2]
        out_ref[:, start : start + widths[3] + widths[4]] = jnp.concatenate(
            [latent_ref[...], router_ref[...]], axis=1
        )
        start += widths[3] + widths[4]
        last = jnp.zeros((block, columns - start - widths[5]), jnp.bfloat16)
        out_ref[:, start:] = jnp.concatenate([routes_ref[...], last], axis=1)

    return pl.pallas_call(
        body,
        out_shape=jax.ShapeDtypeStruct((block, columns), jnp.bfloat16),
        compiler_params=kernel_params(16),
        cost_estimate=short_cost(),
    )(query_weight, expand_weight, output_weight, latent_weight, router_weight, routes)


def unpack_grads(output, joined, widths):
    block = joined.shape[0]
    query_width, expand_width, latent_width = widths
    edge = query_width + expand_width
    parts = 4
    share = block // parts

    def body(sum_ref, joined_ref, output_ref, query_ref, expand_ref, latent_ref, router_ref):
        output_ref[...] = sum_ref[...].astype(jnp.float32).T
        query_ref[...] = head_columns(joined_ref[:, :query_width]).astype(jnp.float32)
        for i in range(parts):
            expand_ref[:, expand_width * i : expand_width * (i + 1)] = joined_ref[
                share * i : share * (i + 1), query_width:edge
            ].astype(jnp.float32)
        narrow = joined_ref[:, edge:].astype(jnp.float32)
        latent_ref[...] = narrow[:, :latent_width]
        router_ref[...] = narrow[:, latent_width:]

    shapes = [
        (output.shape[1], block),
        (block, query_width),
        (share, expand_width * parts),
        (block, latent_width),
        (block, joined.shape[1] - edge - latent_width),
    ]
    return pl.pallas_call(
        body,
        out_shape=[jax.ShapeDtypeStruct(shape, jnp.float32) for shape in shapes],
        compiler_params=kernel_params(16),
        cost_estimate=short_cost(),
    )(output, joined)


def block_grads(places, left, right, tile, core, turned=None, expanded=None, received=None):
    count, width = left.shape
    block = width // (4 * PLANES)
    blocks = 2 * PLANES
    columns = right.shape[1]
    steps = columns // tile
    with_expand = turned is not None
    share = turned.shape[0] // (4 * PLANES) if with_expand else 0
    quarter = expanded.shape[1] // steps if with_expand else 0

    def body(places_ref, left_ref, right_ref, *refs):
        held = refs[-2]
        held_turned = refs[-1]
        out_ref = refs[-3]
        step = pl.program_id(0)

        @pl.when(step == 0)
        def _():
            for i in range(blocks):
                place = places_ref[2 * i + core]
                start = pl.multiple_of(place * block, block)
                held[:, block * i : block * (i + 1)] = left_ref[:, pl.ds(start, block)]
                if with_expand:
                    start = pl.multiple_of(place * share, share)
                    held_turned[share * i : share * (i + 1)] = refs[0][pl.ds(start, share)]

        part = dot_first(held[...], right_ref[...]).reshape(blocks, block, tile)
        lanes = pl.ds(pl.multiple_of(step * tile, 128), tile)
        if received is not None:
            got_ref = refs[-4]
            part = part + got_ref[:, :, lanes].astype(jnp.float32)
        out_ref[:, :, lanes] = part.astype(jnp.bfloat16)
        if with_expand:
            part = dot_plain(held_turned[...], refs[1][...]).reshape(blocks, share, quarter)
            lines = pl.ds(pl.multiple_of(step * share, share), share)
            if received is not None:
                part = part + got_ref[:, lines, columns:].astype(jnp.float32)
            out_ref[:, lines, columns:] = part.astype(jnp.bfloat16)

    whole = lambda shape: pl.BlockSpec(shape, lambda h, places_ref: (0,) * len(shape))
    in_specs = [
        whole(left.shape),
        pl.BlockSpec((count, tile), lambda h, places_ref: (0, h)),
    ]
    operands = [left, right]
    if with_expand:
        in_specs += [
            whole(turned.shape),
            pl.BlockSpec((count, quarter), lambda h, places_ref: (0, h)),
        ]
        operands += [turned, expanded]
    shape = (blocks, block, columns + quarter)
    if received is not None:
        in_specs.append(whole(shape))
        operands.append(received)
    return pl.pallas_call(
        body,
        grid_spec=pltpu.PrefetchScalarGridSpec(
            num_scalar_prefetch=1,
            grid=(steps,),
            in_specs=in_specs,
            out_specs=whole(shape),
            scratch_shapes=[
                pltpu.VMEM((count, blocks * block), jnp.bfloat16),
                pltpu.VMEM((max(blocks * share, 16), count), jnp.bfloat16),
            ],
        ),
        out_shape=jax.ShapeDtypeStruct(shape, jnp.bfloat16),
        compiler_params=kernel_params(40),
        cost_estimate=short_cost(),
    )(places, *operands)


def joined_grads(
    places, normed, query_back, turned, expanded, latent_back, normed_two, logit_grads, wide, narrow
):
    count, width = normed.shape
    block = width // (4 * PLANES)
    blocks = 2 * PLANES
    query_width = query_back.shape[1]
    tile = 384
    steps = query_width // tile
    share = turned.shape[0] // (4 * PLANES)
    quarter = expanded.shape[1] // steps
    latent_width = latent_back.shape[1]
    edge = query_width + quarter

    def body(
        places_ref,
        normed_ref,
        query_ref,
        turned_ref,
        expanded_ref,
        latent_ref,
        two_ref,
        logit_ref,
        wide_ref,
        narrow_ref,
        out_ref,
        held,
        held_turned,
        held_two,
    ):
        step = pl.program_id(0)

        @pl.when(step == 0)
        def _():
            for i in range(blocks):
                place = places_ref[2 * i]
                start = pl.multiple_of(place * block, block)
                held[:, block * i : block * (i + 1)] = normed_ref[:, pl.ds(start, block)]
                held_two[:, block * i : block * (i + 1)] = two_ref[:, pl.ds(start, block)]
                start = pl.multiple_of(place * share, share)
                held_turned[share * i : share * (i + 1)] = turned_ref[pl.ds(start, share)]
            part = jnp.concatenate(
                [
                    dot_first(held[...], latent_ref[...]),
                    dot_first(held_two[...], logit_ref[...]),
                ],
                axis=1,
            ).reshape(blocks, block, narrow.shape[2])
            part = part + narrow_ref[...].astype(jnp.float32)
            out_ref[:, :, edge:] = part.astype(jnp.bfloat16)

        lanes = pl.ds(pl.multiple_of(step * tile, 128), tile)
        part = dot_first(held[...], query_ref[...]).reshape(blocks, block, tile)
        part = part + wide_ref[:, :, lanes].astype(jnp.float32)
        out_ref[:, :, lanes] = part.astype(jnp.bfloat16)
        lines = pl.ds(pl.multiple_of(step * share, share), share)
        part = dot_plain(held_turned[...], expanded_ref[...]).reshape(blocks, share, quarter)
        part = part + wide_ref[:, lines, query_width:].astype(jnp.float32)
        out_ref[:, lines, query_width:edge] = part.astype(jnp.bfloat16)

    whole = lambda shape: pl.BlockSpec(shape, lambda h, places_ref: (0,) * len(shape))
    shape = (blocks, block, edge + narrow.shape[2])
    return pl.pallas_call(
        body,
        grid_spec=pltpu.PrefetchScalarGridSpec(
            num_scalar_prefetch=1,
            grid=(steps,),
            in_specs=[
                whole(normed.shape),
                pl.BlockSpec((count, tile), lambda h, places_ref: (0, h)),
                whole(turned.shape),
                pl.BlockSpec((count, quarter), lambda h, places_ref: (0, h)),
                whole(latent_back.shape),
                whole(normed_two.shape),
                whole(logit_grads.shape),
                whole(wide.shape),
                whole(narrow.shape),
            ],
            out_specs=whole(shape),
            scratch_shapes=[
                pltpu.VMEM((count, blocks * block), jnp.bfloat16),
                pltpu.VMEM((blocks * share, count), jnp.bfloat16),
                pltpu.VMEM((count, blocks * block), jnp.bfloat16),
            ],
        ),
        out_shape=jax.ShapeDtypeStruct(shape, jnp.bfloat16),
        compiler_params=kernel_params(40),
        cost_estimate=short_cost(),
    )(
        places,
        normed,
        query_back,
        turned,
        expanded,
        latent_back,
        normed_two,
        logit_grads,
        wide,
        narrow,
    )


def narrow_grads(places, normed, latent_back, normed_two, logit_grads, core):
    count, width = normed.shape
    block = width // (4 * PLANES)
    widths = [latent_back.shape[1], logit_grads.shape[1]]

    def body(places_ref, normed_ref, two_ref, latent_ref, logit_ref, out_ref):
        parts = [
            dot_first(normed_ref[...], latent_ref[...]),
            dot_first(two_ref[...], logit_ref[...]),
        ]
        out_ref[0] = jnp.concatenate(parts, axis=1).astype(jnp.bfloat16)

    piece = pl.BlockSpec((count, block), lambda i, places_ref: (0, places_ref[2 * i + core]))
    whole = lambda columns: pl.BlockSpec((count, columns), lambda i, places_ref: (0, 0))
    return pl.pallas_call(
        body,
        grid_spec=pltpu.PrefetchScalarGridSpec(
            num_scalar_prefetch=1,
            grid=(2 * PLANES,),
            in_specs=[piece, piece, whole(widths[0]), whole(widths[1])],
            out_specs=pl.BlockSpec((1, block, sum(widths)), lambda i, places_ref: (i, 0, 0)),
        ),
        out_shape=jax.ShapeDtypeStruct((2 * PLANES, block, sum(widths)), jnp.bfloat16),
        compiler_params=kernel_params(24),
        cost_estimate=short_cost(),
    )(places, normed, normed_two, latent_back, logit_grads)


def assemble(blocks, places):
    count = len(blocks)

    def body(places_ref, *refs):
        out, held, sems, out_sems = refs[count:]
        arrivals = [
            pltpu.make_async_copy(refs[i], held.at[i], sems.at[i]) for i in range(count)
        ]
        leaving = [
            pltpu.make_async_copy(held.at[i], out.at[places_ref[i]], out_sems.at[i])
            for i in range(count)
        ]
        for copy in arrivals:
            copy.start()
        for i in range(count):
            arrivals[i].wait()
            leaving[i].start()
        for copy in leaving:
            copy.wait()

    return pl.pallas_call(
        body,
        in_specs=[pl.BlockSpec(memory_space=pltpu.SMEM)]
        + [pl.BlockSpec(memory_space=pl.ANY)] * len(blocks),
        out_specs=pl.BlockSpec(memory_space=pl.ANY),
        out_shape=jax.ShapeDtypeStruct((len(blocks),) + blocks[0].shape, blocks[0].dtype),
        scratch_shapes=[
            pltpu.VMEM((count,) + blocks[0].shape, blocks[0].dtype),
            pltpu.SemaphoreType.DMA((count,)),
            pltpu.SemaphoreType.DMA((count,)),
        ],
        compiler_params=kernel_params(24),
        cost_estimate=short_cost(),
    )(places, *blocks)


def expert_weight_grads(rows, grads, gate_backs, up_backs, hiddens, begin, count, earlier):
    experts, slots, width = rows[0].shape
    units = hiddens[0].shape[2]
    tile = 512
    planes = len(rows)

    def body(*refs):
        rows_in = refs[:planes]
        grads_in = refs[planes : 2 * planes]
        gate_in = refs[2 * planes : 3 * planes]
        up_in = refs[3 * planes : 4 * planes]
        hidden_in = refs[4 * planes : 5 * planes]
        gate_ref, up_ref, down_ref = refs[-3:]
        for left, right, out in (
            (gate_in, rows_in, gate_ref),
            (up_in, rows_in, up_ref),
            (hidden_in, grads_in, down_ref),
        ):
            total = dot_first(left[0][0], right[0][0])
            for p in range(1, planes):
                total = total + dot_first(left[p][0], right[p][0])
            out[0] = total

    wide = pl.BlockSpec((1, slots, tile), lambda j, d: (begin + j, 0, d))
    inner = pl.BlockSpec((1, slots, units), lambda j, d: (begin + j, 0, 0))
    result = pl.BlockSpec((1, units, tile), lambda j, d: (begin + j, 0, d))
    return pl.pallas_call(
        body,
        grid=(count, width // tile),
        in_specs=[wide] * (2 * planes)
        + [inner] * (3 * planes)
        + [pl.BlockSpec(memory_space=pl.ANY)] * len(earlier),
        out_specs=[result] * 3,
        out_shape=[jax.ShapeDtypeStruct((experts, units, width), jnp.float32)] * 3,
        input_output_aliases={5 * planes + i: i for i in range(len(earlier))},
        compiler_params=kernel_params(52),
        cost_estimate=short_cost(),
    )(*rows, *grads, *gate_backs, *up_backs, *hiddens, *earlier)


def swap_halves(values):
    lanes = lax.broadcasted_iota(jnp.int32, values.shape, 1)
    return jnp.where(lanes % 64 < 32, pltpu.roll(values, 96, 1), pltpu.roll(values, 32, 1))


def masked_weights(segment_column, segment_line, query, keys, rope, head_rope):
    count = query.shape[0]
    raw = dot_last(query, keys) + dot_last(rope, head_rope)
    after_key = lax.broadcasted_iota(jnp.int32, (count, count), 0) >= lax.broadcasted_iota(
        jnp.int32, (count, count), 1
    )
    allowed = (segment_column == segment_line) & after_key
    scores = jnp.where(allowed, raw * SCORE_SCALE, -1e30)
    exponent = jnp.exp(scores - jnp.max(scores, axis=1, keepdims=True))
    return exponent / jnp.sum(exponent, axis=1, keepdims=True)


def head_ropes(key_rope):
    zeros = jnp.zeros_like(key_rope)
    return [
        jnp.concatenate([key_rope, zeros], axis=1),
        jnp.concatenate([zeros, key_rope], axis=1),
    ]


def attend(normed, latent_normed, ropes, turns, segments, dense):
    count, width = normed.shape
    rows, block, columns = dense.shape
    pairs = QUERY_COLUMNS // 384
    rank = latent_normed.shape[1]
    share = rank // rows
    flat = dense.reshape(rows * block, columns)
    quarters = dense.reshape(rows, block // share, share, columns)

    def body(
        normed_ref,
        latent_ref,
        rope0_ref,
        rope1_ref,
        cosine_ref,
        sine_ref,
        column_ref,
        line_ref,
        query_weight_ref,
        expand_ref,
        output_ref,
        query_ref,
        keys_ref,
        mixed_ref,
        attended_ref,
        total,
    ):
        step = pl.program_id(0)
        query = dot_plain(normed_ref[...], query_weight_ref[...])
        rope = query[:, 256:]
        rope = rope * cosine_ref[...] + swap_halves(rope) * sine_ref[...]
        query = jnp.concatenate([query[:, :256], rope], axis=1).astype(jnp.bfloat16)
        expand = expand_ref[...].reshape(rank, 512)
        keys = dot_plain(latent_ref[...], expand).astype(jnp.bfloat16)
        query_ref[...] = query
        keys_ref[...] = keys
        mixed = []
        for head, rope_ref in enumerate((rope0_ref, rope1_ref)):
            weights = masked_weights(
                column_ref[:, :1],
                line_ref[:1],
                query[:, 128 * head : 128 * head + 128],
                keys[:, 256 * head : 256 * head + 128],
                query[:, 256:],
                rope_ref[...],
            )
            values = keys[:, 256 * head + 128 : 256 * head + 256]
            mixed.append(dot_plain(weights.astype(jnp.bfloat16), values).astype(jnp.bfloat16))
        mixed = jnp.concatenate(mixed, axis=1)
        mixed_ref[...] = mixed
        part = dot_last(mixed, output_ref[...])

        @pl.when(step == 0)
        def _():
            total[...] = part

        @pl.when(step > 0)
        def _():
            total[...] += part

        @pl.when(step == pairs - 1)
        def _():
            attended_ref[...] = total[...].astype(jnp.bfloat16)

    whole = lambda shape: pl.BlockSpec(shape, lambda h: (0,) * len(shape))
    return pl.pallas_call(
        body,
        grid=(pairs,),
        in_specs=[
            whole((count, width)),
            whole((count, rank)),
            whole((count, 128)),
            whole((count, 128)),
            whole((count, 128)),
            whole((count, 128)),
            whole((count, 128)),
            whole((8, count)),
            pl.BlockSpec((width, 384), lambda h: (0, h)),
            pl.BlockSpec((rows, 1, share, 512), lambda h: (0, h, 0, QUERY_COLUMNS // 512)),
            pl.BlockSpec((width, 256), lambda h: (0, (QUERY_COLUMNS + 512) // 256 + h)),
        ],
        out_specs=[
            pl.BlockSpec((count, 384), lambda h: (0, h)),
            pl.BlockSpec((count, 512), lambda h: (0, h)),
            pl.BlockSpec((count, 256), lambda h: (0, h)),
            whole((count, width)),
        ],
        out_shape=[
            jax.ShapeDtypeStruct((count, 384 * pairs), jnp.bfloat16),
            jax.ShapeDtypeStruct((count, 512 * pairs), jnp.bfloat16),
            jax.ShapeDtypeStruct((count, 256 * pairs), jnp.bfloat16),
            jax.ShapeDtypeStruct((count, width), jnp.bfloat16),
        ],
        scratch_shapes=[pltpu.VMEM((count, width), jnp.float32)],
        compiler_params=kernel_params(44),
        cost_estimate=short_cost(),
    )(normed, latent_normed, *ropes, *turns, *segments, flat, quarters, flat)


def attend_back(upstream, query, keys, ropes, turns, segments, dense, rank):
    count, width = upstream.shape
    rows, block, columns = dense.shape
    pairs = QUERY_COLUMNS // 384
    share = rank // rows
    flat = dense.reshape(rows * block, columns)
    quarters = dense.reshape(rows, block // share, share, columns)

    def body(
        upstream_ref,
        query_ref,
        keys_ref,
        rope0_ref,
        rope1_ref,
        cosine_ref,
        sine_ref,
        column_ref,
        line_ref,
        query_weight_ref,
        expand_ref,
        output_ref,
        query_back_ref,
        keys_back_ref,
        rope_back_ref,
        latent_back_ref,
        input_ref,
        total,
    ):
        step = pl.program_id(0)
        mixed_back = dot_plain(upstream_ref[...], output_ref[...]).astype(jnp.bfloat16)
        query = query_ref[...]
        keys = keys_ref[...]
        rope = query[:, 256:]
        lanes = lax.broadcasted_iota(jnp.int32, (count, 128), 1)
        query_back = []
        keys_back = []
        rope_back = 0.0
        key_rope_back = 0.0
        for head, rope_ref in enumerate((rope0_ref, rope1_ref)):
            query_nope = query[:, 128 * head : 128 * head + 128]
            key_nope = keys[:, 256 * head : 256 * head + 128]
            values = keys[:, 256 * head + 128 : 256 * head + 256]
            mixed_head = mixed_back[:, 128 * head : 128 * head + 128]
            weights = masked_weights(
                column_ref[:, :1], line_ref[:1], query_nope, key_nope, rope, rope_ref[...]
            )
            weight_back = dot_last(mixed_head, values)
            center = jnp.sum(weight_back * weights, axis=1, keepdims=True)
            raw_back = (weights * (weight_back - center) * SCORE_SCALE).astype(jnp.bfloat16)
            query_back.append(dot_plain(raw_back, key_nope))
            rope_back = rope_back + dot_plain(raw_back, rope_ref[...])
            keys_back.append(dot_first(raw_back, query_nope))
            keys_back.append(dot_first(weights.astype(jnp.bfloat16), mixed_head))
            mine = lanes // 64 == head
            key_rope_back = key_rope_back + jnp.where(mine, dot_first(raw_back, rope), 0.0)
        rope_back = rope_back * cosine_ref[...] - swap_halves(rope_back) * sine_ref[...]
        query_back = jnp.concatenate(query_back + [rope_back], axis=1).astype(jnp.bfloat16)
        keys_back = jnp.concatenate(keys_back, axis=1).astype(jnp.bfloat16)
        query_back_ref[...] = query_back
        keys_back_ref[...] = keys_back
        latent_part = dot_last(keys_back, expand_ref[...].reshape(rank, 512))
        input_part = dot_last(query_back, query_weight_ref[...])

        @pl.when(step == 0)
        def _():
            rope_back_ref[...] = key_rope_back
            latent_back_ref[...] = latent_part
            total[...] = input_part

        @pl.when(step > 0)
        def _():
            rope_back_ref[...] += key_rope_back
            latent_back_ref[...] += latent_part
            total[...] += input_part

        @pl.when(step == pairs - 1)
        def _():
            input_ref[...] = total[...].astype(jnp.bfloat16)

    whole = lambda shape: pl.BlockSpec(shape, lambda h: (0,) * len(shape))
    return pl.pallas_call(
        body,
        grid=(pairs,),
        in_specs=[
            whole((count, width)),
            pl.BlockSpec((count, 384), lambda h: (0, h)),
            pl.BlockSpec((count, 512), lambda h: (0, h)),
            whole((count, 128)),
            whole((count, 128)),
            whole((count, 128)),
            whole((count, 128)),
            whole((count, 128)),
            whole((8, count)),
            pl.BlockSpec((width, 384), lambda h: (0, h)),
            pl.BlockSpec((rows, 1, share, 512), lambda h: (0, h, 0, QUERY_COLUMNS // 512)),
            pl.BlockSpec((width, 256), lambda h: (0, (QUERY_COLUMNS + 512) // 256 + h)),
        ],
        out_specs=[
            pl.BlockSpec((count, 384), lambda h: (0, h)),
            pl.BlockSpec((count, 512), lambda h: (0, h)),
            whole((count, 128)),
            whole((count, rank)),
            whole((count, width)),
        ],
        out_shape=[
            jax.ShapeDtypeStruct((count, 384 * pairs), jnp.bfloat16),
            jax.ShapeDtypeStruct((count, 512 * pairs), jnp.bfloat16),
            jax.ShapeDtypeStruct((count, 128), jnp.float32),
            jax.ShapeDtypeStruct((count, rank), jnp.float32),
            jax.ShapeDtypeStruct((count, width), jnp.bfloat16),
        ],
        scratch_shapes=[pltpu.VMEM((count, width), jnp.float32)],
        compiler_params=kernel_params(52),
        cost_estimate=short_cost(),
    )(upstream, query, keys, *ropes, *turns, *segments, flat, quarters, flat)


def on_device(
    inputs,
    segment_ids,
    routes,
    norm_gain,
    query_weight,
    latent_weight,
    latent_gain,
    expand_weight,
    output_weight,
    ffn_gain,
    router_weight,
    expert_gate,
    expert_up,
    expert_down,
    shared_gate,
    shared_up,
    shared_down,
    out_grad,
):
    bf16 = jnp.bfloat16
    f32 = jnp.float32
    rows_count = inputs.shape[0]
    row_devices = lax.axis_size("row")
    row_place = lax.axis_index("row")
    first = lax.axis_index("col") == 0
    expert_count = EXP_DEV * row_devices
    capacity = 4 * rows_count * TOPK // (3 * expert_count)
    segment_row = segment_ids[0]
    places = jnp.arange(rows_count, dtype=jnp.int32)

    steps = jnp.arange(row_devices, dtype=jnp.int32)
    arrival = (((row_place // 4 - steps // 4) % 4) * 4 + ((row_place % 4) ^ (steps % 4))).astype(
        jnp.int32
    )
    block = latent_weight.shape[0]
    share = expand_weight.shape[0]
    quarter = expand_weight.shape[1] * share // block
    query_width = query_weight.shape[1]
    latent_width = latent_weight.shape[1]

    slab = pack_weights(
        query_weight,
        expand_weight,
        output_weight,
        latent_weight,
        router_weight,
        routes.astype(bf16).reshape(block, -1),
    )
    shared_share = shared_gate.shape[1] // row_devices
    blocks = {}
    blocks[0] = slab
    blocks[4], blocks[2], inputs_other, gains_other = together(
        turn_planes(slab),
        swap_rows(slab, 2),
        swap_cols(inputs),
        swap_cols(jnp.stack([norm_gain, ffn_gain])),
    )
    shared_packed = jnp.stack(
        [after(shared_gate, inputs_other).T, after(shared_up, inputs_other).T, shared_down], axis=0
    )
    shared_packed = shared_packed.reshape(3, row_devices, shared_share, -1).transpose(1, 0, 2, 3)
    (
        blocks[8],
        blocks[6],
        blocks[1],
        blocks[3],
        out_grad_other,
    ) = together(
        turn_planes(blocks[4]),
        swap_rows(blocks[4], 2),
        swap_rows(blocks[0], 1),
        swap_rows(blocks[2], 1),
        swap_cols(after(out_grad, inputs_other)),
    )
    upstream_bf16 = jnp.where(
        first,
        jnp.concatenate([out_grad, out_grad_other], axis=1),
        jnp.concatenate([out_grad_other, out_grad], axis=1),
    )
    grad_rows = Spread(sent_rows(upstream_bf16, first))
    blocks[12], blocks[10], blocks[5], blocks[7], got, shared_packed = together(
        turn_planes(blocks[8]),
        swap_rows(blocks[8], 2),
        swap_rows(blocks[4], 1),
        swap_rows(blocks[6], 1),
        swap_cols(grad_rows.sent((0, 0))[0]),
        shared_packed,
    )
    grad_rows.got(got, [0], (0, 0))
    source = jnp.where(
        first,
        jnp.concatenate([inputs, inputs_other], axis=1),
        jnp.concatenate([inputs_other, inputs], axis=1),
    ).astype(f32)
    gains = jnp.stack([norm_gain, ffn_gain])
    gains = jnp.where(
        first,
        jnp.concatenate([gains, gains_other], axis=1),
        jnp.concatenate([gains_other, gains], axis=1),
    )
    gain_one = gains[:1]
    gain_two = gains[1:]
    scale_one = lax.rsqrt(jnp.mean(source * source, axis=1, keepdims=True) + epsilon)
    unit_one = source * scale_one
    normed_one = (unit_one * gain_one).astype(bf16)
    cosine, sine = rotation(rows_count, ROPE)
    turns = (
        jnp.concatenate([cosine] * 4, axis=1),
        jnp.concatenate([-sine, sine, -sine, sine], axis=1),
    )
    segments = (
        jnp.broadcast_to(segment_row[:, None], (rows_count, 128)),
        jnp.broadcast_to(segment_row[None], (8, rows_count)),
    )
    passed, starts = batch(grad_rows.passed((0, 0, 0), (0, 0, 1)))
    (
        blocks[14],
        blocks[9],
        blocks[11],
        passed,
        shared_here,
        normed_one,
        cosine,
        sine,
        turns,
        segments,
    ) = together(
        swap_rows(blocks[12], 2),
        swap_rows(blocks[8], 1),
        swap_rows(blocks[10], 1),
        swap_rows(passed, 1),
        lax.all_to_all(shared_packed, "row", split_axis=0, concat_axis=0, tiled=True),
        normed_one,
        cosine,
        sine,
        turns,
        segments,
    )
    grad_rows.taken(passed, starts, (0, 0, 0), (0, 0, 1))
    grad_rows.held[0, 0] = after(grad_rows.held[0, 0], blocks[14])
    grad_turned = grad_rows.turn(1)
    blocks[13], blocks[15] = together(swap_rows(blocks[12], 1), swap_rows(blocks[14], 1))
    dense = assemble([blocks[i] for i in range(4 * PLANES)], arrival)
    flat_dense = dense.reshape(D, -1)
    latent_full = flat_dense[:, QUERY_COLUMNS + 1536 : QUERY_COLUMNS + 1536 + latent_width]
    router_full = flat_dense[
        :, QUERY_COLUMNS + 1536 + latent_width : QUERY_COLUMNS + 1536 + latent_width + expert_count
    ]
    latent = jnp.dot(normed_one, latent_full, preferred_element_type=f32).astype(bf16)
    compressed = latent[:, :RANK].astype(f32)
    latent_scale = lax.rsqrt(jnp.mean(compressed * compressed, axis=1, keepdims=True) + epsilon)
    latent_unit = compressed * latent_scale
    latent_normed = (latent_unit * latent_gain).astype(bf16)
    key_rope = rotate(latent[:, RANK:].astype(f32), cosine, sine).astype(bf16)
    ropes = head_ropes(key_rope)
    latent_normed, grad_rows.held[0, 1], grad_rows.held[1, 0] = together(
        latent_normed, grad_rows.cross(0), grad_turned
    )

    query, keys, mixed, attended_part = attend(
        normed_one, latent_normed, ropes, turns, segments, dense
    )
    sent, starts = batch(grad_rows.sent((0, 1), (1, 0)))
    passed, passed_starts = batch(grad_rows.passed((0, 1, 0), (1, 0, 0)))
    (
        query,
        attended_part,
        grad_rows.held[2, 0],
        grad_rows.held[1, 1],
        got,
        passed,
    ) = together(
        query,
        attended_part,
        grad_rows.turn(2),
        grad_rows.cross(1),
        swap_cols(sent),
        swap_rows(passed, 1),
    )
    grad_rows.got(got, starts, (0, 1), (1, 0))
    grad_rows.taken(passed, passed_starts, (0, 1, 0), (1, 0, 0))

    picked = {}

    def pick(plane, *others):
        picked[plane] = pick_grads(
            grad_rows.family(plane), after(plane_codes[plane], *others), shared_last, capacity
        )
        return picked[plane]

    def pass_alone(spread, key):
        spread.taken(swap_rows(spread.passed(key)[0], 1), [0], key)

    passed, starts = batch(grad_rows.passed((0, 1, 1), (1, 0, 1), (1, 1, 0)))
    partner_part = jnp.concatenate(
        [
            attended_part[:COMMON],
            jnp.where(first, attended_part[SENT:], attended_part[COMMON:SENT]),
        ],
        axis=0,
    )
    (
        attended_other,
        grad_rows.held[2, 1],
        passed,
    ) = together(
        swap_cols(partner_part),
        grad_rows.cross(2),
        swap_rows(passed, 1),
    )
    grad_rows.taken(passed, starts, (0, 1, 1), (1, 0, 1), (1, 1, 0))
    attended_sent = sent_rows(attended_part, first).astype(f32) + attended_other.astype(f32)
    middle_sent = sent_rows(source, first) + attended_sent
    scale_sent = lax.rsqrt(jnp.mean(middle_sent * middle_sent, axis=1, keepdims=True) + epsilon)
    normed_sent = (middle_sent * scale_sent * gain_two).astype(bf16)
    rows = Spread(normed_sent)

    routes_all = after(flat_dense, normed_sent)[
        :, QUERY_COLUMNS + 1536 + latent_width + expert_count :
    ][:, : rows_count * TOPK // block]
    routes_all = routes_all.reshape(row_devices, rows_count, TOPK).transpose(0, 2, 1)[arrival]
    routes_all = routes_all.astype(jnp.int32)

    routes_all = local_tokens(routes_all, 2, first)
    held_experts = row_place * EXP_DEV + jnp.arange(EXP_DEV, dtype=jnp.int32)
    hits = jnp.any(routes_all[:, :, None, :] == held_experts[None, None, :, None], axis=1)
    upper = (places[:, None] <= places[None, :]).astype(bf16)
    ranks = jnp.einsum("sjt,tu->sju", hits.astype(bf16), upper, preferred_element_type=f32)
    codes = jnp.where(hits, ranks.astype(jnp.int32) - 1, -1)
    codes = jnp.pad(codes, ((0, 0), (0, 8 - EXP_DEV), (0, 0)), constant_values=-1)
    plane_codes = [codes[p * FAMILIES : (p + 1) * FAMILIES] for p in range(PLANES)]

    shared_here = shared_here.transpose(1, 2, 0, 3).reshape(3, shared_share, D)
    shared_here = jnp.pad(shared_here, ((0, 0), (0, SHARED_PAD - shared_share), (0, 0)))
    shared_pair = shared_here[:2].reshape(2 * SHARED_PAD, D)
    shared_last = shared_here[2]

    sent, starts = batch(rows.sent((0, 0)) + grad_rows.sent((1, 1)))
    rows.held[1, 0], rows.held[0, 1], got, shared_pair, shared_last, plane_codes = together(
        rows.turn(1), rows.cross(0), swap_cols(sent), shared_pair, shared_last, plane_codes
    )
    rows.got(got, starts, (0, 0))
    grad_rows.got(got, starts[1:], (1, 1))
    router_turned = router_full.T
    router_held = lax.dynamic_slice_in_dim(
        jnp.concatenate([router_turned, router_turned], axis=0),
        row_place * EXP_DEV,
        expert_count,
        0,
    )
    pass_alone(grad_rows, (1, 1, 1))
    sent, starts = batch(rows.sent((0, 1), (1, 0)))
    passed, passed_starts = batch(rows.passed((0, 0, 0), (0, 0, 1), (0, 1, 0)))
    (
        rows.held[2, 0],
        rows.held[1, 1],
        got,
        passed,
        picked[0],
        picked[1],
        router_held,
    ) = together(
        rows.turn(2),
        rows.cross(1),
        swap_cols(sent),
        swap_rows(passed, 1),
        pick(0),
        pick(1),
        router_held,
    )
    rows.got(got, starts, (0, 1), (1, 0))
    rows.taken(passed, passed_starts, (0, 0, 0), (0, 0, 1), (0, 1, 0))

    experts = (expert_gate, expert_up, expert_down)
    begun = {}
    ran = {}

    def start_plane(plane, *others):
        begun[plane] = pick_rows(
            rows.family(plane),
            grad_rows.family(plane),
            after(plane_codes[plane], *others),
            router_held,
            shared_pair,
            picked[plane][1],
            capacity,
        )
        return begun[plane]

    def run_plane(plane):
        ran[plane] = run_experts(begun[plane][0], picked[plane][0], begun[plane][1], *experts)
        return ran[plane]

    def back_sibling(plane):
        return sum_tokens(
            ran[plane][1],
            plane_codes[plane],
            begun[plane][3],
            shared_pair,
            capacity,
            1,
            None,
            ran[plane][5],
        )

    def back_mine(plane, received):
        return sum_tokens(
            ran[plane][1],
            plane_codes[plane],
            begun[plane][3],
            shared_pair,
            capacity,
            0,
            received,
            ran[plane][5],
        )

    def sum_sibling(plane):
        return sum_tokens(
            ran[plane][0], plane_codes[plane], begun[plane][2], shared_last, capacity, 1
        )[0]

    def sum_mine(plane, received):
        return sum_tokens(
            ran[plane][0], plane_codes[plane], begun[plane][2], shared_last, capacity, 0, received
        )

    def unique_out(mine):
        return swap_cols(mine[1])

    def across_out(mine, unique):
        return swap_rows(add_unique(mine[0], unique, 1), 2)

    def own_sum(mine, unique, crossed):
        return add_unique(mine[0], unique, 0) + crossed

    pass_alone(rows, (0, 1, 1))
    sent, starts = batch(rows.sent((1, 1), (2, 0)))
    passed, passed_starts = batch(rows.passed((1, 0, 0), (1, 1, 0), (1, 0, 1)))
    rows.held[3, 0], rows.held[2, 1], got, passed = together(
        rows.turn(3), rows.cross(2), swap_cols(sent), swap_rows(passed, 1)
    )
    rows.got(got, starts, (1, 1), (2, 0))
    rows.taken(passed, passed_starts, (1, 0, 0), (1, 1, 0), (1, 0, 1))

    pass_alone(rows, (1, 1, 1))
    sent, starts = batch(rows.sent((2, 1), (3, 0)))
    passed, passed_starts = batch(rows.passed((2, 0, 0), (2, 1, 0), (2, 0, 1)))
    begun[1], rows.held[3, 1], grad_rows.held[3, 0], got, passed = together(
        start_plane(1), rows.cross(3), grad_rows.turn(3), swap_cols(sent), swap_rows(passed, 1)
    )
    rows.got(got, starts, (2, 1), (3, 0))
    rows.taken(passed, passed_starts, (2, 0, 0), (2, 1, 0), (2, 0, 1))

    ran[1] = run_plane(1)
    back_1 = back_sibling(1)
    sent, starts = batch(rows.sent((3, 1)) + grad_rows.sent((2, 0), (2, 1)))
    passed = [
        batch(rows.passed((2, 1, 1), (3, 0, 1))),
        batch(rows.passed((3, 0, 0), (3, 1, 0))),
        batch(grad_rows.passed((2, 0, 0), (2, 1, 0))),
    ]
    ran[1], back_1, grad_rows.held[3, 1], got, passed_got = together(
        ran[1],
        back_1,
        grad_rows.cross(3),
        swap_cols(sent),
        [swap_rows(rows_passed, 1) for rows_passed, _ in passed],
    )
    rows.got(got, starts, (3, 1))
    grad_rows.got(got, starts[1:], (2, 0), (2, 1))
    rows.taken(passed_got[0], passed[0][1], (2, 1, 1), (3, 0, 1))
    rows.taken(passed_got[1], passed[1][1], (3, 0, 0), (3, 1, 0))
    grad_rows.taken(passed_got[2], passed[2][1], (2, 0, 0), (2, 1, 0))

    passed, passed_starts = batch(grad_rows.passed((2, 0, 1), (2, 1, 1)))
    grad_rows.taken(swap_rows(passed, 1), passed_starts, (2, 0, 1), (2, 1, 1))
    sent, starts = batch(grad_rows.sent((3, 0), (3, 1)))
    passed, passed_starts = batch(
        rows.passed((3, 1, 1)) + grad_rows.passed((3, 0, 0), (3, 1, 0))
    )
    picked[2] = pick(2)
    begun[2] = start_plane(2)
    picked[2], begun[2], back_got, got, passed = together(
        picked[2], begun[2], swap_rows(back_1[0], 1), swap_cols(sent), swap_rows(passed, 1)
    )
    grad_rows.got(got, starts, (3, 0), (3, 1))
    rows.taken(passed, passed_starts, (3, 1, 1))
    grad_rows.taken(passed, passed_starts[1:], (3, 0, 0), (3, 1, 0))
    passed, passed_starts = batch(grad_rows.passed((3, 0, 1), (3, 1, 1)))
    grad_rows.taken(swap_rows(passed, 1), passed_starts, (3, 0, 1), (3, 1, 1))
    back_mine_1 = back_mine(1, back_got)
    sum_1 = sum_sibling(1)
    back_mine_1, sum_1 = together(back_mine_1, sum_1)

    ran[2] = run_plane(2)
    back_2 = back_sibling(2)
    ran[2], back_2, back_unique, sum_got = together(
        ran[2], back_2, unique_out(back_mine_1), swap_rows(sum_1, 1)
    )
    sum_mine_1 = sum_mine(1, sum_got)

    picked[3] = pick(3)
    begun[3] = start_plane(3)
    picked[3], begun[3], back_got, back_crossed, sum_unique = together(
        picked[3],
        begun[3],
        swap_rows(back_2[0], 1),
        across_out(back_mine_1, back_unique),
        unique_out(sum_mine_1),
    )
    back = own_sum(back_mine_1, back_unique, back_crossed)
    back_mine_2 = back_mine(2, back_got)
    sum_2 = sum_sibling(2)
    attended_rest = after(attended_sent[COMMON:], picked[3]).astype(bf16)
    back_mine_2, sum_2, back, attended_rest = together(
        back_mine_2, sum_2, back, swap_cols(attended_rest)
    )

    ran[3] = run_plane(3)
    back_3 = back_sibling(3)
    ran[3], back_3, back, back_unique, sum_got, sum_crossed = together(
        ran[3],
        back_3,
        turn_planes(back),
        unique_out(back_mine_2),
        swap_rows(sum_2, 1),
        across_out(sum_mine_1, sum_unique),
    )
    result = own_sum(sum_mine_1, sum_unique, sum_crossed)
    sum_mine_2 = sum_mine(2, sum_got)
    sum_mine_2, result = together(sum_mine_2, result)

    attended_rest = after(attended_rest, sum_mine_2).astype(f32)
    attended_mine = attended_sent[COMMON:]
    middle = source + jnp.concatenate(
        [
            attended_sent[:COMMON],
            jnp.where(first, attended_mine, attended_rest),
            jnp.where(first, attended_rest, attended_mine),
        ],
        axis=0,
    )
    scale_two = lax.rsqrt(jnp.mean(middle * middle, axis=1, keepdims=True) + epsilon)
    unit_two = middle * scale_two
    normed_two = (unit_two * gain_two).astype(bf16)
    logits = jnp.dot(normed_two, router_full, preferred_element_type=f32)
    log_total = jax.nn.logsumexp(logits, axis=1, keepdims=True)
    chances = jnp.exp(logits - log_total)

    begun[0] = start_plane(0, sum_mine_2)
    begun[0], back_got, back_crossed, sum_unique, result, normed_two, chances = together(
        begun[0],
        swap_rows(back_3[0], 1),
        across_out(back_mine_2, back_unique),
        unique_out(sum_mine_2),
        turn_planes(result),
        normed_two,
        chances,
    )
    back = back + own_sum(back_mine_2, back_unique, back_crossed)
    back_mine_3 = back_mine(3, back_got)
    sum_3 = sum_sibling(3)
    back_mine_3, sum_3, back = together(back_mine_3, sum_3, back)

    ran[0] = run_plane(0)
    back_0 = back_sibling(0)
    ran[0], back_0, back, back_unique, sum_got, sum_crossed = together(
        ran[0],
        back_0,
        turn_planes(back),
        unique_out(back_mine_3),
        swap_rows(sum_3, 1),
        across_out(sum_mine_2, sum_unique),
    )
    result = result + own_sum(sum_mine_2, sum_unique, sum_crossed)
    sum_mine_3 = sum_mine(3, sum_got)
    sum_mine_3, result = together(sum_mine_3, result)

    kept = [
        (begun[plane][0], picked[plane][0], ran[plane][3], ran[plane][4], ran[plane][2])
        for plane in range(PLANES)
    ]
    kept = [list(part) for part in zip(*kept)]
    half = EXP_DEV // 2
    expert_parts = expert_weight_grads(*kept, 0, half, [])
    expert_parts, back_got, back_crossed, sum_unique, result = together(
        expert_parts,
        swap_rows(back_0[0], 1),
        across_out(back_mine_3, back_unique),
        unique_out(sum_mine_3),
        turn_planes(result),
    )
    back = back + own_sum(back_mine_3, back_unique, back_crossed)
    back_mine_0 = back_mine(0, back_got)
    sum_0 = sum_sibling(0)
    back_mine_0, sum_0, back = together(back_mine_0, sum_0, back)

    expert_parts = expert_weight_grads(*kept, half, EXP_DEV - half, expert_parts)
    expert_parts, back, back_unique, sum_got, common_crossed = together(
        expert_parts,
        turn_planes(back),
        unique_out(back_mine_0),
        swap_rows(sum_0, 1),
        swap_rows(back_mine_0[0][1, :COMMON], 2),
    )
    expert_gate_grad, expert_up_grad, expert_down_grad = expert_parts
    common = back[:COMMON] + back_mine_0[0][0, :COMMON] + common_crossed
    unique_rest = back_mine_0[0][:, COMMON:] + back_unique
    sum_mine_0 = sum_mine(0, sum_got)

    gate_grad_dense = [
        jnp.stack([mine[2], sibling[1]], axis=1)[:, :, :EXP_DEV]
        for mine, sibling in (
            (back_mine_0, back_0),
            (back_mine_1, back_1),
            (back_mine_2, back_2),
            (back_mine_3, back_3),
        )
    ]
    gate_grad_dense = jnp.stack(gate_grad_dense).reshape(row_devices, EXP_DEV, rows_count)
    gate_grad_dense = local_tokens(gate_grad_dense, 2, first)[arrival]
    gate_grad_dense = lax.all_to_all(
        gate_grad_dense, "row", split_axis=0, concat_axis=0, tiled=True
    ).reshape(expert_count, rows_count)
    shared_grads = sum([begun[p][4] for p in range(1, PLANES)], begun[0][4])
    shared_grads = shared_grads.reshape(3, SHARED_PAD, D)[:, :shared_share]
    shared_grads = (
        shared_grads.astype(bf16)
        .reshape(3, shared_share, row_devices, -1)
        .transpose(2, 0, 1, 3)
    )
    gate_grad_dense = gate_grad_dense + swap_cols(gate_grad_dense)
    weighted_gates = gate_grad_dense.T * chances
    logit_grads = (
        weighted_gates - chances * jnp.sum(weighted_gates, axis=1, keepdims=True)
    ).astype(bf16)
    router_back = jnp.einsum("te,de->td", logit_grads, router_full, preferred_element_type=f32)
    unique_crossed, common_other, sum_mine_0, shared_grads, router_back, logit_grads = together(
        swap_rows(unique_rest[1], 2),
        swap_cols(common),
        sum_mine_0,
        shared_grads,
        router_back,
        logit_grads,
    )
    unique_mine = back[COMMON:] + unique_rest[0] + unique_crossed
    shared_grads = lax.all_to_all(shared_grads, "row", split_axis=0, concat_axis=0, tiled=True)
    unique_other = swap_cols(unique_mine)
    upstream = upstream_bf16.astype(f32)
    normed_two_back = router_back + jnp.concatenate(
        [
            common.astype(f32) + common_other.astype(f32),
            jnp.where(first, unique_mine, unique_other).astype(f32),
            jnp.where(first, unique_other, unique_mine).astype(f32),
        ],
        axis=0,
    )
    ffn_gain_part = jnp.sum(normed_two_back * unit_two, axis=0)
    weighted = normed_two_back * gain_two
    average = jnp.mean(weighted * unit_two, axis=1, keepdims=True)
    middle_back = upstream + scale_two * (weighted - unit_two * average)
    attended_back = middle_back.astype(bf16)

    def by_plane(total):
        return total.reshape((PLANES, 2) + total.shape[1:])

    output_sibling = block_grads(arrival, attended_back, mixed, 256, 1)
    query_back, expanded_back, key_rope_back, latent_normed_back, input_part = attend_back(
        attended_back, query, keys, ropes, turns, segments, dense, RANK
    )
    query_back, shared_grads, last_unique, output_got, sum_crossed = together(
        query_back,
        shared_grads,
        unique_out(sum_mine_0),
        swap_rows(output_sibling, 1),
        across_out(after(sum_mine_3, unique_other), sum_unique),
    )
    result = result + own_sum(sum_mine_3, sum_unique, sum_crossed)
    latent_gain_part = jnp.sum(latent_normed_back * latent_unit, axis=0)
    latent_weighted = latent_normed_back * latent_gain
    compressed_back = latent_scale * (
        latent_weighted
        - latent_unit * jnp.mean(latent_weighted * latent_unit, axis=1, keepdims=True)
    )
    key_rope_back = key_rope_back[:, :ROPE] + key_rope_back[:, ROPE:]
    rope_back = unrotate(key_rope_back, cosine, sine)
    latent_part = jnp.concatenate([compressed_back, rope_back], axis=1).astype(bf16)
    latent_turned = latent_normed.T
    wide_sibling = block_grads(
        arrival, normed_one, after(query_back, latent_part), 384, 1, latent_turned, expanded_back
    )
    latent_other, wide_sibling = together(swap_cols(latent_part), wide_sibling)
    latent_back = (latent_part.astype(f32) + latent_other.astype(f32)).astype(bf16)
    narrow_sibling = narrow_grads(arrival, normed_one, latent_back, normed_two, logit_grads, 1)
    weighted_part = jnp.sum(
        after(input_part, wide_sibling).astype(f32) * gain_one * unit_one, axis=1
    )
    wide_got, narrow_sibling, weighted_part = together(
        swap_rows(wide_sibling, 1), narrow_sibling, weighted_part
    )
    output_total = by_plane(
        block_grads(
            arrival, after(attended_back, narrow_sibling), mixed, 256, 0, received=output_got
        )
    )
    input_sent = other_columns(input_part, first)
    small_part = jnp.concatenate([weighted_part, latent_gain_part]).reshape(-1, 128)
    narrow_got = swap_rows(narrow_sibling, 1)
    small_other, narrow_got, output_total, sum_crossed, result = together(
        swap_cols(small_part),
        narrow_got,
        output_total,
        across_out(sum_mine_0, last_unique),
        turn_planes(result),
    )
    sum_sent = result + own_sum(sum_mine_0, last_unique, sum_crossed)
    joined_total = by_plane(
        joined_grads(
            arrival,
            normed_one,
            query_back,
            latent_turned,
            expanded_back,
            latent_back,
            normed_two,
            logit_grads,
            wide_got,
            narrow_got,
        )
    )
    joined_total, crossed_output, input_other = together(
        joined_total,
        swap_rows(output_total[1:, 1], 2),
        swap_cols(after(input_sent, small_other)),
    )
    output_sums = [output_total[p, 0] + crossed_output[p - 1] for p in (1, 2, 3)]

    crossed, crossed_output, moved_output, combined_other = together(
        swap_rows(joined_total[1, 1], 2),
        swap_rows(output_total[0, 1], 2),
        turn_planes(output_sums[0]),
        swap_cols(other_columns(sum_sent, first)),
    )
    moving = joined_total[1, 0] + crossed
    moving_output = output_sums[1] + moved_output
    last_output = output_total[0, 0] + crossed_output

    shared_grads = after(shared_grads, joined_total).transpose(1, 0, 2, 3).reshape(3, row_devices * shared_share, -1)
    shared_grads = shared_grads.astype(f32)
    shared_gate_grad = shared_grads[0].T
    shared_up_grad = shared_grads[1].T
    shared_down_grad = shared_grads[2]

    latent_input = jnp.einsum("tc,dc->td", latent_back, latent_full, preferred_element_type=f32)
    small_sum = (small_part + small_other).reshape(-1)
    weighted_sum = small_sum[:rows_count]
    weighted_sum = weighted_sum + jnp.sum(latent_input * gain_one * unit_one, axis=1)
    normed_one_back = (
        own_columns(input_part, first).astype(f32)
        + input_other.astype(f32)
        + own_columns(latent_input, first)
    )
    own_unit = own_columns(unit_one, first)
    norm_gain_part = jnp.sum(normed_one_back * own_unit, axis=0)
    input_grad = own_columns(middle_back, first) + scale_one * (
        normed_one_back * norm_gain - own_unit * (weighted_sum / D)[:, None]
    )
    gain_grads = jnp.concatenate(
        [norm_gain_part, own_columns(ffn_gain_part, first), small_sum[rows_count:]]
    ).reshape(-1, 128)
    crossed, moved, moved_output, gains_other = together(
        swap_rows(joined_total[2, 1], 2),
        turn_planes(moving),
        turn_planes(moving_output),
        swap_rows(gain_grads, 1),
    )
    moving = joined_total[2, 0] + crossed + moved
    moving_output = output_sums[2] + moved_output
    gain_grads = gain_grads + gains_other
    crossed, moved, moved_output, gains_other = together(
        swap_rows(joined_total[3, 1], 2),
        turn_planes(moving),
        turn_planes(moving_output),
        swap_rows(gain_grads, 2),
    )
    moving = joined_total[3, 0] + crossed + moved
    moving_output = last_output + moved_output
    gain_grads = gain_grads + gains_other
    crossed, moved, others = together(
        swap_rows(joined_total[0, 1], 2),
        turn_planes(moving),
        [swap_rows(gain_grads, bits) for bits in (4, 8, 12)],
    )
    moving = joined_total[0, 0] + crossed + moved
    gain_grads = ((gain_grads + others[0]) + (others[1] + others[2])).reshape(-1)
    output_grad, query_grad, expand_grad, latent_grad, router_grad = unpack_grads(
        moving_output, moving, (query_width, quarter, latent_width)
    )

    combined = merge_rows(own_columns(sum_sent, first), combined_other, first)
    output = (own_columns(middle, first) + combined).astype(bf16)
    width_share = norm_gain.shape[0]
    norm_gain_grad = gain_grads[:width_share]
    ffn_gain_grad = gain_grads[width_share : 2 * width_share]
    latent_gain_grad = gain_grads[2 * width_share :]
    return (
        output,
        input_grad,
        norm_gain_grad,
        query_grad,
        latent_grad,
        latent_gain_grad,
        expand_grad,
        output_grad,
        ffn_gain_grad,
        router_grad,
        expert_gate_grad,
        expert_up_grad,
        expert_down_grad,
        shared_gate_grad,
        shared_up_grad,
        shared_down_grad,
    )


def on_device_general(
    inputs,
    segment_ids,
    routes,
    norm_gain,
    query_weight,
    latent_weight,
    latent_gain,
    expand_weight,
    output_weight,
    ffn_gain,
    router_weight,
    expert_gate,
    expert_up,
    expert_down,
    shared_gate,
    shared_up,
    shared_down,
    out_grad,
):
    bf16 = jnp.bfloat16
    f32 = jnp.float32
    rows_count = inputs.shape[0]
    width_share = inputs.shape[1]
    row_devices = lax.axis_size("row")
    col_devices = lax.axis_size("col")
    col_place = lax.axis_index("col")
    local_heads = query_weight.shape[1] // (NOPE + ROPE)
    expert_count = EXP_DEV * row_devices
    capacity = 4 * rows_count * TOPK // (3 * expert_count)
    score_scale = (NOPE + ROPE) ** (-0.5)
    block_rows = min(512, rows_count)
    segment_row = segment_ids[0]
    places = jnp.arange(rows_count, dtype=jnp.int32)
    (
        query_full,
        latent_full,
        expand_full,
        output_full,
        router_full,
        shared_gate_full,
        shared_up_full,
        shared_down_full,
    ) = (
        lax.all_gather(query_weight, "row", axis=0, tiled=True),
        lax.all_gather(latent_weight, "row", axis=0, tiled=True),
        lax.all_gather(expand_weight, "row", axis=0, tiled=True),
        lax.all_gather(output_weight, "row", axis=1, tiled=True),
        lax.all_gather(router_weight, "row", axis=0, tiled=True),
        lax.all_gather(shared_gate, "row", axis=0, tiled=True),
        lax.all_gather(shared_up, "row", axis=0, tiled=True),
        lax.all_gather(shared_down, "row", axis=1, tiled=True),
    )
    source = inputs.astype(f32)
    scale_one = rms_scale(source)
    unit_one = source * scale_one
    normed_one = spread((unit_one * norm_gain).astype(bf16))
    query = jnp.dot(normed_one, query_full, preferred_element_type=f32).reshape(
        rows_count, local_heads, NOPE + ROPE
    )
    latent = jnp.dot(normed_one, latent_full, preferred_element_type=f32).astype(bf16)
    cosine, sine = rotation(rows_count, ROPE)
    head_cos = cosine[:, None, :]
    head_sin = sine[:, None, :]
    compressed = latent[:, :RANK].astype(f32)
    latent_scale = lax.rsqrt(jnp.mean(compressed * compressed, axis=1, keepdims=True) + epsilon)
    latent_unit = compressed * latent_scale
    latent_normed = (latent_unit * latent_gain).astype(bf16)
    key_rope = rotate(latent[:, RANK:].astype(f32), cosine, sine).astype(bf16)
    expanded = jnp.dot(latent_normed, expand_full, preferred_element_type=f32).reshape(
        rows_count, local_heads, NOPE + VDIM
    )
    key_nope = expanded[..., :NOPE].astype(bf16)
    values_all = expanded[..., NOPE:].astype(bf16)
    query_nope = query[..., :NOPE].astype(bf16)
    query_rope = rotate(query[..., NOPE:], head_cos, head_sin).astype(bf16)

    def block_scores(start):
        ending = start + block_rows
        raw = jnp.einsum("qhd,khd->hqk", query_nope, key_nope, preferred_element_type=f32)
        raw = raw + jnp.einsum("qhd,kd->hqk", query_rope, key_rope, preferred_element_type=f32)
        allowed = (segment_row[start:ending, None] == segment_row[None, :]) & (
            places[None, :] <= places[:, None]
        )
        return jnp.where(allowed[None], raw * score_scale, -1e30)

    start = 0
    scores = block_scores(start)
    top = jnp.max(scores, axis=2, keepdims=True)
    exponent = jnp.exp(scores - top)
    total = jnp.sum(exponent, axis=2, keepdims=True)
    weights = exponent / total
    log_blocks = top + jnp.log(total)
    mixed_blocks = jnp.einsum(
        "hqk,khd->qhd", weights.astype(bf16), values_all, preferred_element_type=f32
    ).astype(bf16)
    mixed = mixed_blocks.reshape(rows_count, local_heads * VDIM)
    attended = mix_sums(jnp.dot(mixed, output_full, preferred_element_type=f32))
    middle = source + attended
    scale_two = rms_scale(middle)
    unit_two = middle * scale_two
    normed_two_share = (unit_two * ffn_gain).astype(bf16)
    normed_two = spread(normed_two_share)
    logits = jnp.dot(normed_two, router_full, preferred_element_type=f32)
    log_total = jax.nn.logsumexp(logits, axis=1, keepdims=True)
    chosen = routes[:, :, None] == jnp.arange(expert_count, dtype=jnp.int32)[None, None, :]
    picked = jnp.sum(jnp.where(chosen, logits[:, None, :], 0.0), axis=2)
    gates = jnp.exp(picked - log_total)
    upstream = out_grad.astype(f32)
    upstream_full = spread(out_grad)
    shared_gate_pre = jnp.dot(normed_two, shared_gate_full, preferred_element_type=f32)
    shared_up_pre = jnp.dot(normed_two, shared_up_full, preferred_element_type=f32)
    shared_hidden = (jax.nn.silu(shared_gate_pre) * shared_up_pre).astype(bf16)
    shared_part = jnp.dot(shared_hidden, shared_down_full, preferred_element_type=f32)
    flat_routes = routes.reshape(-1)
    hits = (flat_routes[:, None] == jnp.arange(expert_count, dtype=jnp.int32)[None, :]).astype(
        jnp.int32
    )
    ranks = jnp.sum((jnp.cumsum(hits, axis=0) - 1) * hits, axis=1)
    owners = jnp.arange(rows_count * TOPK, dtype=jnp.int32) // TOPK
    share_slots = capacity // col_devices
    slot_count = row_devices * share_slots
    buffer_size = EXP_DEV * slot_count
    inside = ranks // share_slots == col_place
    slot_place = jnp.where(
        inside,
        flat_routes % EXP_DEV * slot_count
        + flat_routes // EXP_DEV * share_slots
        + ranks
        - col_place * share_slots,
        buffer_size,
    )
    token_of_slot = (
        jnp.full((buffer_size + 1,), rows_count, jnp.int32).at[slot_place].set(owners)[:buffer_size]
    )
    gate_of_slot = (
        jnp.zeros((buffer_size + 1,), f32).at[slot_place].set(gates.reshape(-1))[:buffer_size]
    )
    position = slot_place.reshape(rows_count, TOPK)
    gate_stack, up_stack, down_stack = (
        lax.all_gather(expert_gate, "col", axis=1, tiled=True),
        lax.all_gather(expert_up, "col", axis=1, tiled=True),
        lax.all_gather(expert_down, "col", axis=1, tiled=True),
    )
    padded_rows = jnp.concatenate([normed_two, jnp.zeros((1, D), bf16)], axis=0)
    outgoing = padded_rows[token_of_slot].reshape(EXP_DEV, slot_count, D)
    arrived = send_rows(outgoing)
    gate_pre = jnp.einsum("jnd,jfd->jnf", arrived, gate_stack, preferred_element_type=f32)
    up_pre = jnp.einsum("jnd,jfd->jnf", arrived, up_stack, preferred_element_type=f32)
    hidden = (jax.nn.silu(gate_pre) * up_pre).astype(bf16)
    expert_result = jnp.einsum(
        "jnf,jfd->jnd", hidden, down_stack, preferred_element_type=f32
    ).astype(bf16)
    returned = return_rows(expert_result).reshape(buffer_size, D)
    returned = jnp.concatenate([returned, jnp.zeros((1, D), bf16)], axis=0)
    slot_values = returned[position].astype(f32)
    combined = mix_sums(jnp.sum(gates[:, :, None] * slot_values, axis=1) + shared_part)
    upstream_wide = upstream_full.astype(f32)
    gate_partial = jnp.sum(upstream_wide[:, None, :] * slot_values, axis=2)
    output = (middle + combined).astype(bf16)
    gate_grads = lax.psum(gate_partial, "col")
    chances = jnp.exp(logits - log_total)
    weighted_gates = gate_grads * gates
    logit_grads = (
        jnp.sum(jnp.where(chosen, weighted_gates[:, :, None], 0.0), axis=1)
        - chances * jnp.sum(weighted_gates, axis=1, keepdims=True)
    ).astype(bf16)
    router_rows = lax.dynamic_slice_in_dim(router_full, col_place * width_share, width_share, 0)
    router_back = jnp.einsum("te,de->td", logit_grads, router_rows, preferred_element_type=f32)
    router_grad_part = jnp.einsum("td,te->de", normed_two, logit_grads, preferred_element_type=f32)
    shared_hidden_back = jnp.einsum(
        "td,fd->tf", upstream_full, shared_down_full, preferred_element_type=f32
    )
    shared_sigmoid = jax.nn.sigmoid(shared_gate_pre)
    shared_gate_back = (
        shared_hidden_back * shared_up_pre * silu_slope(shared_gate_pre, shared_sigmoid)
    ).astype(bf16)
    shared_up_back = (shared_hidden_back * (shared_gate_pre * shared_sigmoid)).astype(bf16)
    shared_input_back = jnp.einsum(
        "tf,df->td", shared_gate_back, shared_gate_full, preferred_element_type=f32
    ) + jnp.einsum("tf,df->td", shared_up_back, shared_up_full, preferred_element_type=f32)
    shared_gate_part = jnp.einsum(
        "td,tf->df", normed_two, shared_gate_back, preferred_element_type=f32
    )
    shared_up_part = jnp.einsum("td,tf->df", normed_two, shared_up_back, preferred_element_type=f32)
    shared_down_part = jnp.einsum(
        "tf,td->fd", shared_hidden, upstream_full, preferred_element_type=f32
    )
    padded_upstream = jnp.concatenate([upstream_wide, jnp.zeros((1, D), f32)], axis=0)
    slot_grads = (
        (gate_of_slot[:, None] * padded_upstream[token_of_slot])
        .astype(bf16)
        .reshape(EXP_DEV, slot_count, D)
    )
    arrived_grads = send_rows(slot_grads)
    hidden_back = jnp.einsum("jnd,jfd->jnf", arrived_grads, down_stack, preferred_element_type=f32)
    gate_sigmoid = jax.nn.sigmoid(gate_pre)
    gate_back = (hidden_back * up_pre * silu_slope(gate_pre, gate_sigmoid)).astype(bf16)
    up_back = (hidden_back * (gate_pre * gate_sigmoid)).astype(bf16)
    row_back = jnp.einsum(
        "jnf,jfd->jnd", gate_back, gate_stack, preferred_element_type=f32
    ) + jnp.einsum("jnf,jfd->jnd", up_back, up_stack, preferred_element_type=f32)
    returned_grads = return_rows(row_back.astype(bf16)).reshape(buffer_size, D)
    returned_grads = jnp.concatenate([returned_grads, jnp.zeros((1, D), bf16)], axis=0)
    routed_back = jnp.sum(returned_grads[position].astype(f32), axis=1)
    normed_two_back = mix_sums(routed_back + shared_input_back) + router_back
    gate_pieces = []
    up_pieces = []
    down_pieces = []
    for expert in range(EXP_DEV):
        gate_piece, up_piece, down_piece = (
            lax.psum_scatter(
                jnp.einsum(
                    "nf,nd->fd", gate_back[expert], arrived[expert], preferred_element_type=f32
                ).astype(jnp.bfloat16),
                "col",
                scatter_dimension=0,
                tiled=True,
            ).astype(jnp.float32),
            lax.psum_scatter(
                jnp.einsum(
                    "nf,nd->fd", up_back[expert], arrived[expert], preferred_element_type=f32
                ).astype(jnp.bfloat16),
                "col",
                scatter_dimension=0,
                tiled=True,
            ).astype(jnp.float32),
            lax.psum_scatter(
                jnp.einsum(
                    "nf,nd->fd", hidden[expert], arrived_grads[expert], preferred_element_type=f32
                ).astype(jnp.bfloat16),
                "col",
                scatter_dimension=0,
                tiled=True,
            ).astype(jnp.float32),
        )
        gate_pieces.append(gate_piece)
        up_pieces.append(up_piece)
        down_pieces.append(down_piece)
    expert_gate_grad = jnp.stack(gate_pieces, axis=0)
    expert_up_grad = jnp.stack(up_pieces, axis=0)
    expert_down_grad = jnp.stack(down_pieces, axis=0)
    ffn_gain_part = jnp.sum(normed_two_back * unit_two, axis=0)
    middle_back = upstream + norm_backward(normed_two_back, unit_two, scale_two, ffn_gain)
    attended_back = spread(middle_back.astype(bf16))
    mixed_back = (
        jnp.einsum("td,vd->tv", attended_back, output_full, preferred_element_type=f32)
        .astype(bf16)
        .reshape(rows_count, local_heads, VDIM)
    )
    output_grad_part = jnp.einsum("tv,td->vd", mixed, attended_back, preferred_element_type=f32)
    start = 0
    ending = start + block_rows
    scores = block_scores(start)
    weights = jnp.exp(scores - log_blocks)
    weight_back = jnp.einsum("qhd,khd->hqk", mixed_back, values_all, preferred_element_type=f32)
    center = jnp.sum(weight_back * weights, axis=2, keepdims=True)
    raw_back = (weights * (weight_back - center) * score_scale).astype(bf16)
    query_nope_back = jnp.einsum("hqk,khd->qhd", raw_back, key_nope, preferred_element_type=f32)
    query_rope_back = jnp.einsum("hqk,kd->qhd", raw_back, key_rope, preferred_element_type=f32)
    key_nope_back = jnp.einsum("hqk,qhd->khd", raw_back, query_nope, preferred_element_type=f32)
    key_rope_back = jnp.einsum("hqk,qhd->kd", raw_back, query_rope, preferred_element_type=f32)
    values_back = jnp.einsum(
        "hqk,qhd->khd", weights.astype(bf16), mixed_back, preferred_element_type=f32
    )
    query_back = jnp.concatenate(
        [query_nope_back, unrotate(query_rope_back, head_cos, head_sin)], axis=2
    )
    query_back = query_back.astype(bf16).reshape(rows_count, local_heads * (NOPE + ROPE))
    expanded_back = (
        jnp.concatenate([key_nope_back, values_back], axis=2)
        .astype(bf16)
        .reshape(rows_count, local_heads * (NOPE + VDIM))
    )
    latent_normed_back = jnp.einsum(
        "tc,rc->tr", expanded_back, expand_full, preferred_element_type=f32
    )
    expand_grad_part = jnp.einsum(
        "tr,tc->rc", latent_normed, expanded_back, preferred_element_type=f32
    )
    latent_gain_part = jnp.sum(latent_normed_back * latent_unit, axis=0)
    latent_weighted = latent_normed_back * latent_gain
    compressed_back = latent_scale * (
        latent_weighted
        - latent_unit * jnp.mean(latent_weighted * latent_unit, axis=1, keepdims=True)
    )
    rope_back = unrotate(key_rope_back, cosine, sine)
    latent_back, latent_gain_col = (
        lax.psum(
            jnp.concatenate([compressed_back, rope_back], axis=1).astype(jnp.bfloat16), "col"
        ).astype(jnp.float32),
        lax.psum(latent_gain_part.astype(jnp.bfloat16), "col").astype(jnp.float32),
    )
    latent_back = latent_back.astype(bf16)
    latent_grad_part = jnp.einsum("td,tc->dc", normed_one, latent_back, preferred_element_type=f32)
    query_grad_part = jnp.einsum("td,tc->dc", normed_one, query_back, preferred_element_type=f32)
    latent_rows = lax.dynamic_slice_in_dim(latent_full, col_place * width_share, width_share, 0)
    input_part = jnp.einsum("tc,dc->td", query_back, query_full, preferred_element_type=f32)
    normed_one_back = mix_sums(input_part) + jnp.einsum(
        "tc,dc->td", latent_back, latent_rows, preferred_element_type=f32
    )
    norm_gain_part = jnp.sum(normed_one_back * unit_one, axis=0)
    input_grad = middle_back + norm_backward(normed_one_back, unit_one, scale_one, norm_gain)
    norm_gain_grad, ffn_gain_grad, latent_gain_grad = lax.psum(
        (norm_gain_part, ffn_gain_part, latent_gain_col), "row"
    )
    (
        query_grad,
        latent_grad,
        expand_grad,
        output_grad,
        router_grad,
        shared_gate_grad,
        shared_up_grad,
        shared_down_grad,
    ) = (
        lax.psum_scatter(
            query_grad_part.astype(jnp.bfloat16), "row", scatter_dimension=0, tiled=True
        ).astype(jnp.float32),
        lax.psum_scatter(
            latent_grad_part.astype(jnp.bfloat16), "row", scatter_dimension=0, tiled=True
        ).astype(jnp.float32),
        lax.psum_scatter(
            expand_grad_part.astype(jnp.bfloat16), "row", scatter_dimension=0, tiled=True
        ).astype(jnp.float32),
        lax.psum_scatter(
            output_grad_part.astype(jnp.bfloat16), "row", scatter_dimension=1, tiled=True
        ).astype(jnp.float32),
        lax.psum_scatter(
            router_grad_part.astype(jnp.bfloat16), "row", scatter_dimension=0, tiled=True
        ).astype(jnp.float32),
        lax.psum_scatter(
            shared_gate_part.astype(jnp.bfloat16), "row", scatter_dimension=0, tiled=True
        ).astype(jnp.float32),
        lax.psum_scatter(
            shared_up_part.astype(jnp.bfloat16), "row", scatter_dimension=0, tiled=True
        ).astype(jnp.float32),
        lax.psum_scatter(
            shared_down_part.astype(jnp.bfloat16), "row", scatter_dimension=1, tiled=True
        ).astype(jnp.float32),
    )
    return (
        output,
        input_grad,
        norm_gain_grad,
        query_grad,
        latent_grad,
        latent_gain_grad,
        expand_grad,
        output_grad,
        ffn_gain_grad,
        router_grad,
        expert_gate_grad,
        expert_up_grad,
        expert_down_grad,
        shared_gate_grad,
        shared_up_grad,
        shared_down_grad,
    )


def solution(mesh):
    in_specs = (
        P("row", "col"),
        P("row", None),
        P("row", None),
        P("col"),
        P("row", "col"),
        P("row", None),
        P(),
        P("row", "col"),
        P("col", "row"),
        P("col"),
        P("row", None),
        P("row", "col", None),
        P("row", "col", None),
        P("row", "col", None),
        P("row", "col"),
        P("row", "col"),
        P("col", "row"),
        P("row", "col"),
    )
    out_specs = (
        P("row", "col"),
        P("row", "col"),
        P("col"),
        P("row", "col"),
        P("row", None),
        P(),
        P("row", "col"),
        P("col", "row"),
        P("col"),
        P("row", None),
        P("row", "col", None),
        P("row", "col", None),
        P("row", "col", None),
        P("row", "col"),
        P("row", "col"),
        P("col", "row"),
    )
    plan = on_device if dict(mesh.shape) == {"row": 16, "col": 2} else on_device_general
    return jax.shard_map(
        plan, mesh=mesh, in_specs=in_specs, out_specs=out_specs, check_vma=False
    )
```
